32 devices in a mesh: section: 2 (over core), seq: 4 (over z), fsdp: 4 (over y, x).
Axes of the slice: x: 2, y: 2, z: 4, core: 2. Of those that a mesh axis runs over, the one named last changes fastest.
Arguments:
- hidden_in: bfloat16 [2, 1024, 640], P(None, ('seq', 'fsdp')), may hold values from -6 to 6
- cotangent: bfloat16 [2, 1024, 640], P(None, ('seq', 'fsdp')), may hold values from -6 to 6
- positions: int32 [2, 1024], P(None, ('seq', 'fsdp')), may hold values from 0 to 1023, as said below
- attn_gain: bfloat16 [2, 640], P('section', 'fsdp'), may hold values from 0.25 to 1.75
- w_query: bfloat16 [2, 640, 1024], P('section', 'fsdp'), may hold values from -0.25 to 0.25
- w_key: bfloat16 [2, 640, 256], P('section', 'fsdp'), may hold values from -0.25 to 0.25
- w_value: bfloat16 [2, 640, 256], P('section', 'fsdp'), may hold values from -0.25 to 0.25
- query_gain: bfloat16 [2, 256], P('section', 'fsdp'), may hold values from 0.25 to 1.75
- key_gain: bfloat16 [2, 256], P('section', 'fsdp'), may hold values from 0.25 to 1.75
- w_output: bfloat16 [2, 1024, 640], P('section', 'fsdp'), may hold values from -0.1875 to 0.1875
- post_attn_gain: bfloat16 [2, 640], P('section', 'fsdp'), may hold values from 0.25 to 1.75
- ffn_gain: bfloat16 [2, 640], P('section', 'fsdp'), may hold values from 0.25 to 1.75
- w_gate: bfloat16 [2, 640, 2048], P('section', 'fsdp'), may hold values from -0.25 to 0.25
- w_up: bfloat16 [2, 640, 2048], P('section', 'fsdp'), may hold values from -0.25 to 0.25
- w_down: bfloat16 [2, 2048, 640], P('section', 'fsdp'), may hold values from -0.125 to 0.125
- post_ffn_gain: bfloat16 [2, 640], P('section', 'fsdp'), may hold values from 0.25 to 1.75
Outputs:
- section_outputs: bfloat16 [2, 2, 1024, 640], P('section', None, ('seq', 'fsdp'))
- input_grads: bfloat16 [2, 2, 1024, 640], P('section', None, ('seq', 'fsdp'))
- grad_attn_gain: float32 [2, 640], P('section', 'fsdp')
- grad_w_query: float32 [2, 640, 1024], P('section', 'fsdp')
- grad_w_key: float32 [2, 640, 256], P('section', 'fsdp')
- grad_w_value: float32 [2, 640, 256], P('section', 'fsdp')
- query_gain_gradient: float32 [2, 256], P('section', 'fsdp')
- grad_key_gain: float32 [2, 256], P('section', 'fsdp')
- grad_w_output: float32 [2, 1024, 640], P('section', 'fsdp')
- grad_post_attn_gain: float32 [2, 640], P('section', 'fsdp')
- grad_ffn_gain: float32 [2, 640], P('section', 'fsdp')
- grad_w_gate: float32 [2, 640, 2048], P('section', 'fsdp')
- grad_w_up: float32 [2, 640, 2048], P('section', 'fsdp')
- grad_w_down: float32 [2, 2048, 640], P('section', 'fsdp')
- grad_post_ffn_gain: float32 [2, 640], P('section', 'fsdp')
The draws below stay inside these ranges and needn't reach their ends.
Inputs may be any that keep to these rules, and one draw needn't show every extreme that they name: `positions`: in every row a document begins at the first token (place 0) and each later token's place is one more than the one before it unless a new document begins there at place 0; one row, chosen by the seed, is a single document of all 1024 tokens.
All inputs are finite; a program needn't handle non-finite values.
Results may differ from the reference program's by a relative error of at most 0.025.
Values may be sent and summed in bfloat16 or wider, within the bound.
No kernel may reach another device: no remote copies, remote signals or barrier semaphores. Data moves between devices by JAX's collectives and lax.ppermute only.
A program may use at most 192 MiB of HBM per device.

```python
import jax
import jax.numpy as jnp
from jax import lax

D = 640
H = 4
HD = 256
FF = 2048
WIN = 512
M = 2
TOKENS = 1024
SECTIONS = 2


def draw_positions(key, part):
    key = jax.random.fold_in(key, 7)
    first_key, second_key = jax.random.split(key)
    marks = jax.random.randint(first_key, (M, TOKENS), 0, max(WIN // 4, 2)) == 0
    whole_row = jax.random.randint(second_key, (), 0, M)
    row_ids = jnp.arange(M, dtype=jnp.int32)[:, None]
    column = jnp.arange(TOKENS, dtype=jnp.int32)[None, :]
    starts = marks & (row_ids != whole_row) | (column == 0)
    anchors = lax.cummax(jnp.where(starts, column, 0), axis=1)
    return (column - anchors).astype(jnp.int32)


def levels(key, extent, cuts, low, top_value):
    def one(dim, shards_of):
        heights = jax.random.uniform(jax.random.fold_in(jax.random.fold_in(key, 6), dim), (shards_of,), jnp.float32, low / len(cuts), top_value / len(cuts))
        return jnp.repeat(jnp.exp(heights), extent[dim] // shards_of).reshape((-1,) + (1,) * (len(extent) - dim - 1))

    level = one(*cuts[0])
    for cut in cuts[1:]:
        level = level * one(*cut)
    return level


def normal_values(key, dims, width, bound, cuts=(), kind=jnp.bfloat16):
    result = width * jax.random.normal(key, dims, jnp.float32)
    if cuts:
        result = result * levels(key, dims, cuts, -0.22, 0.18)
    return jnp.clip(result, -bound, bound).astype(kind)


def setup_inputs(seed: int = 0) -> dict:
    keys = jax.random.split(jax.random.key(seed), 17)
    hidden_in = normal_values(keys[0], (M, TOKENS, D), 1.0, 6.0, ((1, 16),))
    cotangent = normal_values(keys[1], (M, TOKENS, D), 1.0, 6.0, ((1, 16),))
    positions = draw_positions(jax.random.fold_in(keys[16], 71), 0)
    attn_gain = jnp.clip(1.0 + 0.15 * jax.random.normal(keys[3], (SECTIONS, D), jnp.float32), 0.25, 1.75).astype(jnp.bfloat16)
    w_query = normal_values(keys[4], (SECTIONS, D, H * HD), D ** -0.5, 0.25, ((0, 2), (1, 4)))
    w_key = normal_values(keys[5], (SECTIONS, D, HD), D ** -0.5, 0.25, ((0, 2), (1, 4)))
    w_value = normal_values(keys[6], (SECTIONS, D, HD), D ** -0.5, 0.25, ((0, 2), (1, 4)))
    query_gain = jnp.clip(1.0 + 0.15 * jax.random.normal(keys[7], (SECTIONS, HD), jnp.float32), 0.25, 1.75).astype(jnp.bfloat16)
    key_gain = jnp.clip(1.0 + 0.15 * jax.random.normal(keys[8], (SECTIONS, HD), jnp.float32), 0.25, 1.75).astype(jnp.bfloat16)
    w_output = normal_values(keys[9], (SECTIONS, H * HD, D), (H * HD) ** -0.5, 0.1875, ((0, 2), (1, 4)))
    post_attn_gain = jnp.clip(1.0 + 0.15 * jax.random.normal(keys[10], (SECTIONS, D), jnp.float32), 0.25, 1.75).astype(jnp.bfloat16)
    ffn_gain = jnp.clip(1.0 + 0.15 * jax.random.normal(keys[11], (SECTIONS, D), jnp.float32), 0.25, 1.75).astype(jnp.bfloat16)
    w_gate = normal_values(keys[12], (SECTIONS, D, FF), D ** -0.5, 0.25, ((0, 2), (1, 4)))
    w_up = normal_values(keys[13], (SECTIONS, D, FF), D ** -0.5, 0.25, ((0, 2), (1, 4)))
    w_down = normal_values(keys[14], (SECTIONS, FF, D), FF ** -0.5, 0.125, ((0, 2), (1, 4)))
    post_ffn_gain = jnp.clip(1.0 + 0.15 * jax.random.normal(keys[15], (SECTIONS, D), jnp.float32), 0.25, 1.75).astype(jnp.bfloat16)
    return {"hidden_in": hidden_in, "cotangent": cotangent, "positions": positions, "attn_gain": attn_gain, "w_query": w_query, "w_key": w_key, "w_value": w_value, "query_gain": query_gain, "key_gain": key_gain, "w_output": w_output, "post_attn_gain": post_attn_gain, "ffn_gain": ffn_gain, "w_gate": w_gate, "w_up": w_up, "w_down": w_down, "post_ffn_gain": post_ffn_gain}


EPSILON = 1e-06
ROPE_BASE = 10000.0
NEG_LARGE = -1e+30

@jax.custom_vjp
def low(v):
    return lax.optimization_barrier(v.astype(jnp.bfloat16)).astype(jnp.float32)

@jax.custom_vjp
def low_back(v):
    return v

def low_keep(v):
    return (low(v), None)

def low_pass(kept, grad):
    return (grad,)

def back_keep(v):
    return (v, None)

def back_low(kept, grad):
    return (low(grad),)
low.defvjp(low_keep, low_pass)
low_back.defvjp(back_keep, back_low)

def highest(left, right):
    return jnp.dot(left, right, precision=lax.Precision.HIGHEST, preferred_element_type=jnp.float32)

def norm_gain(values, scale_row):
    return values * lax.rsqrt(lax.optimization_barrier(jnp.mean(values * values, axis=-1, keepdims=True)) + EPSILON) * scale_row

def rotate(values, token_pos):
    half_dim = values.shape[-1] // 2
    frequency = ROPE_BASE ** (-2.0 * jnp.arange(half_dim, dtype=jnp.float32) / values.shape[-1])
    angles = token_pos.astype(jnp.float32)[:, None] * frequency[None, :]
    if values.ndim == 3:
        angles = angles[:, None, :]
    cosine = jnp.cos(angles)
    sine_part = jnp.sin(angles)
    first_half = values[..., :half_dim]
    second_half = values[..., half_dim:]
    return jnp.concatenate((first_half * cosine - second_half * sine_part, second_half * cosine + first_half * sine_part), axis=-1)

def qk_post(query_proj, key_proj, query_scale, key_scale, token_pos):
    return (rotate(norm_gain(query_proj, query_scale), token_pos), rotate(norm_gain(key_proj, key_scale), token_pos))

def window_mask(token_pos, key_count):
    distance = WIN + jnp.arange(token_pos.shape[0])[:, None] - jnp.arange(key_count)[None, :]
    return (distance >= 0) & (distance < WIN) & (distance <= token_pos[:, None])

def attention(query_rot, key_rot, value_b, token_pos):
    length = query_rot.shape[0]
    head_dim = key_rot.shape[-1]
    zero_rows = jnp.zeros((WIN, head_dim), jnp.float32)
    key_pad = jnp.concatenate((zero_rows, key_rot), axis=0)
    value_pad = jnp.concatenate((zero_rows, value_b), axis=0)

    def attend_block(block_index):
        row_start = block_index * WIN
        query_blk = lax.dynamic_slice_in_dim(query_rot, row_start, WIN, 0)
        key_blk = lax.dynamic_slice_in_dim(key_pad, row_start, 2 * WIN, 0)
        value_blk = lax.dynamic_slice_in_dim(value_pad, row_start, 2 * WIN, 0)
        pos_blk = lax.dynamic_slice_in_dim(token_pos, row_start, WIN, 0)
        scores = low_back(jnp.einsum('qhd,kd->hqk', query_blk, key_blk, precision=lax.Precision.HIGHEST) * head_dim ** (-0.5))
        allowed = window_mask(pos_blk, 2 * WIN)[None]
        masked = jnp.where(allowed, scores, NEG_LARGE)
        row_peak = lax.optimization_barrier(jnp.max(masked, axis=-1, keepdims=True))
        exponent = jnp.exp(masked - row_peak)
        attention_b = low(exponent / lax.optimization_barrier(jnp.sum(exponent, axis=-1, keepdims=True)))
        return jnp.einsum('hqk,kd->qhd', attention_b, value_blk, precision=lax.Precision.HIGHEST)
    blocks = lax.map(jax.checkpoint(attend_block), jnp.arange(length // WIN, dtype=jnp.int32))
    return blocks.reshape(length, query_rot.shape[1], head_dim)

def layer(residual, weights, token_pos):
    attn_scale, query_weight, key_weight, value_weight, query_scale, key_scale, out_weight, post_attn_scale, ffn_scale, gate_weight, up_weight, down_weight, post_ffn_scale = weights
    length = residual.shape[0]
    head_dim = query_scale.shape[0]
    normed = low(norm_gain(residual, attn_scale))
    query_proj = low_back(highest(normed, query_weight)).reshape(length, -1, head_dim)
    key_proj = low_back(highest(normed, key_weight))
    value_b = low(low_back(highest(normed, value_weight)))
    query_rot, key_rot = qk_post(query_proj, key_proj, query_scale, key_scale, token_pos)
    attended = low(low_back(attention(low(query_rot), low(key_rot), value_b, token_pos))).reshape(length, -1)
    branch = low_back(highest(attended, out_weight))
    mixed = residual + norm_gain(branch, post_attn_scale)
    ffn_in = low(norm_gain(mixed, ffn_scale))
    gate_pre = low_back(highest(ffn_in, gate_weight))
    up_pre = low_back(highest(ffn_in, up_weight))
    activated = low(jax.nn.gelu(gate_pre, approximate=True) * up_pre)
    down_out = low_back(highest(activated, down_weight))
    return mixed + norm_gain(down_out, post_ffn_scale)

def reference(hidden_in, cotangent, positions, attn_gain, w_query, w_key, w_value, query_gain, key_gain, w_output, post_attn_gain, ffn_gain, w_gate, w_up, w_down, post_ffn_gain):
    weights = (attn_gain.astype(jnp.float32), w_query.astype(jnp.float32), w_key.astype(jnp.float32), w_value.astype(jnp.float32), query_gain.astype(jnp.float32), key_gain.astype(jnp.float32), w_output.astype(jnp.float32), post_attn_gain.astype(jnp.float32), ffn_gain.astype(jnp.float32), w_gate.astype(jnp.float32), w_up.astype(jnp.float32), w_down.astype(jnp.float32), post_ffn_gain.astype(jnp.float32))
    inputs = hidden_in.astype(jnp.float32)
    entry = jnp.zeros_like(inputs)

    def model(model_in, model_weights, model_entry):
        first_layer = tuple((weight_arr[0] for weight_arr in model_weights))
        second_layer = tuple((weight_arr[1] for weight_arr in model_weights))

        def one_sequence(packed):
            seq_in, seq_entry, seq_pos = packed
            middle = low(low_back(layer(seq_in, first_layer, seq_pos))) + seq_entry
            return (middle, layer(middle, second_layer, seq_pos))
        return lax.map(jax.checkpoint(one_sequence), (model_in, model_entry, positions))
    (middles, finals), backward_mapping = jax.vjp(model, inputs, weights, entry)
    grad_in, grad_weights, grad_entry = backward_mapping((jnp.zeros_like(middles), cotangent.astype(jnp.float32)))
    section_outputs = jnp.stack((middles, finals)).astype(jnp.bfloat16)
    input_grads = jnp.stack((grad_in, grad_entry)).astype(jnp.bfloat16)
    return (section_outputs, input_grads, grad_weights[0], grad_weights[1], grad_weights[2], grad_weights[3], grad_weights[4], grad_weights[5], grad_weights[6], grad_weights[7], grad_weights[8], grad_weights[9], grad_weights[10], grad_weights[11], grad_weights[12])
```

```python
from functools import partial

import jax
import jax.numpy as jnp
import numpy as np
from jax import lax
from jax.sharding import PartitionSpec as P

WIN = 512
EPSILON = 1e-06
ROPE_BASE = 10000.0
NEG_LARGE = -1e30
AXES = ("section", "seq", "fsdp")
BF = jnp.bfloat16
F32 = jnp.float32


def dot(left, right, spec):
    return jnp.einsum(spec, left, right, preferred_element_type=F32)


def inverse_rms(values):
    return lax.rsqrt(jnp.mean(values * values, axis=-1, keepdims=True) + EPSILON)


def norm_back(values, scale, gain, grad):
    weighted = grad * gain
    inner = jnp.mean(values * weighted, axis=-1, keepdims=True)
    return scale * weighted - values * (scale * scale * scale * inner)


def gain_back(values, scale, grad):
    return jnp.sum((values * scale * grad).reshape(-1, values.shape[-1]), axis=0)


def rope_tables(token_pos, head_dim):
    half = head_dim // 2
    frequency = ROPE_BASE ** (-2.0 * jnp.arange(half, dtype=F32) / head_dim)
    angles = token_pos.astype(F32)[:, None] * frequency[None, :]
    return jnp.cos(angles), jnp.sin(angles)


def rotate(values, cosine, sine):
    half = values.shape[-1] // 2
    first, second = values[..., :half], values[..., half:]
    return jnp.concatenate((first * cosine - second * sine, second * cosine + first * sine), axis=-1)


class Halo:
    def __init__(self, sizes, section, seq, fsdp, rows):
        self.sizes, self.seq, self.fsdp, self.rows = sizes, seq, fsdp, rows
        self.section = section
        self.planes = WIN // (sizes["fsdp"] * rows)
        assert self.planes == 2 and self.planes * sizes["fsdp"] * rows == WIN

    def index(self, section, seq, fsdp):
        return (section * self.sizes["seq"] + seq) * self.sizes["fsdp"] + fsdp

    def along(self, array, section, by):
        pairs = [
            (self.index(section, z, f), self.index(section, z + by, f))
            for z in range(self.sizes["seq"])
            for f in range(self.sizes["fsdp"])
            if 0 <= z + by < self.sizes["seq"]
        ]
        return lax.ppermute(array, AXES, pairs)

    def across(self, array, section, flip):
        pairs = [
            (self.index(section, z, f), self.index(section, z, f ^ flip))
            for z in range(self.sizes["seq"])
            for f in range(self.sizes["fsdp"])
        ]
        return lax.ppermute(array, AXES, pairs)

    def starts(self):
        count = self.sizes["fsdp"]
        places = [(self.seq - back) * count + self.fsdp for back in range(3)]
        for flip in range(1, count):
            other = self.fsdp ^ flip
            places.append((self.seq - 1) * count + other)
            places.append(jnp.where(other < self.fsdp, self.seq, self.seq - 2) * count + other)
        return jnp.stack(places) * self.rows

    def fetch(self, own, section):
        one = self.along(own, section, 1)
        two = self.along(own, section, 2)
        blocks = [own, one, two]
        for flip in range(1, self.sizes["fsdp"]):
            chosen = jnp.where(self.fsdp < (self.fsdp ^ flip), own, two)
            got = self.across(jnp.stack((one, chosen)), section, flip)
            blocks += [got[0], got[1]]
        return jnp.concatenate(blocks, axis=1)

    def give_back(self, grads, section):
        rows = self.rows
        blocks = [grads[:, i * rows : (i + 1) * rows] for i in range(grads.shape[1] // rows)]
        own, one, two = blocks[0], blocks[1], blocks[2]
        for flip in range(1, self.sizes["fsdp"]):
            sent = jnp.stack((blocks[1 + 2 * flip], blocks[2 + 2 * flip])).astype(BF)
            got = self.across(sent, section, flip).astype(F32)
            lower = self.fsdp < (self.fsdp ^ flip)
            one = one + got[0]
            own = own + jnp.where(lower, got[1], 0.0)
            two = two + jnp.where(lower, 0.0, got[1])
        one = self.along(one.astype(BF), section, -1).astype(F32)
        two = self.along(two.astype(BF), section, -2).astype(F32)
        return own + one + two


def attend(query, keys, values, allowed):
    scores = dot(query, keys, "mthd,mkd->mhtk") * query.shape[-1] ** (-0.5)
    masked = jnp.where(allowed, scores, NEG_LARGE)
    exponent = jnp.exp(masked - jnp.max(masked, axis=-1, keepdims=True))
    probs = exponent / jnp.sum(exponent, axis=-1, keepdims=True)
    return dot(probs.astype(BF), values, "mhtk,mkd->mthd"), probs


def attend_back(grad, query, keys, values, probs):
    scale = query.shape[-1] ** (-0.5)
    grad_values = dot(probs.astype(BF), grad, "mhtk,mthd->mkd")
    grad_probs = dot(grad, values, "mthd,mkd->mhtk")
    inner = jnp.sum(probs * grad_probs, axis=-1, keepdims=True)
    grad_scores = (probs * (grad_probs - inner)).astype(BF)
    grad_query = dot(grad_scores, keys, "mhtk,mkd->mthd") * scale
    grad_keys = dot(grad_scores, query, "mhtk,mthd->mkd") * scale
    return grad_query, jnp.concatenate((grad_keys, grad_values), axis=-1)


def gated(gate, up):
    return jax.nn.gelu(gate, approximate=True) * up


def forward(layer_in, weights, tables, allowed, halo, section):
    micro, rows, width = layer_in.shape
    tokens = micro * rows
    cosine, sine = tables
    head_dim = weights["query_gain"].shape[0]
    heads_width = weights["out"].shape[0]
    heads = heads_width // head_dim
    residual = layer_in.astype(F32).reshape(tokens, width)
    scale_in = inverse_rms(residual)
    normed = (residual * scale_in * weights["attn_gain"]).astype(BF)
    qkv = dot(normed, weights["qkv"], "td,dn->tn")
    q = qkv[:, :heads_width].reshape(tokens, heads, head_dim)
    k = qkv[:, heads_width : heads_width + head_dim]
    v = qkv[:, heads_width + head_dim :]
    scale_q, scale_k = inverse_rms(q), inverse_rms(k)
    query = rotate(q * scale_q * weights["query_gain"], cosine[:, None], sine[:, None]).astype(BF)
    key = rotate(k * scale_k * weights["key_gain"], cosine, sine).astype(BF)
    own = jnp.concatenate((key, v.astype(BF)), axis=1).reshape(micro, rows, 2 * head_dim)
    window = halo.fetch(own, section)
    query = query.reshape(micro, rows, heads, head_dim)
    keys, values = window[..., :head_dim], window[..., head_dim:]
    attended, probs = attend(query, keys, values, allowed)
    attended = attended.astype(BF).reshape(tokens, heads_width)
    branch = dot(attended, weights["out"], "tn,nd->td")
    scale_branch = inverse_rms(branch)
    mixed = residual + branch * scale_branch * weights["post_attn_gain"]
    scale_mixed = inverse_rms(mixed)
    ffn_in = (mixed * scale_mixed * weights["ffn_gain"]).astype(BF)
    gate_up = dot(ffn_in, weights["gate_up"], "td,dn->tn")
    hidden = gate_up.shape[1] // 2
    gate, up = gate_up[:, :hidden], gate_up[:, hidden:]
    activated = gated(gate, up).astype(BF)
    down = dot(activated, weights["down"], "tf,fd->td")
    scale_down = inverse_rms(down)
    result = (mixed + down * scale_down * weights["post_ffn_gain"]).astype(BF)
    saved = dict(
        residual=residual, scale_in=scale_in, normed=normed, q=q, k=k, scale_q=scale_q,
        scale_k=scale_k, query=query, keys=keys, values=values, probs=probs, attended=attended,
        branch=branch, scale_branch=scale_branch, mixed=mixed, scale_mixed=scale_mixed,
        ffn_in=ffn_in, gate=gate, up=up, activated=activated, down=down, scale_down=scale_down,
    )
    return result.reshape(micro, rows, width), saved


def back_ffn(upstream, saved, weights):
    top = upstream.astype(F32).reshape(saved["mixed"].shape)
    grad_down = norm_back(saved["down"], saved["scale_down"], weights["post_ffn_gain"], top)
    grad_post_ffn = gain_back(saved["down"], saved["scale_down"], top)
    grad_down = grad_down.astype(BF)
    grad_act = dot(grad_down, weights["down"], "td,fd->tf")
    _, pull = jax.vjp(gated, saved["gate"], saved["up"])
    grad_gate, grad_up = pull(grad_act)
    grad_gate_up = jnp.concatenate((grad_gate.astype(BF), grad_up.astype(BF)), axis=1)
    grad_ffn_in = dot(grad_gate_up, weights["gate_up"], "tn,dn->td")
    grad_mixed = top + norm_back(
        saved["mixed"], saved["scale_mixed"], weights["ffn_gain"], grad_ffn_in
    )
    grad_ffn_gain = gain_back(saved["mixed"], saved["scale_mixed"], grad_ffn_in)
    return dict(
        ffn_in=saved["ffn_in"], gate_up=grad_gate_up, activated=saved["activated"],
        down=grad_down, mixed=grad_mixed, post_ffn_gain=grad_post_ffn, ffn_gain=grad_ffn_gain,
    )


def back_attention(grad_mixed, saved, weights):
    grad_branch = norm_back(
        saved["branch"], saved["scale_branch"], weights["post_attn_gain"], grad_mixed
    ).astype(BF)
    grad_post_attn = gain_back(saved["branch"], saved["scale_branch"], grad_mixed)
    grad_attended = dot(grad_branch, weights["out"], "td,nd->tn").astype(BF)
    grad_attended = grad_attended.reshape(saved["query"].shape)
    grad_query, grad_window = attend_back(
        grad_attended, saved["query"], saved["keys"], saved["values"], saved["probs"]
    )
    return dict(
        branch=grad_branch, post_attn_gain=grad_post_attn, query=grad_query, window=grad_window
    )


def back_project(grad_mixed, grad_query, grad_own, saved, weights, tables):
    cosine, sine = tables
    tokens, heads, head_dim = saved["q"].shape
    grad_own = grad_own.reshape(tokens, 2 * head_dim)
    grad_key = rotate(grad_own[:, :head_dim], cosine, -sine)
    grad_query = rotate(
        grad_query.reshape(tokens, heads, head_dim), cosine[:, None], -sine[:, None]
    )
    grad_query_gain = gain_back(saved["q"], saved["scale_q"], grad_query)
    grad_key_gain = gain_back(saved["k"], saved["scale_k"], grad_key)
    grad_q = norm_back(saved["q"], saved["scale_q"], weights["query_gain"], grad_query)
    grad_k = norm_back(saved["k"], saved["scale_k"], weights["key_gain"], grad_key)
    grad_qkv = jnp.concatenate(
        (
            grad_q.astype(BF).reshape(tokens, heads * head_dim),
            grad_k.astype(BF),
            grad_own[:, head_dim:].astype(BF),
        ),
        axis=1,
    )
    grad_normed = dot(grad_qkv, weights["qkv"], "tn,dn->td")
    grad_attn_gain = gain_back(saved["residual"], saved["scale_in"], grad_normed)
    grad_in = grad_mixed + norm_back(
        saved["residual"], saved["scale_in"], weights["attn_gain"], grad_normed
    )
    return dict(
        qkv=grad_qkv, grad_in=grad_in.astype(BF), attn_gain=grad_attn_gain,
        query_gain=grad_query_gain, key_gain=grad_key_gain,
    )


def body(sizes, hidden_in, cotangent, positions, attn_gain, w_query, w_key, w_value, query_gain,
         key_gain, w_output, post_attn_gain, ffn_gain, w_gate, w_up, w_down, post_ffn_gain):
    section = lax.axis_index("section")
    seq = lax.axis_index("seq")
    fsdp = lax.axis_index("fsdp")
    micro, rows, width = hidden_in.shape
    shard = w_query.shape[1]
    shards = sizes["fsdp"]
    heads_width, head_dim = w_query.shape[2], w_key.shape[2]

    def column(values):
        return jnp.pad(values[0], (0, shard - values.shape[1]))[:, None]

    gains = (attn_gain, post_attn_gain, ffn_gain, post_ffn_gain, query_gain, key_gain)
    columns = jnp.concatenate([column(g) for g in gains], axis=1)
    columns = jnp.pad(columns, ((0, 0), (0, 128 - len(gains))))
    first = jnp.concatenate((w_query[0], w_key[0], w_value[0], columns), axis=1)
    gather = partial(lax.all_gather, axis_name="fsdp", axis=0, tiled=True)
    first = gather(first)
    qkv_width = heads_width + 2 * head_dim
    gain_rows = first[:, qkv_width : qkv_width + len(gains)].astype(F32).T
    part = query_gain.shape[1]
    head_gains = gain_rows[4:].reshape(2, shards, shard)[:, :, :part].reshape(2, shards * part)
    weights = dict(
        qkv=first[:, :qkv_width],
        out=gather(w_output[0]),
        gate_up=gather(jnp.concatenate((w_gate[0], w_up[0]), axis=1)),
        down=gather(w_down[0]),
        attn_gain=gain_rows[0], post_attn_gain=gain_rows[1], ffn_gain=gain_rows[2],
        post_ffn_gain=gain_rows[3], query_gain=head_gains[0], key_gain=head_gains[1],
    )

    halo = Halo(sizes, section, seq, fsdp, rows)
    tables = rope_tables(positions.reshape(micro * rows), head_dim)
    query_place = (seq * shards + fsdp) * rows + jnp.arange(rows)
    key_place = (halo.starts()[:, None] + jnp.arange(rows)[None, :]).reshape(-1)
    distance = (query_place[:, None] - key_place[None, :])[None]
    allowed = (distance >= 0) & (distance < WIN) & (distance <= positions[:, :, None])
    allowed = allowed[:, None]

    def to_section(array, target):
        pairs = [
            (halo.index(1 - target, z, f), halo.index(target, z, f))
            for z in range(sizes["seq"])
            for f in range(shards)
        ]
        return lax.ppermute(array, AXES, pairs)

    result_a, saved_a = forward(hidden_in, weights, tables, allowed, halo, 0)
    middle = to_section(result_a, 1)
    result_b, saved_b = forward(middle, weights, tables, allowed, halo, 1)
    ffn_b = back_ffn(cotangent, saved_b, weights)
    attn_b = back_attention(ffn_b["mixed"], saved_b, weights)
    own_b = halo.give_back(attn_b["window"], 1)
    proj_b = back_project(ffn_b["mixed"], attn_b["query"], own_b, saved_b, weights, tables)
    grad_b = proj_b["grad_in"].reshape(micro, rows, width)
    upstream = to_section(grad_b, 0)

    is_first = section == 0

    def scatter(array):
        summed = lax.psum_scatter(array.astype(BF), "fsdp", scatter_dimension=0, tiled=True)
        return lax.psum(summed, "seq").astype(F32)

    ffn = lax.cond(is_first, lambda: back_ffn(upstream, saved_a, weights), lambda: ffn_b)
    grad_gate_up = scatter(dot(ffn["ffn_in"], ffn["gate_up"], "td,tn->dn"))
    grad_down = scatter(dot(ffn["activated"], ffn["down"], "tf,td->fd"))
    attn = lax.cond(
        is_first, lambda: back_attention(ffn["mixed"], saved_a, weights), lambda: attn_b
    )
    own = halo.give_back(attn["window"], 0)
    proj = lax.cond(
        is_first,
        lambda: back_project(ffn["mixed"], attn["query"], own, saved_a, weights, tables),
        lambda: proj_b,
    )
    attended = jnp.where(is_first, saved_a["attended"], saved_b["attended"])
    normed = jnp.where(is_first, saved_a["normed"], saved_b["normed"])
    grad_out = scatter(dot(attended, attn["branch"], "tn,td->nd"))

    def spread(values):
        return jnp.pad(values.reshape(shards, part), ((0, 0), (0, shard - part))).reshape(-1)

    gain_grads = jnp.stack(
        (
            proj["attn_gain"], attn["post_attn_gain"], ffn["ffn_gain"], ffn["post_ffn_gain"],
            spread(proj["query_gain"]), spread(proj["key_gain"]),
        ),
        axis=1,
    )
    gain_grads = jnp.pad(gain_grads, ((0, 0), (0, 128 - len(gains))))
    grad_first = scatter(
        jnp.concatenate((dot(normed, proj["qkv"], "td,tn->dn"), gain_grads), axis=1)
    )
    gain_out = grad_first[:, qkv_width : qkv_width + len(gains)].T

    section_outputs = jnp.where(is_first, result_a, result_b)[None]
    input_grads = proj["grad_in"].reshape(micro, rows, width)[None]
    hidden = w_gate.shape[2]
    return (
        section_outputs,
        input_grads,
        gain_out[0:1],
        grad_first[None, :, :heads_width],
        grad_first[None, :, heads_width : heads_width + head_dim],
        grad_first[None, :, heads_width + head_dim : qkv_width],
        gain_out[4:5, :part],
        gain_out[5:6, :part],
        grad_out[None],
        gain_out[1:2],
        gain_out[2:3],
        grad_gate_up[None, :, :hidden],
        grad_gate_up[None, :, hidden:],
        grad_down[None],
        gain_out[3:4],
    )


def solution(mesh):
    rows = P(None, ("seq", "fsdp"), None)
    vector, matrix = P("section", "fsdp"), P("section", "fsdp", None)
    weights = (vector, matrix, matrix, matrix, vector, vector, matrix, vector, vector, matrix,
               matrix, matrix, vector)
    out_rows = P("section", None, ("seq", "fsdp"), None)
    return jax.shard_map(
        partial(body, dict(mesh.shape)),
        mesh=mesh,
        in_specs=(rows, rows, P(None, ("seq", "fsdp"))) + weights,
        out_specs=(out_rows, out_rows) + weights,
        check_vma=False,
    )
```

```python
from functools import partial

import jax
import jax.numpy as jnp
import numpy as np
from jax import lax
from jax.sharding import PartitionSpec as P

WIN = 512
EPSILON = 1e-06
ROPE_BASE = 10000.0
NEG_LARGE = -1e30
AXES = ("section", "seq", "fsdp")
BF = jnp.bfloat16
F32 = jnp.float32


def dot(left, right, spec):
    return jnp.einsum(spec, left, right, preferred_element_type=F32)


def inverse_rms(values):
    return lax.rsqrt(jnp.mean(values * values, axis=-1, keepdims=True) + EPSILON)


def norm_back(values, scale, gain, grad):
    weighted = grad * gain
    inner = jnp.mean(values * weighted, axis=-1, keepdims=True)
    return scale * weighted - values * (scale * scale * scale * inner)


def gain_back(values, scale, grad):
    return jnp.sum((values * scale * grad).reshape(-1, values.shape[-1]), axis=0)


def rope_tables(token_pos, head_dim):
    half = head_dim // 2
    frequency = ROPE_BASE ** (-2.0 * jnp.arange(half, dtype=F32) / head_dim)
    angles = token_pos.astype(F32)[:, None] * frequency[None, :]
    return jnp.cos(angles), jnp.sin(angles)


def rotate(values, cosine, sine):
    half = values.shape[-1] // 2
    first, second = values[..., :half], values[..., half:]
    return jnp.concatenate((first * cosine - second * sine, second * cosine + first * sine), axis=-1)


class Halo:
    def __init__(self, sizes, section, seq, fsdp, rows):
        self.sizes, self.seq, self.fsdp, self.rows = sizes, seq, fsdp, rows
        self.section = section
        self.planes = WIN // (sizes["fsdp"] * rows)
        assert self.planes == 2 and self.planes * sizes["fsdp"] * rows == WIN

    def index(self, section, seq, fsdp):
        return (section * self.sizes["seq"] + seq) * self.sizes["fsdp"] + fsdp

    def along(self, array, section, by):
        pairs = [
            (self.index(section, z, f), self.index(section, z + by, f))
            for z in range(self.sizes["seq"])
            for f in range(self.sizes["fsdp"])
            if 0 <= z + by < self.sizes["seq"]
        ]
        return lax.ppermute(array, AXES, pairs)

    def across(self, array, section, flip):
        pairs = [
            (self.index(section, z, f), self.index(section, z, f ^ flip))
            for z in range(self.sizes["seq"])
            for f in range(self.sizes["fsdp"])
        ]
        return lax.ppermute(array, AXES, pairs)

    def exchange(self, array, section, span):
        pairs = [
            (self.index(section, z, f), self.index(section, z ^ span, f))
            for z in range(self.sizes["seq"])
            for f in range(self.sizes["fsdp"])
        ]
        return lax.ppermute(array, AXES, pairs)

    def starts(self):
        count = self.sizes["fsdp"]
        places = [(self.seq - back) * count + self.fsdp for back in range(3)]
        for flip in range(1, count):
            other = self.fsdp ^ flip
            places.append((self.seq - 1) * count + other)
            places.append(jnp.where(other < self.fsdp, self.seq, self.seq - 2) * count + other)
        return jnp.stack(places) * self.rows

    def fetch(self, own, section):
        one = self.along(own, section, 1)
        two = self.along(own, section, 2)
        blocks = [own, one, two]
        for flip in range(1, self.sizes["fsdp"]):
            chosen = jnp.where(self.fsdp < (self.fsdp ^ flip), own, two)
            got = self.across(jnp.stack((one, chosen)), section, flip)
            blocks += [got[0], got[1]]
        return jnp.concatenate(blocks, axis=1)

    def give_back(self, grads, section):
        rows = self.rows
        blocks = [grads[:, i * rows : (i + 1) * rows] for i in range(grads.shape[1] // rows)]
        own, one, two = blocks[0], blocks[1], blocks[2]
        for flip in range(1, self.sizes["fsdp"]):
            sent = jnp.stack((blocks[1 + 2 * flip], blocks[2 + 2 * flip])).astype(BF)
            got = self.across(sent, section, flip).astype(F32)
            lower = self.fsdp < (self.fsdp ^ flip)
            one = one + got[0]
            own = own + jnp.where(lower, got[1], 0.0)
            two = two + jnp.where(lower, 0.0, got[1])
        one = self.along(one.astype(BF), section, -1).astype(F32)
        two = self.along(two.astype(BF), section, -2).astype(F32)
        return own + one + two


def attend(query, keys, values, allowed):
    scores = dot(query, keys, "mthd,mkd->mhtk") * query.shape[-1] ** (-0.5)
    masked = jnp.where(allowed, scores, NEG_LARGE)
    exponent = jnp.exp(masked - jnp.max(masked, axis=-1, keepdims=True))
    probs = exponent / jnp.sum(exponent, axis=-1, keepdims=True)
    return dot(probs.astype(BF), values, "mhtk,mkd->mthd"), probs


def attend_back(grad, query, keys, values, probs):
    scale = query.shape[-1] ** (-0.5)
    grad_values = dot(probs.astype(BF), grad, "mhtk,mthd->mkd")
    grad_probs = dot(grad, values, "mthd,mkd->mhtk")
    inner = jnp.sum(probs * grad_probs, axis=-1, keepdims=True)
    grad_scores = (probs * (grad_probs - inner)).astype(BF)
    grad_query = dot(grad_scores, keys, "mhtk,mkd->mthd") * scale
    grad_keys = dot(grad_scores, query, "mhtk,mthd->mkd") * scale
    return grad_query, jnp.concatenate((grad_keys, grad_values), axis=-1)


def gated(gate, up):
    return jax.nn.gelu(gate, approximate=True) * up


def forward(layer_in, weights, tables, allowed, halo, section):
    micro, rows, width = layer_in.shape
    tokens = micro * rows
    cosine, sine = tables
    head_dim = weights["query_gain"].shape[0]
    heads_width = weights["out"].shape[0]
    heads = heads_width // head_dim
    residual = layer_in.astype(F32).reshape(tokens, width)
    scale_in = inverse_rms(residual)
    normed = (residual * scale_in * weights["attn_gain"]).astype(BF)
    qkv = dot(normed, weights["qkv"], "td,dn->tn")
    q = qkv[:, :heads_width].reshape(tokens, heads, head_dim)
    k = qkv[:, heads_width : heads_width + head_dim]
    v = qkv[:, heads_width + head_dim :]
    scale_q, scale_k = inverse_rms(q), inverse_rms(k)
    query = rotate(q * scale_q * weights["query_gain"], cosine[:, None], sine[:, None]).astype(BF)
    key = rotate(k * scale_k * weights["key_gain"], cosine, sine).astype(BF)
    own = jnp.concatenate((key, v.astype(BF)), axis=1).reshape(micro, rows, 2 * head_dim)
    window = halo.fetch(own, section)
    query = query.reshape(micro, rows, heads, head_dim)
    keys, values = window[..., :head_dim], window[..., head_dim:]
    attended, probs = attend(query, keys, values, allowed)
    attended = attended.astype(BF).reshape(tokens, heads_width)
    branch = dot(attended, weights["out"], "tn,nd->td")
    scale_branch = inverse_rms(branch)
    mixed = residual + branch * scale_branch * weights["post_attn_gain"]
    scale_mixed = inverse_rms(mixed)
    ffn_in = (mixed * scale_mixed * weights["ffn_gain"]).astype(BF)
    gate_up = dot(ffn_in, weights["gate_up"], "td,dn->tn")
    hidden = gate_up.shape[1] // 2
    gate, up = gate_up[:, :hidden], gate_up[:, hidden:]
    activated = gated(gate, up).astype(BF)
    down = dot(activated, weights["down"], "tf,fd->td")
    scale_down = inverse_rms(down)
    result = (mixed + down * scale_down * weights["post_ffn_gain"]).astype(BF)
    saved = dict(
        residual=residual, scale_in=scale_in, normed=normed, q=q, k=k, scale_q=scale_q,
        scale_k=scale_k, query=query, keys=keys, values=values, probs=probs, attended=attended,
        branch=branch, scale_branch=scale_branch, mixed=mixed, scale_mixed=scale_mixed,
        ffn_in=ffn_in, gate=gate, up=up, activated=activated, down=down, scale_down=scale_down,
    )
    return result.reshape(micro, rows, width), saved


def back_ffn(upstream, saved, weights):
    top = upstream.astype(F32).reshape(saved["mixed"].shape)
    grad_down = norm_back(saved["down"], saved["scale_down"], weights["post_ffn_gain"], top)
    grad_post_ffn = gain_back(saved["down"], saved["scale_down"], top)
    grad_down = grad_down.astype(BF)
    grad_act = dot(grad_down, weights["down"], "td,fd->tf")
    _, pull = jax.vjp(gated, saved["gate"], saved["up"])
    grad_gate, grad_up = pull(grad_act)
    grad_gate_up = jnp.concatenate((grad_gate.astype(BF), grad_up.astype(BF)), axis=1)
    grad_ffn_in = dot(grad_gate_up, weights["gate_up"], "tn,dn->td")
    grad_mixed = top + norm_back(
        saved["mixed"], saved["scale_mixed"], weights["ffn_gain"], grad_ffn_in
    )
    grad_ffn_gain = gain_back(saved["mixed"], saved["scale_mixed"], grad_ffn_in)
    return dict(
        ffn_in=saved["ffn_in"], gate_up=grad_gate_up, activated=saved["activated"],
        down=grad_down, mixed=grad_mixed, post_ffn_gain=grad_post_ffn, ffn_gain=grad_ffn_gain,
    )


def back_attention(grad_mixed, saved, weights):
    grad_branch = norm_back(
        saved["branch"], saved["scale_branch"], weights["post_attn_gain"], grad_mixed
    ).astype(BF)
    grad_post_attn = gain_back(saved["branch"], saved["scale_branch"], grad_mixed)
    grad_attended = dot(grad_branch, weights["out"], "td,nd->tn").astype(BF)
    grad_attended = grad_attended.reshape(saved["query"].shape)
    grad_query, grad_window = attend_back(
        grad_attended, saved["query"], saved["keys"], saved["values"], saved["probs"]
    )
    return dict(
        branch=grad_branch, post_attn_gain=grad_post_attn, query=grad_query, window=grad_window
    )


def back_project(grad_mixed, grad_query, grad_own, saved, weights, tables):
    cosine, sine = tables
    tokens, heads, head_dim = saved["q"].shape
    grad_own = grad_own.reshape(tokens, 2 * head_dim)
    grad_key = rotate(grad_own[:, :head_dim], cosine, -sine)
    grad_query = rotate(
        grad_query.reshape(tokens, heads, head_dim), cosine[:, None], -sine[:, None]
    )
    grad_query_gain = gain_back(saved["q"], saved["scale_q"], grad_query)
    grad_key_gain = gain_back(saved["k"], saved["scale_k"], grad_key)
    grad_q = norm_back(saved["q"], saved["scale_q"], weights["query_gain"], grad_query)
    grad_k = norm_back(saved["k"], saved["scale_k"], weights["key_gain"], grad_key)
    grad_qkv = jnp.concatenate(
        (
            grad_q.astype(BF).reshape(tokens, heads * head_dim),
            grad_k.astype(BF),
            grad_own[:, head_dim:].astype(BF),
        ),
        axis=1,
    )
    grad_normed = dot(grad_qkv, weights["qkv"], "tn,dn->td")
    grad_attn_gain = gain_back(saved["residual"], saved["scale_in"], grad_normed)
    grad_in = grad_mixed + norm_back(
        saved["residual"], saved["scale_in"], weights["attn_gain"], grad_normed
    )
    return dict(
        qkv=grad_qkv, grad_in=grad_in.astype(BF), attn_gain=grad_attn_gain,
        query_gain=grad_query_gain, key_gain=grad_key_gain,
    )


def body(sizes, hidden_in, cotangent, positions, attn_gain, w_query, w_key, w_value, query_gain,
         key_gain, w_output, post_attn_gain, ffn_gain, w_gate, w_up, w_down, post_ffn_gain):
    section = lax.axis_index("section")
    seq = lax.axis_index("seq")
    fsdp = lax.axis_index("fsdp")
    micro, rows, width = hidden_in.shape
    shard = w_query.shape[1]
    shards = sizes["fsdp"]
    heads_width, head_dim = w_query.shape[2], w_key.shape[2]
    qkv_width = heads_width + 2 * head_dim
    hidden = w_gate.shape[2]
    part = query_gain.shape[1]
    halo = Halo(sizes, section, seq, fsdp, rows)

    def column(values):
        return jnp.pad(values[0], (0, shard - values.shape[1]))[:, None]

    gains = (attn_gain, post_attn_gain, ffn_gain, post_ffn_gain, query_gain, key_gain)
    columns = jnp.concatenate([column(g) for g in gains], axis=1)
    columns = jnp.pad(columns, ((0, 0), (0, 128 - len(gains))))
    own_shards = (
        jnp.concatenate((w_query[0], w_key[0], w_value[0], columns), axis=1),
        w_output[0],
        jnp.concatenate((w_gate[0], w_up[0]), axis=1),
        w_down[0],
    )

    def gather(array, target):
        count = array.shape[0]
        full = jnp.zeros((count * shards, array.shape[1]), array.dtype)
        for flip in range(shards):
            piece = halo.across(array, target, flip) if flip else array
            full = lax.dynamic_update_slice_in_dim(full, piece, (fsdp ^ flip) * count, 0)
        return full

    def gather_weights(arrays, target):
        first, out, gate_up, down = [gather(array, target) for array in arrays]
        gain_rows = first[:, qkv_width : qkv_width + len(gains)].astype(F32).T
        head_gains = gain_rows[4:].reshape(2, shards, shard)[:, :, :part]
        head_gains = head_gains.reshape(2, shards * part)
        return dict(
            qkv=first[:, :qkv_width], out=out, gate_up=gate_up, down=down,
            attn_gain=gain_rows[0], post_attn_gain=gain_rows[1], ffn_gain=gain_rows[2],
            post_ffn_gain=gain_rows[3], query_gain=head_gains[0], key_gain=head_gains[1],
        )

    tables = rope_tables(positions.reshape(micro * rows), head_dim)
    query_place = (seq * shards + fsdp) * rows + jnp.arange(rows)
    key_place = (halo.starts()[:, None] + jnp.arange(rows)[None, :]).reshape(-1)
    distance = (query_place[:, None] - key_place[None, :])[None]
    allowed = (distance >= 0) & (distance < WIN) & (distance <= positions[:, :, None])
    allowed = allowed[:, None]

    def to_section(array, target):
        pairs = [
            (halo.index(1 - target, z, f), halo.index(target, z, f))
            for z in range(sizes["seq"])
            for f in range(shards)
        ]
        return lax.ppermute(array, AXES, pairs)

    def columns_of(array, flip):
        count = array.shape[1] // shards
        return lax.dynamic_slice_in_dim(array, (fsdp ^ flip) * count, count, 1)

    def fold(array):
        return jnp.concatenate([array[i * shard : (i + 1) * shard] for i in range(shards)], axis=1)

    def unfold(array):
        count = array.shape[1] // shards
        return jnp.concatenate(
            [array[:, i * count : (i + 1) * count] for i in range(shards)], axis=0
        ).T

    def ffn_block(ffn, saved, flip):
        return jnp.concatenate(
            (
                dot(columns_of(saved["ffn_in"], flip), ffn["gate_up"], "td,tn->dn"),
                fold(dot(ffn["down"], columns_of(saved["activated"], flip), "td,tf->df")),
            ),
            axis=1,
        )

    def attention_block(attn, proj, gain_grads, saved, flip):
        return jnp.concatenate(
            (
                dot(columns_of(saved["normed"], flip), proj["qkv"], "td,tn->dn"),
                lax.dynamic_slice_in_dim(gain_grads, (fsdp ^ flip) * shard, shard, 0),
                fold(dot(attn["branch"], columns_of(saved["attended"], flip), "td,tn->dn")),
            ),
            axis=1,
        )

    def spread(values):
        return jnp.pad(values.reshape(shards, part), ((0, 0), (0, shard - part))).reshape(-1)

    def gain_columns(ffn, attn, proj):
        stacked = jnp.stack(
            (
                proj["attn_gain"], attn["post_attn_gain"], ffn["ffn_gain"], ffn["post_ffn_gain"],
                spread(proj["query_gain"]), spread(proj["key_gain"]),
            ),
            axis=1,
        )
        return jnp.pad(stacked, ((0, 0), (0, 128 - len(gains))))

    def blocks_of(block):
        return [block(flip).astype(BF) for flip in range(1, shards)], block(0)

    def sum_plane(blocks, target):
        sent, own = blocks
        got = [halo.across(piece, target, 1 + i).astype(F32) for i, piece in enumerate(sent)]
        return sum(got, own).astype(BF)

    def sum_seq(array, target):
        steps = []
        span = 1
        while span < sizes["seq"]:
            bit = (seq // span) % 2
            half = array.shape[1] // 2
            keep = lax.dynamic_slice_in_dim(array, bit * half, half, 1)
            send = lax.dynamic_slice_in_dim(array, (1 - bit) * half, half, 1)
            got = halo.exchange(send, target, span)
            array = (keep.astype(F32) + got.astype(F32)).astype(BF)
            steps.append((span, bit))
            span *= 2
        for span, bit in reversed(steps):
            got = halo.exchange(array, target, span)
            array = jnp.concatenate(
                (jnp.where(bit == 0, array, got), jnp.where(bit == 0, got, array)), axis=1
            )
        return array

    first = gather_weights(own_shards, 0)
    result_a, saved_a = forward(hidden_in, first, tables, allowed, halo, 0)
    token = to_section(saved_a["keys"][:1, -16:, :64], 1)
    later, token = lax.optimization_barrier((own_shards, token))
    tied = lax.dynamic_update_slice(later[0], token[0], (0, later[0].shape[1] - token.shape[2]))
    second = gather_weights((tied,) + later[1:], 1)
    middle = to_section(result_a, 1)
    result_b, saved_b = forward(middle, second, tables, allowed, halo, 1)

    ffn_b = back_ffn(cotangent, saved_b, second)
    attn_b = back_attention(ffn_b["mixed"], saved_b, second)
    own_b = halo.give_back(attn_b["window"], 1)
    proj_b = back_project(ffn_b["mixed"], attn_b["query"], own_b, saved_b, second, tables)
    upstream = to_section(proj_b["grad_in"].reshape(micro, rows, width), 0)
    gains_b = gain_columns(ffn_b, attn_b, proj_b)
    ffn_blocks = blocks_of(partial(ffn_block, ffn_b, saved_b))
    attn_blocks = blocks_of(partial(attention_block, attn_b, proj_b, gains_b, saved_b))
    upstream, ffn_blocks, attn_blocks = lax.optimization_barrier(
        (upstream, ffn_blocks, attn_blocks)
    )
    ffn_sum_b = sum_plane(ffn_blocks, 1)
    attn_sum_b = sum_plane(attn_blocks, 1)

    ffn_a = back_ffn(upstream, saved_a, first)
    ffn_sum_a = sum_plane(blocks_of(partial(ffn_block, ffn_a, saved_a)), 0)
    attn_a = back_attention(ffn_a["mixed"], saved_a, first)
    own_a = halo.give_back(attn_a["window"], 0)
    proj_a = back_project(ffn_a["mixed"], attn_a["query"], own_a, saved_a, first, tables)
    gains_a = gain_columns(ffn_a, attn_a, proj_a)
    attn_sum_a = sum_plane(
        blocks_of(partial(attention_block, attn_a, proj_a, gains_a, saved_a)), 0
    )

    is_first = section == 0
    attn_cols = attn_sum_a.shape[1]
    padded = -(-attn_cols // (128 * sizes["seq"])) * 128 * sizes["seq"]

    def total(ours, theirs, target_a=0, target_b=1):
        return jnp.where(is_first, sum_seq(ours, target_a), sum_seq(theirs, target_b)).astype(F32)

    def widen(array):
        return jnp.pad(array, ((0, 0), (0, padded - attn_cols)))

    ffn_total = total(ffn_sum_a, ffn_sum_b)
    attn_total = total(widen(attn_sum_a), widen(attn_sum_b))
    gain_out = attn_total[:, qkv_width : qkv_width + len(gains)].T
    grad_down = unfold(ffn_total[:, 2 * hidden :])
    grad_out = unfold(attn_total[:, qkv_width + 128 : qkv_width + 128 + heads_width])
    section_outputs = jnp.where(is_first, result_a, result_b)[None]
    input_grads = jnp.where(is_first, proj_a["grad_in"], proj_b["grad_in"])
    return (
        section_outputs,
        input_grads.reshape(micro, rows, width)[None],
        gain_out[0:1],
        attn_total[None, :, :heads_width],
        attn_total[None, :, heads_width : heads_width + head_dim],
        attn_total[None, :, heads_width + head_dim : qkv_width],
        gain_out[4:5, :part],
        gain_out[5:6, :part],
        grad_out[None],
        gain_out[1:2],
        gain_out[2:3],
        ffn_total[None, :, :hidden],
        ffn_total[None, :, hidden : 2 * hidden],
        grad_down[None],
        gain_out[3:4],
    )


def solution(mesh):
    rows = P(None, ("seq", "fsdp"), None)
    vector, matrix = P("section", "fsdp"), P("section", "fsdp", None)
    weights = (vector, matrix, matrix, matrix, vector, vector, matrix, vector, vector, matrix,
               matrix, matrix, vector)
    out_rows = P("section", None, ("seq", "fsdp"), None)
    return jax.shard_map(
        partial(body, dict(mesh.shape)),
        mesh=mesh,
        in_specs=(rows, rows, P(None, ("seq", "fsdp"))) + weights,
        out_specs=(out_rows, out_rows) + weights,
        check_vma=False,
    )
```

```python
import functools

import jax
import jax.numpy as jnp
from jax import lax
from jax.experimental import pallas as pl
from jax.experimental.pallas import tpu as pltpu
from jax.sharding import PartitionSpec as P

WIN = 512
EPSILON = 1e-06
ROPE_BASE = 10000.0
NEG_LARGE = -1e30
AXES = ("section", "seq", "fsdp")
BF = jnp.bfloat16
F32 = jnp.float32
GAIN_ROWS = 16
INTERPRET = False


def mm(left, right):
    return lax.dot_general(left, right, (((1,), (0,)), ((), ())), preferred_element_type=F32)


def mm_nt(left, right):
    return lax.dot_general(left, right, (((1,), (1,)), ((), ())), preferred_element_type=F32)


def mm_tn(left, right):
    return lax.dot_general(left, right, (((0,), (0,)), ((), ())), preferred_element_type=F32)


def inverse_rms(values):
    return lax.rsqrt(jnp.mean(values * values, axis=-1, keepdims=True) + EPSILON)


def norm_back(values, scale, gain, grad):
    weighted = grad * gain
    inner = jnp.mean(values * weighted, axis=-1, keepdims=True)
    return scale * weighted - values * (scale * scale * scale * inner)


def gain_back(values, scale, grad):
    return jnp.sum(values * scale * grad, axis=0, keepdims=True)


def call(kernel, info, arrays, outs, scratch=(), flops=0):
    smem = pl.BlockSpec(memory_space=pltpu.SMEM)
    vmem = pl.BlockSpec(memory_space=pltpu.VMEM)
    size = sum(a.size * a.dtype.itemsize for a in arrays)
    size += sum(a.size * a.dtype.itemsize for a in outs)
    return pl.pallas_call(
        kernel,
        out_shape=outs,
        in_specs=[smem] + [vmem] * len(arrays),
        out_specs=[vmem] * len(outs),
        scratch_shapes=list(scratch),
        compiler_params=pltpu.CompilerParams(vmem_limit_bytes=40 * 1024 * 1024),
        cost_estimate=pl.CostEstimate(flops=flops, bytes_accessed=size, transcendentals=0),
        interpret=INTERPRET,
    )(info, *arrays)


def shape(dims, kind):
    return jax.ShapeDtypeStruct(tuple(dims), kind)


def slot(index, width):
    return pl.ds(pl.multiple_of(index * width, width), width)


def gains_kernel(info, *refs):
    pieces, out, held = refs[:-2], refs[-2], refs[-1]
    count = len(pieces)
    shard = out.shape[1] // count
    rows = pieces[0].shape[0] - GAIN_ROWS
    part = shard * 2 // 5
    for flip, piece in enumerate(pieces):
        held[info[0] ^ flip] = piece[rows : rows + GAIN_ROWS, : held.shape[2]].astype(F32)
    out[...] = jnp.zeros_like(out)
    for place in range(count):
        for row in range(4):
            out[row : row + 1, place * shard : (place + 1) * shard] = held[
                place, 0:1, row * shard : (row + 1) * shard
            ]
        for row in range(2):
            start = 4 * shard + row * part
            out[4 + row : 5 + row, place * part : (place + 1) * part] = held[
                place, 0:1, start : start + part
            ]


def project_kernel(info, x, gains, cosine, sine, *refs):
    pieces = refs[:-4]
    blocks, qkv, query, own = refs[-4:]
    shard = blocks.shape[2]
    half = cosine.shape[1]
    head = 2 * half
    residual = x[...].astype(F32)
    normed = residual * inverse_rms(residual) * gains[0:1, :]
    for place in range(len(pieces)):
        blocks[place] = normed[:, place * shard : (place + 1) * shard].astype(BF)
    total = None
    for flip, piece in enumerate(pieces):
        term = mm(blocks[info[0] ^ flip], piece[:shard, :])
        total = term if total is None else total + term
    qkv[...] = total
    cos, sin = cosine[...], sine[...]
    heads = query.shape[1] // head
    for index in range(heads + 1):
        raw = total[:, index * head : (index + 1) * head]
        row = 4 if index < heads else 5
        normal = raw * inverse_rms(raw) * gains[row : row + 1, :head]
        one, two = normal[:, :half], normal[:, half:]
        target, start = (query, index * head) if index < heads else (own, 0)
        target[:, start : start + half] = (one * cos - two * sin).astype(BF)
        target[:, start + half : start + head] = (two * cos + one * sin).astype(BF)
    own[:, head:] = total[:, (heads + 1) * head :].astype(BF)


def select_kernel(info, own, one, two, *outs):
    for index, out in enumerate(outs):
        lower = (info[0] < (info[0] ^ (index + 1))).astype(F32)
        out[0] = one[...]
        mixed = own[...].astype(F32) * lower + two[...].astype(F32) * (1.0 - lower)
        out[1] = mixed.astype(BF)


def attend_kernel(micro, info, query, own, one, two, *refs):
    got = refs[:3]
    x, gains, limit, query_place, key_place = refs[3:8]
    pieces = refs[8:12]
    window, probs, attended, branch, mixed, blocks = refs[12:]
    rows = own.shape[0] // micro
    head = own.shape[1] // 2
    heads = query.shape[1] // head
    shard = blocks.shape[2]
    for m in range(micro):
        span = slice(m * rows, (m + 1) * rows)
        parts = [own[span], one[span], two[span]]
        for ref in got:
            parts += [ref[0, span], ref[1, span]]
        for index, part in enumerate(parts):
            window[m, index * rows : (index + 1) * rows] = part
        distance = query_place[span] - key_place[...]
        allowed = (distance >= 0) & (distance <= limit[span])
        bias = jnp.where(allowed, 0.0, NEG_LARGE)
        bias = jnp.concatenate([bias] * heads, axis=0)
        stacked = jnp.concatenate(
            [query[span, h * head : (h + 1) * head] for h in range(heads)], axis=0
        )
        scores = mm_nt(stacked, window[m, :, :head]) * head ** (-0.5) + bias
        exponent = jnp.exp(scores - jnp.max(scores, axis=-1, keepdims=True))
        chance = exponent / jnp.sum(exponent, axis=-1, keepdims=True)
        probs[m] = chance
        result = mm(chance.astype(BF), window[m, :, head:]).astype(BF)
        for h in range(heads):
            attended[span, h * head : (h + 1) * head] = result[h * rows : (h + 1) * rows]
    total = None
    for flip, piece in enumerate(pieces):
        term = mm(attended[:, slot(info[0] ^ flip, head)], piece[...])
        total = term if total is None else total + term
    branch[...] = total
    value = x[...].astype(F32) + total * inverse_rms(total) * gains[1:2, :]
    mixed[...] = value
    normed = value * inverse_rms(value) * gains[2:3, :]
    for place in range(len(pieces)):
        blocks[place] = normed[:, place * shard : (place + 1) * shard].astype(BF)


def gelu_parts(gate):
    c = 0.7978845608028654
    inner = jnp.tanh(c * (gate + 0.044715 * gate * gate * gate))
    value = 0.5 * gate * (1.0 + inner)
    slope = 0.5 * (1.0 + inner) + 0.5 * gate * (1.0 - inner * inner) * c * (
        1.0 + 3 * 0.044715 * gate * gate
    )
    return value, slope


def ffn_kernel(info, blocks, mixed, gains, *refs):
    gate_up_pieces, down_pieces = refs[:4], refs[4:8]
    gate_up, activated, down, result = refs[8:]
    hidden = activated.shape[1]
    width = 512
    for start in range(0, hidden, width):
        both = []
        for base in (start, hidden + start):
            total = None
            for flip, piece in enumerate(gate_up_pieces):
                term = mm(blocks[info[0] ^ flip], piece[:, base : base + width])
                total = term if total is None else total + term
            gate_up[:, base : base + width] = total
            both.append(total)
        value, _ = gelu_parts(both[0])
        activated[:, start : start + width] = (value * both[1]).astype(BF)
    total = None
    for flip, piece in enumerate(down_pieces):
        term = mm(activated[:, slot(info[0] ^ flip, piece.shape[0])], piece[...])
        total = term if total is None else total + term
    down[...] = total
    result[...] = (mixed[...] + total * inverse_rms(total) * gains[3:4, :]).astype(BF)


def ffn_back_kernel(info, upstream, mixed, down, gate_up, activated, blocks, gains, *refs):
    gate_up_pieces, down_pieces = refs[:4], refs[4:8]
    packs, grad_mixed, gain_rows = refs[8:12], refs[12], refs[13]
    grad_act, grad_gate_up, held, natural = refs[14:]
    hidden = activated.shape[1]
    model = mixed.shape[1]
    shard = blocks.shape[2]
    top = upstream[...].astype(F32)
    raw = down[...]
    scale = inverse_rms(raw)
    grad_down = norm_back(raw, scale, gains[3:4, :], top).astype(BF)
    gain_rows[...] = jnp.zeros_like(gain_rows)
    gain_rows[3:4, :] = gain_back(raw, scale, top)
    act_at = 2 * hidden + model
    block_at = act_at + hidden // 4
    for flip, piece in enumerate(down_pieces):
        grad_act[:, slot(info[0] ^ flip, piece.shape[0])] = mm_nt(grad_down, piece[...])
    for flip, pack in enumerate(packs):
        pack[:, 2 * hidden : act_at] = grad_down
        pack[:, act_at:block_at] = activated[:, slot(info[0] ^ flip, hidden // 4)]
        pack[:, block_at:] = jnp.zeros_like(pack[:, block_at:])
        pack[:, block_at : block_at + shard] = blocks[info[0] ^ flip]
    width = 512
    for start in range(0, hidden, width):
        value, slope = gelu_parts(gate_up[:, start : start + width])
        up = gate_up[:, hidden + start : hidden + start + width]
        grad = grad_act[:, start : start + width]
        grad_gate_up[:, start : start + width] = (grad * up * slope).astype(BF)
        grad_gate_up[:, hidden + start : hidden + start + width] = (grad * value).astype(BF)
    for pack in packs:
        pack[:, : 2 * hidden] = grad_gate_up[...]
    for flip, piece in enumerate(gate_up_pieces):
        held[info[0] ^ flip] = mm_nt(grad_gate_up[...], piece[...])
    for place in range(4):
        natural[:, place * shard : (place + 1) * shard] = held[place]
    grad_in = natural[...]
    raw = mixed[...]
    scale = inverse_rms(raw)
    gain_rows[2:3, :] = gain_back(raw, scale, grad_in)
    grad_mixed[...] = top + norm_back(raw, scale, gains[2:3, :], grad_in)


def attend_back_kernel(micro, info, grad_mixed, branch, window, probs, query, gains, *refs):
    pieces = refs[:4]
    grad_branch, grad_query, own, one, two = refs[4:9]
    gives, gain_rows, grad_attended = refs[9:12], refs[12], refs[13]
    rows = own.shape[0] // micro
    head = own.shape[1] // 2
    heads = query.shape[1] // head
    factor = head ** (-0.5)
    raw = branch[...]
    scale = inverse_rms(raw)
    grad = grad_mixed[...]
    gain_rows[...] = jnp.zeros_like(gain_rows)
    gain_rows[1:2, :] = gain_back(raw, scale, grad)
    low = norm_back(raw, scale, gains[1:2, :], grad).astype(BF)
    grad_branch[...] = low
    for flip, piece in enumerate(pieces):
        grad_attended[:, slot(info[0] ^ flip, head)] = mm_nt(low, piece[...]).astype(BF)
    for m in range(micro):
        span = slice(m * rows, (m + 1) * rows)
        chance = probs[m]
        keys, values = window[m, :, :head], window[m, :, head:]
        stacked = jnp.concatenate(
            [query[span, h * head : (h + 1) * head] for h in range(heads)], axis=0
        )
        upstream = jnp.concatenate(
            [grad_attended[span, h * head : (h + 1) * head] for h in range(heads)], axis=0
        )
        grad_values = mm_tn(chance.astype(BF), upstream)
        grad_chance = mm_nt(upstream, values)
        inner = jnp.sum(chance * grad_chance, axis=-1, keepdims=True)
        grad_scores = (chance * (grad_chance - inner)).astype(BF)
        grad_stacked = mm(grad_scores, keys) * factor
        grad_keys = mm_tn(grad_scores, stacked) * factor
        for h in range(heads):
            grad_query[span, h * head : (h + 1) * head] = grad_stacked[h * rows : (h + 1) * rows]
        for index, target in enumerate((own, one, two)):
            part = slice(index * rows, (index + 1) * rows)
            target[span, :head] = grad_keys[part]
            target[span, head:] = grad_values[part]
        for index, target in enumerate(gives):
            for side in range(2):
                start = (3 + 2 * index + side) * rows
                target[side, span, :head] = grad_keys[start : start + rows].astype(BF)
                target[side, span, head:] = grad_values[start : start + rows].astype(BF)


def combine_kernel(info, own, one, two, first, second, third, own_out, one_out, two_out):
    total_own, total_one, total_two = own[...], one[...], two[...]
    for index, got in enumerate((first, second, third)):
        lower = (info[0] < (info[0] ^ (index + 1))).astype(F32)
        total_one = total_one + got[0].astype(F32)
        side = got[1].astype(F32)
        total_own = total_own + side * lower
        total_two = total_two + side * (1.0 - lower)
    own_out[...] = total_own
    one_out[...] = total_one.astype(BF)
    two_out[...] = total_two.astype(BF)


def project_back_kernel(info, own, back_one, back_two, grad_query, qkv, cosine, sine, x, grad_mixed,
                        grad_branch, attended, blocks, gains, rows_ffn, rows_attn, *refs):
    pieces = refs[:4]
    packs, grad_in = refs[4:8], refs[8]
    grad_qkv, held, natural, gain_held = refs[9:]
    tokens, model = natural.shape
    shard = blocks.shape[2]
    half = cosine.shape[1]
    head = 2 * half
    heads = grad_query.shape[1] // head
    cos, sin = cosine[...], sine[...]
    grad_own = own[...] + back_one[...].astype(F32) + back_two[...].astype(F32)
    head_gains = [None, None]
    for index in range(heads + 1):
        if index < heads:
            grad = grad_query[:, index * head : (index + 1) * head]
        else:
            grad = grad_own[:, :head]
        one, two = grad[:, :half], grad[:, half:]
        grad = jnp.concatenate((one * cos + two * sin, two * cos - one * sin), axis=1)
        raw = qkv[:, index * head : (index + 1) * head]
        scale = inverse_rms(raw)
        kind = 0 if index < heads else 1
        term = gain_back(raw, scale, grad)
        head_gains[kind] = term if head_gains[kind] is None else head_gains[kind] + term
        back = norm_back(raw, scale, gains[4 + kind : 5 + kind, :head], grad)
        grad_qkv[:, index * head : (index + 1) * head] = back.astype(BF)
    grad_qkv[:, (heads + 1) * head :] = grad_own[:, head:].astype(BF)
    for flip, piece in enumerate(pieces):
        held[info[0] ^ flip] = mm_nt(grad_qkv[...], piece[:shard, :])
    for place in range(4):
        natural[:, place * shard : (place + 1) * shard] = held[place]
    grad_normed = natural[...]
    residual = x[...].astype(F32)
    scale = inverse_rms(residual)
    first_gain = gain_back(residual, scale, grad_normed)
    total = grad_mixed[...] + norm_back(residual, scale, gains[0:1, :], grad_normed)
    grad_in[...] = total.astype(BF)
    gain_held[...] = jnp.zeros_like(gain_held)
    part = head // 4
    four = (first_gain, rows_attn[1:2, :], rows_ffn[2:3, :], rows_ffn[3:4, :])
    for place in range(4):
        for row, values in enumerate(four):
            gain_held[place, row : row + 1, :shard] = values[
                :, place * shard : (place + 1) * shard
            ]
        for row, values in enumerate(head_gains):
            gain_held[place, 4 + row : 5 + row, :part] = values[
                :, place * part : (place + 1) * part
            ]
    wide = grad_qkv.shape[1]
    att_at = wide + model
    block_at = att_at + head
    for flip, pack in enumerate(packs):
        other = info[0] ^ flip
        pack[tokens:, :] = jnp.zeros_like(pack[tokens:, :])
        pack[tokens:, : gain_held.shape[2]] = gain_held[other].astype(BF)
        pack[:tokens, :wide] = grad_qkv[...]
        pack[:tokens, wide:att_at] = grad_branch[...]
        pack[:tokens, att_at:block_at] = attended[:, slot(other, head)]
        pack[:tokens, block_at:] = jnp.zeros_like(pack[:tokens, block_at:])
        pack[:tokens, block_at : block_at + shard] = blocks[other]


def over(packs, tokens, left, right, left_width, right_width):
    total = None
    for pack in packs:
        term = mm_tn(
            pack[:tokens, left : left + left_width], pack[:tokens, right : right + right_width]
        )
        total = term if total is None else total + term
    return total.astype(BF)


def ffn_weights_kernel(shard, model, info, *refs):
    packs, first, second = refs[:4], refs[4], refs[5]
    tokens = packs[0].shape[0]
    wide = first.shape[1]
    quarter = second.shape[1] // 4
    act_at = wide + model
    for start in range(0, wide, 1024):
        first[:, start : start + 1024] = over(
            packs, tokens, act_at + quarter, start, shard, 1024
        )
    for place in range(4):
        second[:, place * quarter : (place + 1) * quarter] = over(
            packs, tokens, wide + place * shard, act_at, shard, quarter
        )


def weights_kernel(shard, model, info, *refs):
    packs, gate_up, down, first, second = refs[:4], refs[4], refs[5], refs[6], refs[7]
    tokens = packs[0].shape[0] - GAIN_ROWS
    head = model // 5 * 2
    wide = packs[0].shape[1] - model - 2 * head
    hidden = gate_up.shape[1]
    first[:, :hidden] = gate_up[...]
    first[:, hidden:] = jnp.zeros_like(first[:, hidden:])
    gains = sum(pack[tokens:, :head].astype(F32) for pack in packs)
    first[:GAIN_ROWS, hidden : hidden + head] = gains.astype(BF)
    att_at = wide + model
    second[:, :wide] = over(packs, tokens, att_at + head, 0, shard, wide)
    for place in range(4):
        start = wide + place * head
        second[:, start : start + head] = over(
            packs, tokens, wide + place * shard, att_at, shard, head
        )
    second[:, wide + 4 * head :] = down[...]


class Links:
    def __init__(self, sizes):
        self.sizes = sizes

    def index(self, section, seq, fsdp):
        return (section * self.sizes["seq"] + seq) * self.sizes["fsdp"] + fsdp

    def send(self, array, section, place):
        pairs = []
        for z in range(self.sizes["seq"]):
            for f in range(self.sizes["fsdp"]):
                to_section, to_z, to_f = place(z, f)
                if 0 <= to_z < self.sizes["seq"]:
                    pairs.append((self.index(section, z, f), self.index(to_section, to_z, to_f)))
        return lax.ppermute(array, AXES, pairs)

    def along(self, array, section, by):
        return self.send(array, section, lambda z, f: (section, z + by, f))

    def across(self, array, section, flip):
        return self.send(array, section, lambda z, f: (section, z, f ^ flip))

    def cross(self, array, section):
        return self.send(array, section, lambda z, f: (1 - section, z, f))

    def swap(self, array):
        pairs = []
        for section in range(2):
            for z in range(self.sizes["seq"]):
                for f in range(self.sizes["fsdp"]):
                    pairs.append((self.index(section, z, f), self.index(1 - section, z, f)))
        return lax.ppermute(array, AXES, pairs)


def body(sizes, hidden_in, cotangent, positions, attn_gain, w_query, w_key, w_value, query_gain,
         key_gain, w_output, post_attn_gain, ffn_gain, w_gate, w_up, w_down, post_ffn_gain):
    section = lax.axis_index("section")
    seq = lax.axis_index("seq")
    fsdp = lax.axis_index("fsdp")
    is_first = section == 0
    micro, rows, model = hidden_in.shape
    tokens = micro * rows
    shard = w_query.shape[1]
    shards = sizes["fsdp"]
    heads_width, head = w_query.shape[2], w_key.shape[2]
    wide = heads_width + 2 * head
    hidden = w_gate.shape[2]
    quarter = hidden // shards
    assert shards == 4 and 2 * shards * rows == WIN and heads_width == shards * head
    links = Links(sizes)
    info = jnp.stack([fsdp, seq, section]).astype(jnp.int32)

    row = jnp.concatenate(
        (attn_gain[0], post_attn_gain[0], ffn_gain[0], post_ffn_gain[0], query_gain[0], key_gain[0])
    )
    row = jnp.pad(row[None], ((0, GAIN_ROWS - 1), (0, wide - row.shape[0])))
    own_shards = (
        jnp.concatenate(
            (jnp.concatenate((w_query[0], w_key[0], w_value[0]), axis=1), row), axis=0
        ),
        w_output[0],
        jnp.concatenate((w_gate[0], w_up[0]), axis=1),
        w_down[0],
    )

    def gather(arrays, target):
        return [
            [array] + [links.across(array, target, flip) for flip in range(1, shards)]
            for array in arrays
        ]

    half = head // 2
    place = positions.reshape(tokens, 1)
    frequency = ROPE_BASE ** (-2.0 * jnp.arange(half, dtype=F32) / head)
    angles = place.astype(F32) * frequency[None, :]
    cosine, sine = jnp.cos(angles), jnp.sin(angles)
    limit = jnp.minimum(place, WIN - 1)
    query_place = jnp.tile((seq * shards + fsdp) * rows + jnp.arange(rows), micro)[:, None]
    starts = [(seq - back) * shards + fsdp for back in range(3)]
    for flip in range(1, shards):
        other = fsdp ^ flip
        starts.append((seq - 1) * shards + other)
        starts.append(jnp.where(other < fsdp, seq, seq - 2) * shards + other)
    key_place = (jnp.stack(starts)[:, None] * rows + jnp.arange(rows)[None, :]).reshape(1, -1)
    query_place, key_place = query_place.astype(jnp.int32), key_place.astype(jnp.int32)
    span = key_place.shape[1]

    def gain_table(pieces):
        return call(
            gains_kernel, info, pieces, [shape((8, model), F32)],
            [pltpu.VMEM((shards, GAIN_ROWS, 768), F32)],
        )[0]

    def forward(x, weights, target):
        first, out, gate_up_w, down_w = weights
        gains = gain_table(first)
        blocks, qkv, query, own = call(
            project_kernel, info, [x, gains, cosine, sine] + first,
            [shape((shards, tokens, shard), BF), shape((tokens, wide), F32),
             shape((tokens, heads_width), BF), shape((tokens, 2 * head), BF)],
            flops=2 * tokens * model * wide,
        )
        one, two = links.along(own, target, 1), links.along(own, target, 2)
        sent = call(
            select_kernel, info, [own, one, two], [shape((2, tokens, 2 * head), BF)] * (shards - 1)
        )
        got = [links.across(array, target, 1 + i) for i, array in enumerate(sent)]
        window, probs, attended, branch, mixed, ffn_blocks = call(
            functools.partial(attend_kernel, micro), info,
            [query, own, one, two] + got + [x, gains, limit, query_place, key_place] + out,
            [shape((micro, span, 2 * head), BF), shape((micro, shards * rows, span), F32),
             shape((tokens, heads_width), BF), shape((tokens, model), F32),
             shape((tokens, model), F32), shape((shards, tokens, shard), BF)],
            flops=2 * tokens * heads_width * (2 * span + model),
        )
        gate_up, activated, down, result = call(
            ffn_kernel, info, [ffn_blocks, mixed, gains] + gate_up_w + down_w,
            [shape((tokens, 2 * hidden), F32), shape((tokens, hidden), BF),
             shape((tokens, model), F32), shape((tokens, model), BF)],
            flops=6 * tokens * hidden * model,
        )
        saved = dict(
            x=x, gains=gains, blocks=blocks, qkv=qkv, query=query, window=window, probs=probs,
            attended=attended, branch=branch, mixed=mixed, ffn_blocks=ffn_blocks, gate_up=gate_up,
            activated=activated, down=down,
        )
        return result, saved

    def back_ffn(upstream, s, weights):
        _, _, gate_up_w, down_w = weights
        outs = call(
            ffn_back_kernel, info,
            [upstream, s["mixed"], s["down"], s["gate_up"], s["activated"], s["ffn_blocks"],
             s["gains"]] + gate_up_w + down_w,
            [shape((tokens, 2 * hidden + model + quarter + 256), BF)] * shards
            + [shape((tokens, model), F32), shape((8, model), F32)],
            [pltpu.VMEM((tokens, hidden), F32), pltpu.VMEM((tokens, 2 * hidden), BF),
             pltpu.VMEM((shards, tokens, shard), F32), pltpu.VMEM((tokens, model), F32)],
            flops=6 * tokens * hidden * model,
        )
        return outs[:shards], outs[shards], outs[shards + 1]

    def back_attend(grad_mixed, s, weights):
        pair = [shape((tokens, 2 * head), F32)] * 3
        outs = call(
            functools.partial(attend_back_kernel, micro), info,
            [grad_mixed, s["branch"], s["window"], s["probs"], s["query"], s["gains"]] + weights[1],
            [shape((tokens, model), BF), shape((tokens, heads_width), F32)] + pair
            + [shape((2, tokens, 2 * head), BF)] * (shards - 1) + [shape((8, model), F32)],
            [pltpu.VMEM((tokens, heads_width), BF)],
            flops=2 * tokens * heads_width * (4 * span + model),
        )
        return outs[0], outs[1], outs[2:5], outs[5:8], outs[8]

    def back_window(kept, gives, target):
        got = [links.across(array, target, 1 + i) for i, array in enumerate(gives)]
        own, one, two = call(
            combine_kernel, info, list(kept) + got,
            [shape((tokens, 2 * head), F32)] + [shape((tokens, 2 * head), BF)] * 2,
        )
        return own, links.along(one, target, -1), links.along(two, target, -2)

    def back_project(window_grads, grad_query, grad_mixed, grad_branch, rows_ffn, rows_attn, s,
                     weights):
        outs = call(
            project_back_kernel, info,
            list(window_grads) + [grad_query, s["qkv"], cosine, sine, s["x"], grad_mixed,
            grad_branch, s["attended"], s["blocks"], s["gains"], rows_ffn, rows_attn] + weights[0],
            [shape((tokens + GAIN_ROWS, wide + model + head + 256), BF)] * shards
            + [shape((tokens, model), BF)],
            [pltpu.VMEM((tokens, wide), BF), pltpu.VMEM((shards, tokens, shard), F32),
             pltpu.VMEM((tokens, model), F32), pltpu.VMEM((shards, GAIN_ROWS, 256), F32)],
            flops=2 * tokens * wide * model,
        )
        return outs[:shards], outs[shards]

    def exchange(packs, target):
        return [packs[0]] + [links.across(packs[i], target, i) for i in range(1, shards)]

    total_width = 2 * hidden + 512

    def ffn_weights(packs):
        return call(
            functools.partial(ffn_weights_kernel, shard, model), info, list(packs),
            [shape((shard, 2 * hidden), BF), shape((shard, hidden), BF)],
            flops=2 * shards * tokens * shard * 3 * hidden,
        )

    def attn_weights(packs, ffn):
        return call(
            functools.partial(weights_kernel, shard, model), info, list(packs) + list(ffn),
            [shape((shard, total_width), BF)] * 2,
            flops=2 * shards * tokens * shard * (total_width - hidden),
        )

    tie = lax.optimization_barrier

    def backward(upstream, s, weights, target, other=None):
        ffn_packs, grad_mixed, rows_ffn = back_ffn(upstream, s, weights)
        ffn_packs = exchange(ffn_packs, target)
        grad_branch, grad_query, kept, gives, rows_attn = back_attend(grad_mixed, s, weights)
        window_grads = back_window(kept, gives, target)
        if other is not None:
            ffn = ffn_weights(ffn_packs)
            window_grads, ffn, other = tie((window_grads, ffn, other))
        attn_packs, grad_in = back_project(
            window_grads, grad_query, grad_mixed, grad_branch, rows_ffn, rows_attn, s, weights
        )
        if other is None:
            ffn = ffn_weights(ffn_packs)
        return ffn, attn_packs, grad_in, other

    first = gather(own_shards, 0)
    x_first = hidden_in.reshape(tokens, model)
    result_a, saved_a = forward(x_first, first, 0)
    token = links.cross(saved_a["window"][0, -16:, :128], 0)
    later, token = lax.optimization_barrier((own_shards, token))
    tied = lax.dynamic_update_slice(later[0], token, (shard, wide - token.shape[1]))
    second = gather((tied,) + later[1:], 1)
    middle = links.cross(result_a, 0)
    result_b, saved_b = forward(middle, second, 1)

    ffn, attn_packs, grad_b, _ = backward(cotangent.reshape(tokens, model), saved_b, second, 1)
    upstream = links.cross(grad_b, 1)
    b_first, b_second = attn_weights(exchange(attn_packs, 1), ffn)
    upstream, b_first, b_second = tie((upstream, b_first, b_second))
    half_b = jnp.where(is_first, links.cross(b_first, 1), b_second)

    ffn, attn_packs, grad_a, half_b = backward(upstream, saved_a, first, 0, half_b)
    part_b = lax.psum(half_b, "seq")
    attn_packs, part_b = tie((exchange(attn_packs, 0), part_b))
    a_first, a_second = attn_weights(attn_packs, ffn)
    half_a = jnp.where(is_first, a_first, links.cross(a_second, 0))
    part_a = lax.psum(half_a, "seq")

    mine = jnp.where(is_first, part_a, part_b)
    theirs = links.swap(jnp.where(is_first, part_b, part_a))
    total_first = jnp.where(is_first, mine, theirs)
    total_second = jnp.where(is_first, theirs, mine).astype(F32)
    gain_out = total_first[:8, 2 * hidden : 2 * hidden + shard].astype(F32)

    def unfold(array):
        count = array.shape[1] // shards
        return jnp.concatenate(
            [array[:, i * count : (i + 1) * count] for i in range(shards)], axis=0
        ).T

    part = head // shards
    section_outputs = jnp.where(is_first, result_a, result_b).reshape(1, micro, rows, model)
    input_grads = jnp.where(is_first, grad_a, grad_b).reshape(1, micro, rows, model)
    return (
        section_outputs,
        input_grads,
        gain_out[0:1],
        total_second[None, :, :heads_width],
        total_second[None, :, heads_width : heads_width + head],
        total_second[None, :, heads_width + head : wide],
        gain_out[4:5, :part],
        gain_out[5:6, :part],
        unfold(total_second[:, wide : wide + heads_width])[None],
        gain_out[1:2],
        gain_out[2:3],
        total_first[None, :, :hidden].astype(F32),
        total_first[None, :, hidden : 2 * hidden].astype(F32),
        unfold(total_second[:, wide + heads_width :])[None],
        gain_out[3:4],
    )


def solution(mesh):
    rows = P(None, ("seq", "fsdp"), None)
    vector, matrix = P("section", "fsdp"), P("section", "fsdp", None)
    weights = (vector, matrix, matrix, matrix, vector, vector, matrix, vector, vector, matrix,
               matrix, matrix, vector)
    out_rows = P("section", None, ("seq", "fsdp"), None)
    return jax.shard_map(
        functools.partial(body, dict(mesh.shape)),
        mesh=mesh,
        in_specs=(rows, rows, P(None, ("seq", "fsdp"))) + weights,
        out_specs=(out_rows, out_rows) + weights,
        check_vma=False,
    )
```

```python
import functools

import jax
import jax.numpy as jnp
from jax import lax
from jax.experimental import pallas as pl
from jax.experimental.pallas import tpu as pltpu
from jax.sharding import PartitionSpec as P

WIN = 512
EPSILON = 1e-06
ROPE_BASE = 10000.0
NEG_LARGE = -1e30
AXES = ("section", "seq", "fsdp")
BF = jnp.bfloat16
F32 = jnp.float32
GAIN_ROWS = 16
INTERPRET = False


def mm(left, right):
    return lax.dot_general(left, right, (((1,), (0,)), ((), ())), preferred_element_type=F32)


def mm_nt(left, right):
    return lax.dot_general(left, right, (((1,), (1,)), ((), ())), preferred_element_type=F32)


def mm_tn(left, right):
    return lax.dot_general(left, right, (((0,), (0,)), ((), ())), preferred_element_type=F32)


def inverse_rms(values):
    return lax.rsqrt(jnp.mean(values * values, axis=-1, keepdims=True) + EPSILON)


def norm_back(values, scale, gain, grad):
    weighted = grad * gain
    inner = jnp.mean(values * weighted, axis=-1, keepdims=True)
    return scale * weighted - values * (scale * scale * scale * inner)


def gain_back(values, scale, grad):
    return jnp.sum(values * scale * grad, axis=0, keepdims=True)


def call(kernel, info, arrays, outs, scratch=(), flops=0, section=None):
    if section is not None:
        inner = kernel

        def kernel(info, *refs):
            @pl.when(info[2] == section)
            def _():
                inner(info, *refs)

    smem = pl.BlockSpec(memory_space=pltpu.SMEM)
    vmem = pl.BlockSpec(memory_space=pltpu.VMEM)
    size = sum(a.size * a.dtype.itemsize for a in arrays)
    size += sum(a.size * a.dtype.itemsize for a in outs)
    return pl.pallas_call(
        kernel,
        out_shape=outs,
        in_specs=[smem] + [vmem] * len(arrays),
        out_specs=[vmem] * len(outs),
        scratch_shapes=list(scratch),
        compiler_params=pltpu.CompilerParams(vmem_limit_bytes=40 * 1024 * 1024),
        cost_estimate=pl.CostEstimate(flops=flops, bytes_accessed=size, transcendentals=0),
        interpret=INTERPRET,
    )(info, *arrays)


def shape(dims, kind):
    return jax.ShapeDtypeStruct(tuple(dims), kind)


def slot(index, width):
    return pl.ds(pl.multiple_of(index * width, width), width)


def gains_kernel(info, *refs):
    pieces, out, held = refs[:-2], refs[-2], refs[-1]
    count = len(pieces)
    shard = out.shape[1] // count
    rows = pieces[0].shape[0] - GAIN_ROWS
    part = shard * 2 // 5
    for flip, piece in enumerate(pieces):
        held[info[0] ^ flip] = piece[rows : rows + GAIN_ROWS, : held.shape[2]].astype(F32)
    out[...] = jnp.zeros_like(out)
    for place in range(count):
        for row in range(4):
            out[row : row + 1, place * shard : (place + 1) * shard] = held[
                place, 0:1, row * shard : (row + 1) * shard
            ]
        for row in range(2):
            start = 4 * shard + row * part
            out[4 + row : 5 + row, place * part : (place + 1) * part] = held[
                place, 0:1, start : start + part
            ]


def prepare_kernel(info, query, key, value, *refs):
    gains, out = refs[:-1], refs[-1]
    shard = query.shape[1]
    start = 0
    for ref in (query, key, value):
        out[:shard, start : start + ref.shape[2]] = ref[0]
        start += ref.shape[2]
    out[shard:, :] = jnp.zeros_like(out[shard:, :])
    start = 0
    for ref in gains:
        out[shard : shard + 1, start : start + ref.shape[1]] = ref[...]
        start += ref.shape[1]


def rope_store(target, rows, start, normal, cos, sin):
    half = cos.shape[1]
    one, two = normal[:, :half], normal[:, half:]
    target[rows, start : start + half] = (one * cos - two * sin).astype(BF)
    target[rows, start + half : start + 2 * half] = (two * cos + one * sin).astype(BF)


def project_window_kernel(micro, info, x, one, two, *refs):
    got, (gains, cosine, sine, wide_cos, wide_sin) = refs[:3], refs[3:8]
    pieces = refs[8:12]
    blocks, qkv, query, window, held = refs[12:]
    rows = x.shape[0] // micro
    shard = blocks.shape[2]
    head = window.shape[2] // 2
    heads_width = query.shape[1]
    for m in range(micro):
        span = slice(m * rows, (m + 1) * rows)
        parts = [x[span], one[span], two[span]]
        for ref in got:
            parts += [ref[0, span], ref[1, span]]
        values = jnp.concatenate(parts, axis=0).astype(F32)
        normed = values * inverse_rms(values) * gains[0:1, :]
        for place in range(len(pieces)):
            held[place] = normed[:, place * shard : (place + 1) * shard].astype(BF)
        total = None
        for flip, piece in enumerate(pieces):
            term = mm(held[info[0] ^ flip], piece[:shard, heads_width:])
            total = term if total is None else total + term
        for place in range(len(pieces)):
            blocks[place, span] = held[place, :rows]
        qkv[span, heads_width:] = total[:rows]
        raw = total[:, :head]
        normal = raw * inverse_rms(raw) * gains[5:6, :head]
        rope_store(window.at[m], slice(None), 0, normal, wide_cos[...], wide_sin[...])
        window[m, :, head:] = total[:, head:].astype(BF)
    total = None
    for flip, piece in enumerate(pieces):
        term = mm(blocks[info[0] ^ flip], piece[:shard, :heads_width])
        total = term if total is None else total + term
    qkv[:, :heads_width] = total
    for start in range(0, heads_width, head):
        raw = total[:, start : start + head]
        normal = raw * inverse_rms(raw) * gains[4:5, :head]
        rope_store(query, slice(None), start, normal, cosine[...], sine[...])


def finish_kernel(info, part_a, part_b, theirs, *outs):
    query, key, value, out, gate, up, down = outs[:7]
    vectors = outs[7:]
    shard, hidden = gate.shape[1], gate.shape[2]

    def emit(first, second):
        gate[0] = first[:, :hidden].astype(F32)
        up[0] = first[:, hidden : 2 * hidden].astype(F32)
        for row, ref in enumerate(vectors):
            ref[...] = first[:GAIN_ROWS, 2 * hidden : 2 * hidden + ref.shape[1]].astype(F32)[
                row : row + 1
            ]
        start = 0
        for ref in (query, key, value):
            ref[0] = second[:, start : start + ref.shape[2]].astype(F32)
            start += ref.shape[2]
        for ref in (out, down):
            rows = ref.shape[1]
            for place in range(4):
                block = second[:, start : start + rows].astype(F32)
                ref[0, :, place * shard : (place + 1) * shard] = block.T
                start += rows

    @pl.when(info[2] == 0)
    def _():
        emit(part_a, theirs)

    @pl.when(info[2] == 1)
    def _():
        emit(theirs, part_b)


def project_kernel(info, x, gains, cosine, sine, *refs):
    pieces = refs[:-4]
    blocks, qkv, query, own = refs[-4:]
    shard = blocks.shape[2]
    half = cosine.shape[1]
    head = 2 * half
    residual = x[...].astype(F32)
    normed = residual * inverse_rms(residual) * gains[0:1, :]
    for place in range(len(pieces)):
        blocks[place] = normed[:, place * shard : (place + 1) * shard].astype(BF)
    total = None
    for flip, piece in enumerate(pieces):
        term = mm(blocks[info[0] ^ flip], piece[:shard, :])
        total = term if total is None else total + term
    qkv[...] = total
    cos, sin = cosine[...], sine[...]
    heads = query.shape[1] // head
    for index in range(heads + 1):
        raw = total[:, index * head : (index + 1) * head]
        row = 4 if index < heads else 5
        normal = raw * inverse_rms(raw) * gains[row : row + 1, :head]
        one, two = normal[:, :half], normal[:, half:]
        target, start = (query, index * head) if index < heads else (own, 0)
        target[:, start : start + half] = (one * cos - two * sin).astype(BF)
        target[:, start + half : start + head] = (two * cos + one * sin).astype(BF)
    own[:, head:] = total[:, (heads + 1) * head :].astype(BF)


def select_kernel(info, own, one, two, *outs):
    for index, out in enumerate(outs):
        lower = (info[0] < (info[0] ^ (index + 1))).astype(F32)
        out[0] = one[...]
        mixed = own[...].astype(F32) * lower + two[...].astype(F32) * (1.0 - lower)
        out[1] = mixed.astype(BF)


def window_kernel(micro, info, own, one, two, *refs):
    got, window = refs[:3], refs[3]
    rows = own.shape[0] // micro
    for m in range(micro):
        span = slice(m * rows, (m + 1) * rows)
        parts = [own[span], one[span], two[span]]
        for ref in got:
            parts += [ref[0, span], ref[1, span]]
        for index, part in enumerate(parts):
            window[m, index * rows : (index + 1) * rows] = part


def attend_kernel(micro, info, query, *refs):
    x, gains, limit, query_place, key_place = refs[:5]
    pieces = refs[5:9]
    if len(refs) == 9 + 1 + 5:
        window = refs[9]
        outs = refs[10:]
    else:
        window = refs[15]
        outs = refs[16:]
        window_kernel(micro, info, *refs[9:15], window)
    probs, attended, branch, mixed, blocks = outs
    rows = query.shape[0] // micro
    head = window.shape[2] // 2
    heads = query.shape[1] // head
    shard = blocks.shape[2]
    for m in range(micro):
        span = slice(m * rows, (m + 1) * rows)
        distance = query_place[span] - key_place[...]
        allowed = (distance >= 0) & (distance <= limit[span])
        bias = jnp.where(allowed, 0.0, NEG_LARGE)
        bias = jnp.concatenate([bias] * heads, axis=0)
        stacked = jnp.concatenate(
            [query[span, h * head : (h + 1) * head] for h in range(heads)], axis=0
        )
        scores = mm_nt(stacked, window[m, :, :head]) * head ** (-0.5) + bias
        exponent = jnp.exp(scores - jnp.max(scores, axis=-1, keepdims=True))
        chance = exponent / jnp.sum(exponent, axis=-1, keepdims=True)
        probs[m] = chance
        result = mm(chance.astype(BF), window[m, :, head:]).astype(BF)
        for h in range(heads):
            attended[span, h * head : (h + 1) * head] = result[h * rows : (h + 1) * rows]
    total = None
    for flip, piece in enumerate(pieces):
        term = mm(attended[:, slot(info[0] ^ flip, head)], piece[:head, :])
        total = term if total is None else total + term
    branch[...] = total
    value = x[...].astype(F32) + total * inverse_rms(total) * gains[1:2, :]
    mixed[...] = value
    normed = value * inverse_rms(value) * gains[2:3, :]
    for place in range(len(pieces)):
        blocks[place] = normed[:, place * shard : (place + 1) * shard].astype(BF)


def gelu_parts(gate):
    c = 0.7978845608028654
    inner = jnp.tanh(c * (gate + 0.044715 * gate * gate * gate))
    value = 0.5 * gate * (1.0 + inner)
    slope = 0.5 * (1.0 + inner) + 0.5 * gate * (1.0 - inner * inner) * c * (
        1.0 + 3 * 0.044715 * gate * gate
    )
    return value, slope


def ffn_kernel(info, blocks, mixed, gains, *refs):
    gate_up_pieces, down_pieces = refs[:4], refs[4:8]
    gate_up, activated, down, result = refs[8:]
    hidden = activated.shape[1]
    width = 512
    for start in range(0, hidden, width):
        both = []
        for base in (start, hidden + start):
            total = None
            for flip, piece in enumerate(gate_up_pieces):
                term = mm(blocks[info[0] ^ flip], piece[:, base : base + width])
                total = term if total is None else total + term
            gate_up[:, base : base + width] = total
            both.append(total)
        value, _ = gelu_parts(both[0])
        activated[:, start : start + width] = (value * both[1]).astype(BF)
    total = None
    for flip, piece in enumerate(down_pieces):
        quarter = hidden // 4
        term = mm(activated[:, slot(info[0] ^ flip, quarter)], piece[-quarter:, :])
        total = term if total is None else total + term
    down[...] = total
    result[...] = (mixed[...] + total * inverse_rms(total) * gains[3:4, :]).astype(BF)


def ffn_back_kernel(info, upstream, mixed, down, gate_up, activated, blocks, gains, *refs):
    gate_up_pieces, down_pieces = refs[:4], refs[4:8]
    packs, grad_mixed, gain_rows = refs[8:12], refs[12], refs[13]
    grad_act, grad_gate_up, held, natural = refs[14:]
    hidden = activated.shape[1]
    model = mixed.shape[1]
    shard = blocks.shape[2]
    top = upstream[...].astype(F32)
    raw = down[...]
    scale = inverse_rms(raw)
    grad_down = norm_back(raw, scale, gains[3:4, :], top).astype(BF)
    gain_rows[...] = jnp.zeros_like(gain_rows)
    gain_rows[3:4, :] = gain_back(raw, scale, top)
    act_at = 2 * hidden + model
    block_at = act_at + hidden // 4
    for flip, piece in enumerate(down_pieces):
        quarter = hidden // 4
        grad_act[:, slot(info[0] ^ flip, quarter)] = mm_nt(grad_down, piece[-quarter:, :])
    for flip, pack in enumerate(packs):
        pack[:, 2 * hidden : act_at] = grad_down
        pack[:, act_at:block_at] = activated[:, slot(info[0] ^ flip, hidden // 4)]
        pack[:, block_at:] = jnp.zeros_like(pack[:, block_at:])
        pack[:, block_at : block_at + shard] = blocks[info[0] ^ flip]
    width = 512
    for start in range(0, hidden, width):
        value, slope = gelu_parts(gate_up[:, start : start + width])
        up = gate_up[:, hidden + start : hidden + start + width]
        grad = grad_act[:, start : start + width]
        grad_gate_up[:, start : start + width] = (grad * up * slope).astype(BF)
        grad_gate_up[:, hidden + start : hidden + start + width] = (grad * value).astype(BF)
    for pack in packs:
        pack[:, : 2 * hidden] = grad_gate_up[...]
    for flip, piece in enumerate(gate_up_pieces):
        held[info[0] ^ flip] = mm_nt(grad_gate_up[...], piece[...])
    for place in range(4):
        natural[:, place * shard : (place + 1) * shard] = held[place]
    grad_in = natural[...]
    raw = mixed[...]
    scale = inverse_rms(raw)
    gain_rows[2:3, :] = gain_back(raw, scale, grad_in)
    grad_mixed[...] = top + norm_back(raw, scale, gains[2:3, :], grad_in)


def attend_back_kernel(micro, info, grad_mixed, branch, window, probs, query, gains, *refs):
    pieces = refs[:4]
    grad_branch, grad_query, own, one, two = refs[4:9]
    gives, gain_rows, grad_attended = refs[9:12], refs[12], refs[13]
    rows = own.shape[0] // micro
    head = own.shape[1] // 2
    heads = query.shape[1] // head
    factor = head ** (-0.5)
    raw = branch[...]
    scale = inverse_rms(raw)
    grad = grad_mixed[...]
    gain_rows[...] = jnp.zeros_like(gain_rows)
    gain_rows[1:2, :] = gain_back(raw, scale, grad)
    low = norm_back(raw, scale, gains[1:2, :], grad).astype(BF)
    grad_branch[...] = low
    for flip, piece in enumerate(pieces):
        grad_attended[:, slot(info[0] ^ flip, head)] = mm_nt(low, piece[:head, :]).astype(BF)
    for m in range(micro):
        span = slice(m * rows, (m + 1) * rows)
        chance = probs[m]
        keys, values = window[m, :, :head], window[m, :, head:]
        stacked = jnp.concatenate(
            [query[span, h * head : (h + 1) * head] for h in range(heads)], axis=0
        )
        upstream = jnp.concatenate(
            [grad_attended[span, h * head : (h + 1) * head] for h in range(heads)], axis=0
        )
        grad_values = mm_tn(chance.astype(BF), upstream)
        grad_chance = mm_nt(upstream, values)
        inner = jnp.sum(chance * grad_chance, axis=-1, keepdims=True)
        grad_scores = (chance * (grad_chance - inner)).astype(BF)
        grad_stacked = mm(grad_scores, keys) * factor
        grad_keys = mm_tn(grad_scores, stacked) * factor
        for h in range(heads):
            grad_query[span, h * head : (h + 1) * head] = grad_stacked[h * rows : (h + 1) * rows]
        for index, target in enumerate((own, one, two)):
            part = slice(index * rows, (index + 1) * rows)
            target[span, :head] = grad_keys[part]
            target[span, head:] = grad_values[part]
        for index, target in enumerate(gives):
            for side in range(2):
                start = (3 + 2 * index + side) * rows
                target[side, span, :head] = grad_keys[start : start + rows].astype(BF)
                target[side, span, head:] = grad_values[start : start + rows].astype(BF)


def combine_kernel(info, own, one, two, first, second, third, own_out, one_out, two_out):
    total_own, total_one, total_two = own[...], one[...], two[...]
    for index, got in enumerate((first, second, third)):
        lower = (info[0] < (info[0] ^ (index + 1))).astype(F32)
        total_one = total_one + got[0].astype(F32)
        side = got[1].astype(F32)
        total_own = total_own + side * lower
        total_two = total_two + side * (1.0 - lower)
    own_out[...] = total_own
    one_out[...] = total_one.astype(BF)
    two_out[...] = total_two.astype(BF)


def project_back_kernel(info, own, back_one, back_two, grad_query, qkv, cosine, sine, x, grad_mixed,
                        grad_branch, attended, blocks, gains, rows_ffn, rows_attn, *refs):
    pieces = refs[:4]
    packs, grad_in = refs[4:8], refs[8]
    grad_qkv, held, natural, gain_held = refs[9:]
    tokens, model = natural.shape
    shard = blocks.shape[2]
    half = cosine.shape[1]
    head = 2 * half
    heads = grad_query.shape[1] // head
    cos, sin = cosine[...], sine[...]
    grad_own = own[...] + back_one[...].astype(F32) + back_two[...].astype(F32)
    head_gains = [None, None]
    for index in range(heads + 1):
        if index < heads:
            grad = grad_query[:, index * head : (index + 1) * head]
        else:
            grad = grad_own[:, :head]
        one, two = grad[:, :half], grad[:, half:]
        grad = jnp.concatenate((one * cos + two * sin, two * cos - one * sin), axis=1)
        raw = qkv[:, index * head : (index + 1) * head]
        scale = inverse_rms(raw)
        kind = 0 if index < heads else 1
        term = gain_back(raw, scale, grad)
        head_gains[kind] = term if head_gains[kind] is None else head_gains[kind] + term
        back = norm_back(raw, scale, gains[4 + kind : 5 + kind, :head], grad)
        grad_qkv[:, index * head : (index + 1) * head] = back.astype(BF)
    grad_qkv[:, (heads + 1) * head :] = grad_own[:, head:].astype(BF)
    for flip, piece in enumerate(pieces):
        held[info[0] ^ flip] = mm_nt(grad_qkv[...], piece[:shard, :])
    for place in range(4):
        natural[:, place * shard : (place + 1) * shard] = held[place]
    grad_normed = natural[...]
    residual = x[...].astype(F32)
    scale = inverse_rms(residual)
    first_gain = gain_back(residual, scale, grad_normed)
    total = grad_mixed[...] + norm_back(residual, scale, gains[0:1, :], grad_normed)
    grad_in[...] = total.astype(BF)
    gain_held[...] = jnp.zeros_like(gain_held)
    part = head // 4
    four = (first_gain, rows_attn[1:2, :], rows_ffn[2:3, :], rows_ffn[3:4, :])
    for place in range(4):
        for row, values in enumerate(four):
            gain_held[place, row : row + 1, :shard] = values[
                :, place * shard : (place + 1) * shard
            ]
        for row, values in enumerate(head_gains):
            gain_held[place, 4 + row : 5 + row, :part] = values[
                :, place * part : (place + 1) * part
            ]
    wide = grad_qkv.shape[1]
    att_at = wide + model
    block_at = att_at + head
    for flip, pack in enumerate(packs):
        other = info[0] ^ flip
        pack[tokens:, :] = jnp.zeros_like(pack[tokens:, :])
        pack[tokens:, : gain_held.shape[2]] = gain_held[other].astype(BF)
        pack[:tokens, :wide] = grad_qkv[...]
        pack[:tokens, wide:att_at] = grad_branch[...]
        pack[:tokens, att_at:block_at] = attended[:, slot(other, head)]
        pack[:tokens, block_at:] = jnp.zeros_like(pack[:tokens, block_at:])
        pack[:tokens, block_at : block_at + shard] = blocks[other]


def over(packs, tokens, left, right, left_width, right_width):
    total = None
    for pack in packs:
        term = mm_tn(
            pack[:tokens, left : left + left_width], pack[:tokens, right : right + right_width]
        )
        total = term if total is None else total + term
    return total.astype(BF)


def ffn_weights_kernel(shard, model, info, *refs):
    packs, first, second = refs[:4], refs[4], refs[5]
    tokens = packs[0].shape[0]
    wide = first.shape[1]
    quarter = second.shape[1] // 4
    act_at = wide + model
    for start in range(0, wide, 1024):
        first[:, start : start + 1024] = over(
            packs, tokens, act_at + quarter, start, shard, 1024
        )
    for place in range(4):
        second[:, place * quarter : (place + 1) * quarter] = over(
            packs, tokens, wide + place * shard, act_at, shard, quarter
        )


def weights_kernel(shard, model, info, *refs):
    packs, gate_up, down, first, second = refs[:4], refs[4], refs[5], refs[6], refs[7]
    tokens = packs[0].shape[0] - GAIN_ROWS
    head = model // 5 * 2
    wide = packs[0].shape[1] - model - 2 * head
    hidden = gate_up.shape[1]
    first[:, :hidden] = gate_up[...]
    first[:, hidden:] = jnp.zeros_like(first[:, hidden:])
    gains = sum(pack[tokens:, :head].astype(F32) for pack in packs)
    first[:GAIN_ROWS, hidden : hidden + head] = gains.astype(BF)
    att_at = wide + model
    second[:, :wide] = over(packs, tokens, att_at + head, 0, shard, wide)
    for place in range(4):
        start = wide + place * head
        second[:, start : start + head] = over(
            packs, tokens, wide + place * shard, att_at, shard, head
        )
    second[:, wide + 4 * head :] = down[...]


class Links:
    def __init__(self, sizes):
        self.sizes = sizes

    def index(self, section, seq, fsdp):
        return (section * self.sizes["seq"] + seq) * self.sizes["fsdp"] + fsdp

    def send(self, array, section, place):
        pairs = []
        for z in range(self.sizes["seq"]):
            for f in range(self.sizes["fsdp"]):
                to_section, to_z, to_f = place(z, f)
                if 0 <= to_z < self.sizes["seq"]:
                    pairs.append((self.index(section, z, f), self.index(to_section, to_z, to_f)))
        return lax.ppermute(array, AXES, pairs)

    def along(self, array, section, by):
        return self.send(array, section, lambda z, f: (section, z + by, f))

    def across(self, array, section, flip):
        return self.send(array, section, lambda z, f: (section, z, f ^ flip))

    def cross(self, array, section):
        return self.send(array, section, lambda z, f: (1 - section, z, f))

    def swap(self, array):
        pairs = []
        for section in range(2):
            for z in range(self.sizes["seq"]):
                for f in range(self.sizes["fsdp"]):
                    pairs.append((self.index(section, z, f), self.index(1 - section, z, f)))
        return lax.ppermute(array, AXES, pairs)


def body(sizes, hidden_in, cotangent, positions, attn_gain, w_query, w_key, w_value, query_gain,
         key_gain, w_output, post_attn_gain, ffn_gain, w_gate, w_up, w_down, post_ffn_gain):
    section = lax.axis_index("section")
    seq = lax.axis_index("seq")
    fsdp = lax.axis_index("fsdp")
    is_first = section == 0
    micro, rows, model = hidden_in.shape
    tokens = micro * rows
    shard = w_query.shape[1]
    shards = sizes["fsdp"]
    heads_width, head = w_query.shape[2], w_key.shape[2]
    wide = heads_width + 2 * head
    hidden = w_gate.shape[2]
    quarter = hidden // shards
    assert shards == 4 and 2 * shards * rows == WIN and heads_width == shards * head
    links = Links(sizes)
    tie = lax.optimization_barrier
    info = jnp.stack([fsdp, seq, section]).astype(jnp.int32)

    prepared = call(
        prepare_kernel, info,
        [w_query, w_key, w_value, attn_gain, post_attn_gain, ffn_gain, post_ffn_gain, query_gain,
         key_gain],
        [shape((shard + GAIN_ROWS, wide), BF)],
    )[0]
    own_shards = (
        prepared,
        jnp.concatenate((w_output[0], w_down[0]), axis=0),
        jnp.concatenate((w_gate[0], w_up[0]), axis=1),
    )

    def gather_first(array, target):
        return [array] + [links.across(array, target, flip) for flip in range(1, shards)]

    def gather_rest(arrays, target):
        rows_of, columns_of = arrays
        one, two = links.across(columns_of, target, 1), links.across(columns_of, target, 2)
        columns = [columns_of, one, two, links.across(two, target, 1)]
        one, two = links.across(rows_of, target, 1), links.across(rows_of, target, 2)
        return [[rows_of, one, two, links.across(one, target, 2)], columns]

    half = head // 2
    limit = jnp.minimum(positions.reshape(tokens, 1), WIN - 1)
    query_place = jnp.tile((seq * shards + fsdp) * rows + jnp.arange(rows), micro)[:, None]
    starts = [(seq - back) * shards + fsdp for back in range(3)]
    for flip in range(1, shards):
        other = fsdp ^ flip
        starts.append((seq - 1) * shards + other)
        starts.append(jnp.where(other < fsdp, seq, seq - 2) * shards + other)
    key_place = (jnp.stack(starts)[:, None] * rows + jnp.arange(rows)[None, :]).reshape(1, -1)
    query_place, key_place = query_place.astype(jnp.int32), key_place.astype(jnp.int32)
    span = key_place.shape[1]
    frequency = ROPE_BASE ** (-2.0 * jnp.arange(half, dtype=F32) / head)
    angles = key_place.reshape(span, 1).astype(F32) * frequency[None, :]
    wide_cos, wide_sin = jnp.cos(angles), jnp.sin(angles)
    cosine, sine = (jnp.tile(table[:rows], (micro, 1)) for table in (wide_cos, wide_sin))

    def gain_table(pieces, target):
        return call(
            gains_kernel, info, pieces, [shape((8, model), F32)],
            [pltpu.VMEM((shards, GAIN_ROWS, 768), F32)], section=target,
        )[0]

    def fetch(own, target):
        one, two = links.along(own, target, 1), links.along(own, target, 2)
        sent = call(
            select_kernel, info, [own, one, two], [shape((2,) + own.shape, BF)] * (shards - 1),
            section=target,
        )
        return [own, one, two] + [links.across(array, target, 1 + i) for i, array in enumerate(sent)]

    def forward(x, weights, target, x_window=None):
        first, rows_of, gate_up_w = weights
        gains = gain_table(first, target)
        sizes_of = [shape((shards, tokens, shard), BF), shape((tokens, wide), F32),
                    shape((tokens, heads_width), BF)]
        whole = shape((micro, span, 2 * head), BF)
        attend_outs = [
            shape((micro, shards * rows, span), F32), shape((tokens, heads_width), BF),
            shape((tokens, model), F32), shape((tokens, model), F32),
            shape((shards, tokens, shard), BF),
        ]
        attend_ins = [x, gains, limit, query_place, key_place] + rows_of
        if x_window is not None:
            blocks, qkv, query, window = call(
                functools.partial(project_window_kernel, micro), info,
                x_window + [gains, cosine, sine, wide_cos, wide_sin] + first, sizes_of + [whole],
                [pltpu.VMEM((shards, span, shard), BF)], section=target,
                flops=2 * model * (tokens * heads_width + 2 * span * micro * head),
            )
            outs = call(
                functools.partial(attend_kernel, micro), info, [query] + attend_ins + [window],
                attend_outs, section=target,
                flops=2 * tokens * heads_width * (2 * span + model),
            )
        else:
            blocks, qkv, query, own = call(
                project_kernel, info, [x, gains, cosine, sine] + first,
                sizes_of + [shape((tokens, 2 * head), BF)], section=target,
                flops=2 * tokens * model * wide,
            )
            window, *outs = call(
                functools.partial(attend_kernel, micro), info,
                [query] + attend_ins + fetch(own, target), [whole] + attend_outs, section=target,
                flops=2 * tokens * heads_width * (2 * span + model),
            )
        probs, attended, branch, mixed, ffn_blocks = outs
        gate_up, activated, down, result = call(
            ffn_kernel, info, [ffn_blocks, mixed, gains] + gate_up_w + rows_of,
            [shape((tokens, 2 * hidden), F32), shape((tokens, hidden), BF),
             shape((tokens, model), F32), shape((tokens, model), BF)],
            flops=6 * tokens * hidden * model, section=target,
        )
        saved = dict(
            x=x, gains=gains, blocks=blocks, qkv=qkv, query=query, window=window, probs=probs,
            attended=attended, branch=branch, mixed=mixed, ffn_blocks=ffn_blocks, gate_up=gate_up,
            activated=activated, down=down,
        )
        return result, saved

    def back_ffn(upstream, s, weights, target):
        _, rows_of, gate_up_w = weights
        outs = call(
            ffn_back_kernel, info,
            [upstream, s["mixed"], s["down"], s["gate_up"], s["activated"], s["ffn_blocks"],
             s["gains"]] + gate_up_w + rows_of,
            [shape((tokens, 2 * hidden + model + quarter + 256), BF)] * shards
            + [shape((tokens, model), F32), shape((8, model), F32)],
            [pltpu.VMEM((tokens, hidden), F32), pltpu.VMEM((tokens, 2 * hidden), BF),
             pltpu.VMEM((shards, tokens, shard), F32), pltpu.VMEM((tokens, model), F32)],
            flops=6 * tokens * hidden * model, section=target,
        )
        return outs[:shards], outs[shards], outs[shards + 1]

    def back_attend(grad_mixed, s, weights, target):
        pair = [shape((tokens, 2 * head), F32)] * 3
        outs = call(
            functools.partial(attend_back_kernel, micro), info,
            [grad_mixed, s["branch"], s["window"], s["probs"], s["query"], s["gains"]] + weights[1],
            [shape((tokens, model), BF), shape((tokens, heads_width), F32)] + pair
            + [shape((2, tokens, 2 * head), BF)] * (shards - 1) + [shape((8, model), F32)],
            [pltpu.VMEM((tokens, heads_width), BF)],
            flops=2 * tokens * heads_width * (4 * span + model), section=target,
        )
        return outs[0], outs[1], outs[2:5], outs[5:8], outs[8]

    def back_window(kept, gives, target, waiting):
        got = [links.across(array, target, 1 + i) for i, array in enumerate(gives)]
        got, waiting = tie((got, waiting))
        own, one, two = call(
            combine_kernel, info, list(kept) + got,
            [shape((tokens, 2 * head), F32)] + [shape((tokens, 2 * head), BF)] * 2,
            section=target,
        )
        return (own, links.along(one, target, -1), links.along(two, target, -2)), waiting

    def back_project(window_grads, grad_query, grad_mixed, grad_branch, rows_ffn, rows_attn, s,
                     weights, target):
        outs = call(
            project_back_kernel, info,
            list(window_grads) + [grad_query, s["qkv"], cosine, sine, s["x"], grad_mixed,
            grad_branch, s["attended"], s["blocks"], s["gains"], rows_ffn, rows_attn] + weights[0],
            [shape((tokens + GAIN_ROWS, wide + model + head + 256), BF)] * shards
            + [shape((tokens, model), BF)],
            [pltpu.VMEM((tokens, wide), BF), pltpu.VMEM((shards, tokens, shard), F32),
             pltpu.VMEM((tokens, model), F32), pltpu.VMEM((shards, GAIN_ROWS, 256), F32)],
            flops=2 * tokens * wide * model, section=target,
        )
        return outs[:shards], outs[shards]

    def exchange(packs, target):
        return [packs[0]] + [links.across(packs[i], target, i) for i in range(1, shards)]

    total_width = 2 * hidden + 512

    def ffn_weights(packs, target):
        return call(
            functools.partial(ffn_weights_kernel, shard, model), info, list(packs),
            [shape((shard, 2 * hidden), BF), shape((shard, hidden), BF)],
            flops=2 * shards * tokens * shard * 3 * hidden, section=target,
        )

    def attn_weights(packs, ffn, target):
        return call(
            functools.partial(weights_kernel, shard, model), info, list(packs) + list(ffn),
            [shape((shard, total_width), BF)] * 2,
            flops=2 * shards * tokens * shard * (total_width - hidden), section=target,
        )

    def backward(upstream, s, weights, target, other=None):
        ffn_packs, grad_mixed, rows_ffn = back_ffn(upstream, s, weights, target)
        grad_branch, grad_query, kept, gives, rows_attn = back_attend(
            grad_mixed, s, weights, target
        )
        window_grads, (ffn_packs, other) = back_window(kept, gives, target, (ffn_packs, other))
        ffn_packs = exchange(ffn_packs, target)
        if other is not None:
            other = jnp.where(is_first, other[0], other[1])
            window_grads, other = tie((window_grads, other))
        attn_packs, grad_in = back_project(
            window_grads, grad_query, grad_mixed, grad_branch, rows_ffn, rows_attn, s, weights,
            target,
        )
        return ffn_weights(ffn_packs, target), attn_packs, grad_in, other

    x_first = hidden_in.reshape(tokens, model)
    first = [gather_first(prepared, 0)]
    x_window = fetch(x_first, 0)
    x_window[3], rest = tie((x_window[3], own_shards[1:]))
    first += gather_rest(rest, 0)
    result_a, saved_a = forward(x_first, first, 0, x_window)
    token = links.cross(saved_a["query"][-16:, :128], 0)
    tied = lax.dynamic_update_slice(prepared, token, (shard, wide - token.shape[1]))
    second = [gather_first(tied, 1)]
    second[0][1], rest = tie((second[0][1], own_shards[1:]))
    second += gather_rest(rest, 1)
    middle = links.cross(result_a, 0)
    result_b, saved_b = forward(middle, second, 1)

    ffn, attn_packs, grad_b, _ = backward(cotangent.reshape(tokens, model), saved_b, second, 1)
    upstream = links.cross(grad_b, 1)
    b_first, b_second = attn_weights(exchange(attn_packs, 1), ffn, 1)
    upstream, b_first, b_second = tie((upstream, b_first, b_second))
    halves_b = (links.cross(b_first, 1), b_second)

    ffn, attn_packs, grad_a, half_b = backward(upstream, saved_a, first, 0, halves_b)
    part_b = lax.psum(half_b, "seq")
    attn_packs, part_b = tie((exchange(attn_packs, 0), part_b))
    a_first, a_second = attn_weights(attn_packs, ffn, 0)
    part_a = lax.psum(jnp.where(is_first, a_first, links.cross(a_second, 0)), "seq")
    theirs = links.swap(jnp.where(is_first, part_b, part_a))

    part = head // shards
    grads = call(
        finish_kernel, info, [part_a, part_b, theirs],
        [shape((1, shard, heads_width), F32), shape((1, shard, head), F32),
         shape((1, shard, head), F32), shape((1, head, model), F32),
         shape((1, shard, hidden), F32), shape((1, shard, hidden), F32),
         shape((1, quarter, model), F32)]
        + [shape((1, shard), F32)] * 4 + [shape((1, part), F32)] * 2,
    )
    g_query, g_key, g_value, g_out, g_gate, g_up, g_down = grads[:7]
    g_attn, g_post_attn, g_ffn, g_post_ffn, g_query_gain, g_key_gain = grads[7:]
    section_outputs = jnp.where(is_first, result_a, result_b).reshape(1, micro, rows, model)
    input_grads = jnp.where(is_first, grad_a, grad_b).reshape(1, micro, rows, model)
    return (
        section_outputs, input_grads, g_attn, g_query, g_key, g_value, g_query_gain, g_key_gain,
        g_out, g_post_attn, g_ffn, g_gate, g_up, g_down, g_post_ffn,
    )


def solution(mesh):
    rows = P(None, ("seq", "fsdp"), None)
    vector, matrix = P("section", "fsdp"), P("section", "fsdp", None)
    weights = (vector, matrix, matrix, matrix, vector, vector, matrix, vector, vector, matrix,
               matrix, matrix, vector)
    out_rows = P("section", None, ("seq", "fsdp"), None)
    return jax.shard_map(
        functools.partial(body, dict(mesh.shape)),
        mesh=mesh,
        in_specs=(rows, rows, P(None, ("seq", "fsdp"))) + weights,
        out_specs=(out_rows, out_rows) + weights,
        check_vma=False,
    )
```

```python
import functools

import jax
import jax.numpy as jnp
from jax import lax
from jax.experimental import pallas as pl
from jax.experimental.pallas import tpu as pltpu
from jax.sharding import PartitionSpec as P

WIN = 512
EPSILON = 1e-06
ROPE_BASE = 10000.0
NEG_LARGE = -1e30
AXES = ("section", "seq", "fsdp")
BF = jnp.bfloat16
F32 = jnp.float32
GAIN_ROWS = 16
INTERPRET = False


def mm(left, right):
    return lax.dot_general(left, right, (((1,), (0,)), ((), ())), preferred_element_type=F32)


def mm_nt(left, right):
    return lax.dot_general(left, right, (((1,), (1,)), ((), ())), preferred_element_type=F32)


def mm_tn(left, right):
    return lax.dot_general(left, right, (((0,), (0,)), ((), ())), preferred_element_type=F32)


def inverse_rms(values):
    return lax.rsqrt(jnp.mean(values * values, axis=-1, keepdims=True) + EPSILON)


def norm_back(values, scale, gain, grad):
    weighted = grad * gain
    inner = jnp.mean(values * weighted, axis=-1, keepdims=True)
    return scale * weighted - values * (scale * scale * scale * inner)


def gain_back(values, scale, grad):
    return jnp.sum(values * scale * grad, axis=0, keepdims=True)


def call(kernel, info, arrays, outs, scratch=(), flops=0, section=None, far=(), far_out=False):
    if section is not None:
        inner = kernel

        def kernel(info, *refs):
            @pl.when(info[2] == section)
            def _():
                inner(info, *refs)

    smem = pl.BlockSpec(memory_space=pltpu.SMEM)
    vmem = pl.BlockSpec(memory_space=pltpu.VMEM)
    hbm = pl.BlockSpec(memory_space=pl.ANY)
    size = sum(a.size * a.dtype.itemsize for a in arrays)
    size += sum(a.size * a.dtype.itemsize for a in outs)
    return pl.pallas_call(
        kernel,
        out_shape=outs,
        in_specs=[smem] + [hbm if i in far else vmem for i in range(len(arrays))],
        out_specs=[hbm if far_out else vmem] * len(outs),
        scratch_shapes=list(scratch),
        compiler_params=pltpu.CompilerParams(vmem_limit_bytes=24 * 1024 * 1024),
        cost_estimate=pl.CostEstimate(flops=flops, bytes_accessed=size, transcendentals=0),
        interpret=INTERPRET,
    )(info, *arrays)


def shape(dims, kind):
    return jax.ShapeDtypeStruct(tuple(dims), kind)


def slot(index, width):
    return pl.ds(pl.multiple_of(index * width, width), width)


def gains_kernel(info, *refs):
    pieces, out, held = refs[:-2], refs[-2], refs[-1]
    count = len(pieces)
    shard = out.shape[1] // count
    rows = pieces[0].shape[0] - GAIN_ROWS
    part = shard * 2 // 5
    for flip, piece in enumerate(pieces):
        held[info[0] ^ flip] = piece[rows : rows + GAIN_ROWS, : held.shape[2]].astype(F32)
    out[...] = jnp.zeros_like(out)
    for place in range(count):
        for row in range(4):
            out[row : row + 1, place * shard : (place + 1) * shard] = held[
                place, 0:1, row * shard : (row + 1) * shard
            ]
        for row in range(2):
            start = 4 * shard + row * part
            out[4 + row : 5 + row, place * part : (place + 1) * part] = held[
                place, 0:1, start : start + part
            ]


def prepare_kernel(info, query, key, value, *refs):
    gains, out = refs[:-1], refs[-1]
    shard = query.shape[1]
    start = 0
    for ref in (query, key, value):
        out[:shard, start : start + ref.shape[2]] = ref[0]
        start += ref.shape[2]
    out[shard:, :] = jnp.zeros_like(out[shard:, :])
    start = 0
    for ref in gains:
        out[shard : shard + 1, start : start + ref.shape[1]] = ref[...]
        start += ref.shape[1]


def fold_kernel(info, gate, up, out_w, down_w, folded, out_held, down_held, turned, sems):
    shard, hidden = gate.shape[1], gate.shape[2]
    loads = [
        pltpu.make_async_copy(out_w.at[0], out_held, sems.at[0]),
        pltpu.make_async_copy(down_w.at[0], down_held, sems.at[1]),
    ]
    moves = [
        pltpu.make_async_copy(gate.at[0], folded.at[:, pl.ds(0, hidden)], sems.at[2]),
        pltpu.make_async_copy(up.at[0], folded.at[:, pl.ds(hidden, hidden)], sems.at[3]),
    ]
    for copy in loads + moves:
        copy.start()
    start = 0
    for load, held in zip(loads, (out_held, down_held)):
        load.wait()
        rows = held.shape[0]
        for place in range(4):
            block = held[:, place * shard : (place + 1) * shard].astype(F32)
            turned[:, start : start + rows] = block.T.astype(BF)
            start += rows
    last = pltpu.make_async_copy(
        turned, folded.at[:, pl.ds(2 * hidden, turned.shape[1])], sems.at[4]
    )
    last.start()
    for copy in moves + [last]:
        copy.wait()


def load_turned(gathered, held, sems, start, shard):
    width = held.shape[1] // 4
    copies = []
    for place in range(4):
        for row in range(4):
            copy = pltpu.make_async_copy(
                gathered.at[pl.ds(place * shard, shard), pl.ds(start + row * width, width)],
                held.at[pl.ds(row * shard, shard), pl.ds(place * width, width)],
                sems.at[4 * place + row],
            )
            copy.start()
            copies.append(copy)
    return copies


def load_columns(gathered, held, sems, width):
    copies = []
    for index in range(held.shape[1] // width):
        columns = pl.ds(index * width, width)
        copy = pltpu.make_async_copy(
            gathered.at[:, columns], held.at[:, columns], sems.at[index]
        )
        copy.start()
        copies.append(copy)
    return copies


def rope_store(target, rows, start, normal, cos, sin):
    half = cos.shape[1]
    one, two = normal[:, :half], normal[:, half:]
    target[rows, start : start + half] = (one * cos - two * sin).astype(BF)
    target[rows, start + half : start + 2 * half] = (two * cos + one * sin).astype(BF)


def project_window_kernel(micro, info, x, one, two, *refs):
    got, (gains, cosine, sine, wide_cos, wide_sin) = refs[:3], refs[3:8]
    pieces = refs[8:12]
    blocks, qkv, query, window, held = refs[12:]
    rows = x.shape[0] // micro
    shard = blocks.shape[2]
    head = window.shape[2] // 2
    heads_width = query.shape[1]
    for m in range(micro):
        span = slice(m * rows, (m + 1) * rows)
        parts = [x[span], one[span], two[span]]
        for ref in got:
            parts += [ref[0, span], ref[1, span]]
        values = jnp.concatenate(parts, axis=0).astype(F32)
        normed = values * inverse_rms(values) * gains[0:1, :]
        for place in range(len(pieces)):
            held[place] = normed[:, place * shard : (place + 1) * shard].astype(BF)
        total = None
        for flip, piece in enumerate(pieces):
            term = mm(held[info[0] ^ flip], piece[:shard, heads_width:])
            total = term if total is None else total + term
        for place in range(len(pieces)):
            blocks[place, span] = held[place, :rows]
        qkv[span, heads_width:] = total[:rows]
        raw = total[:, :head]
        normal = raw * inverse_rms(raw) * gains[5:6, :head]
        rope_store(window.at[m], slice(None), 0, normal, wide_cos[...], wide_sin[...])
        window[m, :, head:] = total[:, head:].astype(BF)
    total = None
    for flip, piece in enumerate(pieces):
        term = mm(blocks[info[0] ^ flip], piece[:shard, :heads_width])
        total = term if total is None else total + term
    qkv[:, :heads_width] = total
    for start in range(0, heads_width, head):
        raw = total[:, start : start + head]
        normal = raw * inverse_rms(raw) * gains[4:5, :head]
        rope_store(query, slice(None), start, normal, cosine[...], sine[...])


def finish_kernel(info, part_a, part_b, theirs, *outs):
    query, key, value, out, gate, up, down = outs[:7]
    vectors = outs[7:]
    shard, hidden = gate.shape[1], gate.shape[2]

    def emit(first, second):
        gate[0] = first[:, :hidden].astype(F32)
        up[0] = first[:, hidden : 2 * hidden].astype(F32)
        for row, ref in enumerate(vectors):
            ref[...] = first[:GAIN_ROWS, 2 * hidden : 2 * hidden + ref.shape[1]].astype(F32)[
                row : row + 1
            ]
        start = 0
        for ref in (query, key, value):
            ref[0] = second[:, start : start + ref.shape[2]].astype(F32)
            start += ref.shape[2]
        for ref in (out, down):
            rows = ref.shape[1]
            for place in range(4):
                block = second[:, start : start + rows].astype(F32)
                ref[0, :, place * shard : (place + 1) * shard] = block.T
                start += rows

    @pl.when(info[2] == 0)
    def _():
        emit(part_a, theirs)

    @pl.when(info[2] == 1)
    def _():
        emit(theirs, part_b)


def project_kernel(info, x, gains, cosine, sine, *refs):
    pieces = refs[:-4]
    blocks, qkv, query, own = refs[-4:]
    shard = blocks.shape[2]
    half = cosine.shape[1]
    head = 2 * half
    residual = x[...].astype(F32)
    normed = residual * inverse_rms(residual) * gains[0:1, :]
    for place in range(len(pieces)):
        blocks[place] = normed[:, place * shard : (place + 1) * shard].astype(BF)
    total = None
    for flip, piece in enumerate(pieces):
        term = mm(blocks[info[0] ^ flip], piece[:shard, :])
        total = term if total is None else total + term
    qkv[...] = total
    cos, sin = cosine[...], sine[...]
    heads = query.shape[1] // head
    for index in range(heads + 1):
        raw = total[:, index * head : (index + 1) * head]
        row = 4 if index < heads else 5
        normal = raw * inverse_rms(raw) * gains[row : row + 1, :head]
        one, two = normal[:, :half], normal[:, half:]
        target, start = (query, index * head) if index < heads else (own, 0)
        target[:, start : start + half] = (one * cos - two * sin).astype(BF)
        target[:, start + half : start + head] = (two * cos + one * sin).astype(BF)
    own[:, head:] = total[:, (heads + 1) * head :].astype(BF)


def select_kernel(info, own, one, two, *outs):
    for index, out in enumerate(outs):
        lower = (info[0] < (info[0] ^ (index + 1))).astype(F32)
        out[0] = one[...]
        mixed = own[...].astype(F32) * lower + two[...].astype(F32) * (1.0 - lower)
        out[1] = mixed.astype(BF)


def window_kernel(micro, info, own, one, two, *refs):
    got, window = refs[:3], refs[3]
    rows = own.shape[0] // micro
    for m in range(micro):
        span = slice(m * rows, (m + 1) * rows)
        parts = [own[span], one[span], two[span]]
        for ref in got:
            parts += [ref[0, span], ref[1, span]]
        for index, part in enumerate(parts):
            window[m, index * rows : (index + 1) * rows] = part


def attend_kernel(micro, info, gathered, query, x, gains, limit, *refs):
    out_w, sems = refs[-2:]
    model = x.shape[1]
    shard = model // 4
    wide = gathered.shape[1] - 2 * model // 5 * 12
    copies = load_turned(gathered, out_w, sems, wide, shard)
    if len(refs) == 1 + 6 + 2:
        window = refs[0]
        outs = refs[1:-2]
    else:
        window = refs[6]
        outs = refs[7:-2]
        window_kernel(micro, info, *refs[:6], window)
    probs, attended, branch, mixed, blocks, ffn_in = outs
    rows = query.shape[0] // micro
    head = window.shape[2] // 2
    heads = query.shape[1] // head
    count = window.shape[1]
    column = lax.broadcasted_iota(jnp.int32, (rows, count), 1)
    distance = lax.broadcasted_iota(jnp.int32, (rows, count), 0) + info[3]
    for index in range(count // rows):
        inside = (column >= index * rows) & (column < (index + 1) * rows)
        distance = distance - jnp.where(inside, column - index * rows + info[4 + index], 0)
    for m in range(micro):
        span = slice(m * rows, (m + 1) * rows)
        allowed = (distance >= 0) & (distance <= limit[span])
        bias = jnp.where(allowed, 0.0, NEG_LARGE)
        bias = jnp.concatenate([bias] * heads, axis=0)
        stacked = jnp.concatenate(
            [query[span, h * head : (h + 1) * head] for h in range(heads)], axis=0
        )
        scores = mm_nt(stacked, window[m, :, :head]) * head ** (-0.5) + bias
        exponent = jnp.exp(scores - jnp.max(scores, axis=-1, keepdims=True))
        chance = exponent / jnp.sum(exponent, axis=-1, keepdims=True)
        probs[m] = chance
        result = mm(chance.astype(BF), window[m, :, head:]).astype(BF)
        for h in range(heads):
            attended[span, h * head : (h + 1) * head] = result[h * rows : (h + 1) * rows]
    for copy in copies:
        copy.wait()
    total = mm_nt(attended[...], out_w[...])
    branch[...] = total
    value = x[...].astype(F32) + total * inverse_rms(total) * gains[1:2, :]
    mixed[...] = value
    normed = value * inverse_rms(value) * gains[2:3, :]
    ffn_in[...] = normed.astype(BF)
    for place in range(4):
        blocks[place] = normed[:, place * shard : (place + 1) * shard].astype(BF)


def gelu_parts(gate):
    c = 0.7978845608028654
    inner = jnp.tanh(c * (gate + 0.044715 * gate * gate * gate))
    value = 0.5 * gate * (1.0 + inner)
    slope = 0.5 * (1.0 + inner) + 0.5 * gate * (1.0 - inner * inner) * c * (
        1.0 + 3 * 0.044715 * gate * gate
    )
    return value, slope


def ffn_kernel(info, gathered, ffn_in, mixed, gains, gate_up, activated, down, result,
               gate_up_w, down_w, column_sems, sems):
    hidden = activated.shape[1]
    width = 512
    columns = load_columns(gathered, gate_up_w, column_sems, width)
    shard = ffn_in.shape[1] // 4
    copies = load_turned(
        gathered, down_w, sems, gathered.shape[1] - 4 * down_w.shape[1] // 4, shard
    )
    for start in range(0, hidden, width):
        both = []
        for base in (start, hidden + start):
            columns[base // width].wait()
            total = mm(ffn_in[...], gate_up_w[:, base : base + width])
            gate_up[:, base : base + width] = total
            both.append(total)
        value, _ = gelu_parts(both[0])
        activated[:, start : start + width] = (value * both[1]).astype(BF)
    for copy in copies:
        copy.wait()
    total = mm_nt(activated[...], down_w[...])
    down[...] = total
    result[...] = (mixed[...] + total * inverse_rms(total) * gains[3:4, :]).astype(BF)


def ffn_back_kernel(info, gathered, upstream, mixed, down, gate_up, activated, blocks, gains,
                    *refs):
    packs, grad_mixed, gain_rows = refs[:4], refs[4], refs[5]
    grad_gate_up, gate_up_w, down_w, column_sems, sems = refs[6:]
    hidden = activated.shape[1]
    model = mixed.shape[1]
    shard = blocks.shape[2]
    copies = load_turned(
        gathered, down_w, sems, gathered.shape[1] - 4 * down_w.shape[1] // 4, shard
    )
    columns = load_columns(gathered, gate_up_w, column_sems, 512)
    top = upstream[...].astype(F32)
    raw = down[...]
    scale = inverse_rms(raw)
    grad_down = norm_back(raw, scale, gains[3:4, :], top).astype(BF)
    gain_rows[...] = jnp.zeros_like(gain_rows)
    gain_rows[3:4, :] = gain_back(raw, scale, top)
    act_at = 2 * hidden + model
    block_at = act_at + hidden // 4
    for flip, pack in enumerate(packs):
        pack[:, 2 * hidden : act_at] = grad_down
        pack[:, act_at:block_at] = activated[:, slot(info[0] ^ flip, hidden // 4)]
        pack[:, block_at:] = jnp.zeros_like(pack[:, block_at:])
        pack[:, block_at : block_at + shard] = blocks[info[0] ^ flip]
    for copy in copies:
        copy.wait()
    width = 512
    for start in range(0, hidden, width):
        value, slope = gelu_parts(gate_up[:, start : start + width])
        up = gate_up[:, hidden + start : hidden + start + width]
        grad = mm(grad_down, down_w[:, start : start + width])
        grad_gate_up[:, start : start + width] = (grad * up * slope).astype(BF)
        grad_gate_up[:, hidden + start : hidden + start + width] = (grad * value).astype(BF)
    for pack in packs:
        pack[:, : 2 * hidden] = grad_gate_up[...]
    for copy in columns:
        copy.wait()
    grad_in = mm_nt(grad_gate_up[...], gate_up_w[...])
    raw = mixed[...]
    scale = inverse_rms(raw)
    gain_rows[2:3, :] = gain_back(raw, scale, grad_in)
    grad_mixed[...] = top + norm_back(raw, scale, gains[2:3, :], grad_in)


def attend_back_kernel(micro, info, gathered, grad_mixed, branch, window, probs, query, gains,
                       *refs):
    grad_branch, grad_query, own, one, two = refs[:5]
    gives, gain_rows, grad_attended, out_w, sems = refs[5:8], refs[8], refs[9], refs[10], refs[11]
    model = branch.shape[1]
    wide = gathered.shape[1] - 2 * model // 5 * 12
    copies = load_turned(gathered, out_w, sems, wide, model // 4)
    rows = own.shape[0] // micro
    head = own.shape[1] // 2
    heads = query.shape[1] // head
    factor = head ** (-0.5)
    raw = branch[...]
    scale = inverse_rms(raw)
    grad = grad_mixed[...]
    gain_rows[...] = jnp.zeros_like(gain_rows)
    gain_rows[1:2, :] = gain_back(raw, scale, grad)
    low = norm_back(raw, scale, gains[1:2, :], grad).astype(BF)
    grad_branch[...] = low
    for copy in copies:
        copy.wait()
    grad_attended[...] = mm(low, out_w[...]).astype(BF)
    for m in range(micro):
        span = slice(m * rows, (m + 1) * rows)
        chance = probs[m]
        keys, values = window[m, :, :head], window[m, :, head:]
        stacked = jnp.concatenate(
            [query[span, h * head : (h + 1) * head] for h in range(heads)], axis=0
        )
        upstream = jnp.concatenate(
            [grad_attended[span, h * head : (h + 1) * head] for h in range(heads)], axis=0
        )
        grad_values = mm_tn(chance.astype(BF), upstream)
        grad_chance = mm_nt(upstream, values)
        inner = jnp.sum(chance * grad_chance, axis=-1, keepdims=True)
        grad_scores = (chance * (grad_chance - inner)).astype(BF)
        grad_stacked = mm(grad_scores, keys) * factor
        grad_keys = mm_tn(grad_scores, stacked) * factor
        for h in range(heads):
            grad_query[span, h * head : (h + 1) * head] = grad_stacked[h * rows : (h + 1) * rows]
        for index, target in enumerate((own, one, two)):
            part = slice(index * rows, (index + 1) * rows)
            target[span, :head] = grad_keys[part]
            target[span, head:] = grad_values[part]
        for index, target in enumerate(gives):
            for side in range(2):
                start = (3 + 2 * index + side) * rows
                target[side, span, :head] = grad_keys[start : start + rows].astype(BF)
                target[side, span, head:] = grad_values[start : start + rows].astype(BF)


def combine_kernel(info, own, one, two, first, second, third, own_out, one_out, two_out):
    total_own, total_one, total_two = own[...], one[...], two[...]
    for index, got in enumerate((first, second, third)):
        lower = (info[0] < (info[0] ^ (index + 1))).astype(F32)
        total_one = total_one + got[0].astype(F32)
        side = got[1].astype(F32)
        total_own = total_own + side * lower
        total_two = total_two + side * (1.0 - lower)
    own_out[...] = total_own
    one_out[...] = total_one.astype(BF)
    two_out[...] = total_two.astype(BF)


def project_back_kernel(info, own, back_one, back_two, grad_query, qkv, cosine, sine, x, grad_mixed,
                        grad_branch, attended, blocks, gains, rows_ffn, rows_attn, *refs):
    pieces = refs[:4]
    packs, grad_in = refs[4:8], refs[8]
    grad_qkv, held, natural, gain_held = refs[9:]
    tokens, model = natural.shape
    shard = blocks.shape[2]
    half = cosine.shape[1]
    head = 2 * half
    heads = grad_query.shape[1] // head
    cos, sin = cosine[...], sine[...]
    grad_own = own[...] + back_one[...].astype(F32) + back_two[...].astype(F32)
    head_gains = [None, None]
    for index in range(heads + 1):
        if index < heads:
            grad = grad_query[:, index * head : (index + 1) * head]
        else:
            grad = grad_own[:, :head]
        one, two = grad[:, :half], grad[:, half:]
        grad = jnp.concatenate((one * cos + two * sin, two * cos - one * sin), axis=1)
        raw = qkv[:, index * head : (index + 1) * head]
        scale = inverse_rms(raw)
        kind = 0 if index < heads else 1
        term = gain_back(raw, scale, grad)
        head_gains[kind] = term if head_gains[kind] is None else head_gains[kind] + term
        back = norm_back(raw, scale, gains[4 + kind : 5 + kind, :head], grad)
        grad_qkv[:, index * head : (index + 1) * head] = back.astype(BF)
    grad_qkv[:, (heads + 1) * head :] = grad_own[:, head:].astype(BF)
    for flip, piece in enumerate(pieces):
        held[info[0] ^ flip] = mm_nt(grad_qkv[...], piece[:shard, :])
    for place in range(4):
        natural[:, place * shard : (place + 1) * shard] = held[place]
    grad_normed = natural[...]
    residual = x[...].astype(F32)
    scale = inverse_rms(residual)
    first_gain = gain_back(residual, scale, grad_normed)
    total = grad_mixed[...] + norm_back(residual, scale, gains[0:1, :], grad_normed)
    grad_in[...] = total.astype(BF)
    gain_held[...] = jnp.zeros_like(gain_held)
    part = head // 4
    four = (first_gain, rows_attn[1:2, :], rows_ffn[2:3, :], rows_ffn[3:4, :])
    for place in range(4):
        for row, values in enumerate(four):
            gain_held[place, row : row + 1, :shard] = values[
                :, place * shard : (place + 1) * shard
            ]
        for row, values in enumerate(head_gains):
            gain_held[place, 4 + row : 5 + row, :part] = values[
                :, place * part : (place + 1) * part
            ]
    wide = grad_qkv.shape[1]
    att_at = wide + model
    block_at = att_at + head
    for flip, pack in enumerate(packs):
        other = info[0] ^ flip
        pack[tokens:, :] = jnp.zeros_like(pack[tokens:, :])
        pack[tokens:, : gain_held.shape[2]] = gain_held[other].astype(BF)
        pack[:tokens, :wide] = grad_qkv[...]
        pack[:tokens, wide:att_at] = grad_branch[...]
        pack[:tokens, att_at:block_at] = attended[:, slot(other, head)]
        pack[:tokens, block_at:] = jnp.zeros_like(pack[:tokens, block_at:])
        pack[:tokens, block_at : block_at + shard] = blocks[other]


def over(packs, tokens, left, right, left_width, right_width):
    total = None
    for pack in packs:
        term = mm_tn(
            pack[:tokens, left : left + left_width], pack[:tokens, right : right + right_width]
        )
        total = term if total is None else total + term
    return total.astype(BF)


def ffn_weights_kernel(shard, model, info, *refs):
    packs, first, second = refs[:4], refs[4], refs[5]
    tokens = packs[0].shape[0]
    wide = first.shape[1]
    quarter = second.shape[1] // 4
    act_at = wide + model
    for start in range(0, wide, 1024):
        first[:, start : start + 1024] = over(
            packs, tokens, act_at + quarter, start, shard, 1024
        )
    for place in range(4):
        second[:, place * quarter : (place + 1) * quarter] = over(
            packs, tokens, wide + place * shard, act_at, shard, quarter
        )


def weights_kernel(shard, model, info, *refs):
    packs, gate_up, down, first, second = refs[:4], refs[4], refs[5], refs[6], refs[7]
    tokens = packs[0].shape[0] - GAIN_ROWS
    head = model // 5 * 2
    wide = packs[0].shape[1] - model - 2 * head
    hidden = gate_up.shape[1]
    first[:, :hidden] = gate_up[...]
    first[:, hidden:] = jnp.zeros_like(first[:, hidden:])
    gains = sum(pack[tokens:, :head].astype(F32) for pack in packs)
    first[:GAIN_ROWS, hidden : hidden + head] = gains.astype(BF)
    att_at = wide + model
    second[:, :wide] = over(packs, tokens, att_at + head, 0, shard, wide)
    for place in range(4):
        start = wide + place * head
        second[:, start : start + head] = over(
            packs, tokens, wide + place * shard, att_at, shard, head
        )
    second[:, wide + 4 * head :] = down[...]


class Links:
    def __init__(self, sizes):
        self.sizes = sizes

    def index(self, section, seq, fsdp):
        return (section * self.sizes["seq"] + seq) * self.sizes["fsdp"] + fsdp

    def send(self, array, section, place):
        pairs = []
        for z in range(self.sizes["seq"]):
            for f in range(self.sizes["fsdp"]):
                to_section, to_z, to_f = place(z, f)
                if 0 <= to_z < self.sizes["seq"]:
                    pairs.append((self.index(section, z, f), self.index(to_section, to_z, to_f)))
        return lax.ppermute(array, AXES, pairs)

    def along(self, array, section, by):
        return self.send(array, section, lambda z, f: (section, z + by, f))

    def across(self, array, section, flip):
        return self.send(array, section, lambda z, f: (section, z, f ^ flip))

    def cross(self, array, section):
        return self.send(array, section, lambda z, f: (1 - section, z, f))

    def both(self, array, flip):
        pairs = []
        for section in range(2):
            for z in range(self.sizes["seq"]):
                for f in range(self.sizes["fsdp"]):
                    pairs.append((self.index(section, z, f), self.index(section, z, f ^ flip)))
        return lax.ppermute(array, AXES, pairs)

    def swap(self, array):
        pairs = []
        for section in range(2):
            for z in range(self.sizes["seq"]):
                for f in range(self.sizes["fsdp"]):
                    pairs.append((self.index(section, z, f), self.index(1 - section, z, f)))
        return lax.ppermute(array, AXES, pairs)


def body(sizes, hidden_in, cotangent, positions, attn_gain, w_query, w_key, w_value, query_gain,
         key_gain, w_output, post_attn_gain, ffn_gain, w_gate, w_up, w_down, post_ffn_gain):
    section = lax.axis_index("section")
    seq = lax.axis_index("seq")
    fsdp = lax.axis_index("fsdp")
    is_first = section == 0
    micro, rows, model = hidden_in.shape
    tokens = micro * rows
    shard = w_query.shape[1]
    shards = sizes["fsdp"]
    heads_width, head = w_query.shape[2], w_key.shape[2]
    wide = heads_width + 2 * head
    hidden = w_gate.shape[2]
    quarter = hidden // shards
    assert shards == 4 and 2 * shards * rows == WIN and heads_width == shards * head
    links = Links(sizes)
    tie = lax.optimization_barrier
    info = jnp.stack([fsdp, seq, section]).astype(jnp.int32)

    prepared = call(
        prepare_kernel, info,
        [w_query, w_key, w_value, attn_gain, post_attn_gain, ffn_gain, post_ffn_gain, query_gain,
         key_gain],
        [shape((shard + GAIN_ROWS, wide), BF)],
    )[0]
    width_of = 2 * hidden + heads_width + hidden
    folded = call(
        fold_kernel, info, [w_gate, w_up, w_output, w_down], [shape((shard, width_of), BF)],
        [pltpu.VMEM((head, model), BF), pltpu.VMEM((quarter, model), BF),
         pltpu.VMEM((shard, heads_width + hidden), BF), pltpu.SemaphoreType.DMA((5,))],
        far=range(4), far_out=True,
    )[0]
    gathered = lax.all_gather(folded, "fsdp", axis=0, tiled=True)
    first = [prepared] + [links.both(prepared, flip) for flip in range(1, shards)]
    out_scratch = [pltpu.VMEM((model, heads_width), BF), pltpu.SemaphoreType.DMA((16,))]
    ffn_scratch = [pltpu.VMEM((model, 2 * hidden), BF), pltpu.VMEM((model, hidden), BF),
                   pltpu.SemaphoreType.DMA((2 * hidden // 512,)), pltpu.SemaphoreType.DMA((16,))]

    half = head // 2
    limit = jnp.minimum(positions.reshape(tokens, 1), WIN - 1)
    starts = [(seq - back) * shards + fsdp for back in range(3)]
    for flip in range(1, shards):
        other = fsdp ^ flip
        starts.append((seq - 1) * shards + other)
        starts.append(jnp.where(other < fsdp, seq, seq - 2) * shards + other)
    starts = jnp.stack(starts).astype(jnp.int32) * rows
    key_place = (starts[:, None] + jnp.arange(rows, dtype=jnp.int32)[None, :]).reshape(1, -1)
    info = jnp.concatenate((info, starts[:1], starts))
    span = key_place.shape[1]
    frequency = ROPE_BASE ** (-2.0 * jnp.arange(half, dtype=F32) / head)
    angles = key_place.reshape(span, 1).astype(F32) * frequency[None, :]
    wide_cos, wide_sin = jnp.cos(angles), jnp.sin(angles)
    cosine, sine = (jnp.tile(table[:rows], (micro, 1)) for table in (wide_cos, wide_sin))

    def gain_table(pieces, target):
        return call(
            gains_kernel, info, pieces, [shape((8, model), F32)],
            [pltpu.VMEM((shards, GAIN_ROWS, 768), F32)], section=target,
        )[0]

    def fetch(own, target):
        one, two = links.along(own, target, 1), links.along(own, target, 2)
        sent = call(
            select_kernel, info, [own, one, two], [shape((2,) + own.shape, BF)] * (shards - 1),
            section=target,
        )
        return [own, one, two] + [links.across(array, target, 1 + i) for i, array in enumerate(sent)]

    gains = gain_table(first, None)

    def forward(x, target, x_window=None):
        sizes_of = [shape((shards, tokens, shard), BF), shape((tokens, wide), F32),
                    shape((tokens, heads_width), BF)]
        whole = shape((micro, span, 2 * head), BF)
        attend_outs = [
            shape((micro, shards * rows, span), F32), shape((tokens, heads_width), BF),
            shape((tokens, model), F32), shape((tokens, model), F32),
            shape((shards, tokens, shard), BF), shape((tokens, model), BF),
        ]
        if x_window is not None:
            blocks, qkv, query, window = call(
                functools.partial(project_window_kernel, micro), info,
                x_window + [gains, cosine, sine, wide_cos, wide_sin] + first, sizes_of + [whole],
                [pltpu.VMEM((shards, span, shard), BF)], section=target,
                flops=2 * model * (tokens * heads_width + 2 * span * micro * head),
            )
            parts = [window]
        else:
            blocks, qkv, query, own = call(
                project_kernel, info, [x, gains, cosine, sine] + first,
                sizes_of + [shape((tokens, 2 * head), BF)], section=target,
                flops=2 * tokens * model * wide,
            )
            parts = fetch(own, target)
            attend_outs = [whole] + attend_outs
        outs = call(
            functools.partial(attend_kernel, micro), info,
            [gathered, query, x, gains, limit] + parts, attend_outs, out_scratch, section=target,
            flops=2 * tokens * heads_width * (2 * span + model), far=(0,),
        )
        if x_window is None:
            window, *outs = outs
        probs, attended, branch, mixed, ffn_blocks, ffn_in = outs
        gate_up, activated, down, result = call(
            ffn_kernel, info, [gathered, ffn_in, mixed, gains],
            [shape((tokens, 2 * hidden), F32), shape((tokens, hidden), BF),
             shape((tokens, model), F32), shape((tokens, model), BF)], ffn_scratch,
            flops=6 * tokens * hidden * model, section=target, far=(0,),
        )
        saved = dict(
            x=x, blocks=blocks, qkv=qkv, query=query, window=window, probs=probs,
            attended=attended, branch=branch, mixed=mixed, ffn_blocks=ffn_blocks, gate_up=gate_up,
            activated=activated, down=down,
        )
        return result, saved

    def back_ffn(upstream, s, target):
        outs = call(
            ffn_back_kernel, info,
            [gathered, upstream, s["mixed"], s["down"], s["gate_up"], s["activated"],
             s["ffn_blocks"], gains],
            [shape((tokens, 2 * hidden + model + quarter + 256), BF)] * shards
            + [shape((tokens, model), F32), shape((8, model), F32)],
            [pltpu.VMEM((tokens, 2 * hidden), BF)] + ffn_scratch,
            flops=6 * tokens * hidden * model, section=target, far=(0,),
        )
        return outs[:shards], outs[shards], outs[shards + 1]

    def back_attend(grad_mixed, s, target):
        pair = [shape((tokens, 2 * head), F32)] * 3
        outs = call(
            functools.partial(attend_back_kernel, micro), info,
            [gathered, grad_mixed, s["branch"], s["window"], s["probs"], s["query"], gains],
            [shape((tokens, model), BF), shape((tokens, heads_width), F32)] + pair
            + [shape((2, tokens, 2 * head), BF)] * (shards - 1) + [shape((8, model), F32)],
            [pltpu.VMEM((tokens, heads_width), BF)] + out_scratch,
            flops=2 * tokens * heads_width * (4 * span + model), section=target, far=(0,),
        )
        return outs[0], outs[1], outs[2:5], outs[5:8], outs[8]

    def back_window(kept, gives, target, waiting):
        got = [links.across(array, target, 1 + i) for i, array in enumerate(gives)]
        ffn_packs, other = waiting
        got, other = tie((got, other))
        if other is not None:
            other = jnp.where(is_first, other[0], other[1])
            kept, other = tie((kept, other))
        own, one, two = call(
            combine_kernel, info, list(kept) + got,
            [shape((tokens, 2 * head), F32)] + [shape((tokens, 2 * head), BF)] * 2,
            section=target,
        )
        one, two = links.along(one, target, -1), links.along(two, target, -2)
        one, ffn_packs = tie((one, ffn_packs))
        return (own, one, two), ffn_packs, other

    def back_project(window_grads, grad_query, grad_mixed, grad_branch, rows_ffn, rows_attn, s,
                     target):
        outs = call(
            project_back_kernel, info,
            list(window_grads) + [grad_query, s["qkv"], cosine, sine, s["x"], grad_mixed,
            grad_branch, s["attended"], s["blocks"], gains, rows_ffn, rows_attn] + first,
            [shape((tokens + GAIN_ROWS, wide + model + head + 256), BF)] * shards
            + [shape((tokens, model), BF)],
            [pltpu.VMEM((tokens, wide), BF), pltpu.VMEM((shards, tokens, shard), F32),
             pltpu.VMEM((tokens, model), F32), pltpu.VMEM((shards, GAIN_ROWS, 256), F32)],
            flops=2 * tokens * wide * model, section=target,
        )
        return outs[:shards], outs[shards]

    def exchange(packs, target):
        return [packs[0]] + [links.across(packs[i], target, i) for i in range(1, shards)]

    total_width = 2 * hidden + 512

    def ffn_weights(packs, target):
        return call(
            functools.partial(ffn_weights_kernel, shard, model), info, list(packs),
            [shape((shard, 2 * hidden), BF), shape((shard, hidden), BF)],
            flops=2 * shards * tokens * shard * 3 * hidden, section=target,
        )

    def attn_weights(packs, ffn, target):
        return call(
            functools.partial(weights_kernel, shard, model), info, list(packs) + list(ffn),
            [shape((shard, total_width), BF)] * 2,
            flops=2 * shards * tokens * shard * (total_width - hidden), section=target,
        )

    def backward(upstream, s, target, other=None):
        ffn_packs, grad_mixed, rows_ffn = back_ffn(upstream, s, target)
        grad_branch, grad_query, kept, gives, rows_attn = back_attend(grad_mixed, s, target)
        window_grads, ffn_packs, other = back_window(kept, gives, target, (ffn_packs, other))
        ffn_packs = exchange(ffn_packs, target)
        attn_packs, grad_in = back_project(
            window_grads, grad_query, grad_mixed, grad_branch, rows_ffn, rows_attn, s, target
        )
        return ffn_weights(ffn_packs, target), attn_packs, grad_in, other

    x_first = hidden_in.reshape(tokens, model)
    result_a, saved_a = forward(x_first, 0, fetch(x_first, 0))
    middle = links.cross(result_a, 0)
    result_b, saved_b = forward(middle, 1)

    ffn, attn_packs, grad_b, _ = backward(cotangent.reshape(tokens, model), saved_b, 1)
    upstream = links.cross(grad_b, 1)
    b_first, b_second = attn_weights(exchange(attn_packs, 1), ffn, 1)
    upstream, b_first, b_second = tie((upstream, b_first, b_second))
    halves_b = (links.cross(b_first, 1), b_second)

    ffn, attn_packs, grad_a, half_b = backward(upstream, saved_a, 0, halves_b)
    part_b = lax.psum(half_b, "seq")
    attn_packs, part_b = tie((exchange(attn_packs, 0), part_b))
    a_first, a_second = attn_weights(attn_packs, ffn, 0)
    part_a = lax.psum(jnp.where(is_first, a_first, links.cross(a_second, 0)), "seq")
    theirs = links.swap(jnp.where(is_first, part_b, part_a))

    part = head // shards
    grads = call(
        finish_kernel, info, [part_a, part_b, theirs],
        [shape((1, shard, heads_width), F32), shape((1, shard, head), F32),
         shape((1, shard, head), F32), shape((1, head, model), F32),
         shape((1, shard, hidden), F32), shape((1, shard, hidden), F32),
         shape((1, quarter, model), F32)]
        + [shape((1, shard), F32)] * 4 + [shape((1, part), F32)] * 2,
    )
    g_query, g_key, g_value, g_out, g_gate, g_up, g_down = grads[:7]
    g_attn, g_post_attn, g_ffn, g_post_ffn, g_query_gain, g_key_gain = grads[7:]
    section_outputs = jnp.where(is_first, result_a, result_b).reshape(1, micro, rows, model)
    input_grads = jnp.where(is_first, grad_a, grad_b).reshape(1, micro, rows, model)
    return (
        section_outputs, input_grads, g_attn, g_query, g_key, g_value, g_query_gain, g_key_gain,
        g_out, g_post_attn, g_ffn, g_gate, g_up, g_down, g_post_ffn,
    )


def solution(mesh):
    rows = P(None, ("seq", "fsdp"), None)
    vector, matrix = P("section", "fsdp"), P("section", "fsdp", None)
    weights = (vector, matrix, matrix, matrix, vector, vector, matrix, vector, vector, matrix,
               matrix, matrix, vector)
    out_rows = P("section", None, ("seq", "fsdp"), None)
    return jax.shard_map(
        functools.partial(body, dict(mesh.shape)),
        mesh=mesh,
        in_specs=(rows, rows, P(None, ("seq", "fsdp"))) + weights,
        out_specs=(out_rows, out_rows) + weights,
        check_vma=False,
    )
```

```python
import functools

import jax
import jax.numpy as jnp
from jax import lax
from jax.experimental import pallas as pl
from jax.experimental.pallas import tpu as pltpu
from jax.sharding import PartitionSpec as P

WIN = 512
EPSILON = 1e-06
ROPE_BASE = 10000.0
NEG_LARGE = -1e30
AXES = ("section", "seq", "fsdp")
BF = jnp.bfloat16
F32 = jnp.float32
GAIN_ROWS = 16
INTERPRET = False


def mm(left, right):
    return lax.dot_general(left, right, (((1,), (0,)), ((), ())), preferred_element_type=F32)


def mm_nt(left, right):
    return lax.dot_general(left, right, (((1,), (1,)), ((), ())), preferred_element_type=F32)


def mm_tn(left, right):
    return lax.dot_general(left, right, (((0,), (0,)), ((), ())), preferred_element_type=F32)


def inverse_rms(values):
    return lax.rsqrt(jnp.mean(values * values, axis=-1, keepdims=True) + EPSILON)


def norm_back(values, scale, gain, grad):
    weighted = grad * gain
    inner = jnp.mean(values * weighted, axis=-1, keepdims=True)
    return scale * weighted - values * (scale * scale * scale * inner)


def gain_back(values, scale, grad):
    return jnp.sum(values * scale * grad, axis=0, keepdims=True)


def call(kernel, info, arrays, outs, scratch=(), flops=0, section=None, far=(), far_out=False):
    if section is not None:
        inner = kernel

        def kernel(info, *refs):
            @pl.when(info[2] == section)
            def _():
                inner(info, *refs)

    smem = pl.BlockSpec(memory_space=pltpu.SMEM)
    vmem = pl.BlockSpec(memory_space=pltpu.VMEM)
    hbm = pl.BlockSpec(memory_space=pl.ANY)
    return pl.pallas_call(
        kernel,
        out_shape=outs,
        in_specs=[smem] + [hbm if i in far else vmem for i in range(len(arrays))],
        out_specs=[hbm if far_out else vmem] * len(outs),
        scratch_shapes=list(scratch),
        compiler_params=pltpu.CompilerParams(vmem_limit_bytes=24 * 1024 * 1024),
        cost_estimate=pl.CostEstimate(flops=1, bytes_accessed=1, transcendentals=0),
        interpret=INTERPRET,
    )(info, *arrays)


def shape(dims, kind):
    return jax.ShapeDtypeStruct(tuple(dims), kind)


def slot(index, width):
    return pl.ds(pl.multiple_of(index * width, width), width)


def gains_kernel(info, gathered, out, held, sems):
    count, rows, width = held.shape
    shard = out.shape[1] // count
    part = shard * 2 // 5
    copies = []
    for place in range(count):
        source = gathered.at[
            pl.ds(place * shard, rows), pl.ds(gathered.shape[1] - width, width)
        ]
        copies.append(pltpu.make_async_copy(source, held.at[place], sems.at[place]))
    for copy in copies:
        copy.start()
    for copy in copies:
        copy.wait()
    out[...] = jnp.zeros_like(out)
    for place in range(count):
        values = held[place].astype(F32)
        start = place * shard
        for row in range(4):
            out[row : row + 1, start : start + width] = values[2 * row : 2 * row + 1]
            out[row : row + 1, start + width : start + shard] = values[
                2 * row + 1 : 2 * row + 2, : shard - width
            ]
        for row in range(2):
            out[4 + row : 5 + row, place * part : (place + 1) * part] = values[
                8 + row : 9 + row, :part
            ]


def fold_kernel(info, gate, up, query, key, value, out_w, down_w, attn, post_attn, ffn, post_ffn,
                query_gain, key_gain, folded, out_held, down_held, turned, gain_block, sems):
    shard = gate.shape[1]
    loads = [
        pltpu.make_async_copy(out_w.at[0], out_held, sems.at[0]),
        pltpu.make_async_copy(down_w.at[0], down_held, sems.at[1]),
    ]
    for copy in loads:
        copy.start()
    moves = []

    def move(source, start):
        copy = pltpu.make_async_copy(
            source, folded.at[:, pl.ds(start, source.shape[1])], sems.at[2 + len(moves)]
        )
        copy.start()
        moves.append(copy)
        return start + source.shape[1]

    start = move(up.at[0], move(gate.at[0], 0))
    turned_at = start
    start += turned.shape[1]
    for ref in (query, key, value):
        start = move(ref.at[0], start)
    width = gain_block.shape[1]
    gain_block[...] = jnp.zeros_like(gain_block)
    for row, ref in enumerate((attn, post_attn, ffn, post_ffn)):
        gain_block[2 * row : 2 * row + 1, :] = ref[:, :width]
        gain_block[2 * row + 1 : 2 * row + 2, : shard - width] = ref[:, width:]
    for row, ref in enumerate((query_gain, key_gain)):
        gain_block[8 + row : 9 + row, : ref.shape[1]] = ref[...]
    move(gain_block, start)
    start = 0
    for load, held in zip(loads, (out_held, down_held)):
        load.wait()
        rows = held.shape[0]
        for place in range(4):
            block = held[:, place * shard : (place + 1) * shard].astype(F32)
            turned[:, start : start + rows] = block.T.astype(BF)
            start += rows
    move(turned, turned_at)
    for copy in moves:
        copy.wait()


def out_start(model):
    return model // 5 * 32


def down_start(gathered, hidden):
    return gathered.shape[1] - 128 - hidden // 4 * 3 - hidden


def load_turned(gathered, held, sems, start, shard):
    width = held.shape[1] // 4
    copies = []
    for place in range(4):
        for row in range(4):
            copy = pltpu.make_async_copy(
                gathered.at[pl.ds(place * shard, shard), pl.ds(start + row * width, width)],
                held.at[pl.ds(row * shard, shard), pl.ds(place * width, width)],
                sems.at[4 * place + row],
            )
            copy.start()
            copies.append(copy)
    return copies


def load_columns(gathered, held, sems, width):
    copies = []
    for index in range(held.shape[1] // width):
        columns = pl.ds(index * width, width)
        copy = pltpu.make_async_copy(
            gathered.at[:, columns], held.at[:, columns], sems.at[index]
        )
        copy.start()
        copies.append(copy)
    return copies


def rope_store(target, rows, start, normal, cos, sin):
    half = cos.shape[1]
    one, two = normal[:, :half], normal[:, half:]
    target[rows, start : start + half] = (one * cos - two * sin).astype(BF)
    target[rows, start + half : start + 2 * half] = (two * cos + one * sin).astype(BF)


def load_qkv(gathered, held, sem):
    columns = pl.ds(gathered.shape[1] - 128 - held.shape[1], held.shape[1])
    copy = pltpu.make_async_copy(gathered.at[:, columns], held, sem)
    copy.start()
    return copy


def cut(blocks, normed):
    shard = blocks.shape[2]
    for place in range(blocks.shape[0]):
        blocks[place] = normed[:, place * shard : (place + 1) * shard].astype(BF)


def project_window_kernel(micro, info, gathered, x, one, two, *refs):
    got, (gains, cosine, sine, wide_cos, wide_sin) = refs[:3], refs[3:8]
    blocks, qkv, query, window, weight, sem = refs[8:]
    copy = load_qkv(gathered, weight, sem)
    rows = x.shape[0] // micro
    head = window.shape[2] // 2
    heads_width = query.shape[1]

    def normed_of(values):
        return values * inverse_rms(values) * gains[0:1, :]

    normed = normed_of(x[...].astype(F32))
    cut(blocks, normed)
    normed = normed.astype(BF)
    copy.wait()
    total = mm(normed, weight[:, :heads_width])
    qkv[:, :heads_width] = total
    for start in range(0, heads_width, head):
        raw = total[:, start : start + head]
        normal = raw * inverse_rms(raw) * gains[4:5, :head]
        rope_store(query, slice(None), start, normal, cosine[...], sine[...])
    for m in range(micro):
        span = slice(m * rows, (m + 1) * rows)
        parts = [x[span], one[span], two[span]]
        for ref in got:
            parts += [ref[0, span], ref[1, span]]
        values = jnp.concatenate(parts, axis=0).astype(F32)
        total = mm(normed_of(values).astype(BF), weight[:, heads_width:])
        qkv[span, heads_width:] = total[:rows]
        raw = total[:, :head]
        normal = raw * inverse_rms(raw) * gains[5:6, :head]
        rope_store(window.at[m], slice(None), 0, normal, wide_cos[...], wide_sin[...])
        window[m, :, head:] = total[:, head:].astype(BF)


def finish_kernel(info, part_a, part_b, theirs, *outs):
    query, key, value, out, gate, up, down = outs[:7]
    vectors = outs[7:]
    shard, hidden = gate.shape[1], gate.shape[2]

    def emit(first, second):
        gate[0] = first[:, :hidden].astype(F32)
        up[0] = first[:, hidden : 2 * hidden].astype(F32)
        for row, ref in enumerate(vectors):
            ref[...] = first[:GAIN_ROWS, 2 * hidden : 2 * hidden + ref.shape[1]].astype(F32)[
                row : row + 1
            ]
        start = 0
        for ref in (query, key, value):
            ref[0] = second[:, start : start + ref.shape[2]].astype(F32)
            start += ref.shape[2]
        for ref in (out, down):
            rows = ref.shape[1]
            for place in range(4):
                block = second[:, start : start + rows].astype(F32)
                ref[0, :, place * shard : (place + 1) * shard] = block.T
                start += rows

    @pl.when(info[2] == 0)
    def _():
        emit(part_a, theirs)

    @pl.when(info[2] == 1)
    def _():
        emit(theirs, part_b)


def project_kernel(info, gathered, x, gains, cosine, sine, blocks, qkv, query, own, weight, sem):
    copy = load_qkv(gathered, weight, sem)
    head = 2 * cosine.shape[1]
    residual = x[...].astype(F32)
    normed = residual * inverse_rms(residual) * gains[0:1, :]
    cut(blocks, normed)
    copy.wait()
    total = mm(normed.astype(BF), weight[...])
    qkv[...] = total
    heads = query.shape[1] // head
    for index in range(heads + 1):
        raw = total[:, index * head : (index + 1) * head]
        row = 4 if index < heads else 5
        normal = raw * inverse_rms(raw) * gains[row : row + 1, :head]
        target, start = (query, index * head) if index < heads else (own, 0)
        rope_store(target, slice(None), start, normal, cosine[...], sine[...])
    own[:, head:] = total[:, (heads + 1) * head :].astype(BF)


def select_kernel(info, own, one, two, *outs):
    for index, out in enumerate(outs):
        lower = (info[0] < (info[0] ^ (index + 1))).astype(F32)
        out[0] = one[...]
        mixed = own[...].astype(F32) * lower + two[...].astype(F32) * (1.0 - lower)
        out[1] = mixed.astype(BF)


def window_kernel(micro, info, own, one, two, *refs):
    got, window = refs[:3], refs[3]
    rows = own.shape[0] // micro
    for m in range(micro):
        span = slice(m * rows, (m + 1) * rows)
        parts = [own[span], one[span], two[span]]
        for ref in got:
            parts += [ref[0, span], ref[1, span]]
        for index, part in enumerate(parts):
            window[m, index * rows : (index + 1) * rows] = part


def attend_kernel(micro, info, gathered, query, x, gains, limit, *refs):
    out_w, sems = refs[-2:]
    model = x.shape[1]
    shard = model // 4
    copies = load_turned(gathered, out_w, sems, out_start(model), shard)
    if len(refs) == 1 + 6 + 2:
        window = refs[0]
        outs = refs[1:-2]
    else:
        window = refs[6]
        outs = refs[7:-2]
        window_kernel(micro, info, *refs[:6], window)
    probs, attended, branch, mixed, blocks, ffn_in = outs
    rows = query.shape[0] // micro
    head = window.shape[2] // 2
    heads = query.shape[1] // head
    count = window.shape[1]
    column = lax.broadcasted_iota(jnp.int32, (rows, count), 1)
    distance = lax.broadcasted_iota(jnp.int32, (rows, count), 0) + info[3]
    for index in range(count // rows):
        inside = (column >= index * rows) & (column < (index + 1) * rows)
        distance = distance - jnp.where(inside, column - index * rows + info[4 + index], 0)
    for m in range(micro):
        span = slice(m * rows, (m + 1) * rows)
        allowed = (distance >= 0) & (distance <= limit[span])
        bias = jnp.where(allowed, 0.0, NEG_LARGE)
        bias = jnp.concatenate([bias] * heads, axis=0)
        stacked = jnp.concatenate(
            [query[span, h * head : (h + 1) * head] for h in range(heads)], axis=0
        )
        scores = mm_nt(stacked, window[m, :, :head]) * head ** (-0.5) + bias
        exponent = jnp.exp(scores - jnp.max(scores, axis=-1, keepdims=True))
        chance = exponent / jnp.sum(exponent, axis=-1, keepdims=True)
        probs[m] = chance
        result = mm(chance.astype(BF), window[m, :, head:]).astype(BF)
        for h in range(heads):
            attended[span, h * head : (h + 1) * head] = result[h * rows : (h + 1) * rows]
    for copy in copies:
        copy.wait()
    total = mm_nt(attended[...], out_w[...])
    branch[...] = total
    value = x[...].astype(F32) + total * inverse_rms(total) * gains[1:2, :]
    mixed[...] = value
    normed = value * inverse_rms(value) * gains[2:3, :]
    ffn_in[...] = normed.astype(BF)
    for place in range(4):
        blocks[place] = normed[:, place * shard : (place + 1) * shard].astype(BF)


def gelu_parts(gate):
    c = 0.7978845608028654
    inner = jnp.tanh(c * (gate + 0.044715 * gate * gate * gate))
    value = 0.5 * gate * (1.0 + inner)
    slope = 0.5 * (1.0 + inner) + 0.5 * gate * (1.0 - inner * inner) * c * (
        1.0 + 3 * 0.044715 * gate * gate
    )
    return value, slope


def ffn_kernel(info, gathered, ffn_in, mixed, gains, gate_up, activated, down, result,
               gate_up_w, down_w, column_sems, sems):
    hidden = activated.shape[1]
    width = 512
    columns = load_columns(gathered, gate_up_w, column_sems, width)
    shard = ffn_in.shape[1] // 4
    copies = load_turned(gathered, down_w, sems, down_start(gathered, down_w.shape[1]), shard)
    for start in range(0, hidden, width):
        both = []
        for base in (start, hidden + start):
            columns[base // width].wait()
            total = mm(ffn_in[...], gate_up_w[:, base : base + width])
            gate_up[:, base : base + width] = total
            both.append(total)
        value, _ = gelu_parts(both[0])
        activated[:, start : start + width] = (value * both[1]).astype(BF)
    for copy in copies:
        copy.wait()
    total = mm_nt(activated[...], down_w[...])
    down[...] = total
    result[...] = (mixed[...] + total * inverse_rms(total) * gains[3:4, :]).astype(BF)


def ffn_back_kernel(info, gathered, upstream, mixed, down, gate_up, activated, blocks, gains,
                    *refs):
    packs, grad_mixed, gain_rows = refs[:4], refs[4], refs[5]
    grad_gate_up, gate_up_w, down_w, column_sems, sems = refs[6:]
    hidden = activated.shape[1]
    model = mixed.shape[1]
    shard = blocks.shape[2]
    copies = load_turned(gathered, down_w, sems, down_start(gathered, down_w.shape[1]), shard)
    columns = load_columns(gathered, gate_up_w, column_sems, 512)
    top = upstream[...].astype(F32)
    raw = down[...]
    scale = inverse_rms(raw)
    grad_down = norm_back(raw, scale, gains[3:4, :], top).astype(BF)
    gain_rows[...] = jnp.zeros_like(gain_rows)
    gain_rows[3:4, :] = gain_back(raw, scale, top)
    act_at = 2 * hidden + model
    block_at = act_at + hidden // 4
    for flip, pack in enumerate(packs):
        pack[:, 2 * hidden : act_at] = grad_down
        pack[:, act_at:block_at] = activated[:, slot(info[0] ^ flip, hidden // 4)]
        pack[:, block_at:] = jnp.zeros_like(pack[:, block_at:])
        pack[:, block_at : block_at + shard] = blocks[info[0] ^ flip]
    for copy in copies:
        copy.wait()
    width = 512
    for start in range(0, hidden, width):
        value, slope = gelu_parts(gate_up[:, start : start + width])
        up = gate_up[:, hidden + start : hidden + start + width]
        grad = mm(grad_down, down_w[:, start : start + width])
        grad_gate_up[:, start : start + width] = (grad * up * slope).astype(BF)
        grad_gate_up[:, hidden + start : hidden + start + width] = (grad * value).astype(BF)
    for pack in packs:
        pack[:, : 2 * hidden] = grad_gate_up[...]
    for copy in columns:
        copy.wait()
    grad_in = mm_nt(grad_gate_up[...], gate_up_w[...])
    raw = mixed[...]
    scale = inverse_rms(raw)
    gain_rows[2:3, :] = gain_back(raw, scale, grad_in)
    grad_mixed[...] = top + norm_back(raw, scale, gains[2:3, :], grad_in)


def attend_back_kernel(micro, info, gathered, grad_mixed, branch, window, probs, query, gains,
                       *refs):
    grad_branch, grad_query, own, one, two = refs[:5]
    gives, gain_rows, grad_attended, out_w, sems = refs[5:8], refs[8], refs[9], refs[10], refs[11]
    model = branch.shape[1]
    copies = load_turned(gathered, out_w, sems, out_start(model), model // 4)
    rows = own.shape[0] // micro
    head = own.shape[1] // 2
    heads = query.shape[1] // head
    factor = head ** (-0.5)
    raw = branch[...]
    scale = inverse_rms(raw)
    grad = grad_mixed[...]
    gain_rows[...] = jnp.zeros_like(gain_rows)
    gain_rows[1:2, :] = gain_back(raw, scale, grad)
    low = norm_back(raw, scale, gains[1:2, :], grad).astype(BF)
    grad_branch[...] = low
    for copy in copies:
        copy.wait()
    grad_attended[...] = mm(low, out_w[...]).astype(BF)
    for m in range(micro):
        span = slice(m * rows, (m + 1) * rows)
        chance = probs[m]
        keys, values = window[m, :, :head], window[m, :, head:]
        stacked = jnp.concatenate(
            [query[span, h * head : (h + 1) * head] for h in range(heads)], axis=0
        )
        upstream = jnp.concatenate(
            [grad_attended[span, h * head : (h + 1) * head] for h in range(heads)], axis=0
        )
        grad_values = mm_tn(chance.astype(BF), upstream)
        grad_chance = mm_nt(upstream, values)
        inner = jnp.sum(chance * grad_chance, axis=-1, keepdims=True)
        grad_scores = (chance * (grad_chance - inner)).astype(BF)
        grad_stacked = mm(grad_scores, keys) * factor
        grad_keys = mm_tn(grad_scores, stacked) * factor
        for h in range(heads):
            grad_query[span, h * head : (h + 1) * head] = grad_stacked[h * rows : (h + 1) * rows]
        for index, target in enumerate((own, one, two)):
            part = slice(index * rows, (index + 1) * rows)
            target[span, :head] = grad_keys[part]
            target[span, head:] = grad_values[part]
        for index, target in enumerate(gives):
            for side in range(2):
                start = (3 + 2 * index + side) * rows
                target[side, span, :head] = grad_keys[start : start + rows].astype(BF)
                target[side, span, head:] = grad_values[start : start + rows].astype(BF)


def combine_kernel(info, own, one, two, first, second, third, own_out, one_out, two_out):
    total_own, total_one, total_two = own[...], one[...], two[...]
    for index, got in enumerate((first, second, third)):
        lower = (info[0] < (info[0] ^ (index + 1))).astype(F32)
        total_one = total_one + got[0].astype(F32)
        side = got[1].astype(F32)
        total_own = total_own + side * lower
        total_two = total_two + side * (1.0 - lower)
    own_out[...] = total_own
    one_out[...] = total_one.astype(BF)
    two_out[...] = total_two.astype(BF)


def project_back_kernel(info, gathered, own, back_one, back_two, grad_query, qkv, cosine, sine, x, grad_mixed,
                        grad_branch, attended, blocks, gains, rows_ffn, rows_attn, *refs):
    packs, grad_in = refs[:4], refs[4]
    grad_qkv, gain_held, weight, sem = refs[5:]
    copy = load_qkv(gathered, weight, sem)
    tokens, model = x.shape
    shard = blocks.shape[2]
    half = cosine.shape[1]
    head = 2 * half
    heads = grad_query.shape[1] // head
    cos, sin = cosine[...], sine[...]
    grad_own = own[...] + back_one[...].astype(F32) + back_two[...].astype(F32)
    head_gains = [None, None]
    for index in range(heads + 1):
        if index < heads:
            grad = grad_query[:, index * head : (index + 1) * head]
        else:
            grad = grad_own[:, :head]
        one, two = grad[:, :half], grad[:, half:]
        grad = jnp.concatenate((one * cos + two * sin, two * cos - one * sin), axis=1)
        raw = qkv[:, index * head : (index + 1) * head]
        scale = inverse_rms(raw)
        kind = 0 if index < heads else 1
        term = gain_back(raw, scale, grad)
        head_gains[kind] = term if head_gains[kind] is None else head_gains[kind] + term
        back = norm_back(raw, scale, gains[4 + kind : 5 + kind, :head], grad)
        grad_qkv[:, index * head : (index + 1) * head] = back.astype(BF)
    grad_qkv[:, (heads + 1) * head :] = grad_own[:, head:].astype(BF)
    copy.wait()
    grad_normed = mm_nt(grad_qkv[...], weight[...])
    residual = x[...].astype(F32)
    scale = inverse_rms(residual)
    first_gain = gain_back(residual, scale, grad_normed)
    total = grad_mixed[...] + norm_back(residual, scale, gains[0:1, :], grad_normed)
    grad_in[...] = total.astype(BF)
    gain_held[...] = jnp.zeros_like(gain_held)
    part = head // 4
    four = (first_gain, rows_attn[1:2, :], rows_ffn[2:3, :], rows_ffn[3:4, :])
    for place in range(4):
        for row, values in enumerate(four):
            gain_held[place, row : row + 1, :shard] = values[
                :, place * shard : (place + 1) * shard
            ]
        for row, values in enumerate(head_gains):
            gain_held[place, 4 + row : 5 + row, :part] = values[
                :, place * part : (place + 1) * part
            ]
    wide = grad_qkv.shape[1]
    att_at = wide + model
    block_at = att_at + head
    for flip, pack in enumerate(packs):
        other = info[0] ^ flip
        pack[tokens:, :] = jnp.zeros_like(pack[tokens:, :])
        pack[tokens:, : gain_held.shape[2]] = gain_held[other].astype(BF)
        pack[:tokens, :wide] = grad_qkv[...]
        pack[:tokens, wide:att_at] = grad_branch[...]
        pack[:tokens, att_at:block_at] = attended[:, slot(other, head)]
        pack[:tokens, block_at:] = jnp.zeros_like(pack[:tokens, block_at:])
        pack[:tokens, block_at : block_at + shard] = blocks[other]


def over(packs, tokens, left, right, left_width, right_width):
    total = None
    for pack in packs:
        term = mm_tn(
            pack[:tokens, left : left + left_width], pack[:tokens, right : right + right_width]
        )
        total = term if total is None else total + term
    return total.astype(BF)


def ffn_weights_kernel(shard, model, info, *refs):
    packs, first, second = refs[:4], refs[4], refs[5]
    tokens = packs[0].shape[0]
    wide = first.shape[1]
    quarter = second.shape[1] // 4
    act_at = wide + model
    for start in range(0, wide, 1024):
        first[:, start : start + 1024] = over(
            packs, tokens, act_at + quarter, start, shard, 1024
        )
    for place in range(4):
        second[:, place * quarter : (place + 1) * quarter] = over(
            packs, tokens, wide + place * shard, act_at, shard, quarter
        )


def weights_kernel(shard, model, info, *refs):
    packs, gate_up, down, first, second = refs[:4], refs[4], refs[5], refs[6], refs[7]
    tokens = packs[0].shape[0] - GAIN_ROWS
    head = model // 5 * 2
    wide = packs[0].shape[1] - model - 2 * head
    hidden = gate_up.shape[1]
    first[:, :hidden] = gate_up[...]
    first[:, hidden:] = jnp.zeros_like(first[:, hidden:])
    gains = sum(pack[tokens:, :head].astype(F32) for pack in packs)
    first[:GAIN_ROWS, hidden : hidden + head] = gains.astype(BF)
    att_at = wide + model
    second[:, :wide] = over(packs, tokens, att_at + head, 0, shard, wide)
    for place in range(4):
        start = wide + place * head
        second[:, start : start + head] = over(
            packs, tokens, wide + place * shard, att_at, shard, head
        )
    second[:, wide + 4 * head :] = down[...]


class Links:
    def __init__(self, sizes):
        self.sizes = sizes

    def index(self, section, seq, fsdp):
        return (section * self.sizes["seq"] + seq) * self.sizes["fsdp"] + fsdp

    def send(self, array, section, place):
        pairs = []
        for z in range(self.sizes["seq"]):
            for f in range(self.sizes["fsdp"]):
                to_section, to_z, to_f = place(z, f)
                if 0 <= to_z < self.sizes["seq"]:
                    pairs.append((self.index(section, z, f), self.index(to_section, to_z, to_f)))
        return lax.ppermute(array, AXES, pairs)

    def along(self, array, section, by):
        return self.send(array, section, lambda z, f: (section, z + by, f))

    def across(self, array, section, flip):
        return self.send(array, section, lambda z, f: (section, z, f ^ flip))

    def cross(self, array, section):
        return self.send(array, section, lambda z, f: (1 - section, z, f))

    def both(self, array, flip):
        pairs = []
        for section in range(2):
            for z in range(self.sizes["seq"]):
                for f in range(self.sizes["fsdp"]):
                    pairs.append((self.index(section, z, f), self.index(section, z, f ^ flip)))
        return lax.ppermute(array, AXES, pairs)

    def swap(self, array):
        pairs = []
        for section in range(2):
            for z in range(self.sizes["seq"]):
                for f in range(self.sizes["fsdp"]):
                    pairs.append((self.index(section, z, f), self.index(1 - section, z, f)))
        return lax.ppermute(array, AXES, pairs)


def body(sizes, hidden_in, cotangent, positions, attn_gain, w_query, w_key, w_value, query_gain,
         key_gain, w_output, post_attn_gain, ffn_gain, w_gate, w_up, w_down, post_ffn_gain):
    section = lax.axis_index("section")
    seq = lax.axis_index("seq")
    fsdp = lax.axis_index("fsdp")
    is_first = section == 0
    micro, rows, model = hidden_in.shape
    tokens = micro * rows
    shard = w_query.shape[1]
    shards = sizes["fsdp"]
    heads_width, head = w_query.shape[2], w_key.shape[2]
    wide = heads_width + 2 * head
    hidden = w_gate.shape[2]
    quarter = hidden // shards
    assert shards == 4 and 2 * shards * rows == WIN and heads_width == shards * head
    links = Links(sizes)
    tie = lax.optimization_barrier
    info = jnp.stack([fsdp, seq, section]).astype(jnp.int32)

    width_of = 2 * hidden + heads_width + hidden + wide + 128
    folded = call(
        fold_kernel, info,
        [w_gate, w_up, w_query, w_key, w_value, w_output, w_down, attn_gain, post_attn_gain,
         ffn_gain, post_ffn_gain, query_gain, key_gain], [shape((shard, width_of), BF)],
        [pltpu.VMEM((head, model), BF), pltpu.VMEM((quarter, model), BF),
         pltpu.VMEM((shard, heads_width + hidden), BF), pltpu.VMEM((shard, 128), BF),
         pltpu.SemaphoreType.DMA((9,))],
        far=range(7), far_out=True,
    )[0]
    gathered = lax.all_gather(folded, "fsdp", axis=0, tiled=True)
    qkv_scratch = [pltpu.VMEM((model, wide), BF), pltpu.SemaphoreType.DMA]
    out_scratch = [pltpu.VMEM((model, heads_width), BF), pltpu.SemaphoreType.DMA((16,))]
    ffn_scratch = [pltpu.VMEM((model, 2 * hidden), BF), pltpu.VMEM((model, hidden), BF),
                   pltpu.SemaphoreType.DMA((2 * hidden // 512,)), pltpu.SemaphoreType.DMA((16,))]

    half = head // 2
    limit = jnp.minimum(positions.reshape(tokens, 1), WIN - 1)
    starts = [(seq - back) * shards + fsdp for back in range(3)]
    for flip in range(1, shards):
        other = fsdp ^ flip
        starts.append((seq - 1) * shards + other)
        starts.append(jnp.where(other < fsdp, seq, seq - 2) * shards + other)
    starts = jnp.stack(starts).astype(jnp.int32) * rows
    key_place = (starts[:, None] + jnp.arange(rows, dtype=jnp.int32)[None, :]).reshape(1, -1)
    info = jnp.concatenate((info, starts[:1], starts))
    span = key_place.shape[1]
    frequency = ROPE_BASE ** (-2.0 * jnp.arange(half, dtype=F32) / head)
    angles = key_place.reshape(span, 1).astype(F32) * frequency[None, :]
    wide_cos, wide_sin = jnp.cos(angles), jnp.sin(angles)
    cosine, sine = (jnp.tile(table[:rows], (micro, 1)) for table in (wide_cos, wide_sin))

    def fetch(own, target):
        one, two = links.along(own, target, 1), links.along(own, target, 2)
        sent = call(
            select_kernel, info, [own, one, two], [shape((2,) + own.shape, BF)] * (shards - 1),
            section=target,
        )
        return [own, one, two] + [links.across(array, target, 1 + i) for i, array in enumerate(sent)]

    gains = call(
        gains_kernel, info, [gathered], [shape((8, model), F32)],
        [pltpu.VMEM((shards, GAIN_ROWS, 128), BF), pltpu.SemaphoreType.DMA((shards,))], far=(0,),
    )[0]

    def forward(x, target, x_window=None):
        sizes_of = [shape((shards, tokens, shard), BF), shape((tokens, wide), F32),
                    shape((tokens, heads_width), BF)]
        whole = shape((micro, span, 2 * head), BF)
        attend_outs = [
            shape((micro, shards * rows, span), F32), shape((tokens, heads_width), BF),
            shape((tokens, model), F32), shape((tokens, model), F32),
            shape((shards, tokens, shard), BF), shape((tokens, model), BF),
        ]
        if x_window is not None:
            blocks, qkv, query, window = call(
                functools.partial(project_window_kernel, micro), info,
                [gathered] + x_window + [gains, cosine, sine, wide_cos, wide_sin],
                sizes_of + [whole], qkv_scratch, section=target, far=(0,),
                flops=2 * model * (tokens * heads_width + 2 * span * micro * head),
            )
            parts = [window]
        else:
            blocks, qkv, query, own = call(
                project_kernel, info, [gathered, x, gains, cosine, sine],
                sizes_of + [shape((tokens, 2 * head), BF)], qkv_scratch, section=target, far=(0,),
                flops=2 * tokens * model * wide,
            )
            parts = fetch(own, target)
            attend_outs = [whole] + attend_outs
        outs = call(
            functools.partial(attend_kernel, micro), info,
            [gathered, query, x, gains, limit] + parts, attend_outs, out_scratch, section=target,
            flops=2 * tokens * heads_width * (2 * span + model), far=(0,),
        )
        if x_window is None:
            window, *outs = outs
        probs, attended, branch, mixed, ffn_blocks, ffn_in = outs
        gate_up, activated, down, result = call(
            ffn_kernel, info, [gathered, ffn_in, mixed, gains],
            [shape((tokens, 2 * hidden), F32), shape((tokens, hidden), BF),
             shape((tokens, model), F32), shape((tokens, model), BF)], ffn_scratch,
            flops=6 * tokens * hidden * model, section=target, far=(0,),
        )
        saved = dict(
            x=x, blocks=blocks, qkv=qkv, query=query, window=window, probs=probs,
            attended=attended, branch=branch, mixed=mixed, ffn_blocks=ffn_blocks, gate_up=gate_up,
            activated=activated, down=down,
        )
        return result, saved

    def back_ffn(upstream, s, target):
        outs = call(
            ffn_back_kernel, info,
            [gathered, upstream, s["mixed"], s["down"], s["gate_up"], s["activated"],
             s["ffn_blocks"], gains],
            [shape((tokens, 2 * hidden + model + quarter + 256), BF)] * shards
            + [shape((tokens, model), F32), shape((8, model), F32)],
            [pltpu.VMEM((tokens, 2 * hidden), BF)] + ffn_scratch,
            flops=6 * tokens * hidden * model, section=target, far=(0,),
        )
        return outs[:shards], outs[shards], outs[shards + 1]

    def back_attend(grad_mixed, s, target):
        pair = [shape((tokens, 2 * head), F32)] * 3
        outs = call(
            functools.partial(attend_back_kernel, micro), info,
            [gathered, grad_mixed, s["branch"], s["window"], s["probs"], s["query"], gains],
            [shape((tokens, model), BF), shape((tokens, heads_width), F32)] + pair
            + [shape((2, tokens, 2 * head), BF)] * (shards - 1) + [shape((8, model), F32)],
            [pltpu.VMEM((tokens, heads_width), BF)] + out_scratch,
            flops=2 * tokens * heads_width * (4 * span + model), section=target, far=(0,),
        )
        return outs[0], outs[1], outs[2:5], outs[5:8], outs[8]

    def back_window(kept, gives, target, waiting):
        got = [links.across(array, target, 1 + i) for i, array in enumerate(gives)]
        ffn_packs, other = waiting
        if other is not None:
            got, other, ffn_packs = tie((got, other, ffn_packs))
            other = jnp.where(is_first, other[0], other[1])
            kept, other = tie((kept, other))
        own, one, two = call(
            combine_kernel, info, list(kept) + got,
            [shape((tokens, 2 * head), F32)] + [shape((tokens, 2 * head), BF)] * 2,
            section=target,
        )
        one, two = links.along(one, target, -1), links.along(two, target, -2)
        if other is None:
            one, ffn_packs = tie((one, ffn_packs))
        return (own, one, two), ffn_packs, other

    def back_project(window_grads, grad_query, grad_mixed, grad_branch, rows_ffn, rows_attn, s,
                     target):
        outs = call(
            project_back_kernel, info,
            [gathered] + list(window_grads) + [grad_query, s["qkv"], cosine, sine, s["x"], grad_mixed,
            grad_branch, s["attended"], s["blocks"], gains, rows_ffn, rows_attn],
            [shape((tokens + GAIN_ROWS, wide + model + head + 256), BF)] * shards
            + [shape((tokens, model), BF)],
            [pltpu.VMEM((tokens, wide), BF), pltpu.VMEM((shards, GAIN_ROWS, 256), F32)]
            + qkv_scratch,
            flops=2 * tokens * wide * model, section=target, far=(0,),
        )
        return outs[:shards], outs[shards]

    def exchange(packs, target):
        return [packs[0]] + [links.across(packs[i], target, i) for i in range(1, shards)]

    total_width = 2 * hidden + 512

    def ffn_weights(packs, target):
        return call(
            functools.partial(ffn_weights_kernel, shard, model), info, list(packs),
            [shape((shard, 2 * hidden), BF), shape((shard, hidden), BF)],
            flops=2 * shards * tokens * shard * 3 * hidden, section=target,
        )

    def attn_weights(packs, ffn, target):
        return call(
            functools.partial(weights_kernel, shard, model), info, list(packs) + list(ffn),
            [shape((shard, total_width), BF)] * 2,
            flops=2 * shards * tokens * shard * (total_width - hidden), section=target,
        )

    def backward(upstream, s, target, other=None):
        ffn_packs, grad_mixed, rows_ffn = back_ffn(upstream, s, target)
        grad_branch, grad_query, kept, gives, rows_attn = back_attend(grad_mixed, s, target)
        window_grads, ffn_packs, other = back_window(kept, gives, target, (ffn_packs, other))
        ffn_packs = exchange(ffn_packs, target)
        attn_packs, grad_in = back_project(
            window_grads, grad_query, grad_mixed, grad_branch, rows_ffn, rows_attn, s, target
        )
        return ffn_weights(ffn_packs, target), attn_packs, grad_in, other

    x_first = hidden_in.reshape(tokens, model)
    result_a, saved_a = forward(x_first, 0, fetch(x_first, 0))
    middle = links.cross(result_a, 0)
    result_b, saved_b = forward(middle, 1)

    ffn, attn_packs, grad_b, _ = backward(cotangent.reshape(tokens, model), saved_b, 1)
    upstream = links.cross(grad_b, 1)
    upstream, attn_packs = tie((upstream, attn_packs))
    b_first, b_second = attn_weights(exchange(attn_packs, 1), ffn, 1)
    upstream, b_first, b_second = tie((upstream, b_first, b_second))
    halves_b = (links.cross(b_first, 1), b_second)

    ffn, attn_packs, grad_a, half_b = backward(upstream, saved_a, 0, halves_b)
    part_b = lax.psum(half_b, "seq")
    attn_packs, part_b = tie((exchange(attn_packs, 0), part_b))
    a_first, a_second = attn_weights(attn_packs, ffn, 0)
    part_a = lax.psum(jnp.where(is_first, a_first, links.cross(a_second, 0)), "seq")
    theirs = links.swap(jnp.where(is_first, part_b, part_a))

    part = head // shards
    grads = call(
        finish_kernel, info, [part_a, part_b, theirs],
        [shape((1, shard, heads_width), F32), shape((1, shard, head), F32),
         shape((1, shard, head), F32), shape((1, head, model), F32),
         shape((1, shard, hidden), F32), shape((1, shard, hidden), F32),
         shape((1, quarter, model), F32)]
        + [shape((1, shard), F32)] * 4 + [shape((1, part), F32)] * 2,
    )
    g_query, g_key, g_value, g_out, g_gate, g_up, g_down = grads[:7]
    g_attn, g_post_attn, g_ffn, g_post_ffn, g_query_gain, g_key_gain = grads[7:]
    section_outputs = jnp.where(is_first, result_a, result_b).reshape(1, micro, rows, model)
    input_grads = jnp.where(is_first, grad_a, grad_b).reshape(1, micro, rows, model)
    return (
        section_outputs, input_grads, g_attn, g_query, g_key, g_value, g_query_gain, g_key_gain,
        g_out, g_post_attn, g_ffn, g_gate, g_up, g_down, g_post_ffn,
    )


def solution(mesh):
    rows = P(None, ("seq", "fsdp"), None)
    vector, matrix = P("section", "fsdp"), P("section", "fsdp", None)
    weights = (vector, matrix, matrix, matrix, vector, vector, matrix, vector, vector, matrix,
               matrix, matrix, vector)
    out_rows = P("section", None, ("seq", "fsdp"), None)
    return jax.shard_map(
        functools.partial(body, dict(mesh.shape)),
        mesh=mesh,
        in_specs=(rows, rows, P(None, ("seq", "fsdp"))) + weights,
        out_specs=(out_rows, out_rows) + weights,
        check_vma=False,
    )
```

```python
import functools

import jax
import jax.numpy as jnp
from jax import lax
from jax.experimental import pallas as pl
from jax.experimental.pallas import tpu as pltpu
from jax.sharding import PartitionSpec as P

WIN = 512
EPSILON = 1e-06
ROPE_BASE = 10000.0
NEG_LARGE = -1e30
AXES = ("section", "seq", "fsdp")
BF = jnp.bfloat16
F32 = jnp.float32
GAIN_ROWS = 16
INTERPRET = False


def mm(left, right):
    return lax.dot_general(left, right, (((1,), (0,)), ((), ())), preferred_element_type=F32)


def mm_nt(left, right):
    return lax.dot_general(left, right, (((1,), (1,)), ((), ())), preferred_element_type=F32)


def mm_tn(left, right):
    return lax.dot_general(left, right, (((0,), (0,)), ((), ())), preferred_element_type=F32)


def inverse_rms(values):
    return lax.rsqrt(jnp.mean(values * values, axis=-1, keepdims=True) + EPSILON)


def norm_back(values, scale, gain, grad):
    weighted = grad * gain
    inner = jnp.mean(values * weighted, axis=-1, keepdims=True)
    return scale * weighted - values * (scale * scale * scale * inner)


def gain_back(values, scale, grad):
    return jnp.sum(values * scale * grad, axis=0, keepdims=True)


def call(kernel, info, arrays, outs, scratch=(), section=None, pieces=(), staged=False, far=(),
         far_out=False):
    smem = pl.BlockSpec(memory_space=pltpu.SMEM)
    vmem = pl.BlockSpec(memory_space=pltpu.VMEM)
    hbm = pl.BlockSpec(memory_space=pltpu.HBM)
    count, lead = len(arrays), len(pieces)
    scratch = list(scratch)
    if staged:
        scratch += [pltpu.VMEM(a.shape, a.dtype) for a in arrays]
        scratch += [pltpu.SemaphoreType.DMA((count,))]

    def entry(info, *refs):
        ins, rest = refs[lead : lead + count], refs[lead + count :]

        def run(ins=ins, rest=rest):
            if staged:
                rest, held, sems = rest[: -count - 1], rest[-count - 1 : -1], rest[-1]
                copies = [
                    pltpu.make_async_copy(source, target, sems.at[i])
                    for i, (source, target) in enumerate(zip(ins, held))
                ]
                for copy in copies:
                    copy.start()
                for copy in copies:
                    copy.wait()
                ins = held
            kernel(info, *((refs[:lead],) if lead else ()), *ins, *rest)

        if section is None:
            run()
        else:
            pl.when(info[2] == section)(run)

    return pl.pallas_call(
        entry,
        out_shape=outs,
        in_specs=[smem] + [hbm] * lead
        + [hbm if staged or i in far else vmem for i in range(count)],
        out_specs=[hbm if far_out else vmem] * len(outs),
        scratch_shapes=scratch,
        compiler_params=pltpu.CompilerParams(vmem_limit_bytes=32 * 1024 * 1024),
        cost_estimate=pl.CostEstimate(flops=1, bytes_accessed=1, transcendentals=0),
        interpret=INTERPRET,
    )(info, *pieces, *arrays)


def shape(dims, kind):
    return jax.ShapeDtypeStruct(tuple(dims), kind)


def slot(index, width):
    return pl.ds(pl.multiple_of(index * width, width), width)


def layout(model):
    unit = model // 5
    return unit * 32, unit * 40, unit * 56, unit * 68


def sources(pieces, start):
    own, one, two, left, right = pieces
    split = left.shape[1]
    last = (left, start) if start < split else (right, start - split)
    return [(own, start), (one, start), (two, start), last]


def gains_kernel(info, gathered, out, held, sems):
    count, rows, width = held.shape
    shard = out.shape[1] // count
    part = shard * 2 // 5
    copies = []
    for flip, (piece, start) in enumerate(sources(gathered, layout(out.shape[1])[3])):
        source = piece.at[pl.ds(0, rows), pl.ds(start, width)]
        copies.append(pltpu.make_async_copy(source, held.at[info[0] ^ flip], sems.at[flip]))
    for copy in copies:
        copy.start()
    for copy in copies:
        copy.wait()
    out[...] = jnp.zeros_like(out)
    for place in range(count):
        values = held[place].astype(F32)
        start = place * shard
        for row in range(4):
            out[row : row + 1, start : start + width] = values[2 * row : 2 * row + 1]
            out[row : row + 1, start + width : start + shard] = values[
                2 * row + 1 : 2 * row + 2, : shard - width
            ]
        for row in range(2):
            out[4 + row : 5 + row, place * part : (place + 1) * part] = values[
                8 + row : 9 + row, :part
            ]


def fold_kernel(info, gate, up, query, key, value, out_w, down_w, attn, post_attn, ffn, post_ffn,
                query_gain, key_gain, folded, out_held, down_held, turned, gain_block, *rest):
    shard = gate.shape[1]
    vectors, sems = rest[:-1], rest[-1]
    loads = [
        pltpu.make_async_copy(out_w.at[0], out_held, sems.at[0]),
        pltpu.make_async_copy(down_w.at[0], down_held, sems.at[1]),
    ]
    small = [
        pltpu.make_async_copy(source, held, sems.at[9 + i])
        for i, (source, held) in enumerate(
            zip((attn, post_attn, ffn, post_ffn, query_gain, key_gain), vectors)
        )
    ]
    for copy in loads + small:
        copy.start()
    moves = []

    def move(source, start):
        copy = pltpu.make_async_copy(
            source, folded.at[:, pl.ds(start, source.shape[1])], sems.at[2 + len(moves)]
        )
        copy.start()
        moves.append(copy)
        return start + source.shape[1]

    start = move(up.at[0], move(gate.at[0], 0))
    turned_at = start
    start += turned.shape[1]
    for ref in (query, key, value):
        start = move(ref.at[0], start)
    width = gain_block.shape[1]
    gain_block[...] = jnp.zeros_like(gain_block)
    wait_all(small)
    for row, ref in enumerate(vectors[:4]):
        gain_block[2 * row : 2 * row + 1, :] = ref[:, :width]
        gain_block[2 * row + 1 : 2 * row + 2, : shard - width] = ref[:, width:]
    for row, ref in enumerate(vectors[4:]):
        gain_block[8 + row : 9 + row, : ref.shape[1]] = ref[...]
    move(gain_block, start)
    start = 0
    for load, held in zip(loads, (out_held, down_held)):
        load.wait()
        rows = held.shape[0]
        for place in range(4):
            block = held[:, place * shard : (place + 1) * shard].astype(F32)
            turned[:, start : start + rows] = block.T.astype(BF)
            start += rows
    move(turned, turned_at)
    for copy in moves:
        copy.wait()


def load_turned(info, gathered, held, sems, start):
    width, shard = held.shape[1] // 4, held.shape[0] // 4
    copies = []
    for flip, (piece, column) in enumerate(sources(gathered, start)):
        for row in range(4):
            copy = pltpu.make_async_copy(
                piece.at[:, pl.ds(column + row * width, width)],
                held.at[pl.ds(row * shard, shard), slot(info[0] ^ flip, width)],
                sems.at[4 * flip + row],
            )
            copy.start()
            copies.append(copy)
    return copies


def load_rows(info, gathered, held, sems, start):
    shard, width = held.shape[0] // 4, held.shape[1]
    copies = []
    for flip, (piece, column) in enumerate(sources(gathered, start)):
        copy = pltpu.make_async_copy(
            piece.at[:, pl.ds(column, width)], held.at[slot(info[0] ^ flip, shard)], sems.at[flip]
        )
        copy.start()
        copies.append(copy)
    return copies


def wait_all(copies):
    for copy in copies:
        copy.wait()


def rope_store(target, rows, start, normal, cos, sin):
    half = cos.shape[1]
    one, two = normal[:, :half], normal[:, half:]
    target[rows, start : start + half] = (one * cos - two * sin).astype(BF)
    target[rows, start + half : start + 2 * half] = (two * cos + one * sin).astype(BF)


def cut(blocks, normed):
    shard = blocks.shape[2]
    for place in range(blocks.shape[0]):
        blocks[place] = normed[:, place * shard : (place + 1) * shard].astype(BF)


def project_window_kernel(micro, info, gathered, x, one, two, *refs):
    got, (gains, cosine, sine, wide_cos, wide_sin) = refs[:3], refs[3:8]
    blocks, qkv, query, window, weight, sems = refs[8:]
    copies = load_rows(info, gathered, weight, sems, layout(x.shape[1])[2])
    rows = x.shape[0] // micro
    head = window.shape[2] // 2
    heads_width = query.shape[1]

    def normed_of(values):
        return values * inverse_rms(values) * gains[0:1, :]

    normed = normed_of(x[...].astype(F32))
    cut(blocks, normed)
    normed = normed.astype(BF)
    wait_all(copies)
    total = mm(normed, weight[:, :heads_width])
    qkv[:, :heads_width] = total
    for start in range(0, heads_width, head):
        raw = total[:, start : start + head]
        normal = raw * inverse_rms(raw) * gains[4:5, :head]
        rope_store(query, slice(None), start, normal, cosine[...], sine[...])
    for m in range(micro):
        span = slice(m * rows, (m + 1) * rows)
        parts = [x[span], one[span], two[span]]
        for ref in got:
            parts += [ref[0, span], ref[1, span]]
        values = jnp.concatenate(parts, axis=0).astype(F32)
        total = mm(normed_of(values).astype(BF), weight[:, heads_width:])
        qkv[span, heads_width:] = total[:rows]
        raw = total[:, :head]
        normal = raw * inverse_rms(raw) * gains[5:6, :head]
        rope_store(window.at[m], slice(None), 0, normal, wide_cos[...], wide_sin[...])
        window[m, :, head:] = total[:, head:].astype(BF)


def finish_kernel(info, part_a, part_b, theirs, *outs):
    query, key, value, out, gate, up, down = outs[:7]
    vectors = outs[7:]
    shard, hidden = gate.shape[1], gate.shape[2]

    def emit(first, second):
        gate[0] = first[:, :hidden].astype(F32)
        up[0] = first[:, hidden : 2 * hidden].astype(F32)
        for row, ref in enumerate(vectors):
            ref[...] = first[:GAIN_ROWS, 2 * hidden : 2 * hidden + ref.shape[1]].astype(F32)[
                row : row + 1
            ]
        start = 0
        for ref in (query, key, value):
            ref[0] = second[:, start : start + ref.shape[2]].astype(F32)
            start += ref.shape[2]
        for ref in (out, down):
            rows = ref.shape[1]
            for place in range(4):
                block = second[:, start : start + rows].astype(F32)
                ref[0, :, place * shard : (place + 1) * shard] = block.T
                start += rows

    @pl.when(info[2] == 0)
    def _():
        emit(part_a, theirs)

    @pl.when(info[2] == 1)
    def _():
        emit(theirs, part_b)


def project_kernel(info, gathered, x, gains, cosine, sine, token, blocks, qkv, query, own, weight,
                   sems):
    copies = load_rows(info, gathered, weight, sems, layout(x.shape[1])[2])
    head = 2 * cosine.shape[1]
    residual = x[...].astype(F32)
    normed = residual * inverse_rms(residual) * gains[0:1, :]
    cut(blocks, normed)
    wait_all(copies)
    total = mm(normed.astype(BF), weight[...])
    qkv[...] = total
    heads = query.shape[1] // head
    for index in range(heads + 1):
        raw = total[:, index * head : (index + 1) * head]
        row = 4 if index < heads else 5
        normal = raw * inverse_rms(raw) * gains[row : row + 1, :head]
        target, start = (query, index * head) if index < heads else (own, 0)
        rope_store(target, slice(None), start, normal, cosine[...], sine[...])
    own[:, head:] = total[:, (heads + 1) * head :].astype(BF)


def select_kernel(info, own, one, two, *outs):
    for index, out in enumerate(outs):
        lower = (info[0] < (info[0] ^ (index + 1))).astype(F32)
        out[0] = one[...]
        mixed = own[...].astype(F32) * lower + two[...].astype(F32) * (1.0 - lower)
        out[1] = mixed.astype(BF)


def window_kernel(micro, info, own, one, two, *refs):
    got, window = refs[:3], refs[3]
    rows = own.shape[0] // micro
    for m in range(micro):
        span = slice(m * rows, (m + 1) * rows)
        parts = [own[span], one[span], two[span]]
        for ref in got:
            parts += [ref[0, span], ref[1, span]]
        for index, part in enumerate(parts):
            window[m, index * rows : (index + 1) * rows] = part


def attend_kernel(micro, info, gathered, query, x, gains, limit, *refs):
    out_w, sems = refs[-2:]
    model = x.shape[1]
    shard = model // 4
    copies = load_turned(info, gathered, out_w, sems, layout(model)[0])
    if len(refs) == 1 + 6 + 2:
        window = refs[0]
        outs = refs[1:-2]
    else:
        window = refs[6]
        outs = refs[7:-2]
        window_kernel(micro, info, *refs[:6], window)
    probs, attended, branch, mixed, blocks, ffn_in = outs
    rows = query.shape[0] // micro
    head = window.shape[2] // 2
    heads = query.shape[1] // head
    count = window.shape[1]
    column = lax.broadcasted_iota(jnp.int32, (rows, count), 1)
    distance = lax.broadcasted_iota(jnp.int32, (rows, count), 0) + info[3]
    for index in range(count // rows):
        inside = (column >= index * rows) & (column < (index + 1) * rows)
        distance = distance - jnp.where(inside, column - index * rows + info[4 + index], 0)
    for m in range(micro):
        span = slice(m * rows, (m + 1) * rows)
        allowed = (distance >= 0) & (distance <= limit[span])
        bias = jnp.where(allowed, 0.0, NEG_LARGE)
        bias = jnp.concatenate([bias] * heads, axis=0)
        stacked = jnp.concatenate(
            [query[span, h * head : (h + 1) * head] for h in range(heads)], axis=0
        )
        scores = mm_nt(stacked, window[m, :, :head]) * head ** (-0.5) + bias
        exponent = jnp.exp(scores - jnp.max(scores, axis=-1, keepdims=True))
        chance = exponent / jnp.sum(exponent, axis=-1, keepdims=True)
        probs[m] = chance
        result = mm(chance.astype(BF), window[m, :, head:]).astype(BF)
        for h in range(heads):
            attended[span, h * head : (h + 1) * head] = result[h * rows : (h + 1) * rows]
    for copy in copies:
        copy.wait()
    total = mm_nt(attended[...], out_w[...])
    branch[...] = total
    value = x[...].astype(F32) + total * inverse_rms(total) * gains[1:2, :]
    mixed[...] = value
    normed = value * inverse_rms(value) * gains[2:3, :]
    ffn_in[...] = normed.astype(BF)
    for place in range(4):
        blocks[place] = normed[:, place * shard : (place + 1) * shard].astype(BF)


def gelu_parts(gate):
    c = 0.7978845608028654
    inner = jnp.tanh(c * (gate + 0.044715 * gate * gate * gate))
    value = 0.5 * gate * (1.0 + inner)
    slope = 0.5 * (1.0 + inner) + 0.5 * gate * (1.0 - inner * inner) * c * (
        1.0 + 3 * 0.044715 * gate * gate
    )
    return value, slope


def ffn_kernel(info, gathered, ffn_in, mixed, gains, gate_up, activated, down, result,
               gate_up_w, down_w, column_sems, sems):
    hidden = activated.shape[1]
    width = 512
    columns = load_rows(info, gathered, gate_up_w, column_sems, 0)
    copies = load_turned(info, gathered, down_w, sems, layout(mixed.shape[1])[1])
    wait_all(columns)
    for start in range(0, hidden, width):
        both = []
        for base in (start, hidden + start):
            total = mm(ffn_in[...], gate_up_w[:, base : base + width])
            gate_up[:, base : base + width] = total
            both.append(total)
        value, _ = gelu_parts(both[0])
        activated[:, start : start + width] = (value * both[1]).astype(BF)
    for copy in copies:
        copy.wait()
    total = mm_nt(activated[...], down_w[...])
    down[...] = total
    result[...] = (mixed[...] + total * inverse_rms(total) * gains[3:4, :]).astype(BF)


def ffn_back_kernel(info, gathered, upstream, mixed, down, gate_up, activated, blocks, gains,
                    *refs):
    packs, grad_mixed, gain_rows = refs[:4], refs[4], refs[5]
    grad_gate_up, gate_up_w, down_w, column_sems, sems = refs[6:]
    hidden = activated.shape[1]
    model = mixed.shape[1]
    shard = blocks.shape[2]
    copies = load_turned(info, gathered, down_w, sems, layout(mixed.shape[1])[1])
    columns = load_rows(info, gathered, gate_up_w, column_sems, 0)
    top = upstream[...].astype(F32)
    raw = down[...]
    scale = inverse_rms(raw)
    grad_down = norm_back(raw, scale, gains[3:4, :], top).astype(BF)
    gain_rows[...] = jnp.zeros_like(gain_rows)
    gain_rows[3:4, :] = gain_back(raw, scale, top)
    act_at = 2 * hidden + model
    block_at = act_at + hidden // 4
    for flip, pack in enumerate(packs):
        pack[:, 2 * hidden : act_at] = grad_down
        pack[:, act_at:block_at] = activated[:, slot(info[0] ^ flip, hidden // 4)]
        pack[:, block_at:] = jnp.zeros_like(pack[:, block_at:])
        pack[:, block_at : block_at + shard] = blocks[info[0] ^ flip]
    for copy in copies:
        copy.wait()
    width = 512
    for start in range(0, hidden, width):
        value, slope = gelu_parts(gate_up[:, start : start + width])
        up = gate_up[:, hidden + start : hidden + start + width]
        grad = mm(grad_down, down_w[:, start : start + width])
        grad_gate_up[:, start : start + width] = (grad * up * slope).astype(BF)
        grad_gate_up[:, hidden + start : hidden + start + width] = (grad * value).astype(BF)
    for pack in packs:
        pack[:, : 2 * hidden] = grad_gate_up[...]
    for copy in columns:
        copy.wait()
    grad_in = mm_nt(grad_gate_up[...], gate_up_w[...])
    raw = mixed[...]
    scale = inverse_rms(raw)
    gain_rows[2:3, :] = gain_back(raw, scale, grad_in)
    grad_mixed[...] = top + norm_back(raw, scale, gains[2:3, :], grad_in)


def attend_back_kernel(micro, info, gathered, grad_mixed, branch, window, probs, query, gains,
                       *refs):
    grad_branch, grad_query, own, one, two = refs[:5]
    gives, gain_rows, grad_attended, out_w, sems = refs[5:8], refs[8], refs[9], refs[10], refs[11]
    model = branch.shape[1]
    copies = load_turned(info, gathered, out_w, sems, layout(model)[0])
    rows = own.shape[0] // micro
    head = own.shape[1] // 2
    heads = query.shape[1] // head
    factor = head ** (-0.5)
    raw = branch[...]
    scale = inverse_rms(raw)
    grad = grad_mixed[...]
    gain_rows[...] = jnp.zeros_like(gain_rows)
    gain_rows[1:2, :] = gain_back(raw, scale, grad)
    low = norm_back(raw, scale, gains[1:2, :], grad).astype(BF)
    grad_branch[...] = low
    for copy in copies:
        copy.wait()
    grad_attended[...] = mm(low, out_w[...]).astype(BF)
    for m in range(micro):
        span = slice(m * rows, (m + 1) * rows)
        chance = probs[m]
        keys, values = window[m, :, :head], window[m, :, head:]
        stacked = jnp.concatenate(
            [query[span, h * head : (h + 1) * head] for h in range(heads)], axis=0
        )
        upstream = jnp.concatenate(
            [grad_attended[span, h * head : (h + 1) * head] for h in range(heads)], axis=0
        )
        grad_values = mm_tn(chance.astype(BF), upstream)
        grad_chance = mm_nt(upstream, values)
        inner = jnp.sum(chance * grad_chance, axis=-1, keepdims=True)
        grad_scores = (chance * (grad_chance - inner)).astype(BF)
        grad_stacked = mm(grad_scores, keys) * factor
        grad_keys = mm_tn(grad_scores, stacked) * factor
        for h in range(heads):
            grad_query[span, h * head : (h + 1) * head] = grad_stacked[h * rows : (h + 1) * rows]
        for index, target in enumerate((own, one, two)):
            part = slice(index * rows, (index + 1) * rows)
            target[span, :head] = grad_keys[part]
            target[span, head:] = grad_values[part]
        for index, target in enumerate(gives):
            for side in range(2):
                start = (3 + 2 * index + side) * rows
                target[side, span, :head] = grad_keys[start : start + rows].astype(BF)
                target[side, span, head:] = grad_values[start : start + rows].astype(BF)


def combine_kernel(info, own, one, two, first, second, third, own_out, one_out, two_out):
    total_own, total_one, total_two = own[...], one[...], two[...]
    for index, got in enumerate((first, second, third)):
        lower = (info[0] < (info[0] ^ (index + 1))).astype(F32)
        total_one = total_one + got[0].astype(F32)
        side = got[1].astype(F32)
        total_own = total_own + side * lower
        total_two = total_two + side * (1.0 - lower)
    own_out[...] = total_own
    one_out[...] = total_one.astype(BF)
    two_out[...] = total_two.astype(BF)


def project_back_kernel(info, gathered, own, back_one, back_two, grad_query, qkv, cosine, sine, x, grad_mixed,
                        grad_branch, attended, blocks, gains, rows_ffn, rows_attn, *refs):
    packs, grad_in = refs[:4], refs[4]
    grad_qkv, gain_held, weight, sems = refs[5:]
    copies = load_rows(info, gathered, weight, sems, layout(x.shape[1])[2])
    tokens, model = x.shape
    shard = blocks.shape[2]
    half = cosine.shape[1]
    head = 2 * half
    heads = grad_query.shape[1] // head
    cos, sin = cosine[...], sine[...]
    grad_own = own[...] + back_one[...].astype(F32) + back_two[...].astype(F32)
    head_gains = [None, None]
    for index in range(heads + 1):
        if index < heads:
            grad = grad_query[:, index * head : (index + 1) * head]
        else:
            grad = grad_own[:, :head]
        one, two = grad[:, :half], grad[:, half:]
        grad = jnp.concatenate((one * cos + two * sin, two * cos - one * sin), axis=1)
        raw = qkv[:, index * head : (index + 1) * head]
        scale = inverse_rms(raw)
        kind = 0 if index < heads else 1
        term = gain_back(raw, scale, grad)
        head_gains[kind] = term if head_gains[kind] is None else head_gains[kind] + term
        back = norm_back(raw, scale, gains[4 + kind : 5 + kind, :head], grad)
        grad_qkv[:, index * head : (index + 1) * head] = back.astype(BF)
    grad_qkv[:, (heads + 1) * head :] = grad_own[:, head:].astype(BF)
    wait_all(copies)
    grad_normed = mm_nt(grad_qkv[...], weight[...])
    residual = x[...].astype(F32)
    scale = inverse_rms(residual)
    first_gain = gain_back(residual, scale, grad_normed)
    total = grad_mixed[...] + norm_back(residual, scale, gains[0:1, :], grad_normed)
    grad_in[...] = total.astype(BF)
    gain_held[...] = jnp.zeros_like(gain_held)
    part = head // 4
    four = (first_gain, rows_attn[1:2, :], rows_ffn[2:3, :], rows_ffn[3:4, :])
    for place in range(4):
        for row, values in enumerate(four):
            gain_held[place, row : row + 1, :shard] = values[
                :, place * shard : (place + 1) * shard
            ]
        for row, values in enumerate(head_gains):
            gain_held[place, 4 + row : 5 + row, :part] = values[
                :, place * part : (place + 1) * part
            ]
    wide = grad_qkv.shape[1]
    att_at = wide + model
    block_at = att_at + head
    for flip, pack in enumerate(packs):
        other = info[0] ^ flip
        pack[tokens:, :] = jnp.zeros_like(pack[tokens:, :])
        pack[tokens:, : gain_held.shape[2]] = gain_held[other].astype(BF)
        pack[:tokens, :wide] = grad_qkv[...]
        pack[:tokens, wide:att_at] = grad_branch[...]
        pack[:tokens, att_at:block_at] = attended[:, slot(other, head)]
        pack[:tokens, block_at:] = jnp.zeros_like(pack[:tokens, block_at:])
        pack[:tokens, block_at : block_at + shard] = blocks[other]


def over(packs, tokens, left, right, left_width, right_width):
    total = None
    for pack in packs:
        term = mm_tn(
            pack[:tokens, left : left + left_width], pack[:tokens, right : right + right_width]
        )
        total = term if total is None else total + term
    return total.astype(BF)


def ffn_weights_kernel(shard, model, info, *refs):
    packs, first, second = refs[:4], refs[4], refs[5]
    tokens = packs[0].shape[0]
    wide = first.shape[1]
    quarter = second.shape[1] // 4
    act_at = wide + model
    for start in range(0, wide, 1024):
        first[:, start : start + 1024] = over(
            packs, tokens, act_at + quarter, start, shard, 1024
        )
    for place in range(4):
        second[:, place * quarter : (place + 1) * quarter] = over(
            packs, tokens, wide + place * shard, act_at, shard, quarter
        )


def weights_kernel(shard, model, info, *refs):
    packs, gate_up, down, first, second = refs[:4], refs[4], refs[5], refs[6], refs[7]
    tokens = packs[0].shape[0] - GAIN_ROWS
    head = model // 5 * 2
    wide = packs[0].shape[1] - model - 2 * head
    hidden = gate_up.shape[1]
    first[:, :hidden] = gate_up[...]
    first[:, hidden:] = jnp.zeros_like(first[:, hidden:])
    gains = sum(pack[tokens:, :head].astype(F32) for pack in packs)
    first[:GAIN_ROWS, hidden : hidden + head] = gains.astype(BF)
    att_at = wide + model
    second[:, :wide] = over(packs, tokens, att_at + head, 0, shard, wide)
    for place in range(4):
        start = wide + place * head
        second[:, start : start + head] = over(
            packs, tokens, wide + place * shard, att_at, shard, head
        )
    second[:, wide + 4 * head :] = down[...]


class Links:
    def __init__(self, sizes):
        self.sizes = sizes

    def index(self, section, seq, fsdp):
        return (section * self.sizes["seq"] + seq) * self.sizes["fsdp"] + fsdp

    def send(self, array, section, place):
        pairs = []
        for z in range(self.sizes["seq"]):
            for f in range(self.sizes["fsdp"]):
                to_section, to_z, to_f = place(z, f)
                if 0 <= to_z < self.sizes["seq"]:
                    pairs.append((self.index(section, z, f), self.index(to_section, to_z, to_f)))
        return lax.ppermute(array, AXES, pairs)

    def along(self, array, section, by):
        return self.send(array, section, lambda z, f: (section, z + by, f))

    def across(self, array, section, flip):
        return self.send(array, section, lambda z, f: (section, z, f ^ flip))

    def cross(self, array, section):
        return self.send(array, section, lambda z, f: (1 - section, z, f))

    def both(self, array, flip):
        pairs = []
        for section in range(2):
            for z in range(self.sizes["seq"]):
                for f in range(self.sizes["fsdp"]):
                    pairs.append((self.index(section, z, f), self.index(section, z, f ^ flip)))
        return lax.ppermute(array, AXES, pairs)

    def swap(self, array):
        pairs = []
        for section in range(2):
            for z in range(self.sizes["seq"]):
                for f in range(self.sizes["fsdp"]):
                    pairs.append((self.index(section, z, f), self.index(1 - section, z, f)))
        return lax.ppermute(array, AXES, pairs)


def body(sizes, hidden_in, cotangent, positions, attn_gain, w_query, w_key, w_value, query_gain,
         key_gain, w_output, post_attn_gain, ffn_gain, w_gate, w_up, w_down, post_ffn_gain):
    section = lax.axis_index("section")
    seq = lax.axis_index("seq")
    fsdp = lax.axis_index("fsdp")
    is_first = section == 0
    micro, rows, model = hidden_in.shape
    tokens = micro * rows
    shard = w_query.shape[1]
    shards = sizes["fsdp"]
    heads_width, head = w_query.shape[2], w_key.shape[2]
    wide = heads_width + 2 * head
    hidden = w_gate.shape[2]
    quarter = hidden // shards
    assert shards == 4 and 2 * shards * rows == WIN and heads_width == shards * head
    links = Links(sizes)
    tie = lax.optimization_barrier
    info = jnp.stack([fsdp, seq, section]).astype(jnp.int32)

    width_of = 2 * hidden + heads_width + hidden + wide + 128
    folded = call(
        fold_kernel, info,
        [w_gate, w_up, w_query, w_key, w_value, w_output, w_down, attn_gain, post_attn_gain,
         ffn_gain, post_ffn_gain, query_gain, key_gain], [shape((shard, width_of), BF)],
        [pltpu.VMEM((head, model), BF), pltpu.VMEM((quarter, model), BF),
         pltpu.VMEM((shard, heads_width + hidden), BF), pltpu.VMEM((shard, 128), BF)]
        + [pltpu.VMEM((1, shard), BF)] * 4 + [pltpu.VMEM((1, query_gain.shape[1]), BF)] * 2
        + [pltpu.SemaphoreType.DMA((15,))],
        far=range(13), far_out=True,
    )[0]

    def gather(array, target):
        split = 2 * hidden
        one, two = links.across(array, target, 1), links.across(array, target, 2)
        left = links.across(two[:, :split], target, 1)
        return [array, one, two, left, links.across(one[:, split:], target, 2)]

    def gain_table(pieces, target):
        return call(
            gains_kernel, info, [], [shape((8, model), F32)],
            [pltpu.VMEM((shards, GAIN_ROWS, 128), BF), pltpu.SemaphoreType.DMA((shards,))],
            pieces=pieces, section=target,
        )[0]

    qkv_scratch = [pltpu.VMEM((model, wide), BF), pltpu.SemaphoreType.DMA((shards,))]
    out_scratch = [pltpu.VMEM((model, heads_width), BF), pltpu.SemaphoreType.DMA((16,))]
    ffn_scratch = [pltpu.VMEM((model, 2 * hidden), BF), pltpu.VMEM((model, hidden), BF),
                   pltpu.SemaphoreType.DMA((shards,)), pltpu.SemaphoreType.DMA((16,))]

    half = head // 2
    limit = jnp.minimum(positions.reshape(tokens, 1), WIN - 1)
    starts = [(seq - back) * shards + fsdp for back in range(3)]
    for flip in range(1, shards):
        other = fsdp ^ flip
        starts.append((seq - 1) * shards + other)
        starts.append(jnp.where(other < fsdp, seq, seq - 2) * shards + other)
    starts = jnp.stack(starts).astype(jnp.int32) * rows
    key_place = (starts[:, None] + jnp.arange(rows, dtype=jnp.int32)[None, :]).reshape(1, -1)
    info = jnp.concatenate((info, starts[:1], starts))
    span = key_place.shape[1]
    frequency = ROPE_BASE ** (-2.0 * jnp.arange(half, dtype=F32) / head)
    angles = key_place.reshape(span, 1).astype(F32) * frequency[None, :]
    wide_cos, wide_sin = jnp.cos(angles), jnp.sin(angles)
    cosine, sine = (jnp.tile(table[:rows], (micro, 1)) for table in (wide_cos, wide_sin))

    def fetch(own, target, waiting=None):
        one, two = links.along(own, target, 1), links.along(own, target, 2)
        if waiting is not None:
            one, two, waiting = tie((one, two, waiting))
        sent = call(
            select_kernel, info, [own, one, two], [shape((2,) + own.shape, BF)] * (shards - 1),
            section=target,
        )
        got = [links.across(array, target, 1 + i) for i, array in enumerate(sent)]
        return [own, one, two] + got, waiting

    def forward(x, pieces, target, x_window=None, token=None):
        gains = gain_table(pieces, target)
        sizes_of = [shape((shards, tokens, shard), BF), shape((tokens, wide), F32),
                    shape((tokens, heads_width), BF)]
        whole = shape((micro, span, 2 * head), BF)
        attend_outs = [
            shape((micro, shards * rows, span), F32), shape((tokens, heads_width), BF),
            shape((tokens, model), F32), shape((tokens, model), F32),
            shape((shards, tokens, shard), BF), shape((tokens, model), BF),
        ]
        if x_window is not None:
            blocks, qkv, query, window = call(
                functools.partial(project_window_kernel, micro), info,
                x_window + [gains, cosine, sine, wide_cos, wide_sin],
                sizes_of + [whole], qkv_scratch, section=target, pieces=pieces,
            )
            parts = [window]
        else:
            blocks, qkv, query, own = call(
                project_kernel, info, [x, gains, cosine, sine, token],
                sizes_of + [shape((tokens, 2 * head), BF)], qkv_scratch, section=target,
                pieces=pieces,
            )
            parts, _ = fetch(own, target)
            attend_outs = [whole] + attend_outs
        outs = call(
            functools.partial(attend_kernel, micro), info,
            [query, x, gains, limit] + parts, attend_outs, out_scratch, section=target,
            pieces=pieces,
        )
        if x_window is None:
            window, *outs = outs
        probs, attended, branch, mixed, ffn_blocks, ffn_in = outs
        gate_up, activated, down, result = call(
            ffn_kernel, info, [ffn_in, mixed, gains],
            [shape((tokens, 2 * hidden), F32), shape((tokens, hidden), BF),
             shape((tokens, model), F32), shape((tokens, model), BF)], ffn_scratch,
            section=target, pieces=pieces,
        )
        saved = dict(
            x=x, gains=gains, pieces=pieces, blocks=blocks, qkv=qkv, query=query, window=window, probs=probs,
            attended=attended, branch=branch, mixed=mixed, ffn_blocks=ffn_blocks, gate_up=gate_up,
            activated=activated, down=down,
        )
        return result, saved

    def back_ffn(upstream, s, target):
        outs = call(
            ffn_back_kernel, info,
            [upstream, s["mixed"], s["down"], s["gate_up"], s["activated"], s["ffn_blocks"],
             s["gains"]],
            [shape((tokens, 2 * hidden + model + quarter + 256), BF)] * shards
            + [shape((tokens, model), F32), shape((8, model), F32)],
            [pltpu.VMEM((tokens, 2 * hidden), BF)] + ffn_scratch,
            section=target, pieces=s["pieces"], staged=target == 0,
        )
        return outs[:shards], outs[shards], outs[shards + 1]

    def back_attend(grad_mixed, s, target):
        pair = [shape((tokens, 2 * head), F32)] * 3
        outs = call(
            functools.partial(attend_back_kernel, micro), info,
            [grad_mixed, s["branch"], s["window"], s["probs"], s["query"], s["gains"]],
            [shape((tokens, model), BF), shape((tokens, heads_width), F32)] + pair
            + [shape((2, tokens, 2 * head), BF)] * (shards - 1) + [shape((8, model), F32)],
            [pltpu.VMEM((tokens, heads_width), BF)] + out_scratch,
            section=target, pieces=s["pieces"], staged=target == 0,
        )
        return outs[0], outs[1], outs[2:5], outs[5:8], outs[8]

    def back_window(kept, gives, target, waiting):
        got = [links.across(array, target, 1 + i) for i, array in enumerate(gives)]
        ffn_packs, other = waiting
        if other is not None:
            got, other, ffn_packs = tie((got, other, ffn_packs))
            other = jnp.where(is_first, other[0], other[1])
            kept, other = tie((kept, other))
        own, one, two = call(
            combine_kernel, info, list(kept) + got,
            [shape((tokens, 2 * head), F32)] + [shape((tokens, 2 * head), BF)] * 2,
            section=target, staged=target == 0,
        )
        one, two = links.along(one, target, -1), links.along(two, target, -2)
        if other is None:
            one, ffn_packs = tie((one, ffn_packs))
        return (own, one, two), ffn_packs, other

    def back_project(window_grads, grad_query, grad_mixed, grad_branch, rows_ffn, rows_attn, s,
                     target):
        outs = call(
            project_back_kernel, info,
            list(window_grads) + [grad_query, s["qkv"], cosine, sine, s["x"], grad_mixed,
            grad_branch, s["attended"], s["blocks"], s["gains"], rows_ffn, rows_attn],
            [shape((tokens + GAIN_ROWS, wide + model + head + 256), BF)] * shards
            + [shape((tokens, model), BF)],
            [pltpu.VMEM((tokens, wide), BF), pltpu.VMEM((shards, GAIN_ROWS, 256), F32)]
            + qkv_scratch,
            section=target, pieces=s["pieces"], staged=target == 0,
        )
        return outs[:shards], outs[shards]

    def exchange(packs, target):
        return [packs[0]] + [links.across(packs[i], target, i) for i in range(1, shards)]

    total_width = 2 * hidden + 512

    def ffn_weights(packs, target):
        return call(
            functools.partial(ffn_weights_kernel, shard, model), info, list(packs),
            [shape((shard, 2 * hidden), BF), shape((shard, hidden), BF)],
            section=target, staged=target == 0,
        )

    def attn_weights(packs, ffn, target):
        return call(
            functools.partial(weights_kernel, shard, model), info, list(packs) + list(ffn),
            [shape((shard, total_width), BF)] * 2,
            section=target, staged=target == 0,
        )

    def backward(upstream, s, target, other=None):
        ffn_packs, grad_mixed, rows_ffn = back_ffn(upstream, s, target)
        grad_branch, grad_query, kept, gives, rows_attn = back_attend(grad_mixed, s, target)
        window_grads, ffn_packs, other = back_window(kept, gives, target, (ffn_packs, other))
        ffn_packs = exchange(ffn_packs, target)
        attn_packs, grad_in = back_project(
            window_grads, grad_query, grad_mixed, grad_branch, rows_ffn, rows_attn, s, target
        )
        return ffn_weights(ffn_packs, target), attn_packs, grad_in, other

    x_first = hidden_in.reshape(tokens, model)
    x_window, folded = fetch(x_first, 0, folded)
    pieces = gather(folded, 0)
    token = links.cross(pieces[1][:16, :128], 0)
    result_a, saved_a = forward(x_first, pieces, 0, x_window)
    later, token = tie((folded, token))
    pieces = gather(later, 1)
    middle = links.cross(result_a, 0)
    result_b, saved_b = forward(middle, pieces, 1, token=token)

    ffn, attn_packs, grad_b, _ = backward(cotangent.reshape(tokens, model), saved_b, 1)
    upstream = links.cross(grad_b, 1)
    upstream, attn_packs = tie((upstream, attn_packs))
    b_first, b_second = attn_weights(exchange(attn_packs, 1), ffn, 1)
    upstream, b_first, b_second = tie((upstream, b_first, b_second))
    halves_b = (links.cross(b_first, 1), b_second)

    ffn, attn_packs, grad_a, half_b = backward(upstream, saved_a, 0, halves_b)
    part_b = lax.psum(half_b, "seq")
    attn_packs, part_b = tie((exchange(attn_packs, 0), part_b))
    a_first, a_second = attn_weights(attn_packs, ffn, 0)
    part_a = lax.psum(jnp.where(is_first, a_first, links.cross(a_second, 0)), "seq")
    theirs = links.swap(jnp.where(is_first, part_b, part_a))

    part = head // shards
    grads = call(
        finish_kernel, info, [part_a, part_b, theirs],
        [shape((1, shard, heads_width), F32), shape((1, shard, head), F32),
         shape((1, shard, head), F32), shape((1, head, model), F32),
         shape((1, shard, hidden), F32), shape((1, shard, hidden), F32),
         shape((1, quarter, model), F32)]
        + [shape((1, shard), F32)] * 4 + [shape((1, part), F32)] * 2,
    )
    g_query, g_key, g_value, g_out, g_gate, g_up, g_down = grads[:7]
    g_attn, g_post_attn, g_ffn, g_post_ffn, g_query_gain, g_key_gain = grads[7:]
    section_outputs = jnp.where(is_first, result_a, result_b).reshape(1, micro, rows, model)
    input_grads = jnp.where(is_first, grad_a, grad_b).reshape(1, micro, rows, model)
    return (
        section_outputs, input_grads, g_attn, g_query, g_key, g_value, g_query_gain, g_key_gain,
        g_out, g_post_attn, g_ffn, g_gate, g_up, g_down, g_post_ffn,
    )


def solution(mesh):
    rows = P(None, ("seq", "fsdp"), None)
    vector, matrix = P("section", "fsdp"), P("section", "fsdp", None)
    weights = (vector, matrix, matrix, matrix, vector, vector, matrix, vector, vector, matrix,
               matrix, matrix, vector)
    out_rows = P("section", None, ("seq", "fsdp"), None)
    return jax.shard_map(
        functools.partial(body, dict(mesh.shape)),
        mesh=mesh,
        in_specs=(rows, rows, P(None, ("seq", "fsdp"))) + weights,
        out_specs=(out_rows, out_rows) + weights,
        check_vma=False,
    )
```

```python
import functools

import jax
import jax.numpy as jnp
from jax import lax
from jax.experimental import pallas as pl
from jax.experimental.pallas import tpu as pltpu
from jax.sharding import PartitionSpec as P

WIN = 512
EPSILON = 1e-06
ROPE_BASE = 10000.0
NEG_LARGE = -1e30
AXES = ("section", "seq", "fsdp")
BF = jnp.bfloat16
F32 = jnp.float32
GAIN_ROWS = 16
INTERPRET = False


def mm(left, right):
    return lax.dot_general(left, right, (((1,), (0,)), ((), ())), preferred_element_type=F32)


def mm_nt(left, right):
    return lax.dot_general(left, right, (((1,), (1,)), ((), ())), preferred_element_type=F32)


def mm_tn(left, right):
    return lax.dot_general(left, right, (((0,), (0,)), ((), ())), preferred_element_type=F32)


def inverse_rms(values):
    return lax.rsqrt(jnp.mean(values * values, axis=-1, keepdims=True) + EPSILON)


def norm_back(values, scale, gain, grad):
    weighted = grad * gain
    inner = jnp.mean(values * weighted, axis=-1, keepdims=True)
    return scale * weighted - values * (scale * scale * scale * inner)


def gain_back(values, scale, grad):
    return jnp.sum(values * scale * grad, axis=0, keepdims=True)


def call(kernel, info, arrays, outs, scratch=(), section=None, pieces=(), staged=True,
         far_out=False):
    smem = pl.BlockSpec(memory_space=pltpu.SMEM)
    vmem = pl.BlockSpec(memory_space=pltpu.VMEM)
    hbm = pl.BlockSpec(memory_space=pltpu.HBM)
    count, lead = len(arrays), len(pieces)
    scratch = list(scratch)
    staged = staged and count > 0
    if staged:
        scratch += [pltpu.VMEM(a.shape, a.dtype) for a in arrays]
        scratch += [pltpu.SemaphoreType.DMA((count,))]

    def entry(info, *refs):
        ins, rest = refs[lead : lead + count], refs[lead + count :]

        def run(ins=ins, rest=rest):
            if staged:
                rest, held, sems = rest[: -count - 1], rest[-count - 1 : -1], rest[-1]
                copies = [
                    pltpu.make_async_copy(source, target, sems.at[i])
                    for i, (source, target) in enumerate(zip(ins, held))
                ]
                for copy in copies:
                    copy.start()
                for copy in copies:
                    copy.wait()
                ins = held
            kernel(info, *((refs[:lead],) if lead else ()), *ins, *rest)

        if section is None:
            run()
        else:
            pl.when(info[2] == section)(run)

    return pl.pallas_call(
        entry,
        out_shape=outs,
        in_specs=[smem] + [hbm] * lead
        + [hbm if staged or far_out else vmem] * count,
        out_specs=[hbm if far_out else vmem] * len(outs),
        scratch_shapes=scratch,
        compiler_params=pltpu.CompilerParams(vmem_limit_bytes=58 * 1024 * 1024),
        cost_estimate=pl.CostEstimate(flops=1, bytes_accessed=1, transcendentals=0),
        interpret=INTERPRET,
    )(info, *pieces, *arrays)


def shape(dims, kind):
    return jax.ShapeDtypeStruct(tuple(dims), kind)


def slot(index, width):
    return pl.ds(pl.multiple_of(index * width, width), width)


def layout(model):
    unit = model // 5
    return unit * 32, unit * 40, unit * 56, unit * 68


def sources(pieces, start):
    own, one, two, left, right = pieces
    split = left.shape[1]
    last = (left, start) if start < split else (right, start - split)
    return [(own, start), (one, start), (two, start), last]


def gains_kernel(info, gathered, out, held, sems):
    count, rows, width = held.shape
    shard = out.shape[1] // count
    part = shard * 2 // 5
    copies = []
    for flip, (piece, start) in enumerate(sources(gathered, layout(out.shape[1])[3])):
        source = piece.at[pl.ds(0, rows), pl.ds(start, width)]
        copies.append(pltpu.make_async_copy(source, held.at[info[0] ^ flip], sems.at[flip]))
    for copy in copies:
        copy.start()
    for copy in copies:
        copy.wait()
    out[...] = jnp.zeros_like(out)
    for place in range(count):
        values = held[place].astype(F32)
        start = place * shard
        for row in range(4):
            out[row : row + 1, start : start + width] = values[2 * row : 2 * row + 1]
            out[row : row + 1, start + width : start + shard] = values[
                2 * row + 1 : 2 * row + 2, : shard - width
            ]
        for row in range(2):
            out[4 + row : 5 + row, place * part : (place + 1) * part] = values[
                8 + row : 9 + row, :part
            ]


def fold_kernel(info, gate, up, query, key, value, out_w, down_w, attn, post_attn, ffn, post_ffn,
                query_gain, key_gain, folded, out_held, down_held, turned, gain_block, *rest):
    shard = gate.shape[1]
    vectors, sems = rest[:-1], rest[-1]
    loads = [
        pltpu.make_async_copy(out_w.at[0], out_held, sems.at[0]),
        pltpu.make_async_copy(down_w.at[0], down_held, sems.at[1]),
    ]
    small = [
        pltpu.make_async_copy(source, held, sems.at[9 + i])
        for i, (source, held) in enumerate(
            zip((attn, post_attn, ffn, post_ffn, query_gain, key_gain), vectors)
        )
    ]
    for copy in loads + small:
        copy.start()
    moves = []

    def move(source, start):
        copy = pltpu.make_async_copy(
            source, folded.at[:, pl.ds(start, source.shape[1])], sems.at[2 + len(moves)]
        )
        copy.start()
        moves.append(copy)
        return start + source.shape[1]

    start = move(up.at[0], move(gate.at[0], 0))
    turned_at = start
    start += turned.shape[1]
    for ref in (query, key, value):
        start = move(ref.at[0], start)
    width = gain_block.shape[1]
    gain_block[...] = jnp.zeros_like(gain_block)
    wait_all(small)
    for row, ref in enumerate(vectors[:4]):
        gain_block[2 * row : 2 * row + 1, :] = ref[:, :width]
        gain_block[2 * row + 1 : 2 * row + 2, : shard - width] = ref[:, width:]
    for row, ref in enumerate(vectors[4:]):
        gain_block[8 + row : 9 + row, : ref.shape[1]] = ref[...]
    move(gain_block, start)
    start = 0
    for load, held in zip(loads, (out_held, down_held)):
        load.wait()
        rows = held.shape[0]
        for place in range(4):
            block = held[:, place * shard : (place + 1) * shard].astype(F32)
            turned[:, start : start + rows] = block.T.astype(BF)
            start += rows
    move(turned, turned_at)
    for copy in moves:
        copy.wait()


def load_turned(info, gathered, held, sems, start):
    width, shard = held.shape[1] // 4, held.shape[0] // 4
    copies = []
    for flip, (piece, column) in enumerate(sources(gathered, start)):
        for row in range(4):
            copy = pltpu.make_async_copy(
                piece.at[:, pl.ds(column + row * width, width)],
                held.at[pl.ds(row * shard, shard), slot(info[0] ^ flip, width)],
                sems.at[4 * flip + row],
            )
            copy.start()
            copies.append(copy)
    return copies


def load_rows(info, gathered, held, sems, start):
    shard, width = held.shape[0] // 4, held.shape[1]
    copies = []
    for flip, (piece, column) in enumerate(sources(gathered, start)):
        copy = pltpu.make_async_copy(
            piece.at[:, pl.ds(column, width)], held.at[slot(info[0] ^ flip, shard)], sems.at[flip]
        )
        copy.start()
        copies.append(copy)
    return copies


def wait_all(copies):
    for copy in copies:
        copy.wait()


def rope_store(target, rows, start, normal, cos, sin):
    half = cos.shape[1]
    one, two = normal[:, :half], normal[:, half:]
    target[rows, start : start + half] = (one * cos - two * sin).astype(BF)
    target[rows, start + half : start + 2 * half] = (two * cos + one * sin).astype(BF)


def cut(blocks, normed):
    shard = blocks.shape[2]
    for place in range(blocks.shape[0]):
        blocks[place] = normed[:, place * shard : (place + 1) * shard].astype(BF)


def project_window_kernel(micro, info, gathered, x, one, two, *refs):
    got, (gains, cosine, sine, wide_cos, wide_sin) = refs[:3], refs[3:8]
    blocks, qkv, query, window, weight, sems = refs[8:]
    copies = load_rows(info, gathered, weight, sems, layout(x.shape[1])[2])
    rows = x.shape[0] // micro
    head = window.shape[2] // 2
    heads_width = query.shape[1]

    def normed_of(values):
        return values * inverse_rms(values) * gains[0:1, :]

    normed = normed_of(x[...].astype(F32))
    cut(blocks, normed)
    normed = normed.astype(BF)
    wait_all(copies)
    total = mm(normed, weight[:, :heads_width])
    qkv[:, :heads_width] = total
    for start in range(0, heads_width, head):
        raw = total[:, start : start + head]
        normal = raw * inverse_rms(raw) * gains[4:5, :head]
        rope_store(query, slice(None), start, normal, cosine[...], sine[...])
    for m in range(micro):
        span = slice(m * rows, (m + 1) * rows)
        parts = [x[span], one[span], two[span]]
        for ref in got:
            parts += [ref[0, span], ref[1, span]]
        values = jnp.concatenate(parts, axis=0).astype(F32)
        total = mm(normed_of(values).astype(BF), weight[:, heads_width:])
        qkv[span, heads_width:] = total[:rows]
        raw = total[:, :head]
        normal = raw * inverse_rms(raw) * gains[5:6, :head]
        rope_store(window.at[m], slice(None), 0, normal, wide_cos[...], wide_sin[...])
        window[m, :, head:] = total[:, head:].astype(BF)


def finish_kernel(info, part_a, part_b, theirs, *outs):
    query, key, value, out, gate, up, down = outs[:7]
    vectors = outs[7:]
    shard, hidden = gate.shape[1], gate.shape[2]

    def emit(first, second):
        gate[0] = first[:, :hidden].astype(F32)
        up[0] = first[:, hidden : 2 * hidden].astype(F32)
        for row, ref in enumerate(vectors):
            ref[...] = first[:GAIN_ROWS, 2 * hidden : 2 * hidden + ref.shape[1]].astype(F32)[
                row : row + 1
            ]
        start = 0
        for ref in (query, key, value):
            ref[0] = second[:, start : start + ref.shape[2]].astype(F32)
            start += ref.shape[2]
        for ref in (out, down):
            rows = ref.shape[1]
            for place in range(4):
                block = second[:, start : start + rows].astype(F32)
                ref[0, :, place * shard : (place + 1) * shard] = block.T
                start += rows

    @pl.when(info[2] == 0)
    def _():
        emit(part_a, theirs)

    @pl.when(info[2] == 1)
    def _():
        emit(theirs, part_b)


def project_kernel(info, gathered, x, gains, cosine, sine, token, blocks, qkv, query, own, weight,
                   sems):
    copies = load_rows(info, gathered, weight, sems, layout(x.shape[1])[2])
    head = 2 * cosine.shape[1]
    residual = x[...].astype(F32)
    normed = residual * inverse_rms(residual) * gains[0:1, :]
    cut(blocks, normed)
    wait_all(copies)
    total = mm(normed.astype(BF), weight[...])
    qkv[...] = total
    heads = query.shape[1] // head
    for index in range(heads + 1):
        raw = total[:, index * head : (index + 1) * head]
        row = 4 if index < heads else 5
        normal = raw * inverse_rms(raw) * gains[row : row + 1, :head]
        target, start = (query, index * head) if index < heads else (own, 0)
        rope_store(target, slice(None), start, normal, cosine[...], sine[...])
    own[:, head:] = total[:, (heads + 1) * head :].astype(BF)


def select_kernel(info, own, one, two, *outs):
    for index, out in enumerate(outs):
        lower = (info[0] < (info[0] ^ (index + 1))).astype(F32)
        out[0] = one[...]
        mixed = own[...].astype(F32) * lower + two[...].astype(F32) * (1.0 - lower)
        out[1] = mixed.astype(BF)


def window_kernel(micro, info, own, one, two, *refs):
    got, window = refs[:3], refs[3]
    rows = own.shape[0] // micro
    for m in range(micro):
        span = slice(m * rows, (m + 1) * rows)
        parts = [own[span], one[span], two[span]]
        for ref in got:
            parts += [ref[0, span], ref[1, span]]
        for index, part in enumerate(parts):
            window[m, index * rows : (index + 1) * rows] = part


def attend_kernel(micro, info, gathered, query, x, gains, limit, *refs):
    out_w, sems = refs[-2:]
    model = x.shape[1]
    shard = model // 4
    copies = load_turned(info, gathered, out_w, sems, layout(model)[0])
    if len(refs) == 1 + 6 + 2:
        window = refs[0]
        outs = refs[1:-2]
    else:
        window = refs[6]
        outs = refs[7:-2]
        window_kernel(micro, info, *refs[:6], window)
    probs, attended, branch, mixed, blocks, ffn_in = outs
    rows = query.shape[0] // micro
    head = window.shape[2] // 2
    heads = query.shape[1] // head
    count = window.shape[1]
    column = lax.broadcasted_iota(jnp.int32, (rows, count), 1)
    distance = lax.broadcasted_iota(jnp.int32, (rows, count), 0) + info[3]
    for index in range(count // rows):
        inside = (column >= index * rows) & (column < (index + 1) * rows)
        distance = distance - jnp.where(inside, column - index * rows + info[4 + index], 0)
    for m in range(micro):
        span = slice(m * rows, (m + 1) * rows)
        allowed = (distance >= 0) & (distance <= limit[span])
        bias = jnp.where(allowed, 0.0, NEG_LARGE)
        bias = jnp.concatenate([bias] * heads, axis=0)
        stacked = jnp.concatenate(
            [query[span, h * head : (h + 1) * head] for h in range(heads)], axis=0
        )
        scores = mm_nt(stacked, window[m, :, :head]) * head ** (-0.5) + bias
        exponent = jnp.exp(scores - jnp.max(scores, axis=-1, keepdims=True))
        chance = exponent / jnp.sum(exponent, axis=-1, keepdims=True)
        probs[m] = chance
        result = mm(chance.astype(BF), window[m, :, head:]).astype(BF)
        for h in range(heads):
            attended[span, h * head : (h + 1) * head] = result[h * rows : (h + 1) * rows]
    for copy in copies:
        copy.wait()
    total = mm_nt(attended[...], out_w[...])
    branch[...] = total
    value = x[...].astype(F32) + total * inverse_rms(total) * gains[1:2, :]
    mixed[...] = value
    normed = value * inverse_rms(value) * gains[2:3, :]
    ffn_in[...] = normed.astype(BF)
    for place in range(4):
        blocks[place] = normed[:, place * shard : (place + 1) * shard].astype(BF)


def gelu_parts(gate):
    c = 0.7978845608028654
    inner = jnp.tanh(c * (gate + 0.044715 * gate * gate * gate))
    value = 0.5 * gate * (1.0 + inner)
    slope = 0.5 * (1.0 + inner) + 0.5 * gate * (1.0 - inner * inner) * c * (
        1.0 + 3 * 0.044715 * gate * gate
    )
    return value, slope


def ffn_kernel(info, gathered, ffn_in, mixed, gains, gate_up, activated, down, result,
               gate_up_w, down_w, column_sems, sems):
    hidden = activated.shape[1]
    width = 512
    columns = load_rows(info, gathered, gate_up_w, column_sems, 0)
    copies = load_turned(info, gathered, down_w, sems, layout(mixed.shape[1])[1])
    wait_all(columns)
    for start in range(0, hidden, width):
        both = []
        for base in (start, hidden + start):
            total = mm(ffn_in[...], gate_up_w[:, base : base + width])
            gate_up[:, base : base + width] = total
            both.append(total)
        value, _ = gelu_parts(both[0])
        activated[:, start : start + width] = (value * both[1]).astype(BF)
    for copy in copies:
        copy.wait()
    total = mm_nt(activated[...], down_w[...])
    down[...] = total
    result[...] = (mixed[...] + total * inverse_rms(total) * gains[3:4, :]).astype(BF)


def ffn_back_kernel(info, gathered, upstream, mixed, down, gate_up, activated, blocks, gains,
                    *refs):
    packs, grad_mixed, gain_rows = refs[:4], refs[4], refs[5]
    grad_gate_up, gate_up_w, down_w, column_sems, sems = refs[6:]
    hidden = activated.shape[1]
    model = mixed.shape[1]
    shard = blocks.shape[2]
    copies = load_turned(info, gathered, down_w, sems, layout(mixed.shape[1])[1])
    columns = load_rows(info, gathered, gate_up_w, column_sems, 0)
    top = upstream[...].astype(F32)
    raw = down[...]
    scale = inverse_rms(raw)
    grad_down = norm_back(raw, scale, gains[3:4, :], top).astype(BF)
    gain_rows[...] = jnp.zeros_like(gain_rows)
    gain_rows[3:4, :] = gain_back(raw, scale, top)
    act_at = 2 * hidden + model
    block_at = act_at + hidden // 4
    for flip, pack in enumerate(packs):
        pack[:, 2 * hidden : act_at] = grad_down
        pack[:, act_at:block_at] = activated[:, slot(info[0] ^ flip, hidden // 4)]
        pack[:, block_at:] = jnp.zeros_like(pack[:, block_at:])
        pack[:, block_at : block_at + shard] = blocks[info[0] ^ flip]
    for copy in copies:
        copy.wait()
    width = 512
    for start in range(0, hidden, width):
        value, slope = gelu_parts(gate_up[:, start : start + width])
        up = gate_up[:, hidden + start : hidden + start + width]
        grad = mm(grad_down, down_w[:, start : start + width])
        grad_gate_up[:, start : start + width] = (grad * up * slope).astype(BF)
        grad_gate_up[:, hidden + start : hidden + start + width] = (grad * value).astype(BF)
    for pack in packs:
        pack[:, : 2 * hidden] = grad_gate_up[...]
    for copy in columns:
        copy.wait()
    grad_in = mm_nt(grad_gate_up[...], gate_up_w[...])
    raw = mixed[...]
    scale = inverse_rms(raw)
    gain_rows[2:3, :] = gain_back(raw, scale, grad_in)
    grad_mixed[...] = top + norm_back(raw, scale, gains[2:3, :], grad_in)


def attend_back_kernel(micro, info, gathered, grad_mixed, branch, window, probs, query, gains,
                       *refs):
    grad_branch, grad_query, own, one, two = refs[:5]
    gives, gain_rows, grad_attended, out_w, sems = refs[5:8], refs[8], refs[9], refs[10], refs[11]
    model = branch.shape[1]
    copies = load_turned(info, gathered, out_w, sems, layout(model)[0])
    rows = own.shape[0] // micro
    head = own.shape[1] // 2
    heads = query.shape[1] // head
    factor = head ** (-0.5)
    raw = branch[...]
    scale = inverse_rms(raw)
    grad = grad_mixed[...]
    gain_rows[...] = jnp.zeros_like(gain_rows)
    gain_rows[1:2, :] = gain_back(raw, scale, grad)
    low = norm_back(raw, scale, gains[1:2, :], grad).astype(BF)
    grad_branch[...] = low
    for copy in copies:
        copy.wait()
    grad_attended[...] = mm(low, out_w[...]).astype(BF)
    for m in range(micro):
        span = slice(m * rows, (m + 1) * rows)
        chance = probs[m]
        keys, values = window[m, :, :head], window[m, :, head:]
        stacked = jnp.concatenate(
            [query[span, h * head : (h + 1) * head] for h in range(heads)], axis=0
        )
        upstream = jnp.concatenate(
            [grad_attended[span, h * head : (h + 1) * head] for h in range(heads)], axis=0
        )
        grad_values = mm_tn(chance.astype(BF), upstream)
        grad_chance = mm_nt(upstream, values)
        inner = jnp.sum(chance * grad_chance, axis=-1, keepdims=True)
        grad_scores = (chance * (grad_chance - inner)).astype(BF)
        grad_stacked = mm(grad_scores, keys) * factor
        grad_keys = mm_tn(grad_scores, stacked) * factor
        for h in range(heads):
            grad_query[span, h * head : (h + 1) * head] = grad_stacked[h * rows : (h + 1) * rows]
        for index, target in enumerate((own, one, two)):
            part = slice(index * rows, (index + 1) * rows)
            target[span, :head] = grad_keys[part]
            target[span, head:] = grad_values[part]
        for index, target in enumerate(gives):
            for side in range(2):
                start = (3 + 2 * index + side) * rows
                target[side, span, :head] = grad_keys[start : start + rows].astype(BF)
                target[side, span, head:] = grad_values[start : start + rows].astype(BF)


def combine_kernel(info, own, one, two, first, second, third, own_out, one_out, two_out):
    total_own, total_one, total_two = own[...], one[...], two[...]
    for index, got in enumerate((first, second, third)):
        lower = (info[0] < (info[0] ^ (index + 1))).astype(F32)
        total_one = total_one + got[0].astype(F32)
        side = got[1].astype(F32)
        total_own = total_own + side * lower
        total_two = total_two + side * (1.0 - lower)
    own_out[...] = total_own
    one_out[...] = total_one.astype(BF)
    two_out[...] = total_two.astype(BF)


def project_back_kernel(info, gathered, own, back_one, back_two, grad_query, qkv, cosine, sine, x, grad_mixed,
                        grad_branch, attended, blocks, gains, rows_ffn, rows_attn, *refs):
    packs, grad_in = refs[:4], refs[4]
    grad_qkv, gain_held, weight, sems = refs[5:]
    copies = load_rows(info, gathered, weight, sems, layout(x.shape[1])[2])
    tokens, model = x.shape
    shard = blocks.shape[2]
    half = cosine.shape[1]
    head = 2 * half
    heads = grad_query.shape[1] // head
    cos, sin = cosine[...], sine[...]
    grad_own = own[...] + back_one[...].astype(F32) + back_two[...].astype(F32)
    head_gains = [None, None]
    for index in range(heads + 1):
        if index < heads:
            grad = grad_query[:, index * head : (index + 1) * head]
        else:
            grad = grad_own[:, :head]
        one, two = grad[:, :half], grad[:, half:]
        grad = jnp.concatenate((one * cos + two * sin, two * cos - one * sin), axis=1)
        raw = qkv[:, index * head : (index + 1) * head]
        scale = inverse_rms(raw)
        kind = 0 if index < heads else 1
        term = gain_back(raw, scale, grad)
        head_gains[kind] = term if head_gains[kind] is None else head_gains[kind] + term
        back = norm_back(raw, scale, gains[4 + kind : 5 + kind, :head], grad)
        grad_qkv[:, index * head : (index + 1) * head] = back.astype(BF)
    grad_qkv[:, (heads + 1) * head :] = grad_own[:, head:].astype(BF)
    wait_all(copies)
    grad_normed = mm_nt(grad_qkv[...], weight[...])
    residual = x[...].astype(F32)
    scale = inverse_rms(residual)
    first_gain = gain_back(residual, scale, grad_normed)
    total = grad_mixed[...] + norm_back(residual, scale, gains[0:1, :], grad_normed)
    grad_in[...] = total.astype(BF)
    gain_held[...] = jnp.zeros_like(gain_held)
    part = head // 4
    four = (first_gain, rows_attn[1:2, :], rows_ffn[2:3, :], rows_ffn[3:4, :])
    for place in range(4):
        for row, values in enumerate(four):
            gain_held[place, row : row + 1, :shard] = values[
                :, place * shard : (place + 1) * shard
            ]
        for row, values in enumerate(head_gains):
            gain_held[place, 4 + row : 5 + row, :part] = values[
                :, place * part : (place + 1) * part
            ]
    wide = grad_qkv.shape[1]
    att_at = wide + model
    block_at = att_at + head
    for flip, pack in enumerate(packs):
        other = info[0] ^ flip
        pack[tokens:, :] = jnp.zeros_like(pack[tokens:, :])
        pack[tokens:, : gain_held.shape[2]] = gain_held[other].astype(BF)
        pack[:tokens, :wide] = grad_qkv[...]
        pack[:tokens, wide:att_at] = grad_branch[...]
        pack[:tokens, att_at:block_at] = attended[:, slot(other, head)]
        pack[:tokens, block_at:] = jnp.zeros_like(pack[:tokens, block_at:])
        pack[:tokens, block_at : block_at + shard] = blocks[other]


def over(packs, tokens, left, right, left_width, right_width):
    total = None
    for pack in packs:
        term = mm_tn(
            pack[:tokens, left : left + left_width], pack[:tokens, right : right + right_width]
        )
        total = term if total is None else total + term
    return total.astype(BF)


def ffn_weights_kernel(shard, model, info, *refs):
    packs, first, second = refs[:4], refs[4], refs[5]
    tokens = packs[0].shape[0]
    wide = first.shape[1]
    quarter = second.shape[1] // 4
    act_at = wide + model
    for start in range(0, wide, 1024):
        first[:, start : start + 1024] = over(
            packs, tokens, act_at + quarter, start, shard, 1024
        )
    for place in range(4):
        second[:, place * quarter : (place + 1) * quarter] = over(
            packs, tokens, wide + place * shard, act_at, shard, quarter
        )


def weights_kernel(shard, model, info, *refs):
    packs, gate_up, down, first, second = refs[:4], refs[4], refs[5], refs[6], refs[7]
    tokens = packs[0].shape[0] - GAIN_ROWS
    head = model // 5 * 2
    wide = packs[0].shape[1] - model - 2 * head
    hidden = gate_up.shape[1]
    first[:, :hidden] = gate_up[...]
    first[:, hidden:] = jnp.zeros_like(first[:, hidden:])
    gains = sum(pack[tokens:, :head].astype(F32) for pack in packs)
    first[:GAIN_ROWS, hidden : hidden + head] = gains.astype(BF)
    att_at = wide + model
    second[:, :wide] = over(packs, tokens, att_at + head, 0, shard, wide)
    for place in range(4):
        start = wide + place * head
        second[:, start : start + head] = over(
            packs, tokens, wide + place * shard, att_at, shard, head
        )
    second[:, wide + 4 * head :] = down[...]


class Links:
    def __init__(self, sizes):
        self.sizes = sizes

    def index(self, section, seq, fsdp):
        return (section * self.sizes["seq"] + seq) * self.sizes["fsdp"] + fsdp

    def send(self, array, section, place):
        pairs = []
        for z in range(self.sizes["seq"]):
            for f in range(self.sizes["fsdp"]):
                to_section, to_z, to_f = place(z, f)
                if 0 <= to_z < self.sizes["seq"]:
                    pairs.append((self.index(section, z, f), self.index(to_section, to_z, to_f)))
        return lax.ppermute(array, AXES, pairs)

    def along(self, array, section, by):
        return self.send(array, section, lambda z, f: (section, z + by, f))

    def across(self, array, section, flip):
        return self.send(array, section, lambda z, f: (section, z, f ^ flip))

    def cross(self, array, section):
        return self.send(array, section, lambda z, f: (1 - section, z, f))

    def both(self, array, flip):
        pairs = []
        for section in range(2):
            for z in range(self.sizes["seq"]):
                for f in range(self.sizes["fsdp"]):
                    pairs.append((self.index(section, z, f), self.index(section, z, f ^ flip)))
        return lax.ppermute(array, AXES, pairs)

    def swap(self, array):
        pairs = []
        for section in range(2):
            for z in range(self.sizes["seq"]):
                for f in range(self.sizes["fsdp"]):
                    pairs.append((self.index(section, z, f), self.index(1 - section, z, f)))
        return lax.ppermute(array, AXES, pairs)


def body(sizes, hidden_in, cotangent, positions, attn_gain, w_query, w_key, w_value, query_gain,
         key_gain, w_output, post_attn_gain, ffn_gain, w_gate, w_up, w_down, post_ffn_gain):
    section = lax.axis_index("section")
    seq = lax.axis_index("seq")
    fsdp = lax.axis_index("fsdp")
    is_first = section == 0
    micro, rows, model = hidden_in.shape
    tokens = micro * rows
    shard = w_query.shape[1]
    shards = sizes["fsdp"]
    heads_width, head = w_query.shape[2], w_key.shape[2]
    wide = heads_width + 2 * head
    hidden = w_gate.shape[2]
    quarter = hidden // shards
    assert shards == 4 and 2 * shards * rows == WIN and heads_width == shards * head
    links = Links(sizes)
    tie = lax.optimization_barrier
    info = jnp.stack([fsdp, seq, section]).astype(jnp.int32)

    width_of = 2 * hidden + heads_width + hidden + wide + 128
    folded = call(
        fold_kernel, info,
        [w_gate, w_up, w_query, w_key, w_value, w_output, w_down, attn_gain, post_attn_gain,
         ffn_gain, post_ffn_gain, query_gain, key_gain], [shape((shard, width_of), BF)],
        [pltpu.VMEM((head, model), BF), pltpu.VMEM((quarter, model), BF),
         pltpu.VMEM((shard, heads_width + hidden), BF), pltpu.VMEM((shard, 128), BF)]
        + [pltpu.VMEM((1, shard), BF)] * 4 + [pltpu.VMEM((1, query_gain.shape[1]), BF)] * 2
        + [pltpu.SemaphoreType.DMA((15,))],
        staged=False, far_out=True,
    )[0]

    def neighbours(array, target):
        return links.across(array, target, 1), links.across(array, target, 2)

    def gather(array, near, target):
        split = 2 * hidden
        one, two = near
        left = links.across(two[:, :split], target, 1)
        return [array, one, two, left, links.across(one[:, split:], target, 2)]

    def gain_table(pieces, target):
        return call(
            gains_kernel, info, [], [shape((8, model), F32)],
            [pltpu.VMEM((shards, GAIN_ROWS, 128), BF), pltpu.SemaphoreType.DMA((shards,))],
            pieces=pieces, section=target,
        )[0]

    qkv_scratch = [pltpu.VMEM((model, wide), BF), pltpu.SemaphoreType.DMA((shards,))]
    out_scratch = [pltpu.VMEM((model, heads_width), BF), pltpu.SemaphoreType.DMA((16,))]
    ffn_scratch = [pltpu.VMEM((model, 2 * hidden), BF), pltpu.VMEM((model, hidden), BF),
                   pltpu.SemaphoreType.DMA((shards,)), pltpu.SemaphoreType.DMA((16,))]

    half = head // 2
    limit = jnp.minimum(positions.reshape(tokens, 1), WIN - 1)
    starts = [(seq - back) * shards + fsdp for back in range(3)]
    for flip in range(1, shards):
        other = fsdp ^ flip
        starts.append((seq - 1) * shards + other)
        starts.append(jnp.where(other < fsdp, seq, seq - 2) * shards + other)
    starts = jnp.stack(starts).astype(jnp.int32) * rows
    key_place = (starts[:, None] + jnp.arange(rows, dtype=jnp.int32)[None, :]).reshape(1, -1)
    info = jnp.concatenate((info, starts[:1], starts))
    span = key_place.shape[1]
    frequency = ROPE_BASE ** (-2.0 * jnp.arange(half, dtype=F32) / head)
    angles = key_place.reshape(span, 1).astype(F32) * frequency[None, :]
    wide_cos, wide_sin = jnp.cos(angles), jnp.sin(angles)
    cosine, sine = (jnp.tile(table[:rows], (micro, 1)) for table in (wide_cos, wide_sin))

    def fetch(own, target, waiting=None):
        one, two = links.along(own, target, 1), links.along(own, target, 2)
        sent = call(
            select_kernel, info, [own, one, two], [shape((2,) + own.shape, BF)] * (shards - 1),
            section=target,
        )
        if waiting is not None:
            last, waiting = tie((sent[-1], waiting))
            sent = [*sent[:-1], last]
        got = [links.across(array, target, 1 + i) for i, array in enumerate(sent)]
        return [own, one, two] + got, waiting

    def forward(x, pieces, target, x_window=None, token=None):
        gains = gain_table(pieces, target)
        sizes_of = [shape((shards, tokens, shard), BF), shape((tokens, wide), F32),
                    shape((tokens, heads_width), BF)]
        whole = shape((micro, span, 2 * head), BF)
        attend_outs = [
            shape((micro, shards * rows, span), F32), shape((tokens, heads_width), BF),
            shape((tokens, model), F32), shape((tokens, model), F32),
            shape((shards, tokens, shard), BF), shape((tokens, model), BF),
        ]
        if x_window is not None:
            blocks, qkv, query, window = call(
                functools.partial(project_window_kernel, micro), info,
                x_window + [gains, cosine, sine, wide_cos, wide_sin],
                sizes_of + [whole], qkv_scratch, section=target, pieces=pieces,
            )
            parts = [window]
        else:
            blocks, qkv, query, own = call(
                project_kernel, info, [x, gains, cosine, sine, token],
                sizes_of + [shape((tokens, 2 * head), BF)], qkv_scratch, section=target,
                pieces=pieces,
            )
            parts, _ = fetch(own, target)
            attend_outs = [whole] + attend_outs
        outs = call(
            functools.partial(attend_kernel, micro), info,
            [query, x, gains, limit] + parts, attend_outs, out_scratch, section=target,
            pieces=pieces,
        )
        if x_window is None:
            window, *outs = outs
        probs, attended, branch, mixed, ffn_blocks, ffn_in = outs
        gate_up, activated, down, result = call(
            ffn_kernel, info, [ffn_in, mixed, gains],
            [shape((tokens, 2 * hidden), F32), shape((tokens, hidden), BF),
             shape((tokens, model), F32), shape((tokens, model), BF)], ffn_scratch,
            section=target, pieces=pieces,
        )
        saved = dict(
            x=x, gains=gains, pieces=pieces, blocks=blocks, qkv=qkv, query=query, window=window, probs=probs,
            attended=attended, branch=branch, mixed=mixed, ffn_blocks=ffn_blocks, gate_up=gate_up,
            activated=activated, down=down,
        )
        return result, saved

    def back_ffn(upstream, s, target):
        outs = call(
            ffn_back_kernel, info,
            [upstream, s["mixed"], s["down"], s["gate_up"], s["activated"], s["ffn_blocks"],
             s["gains"]],
            [shape((tokens, 2 * hidden + model + quarter + 256), BF)] * shards
            + [shape((tokens, model), F32), shape((8, model), F32)],
            [pltpu.VMEM((tokens, 2 * hidden), BF)] + ffn_scratch,
            section=target, pieces=s["pieces"],
        )
        return outs[:shards], outs[shards], outs[shards + 1]

    def back_attend(grad_mixed, s, target):
        pair = [shape((tokens, 2 * head), F32)] * 3
        outs = call(
            functools.partial(attend_back_kernel, micro), info,
            [grad_mixed, s["branch"], s["window"], s["probs"], s["query"], s["gains"]],
            [shape((tokens, model), BF), shape((tokens, heads_width), F32)] + pair
            + [shape((2, tokens, 2 * head), BF)] * (shards - 1) + [shape((8, model), F32)],
            [pltpu.VMEM((tokens, heads_width), BF)] + out_scratch,
            section=target, pieces=s["pieces"],
        )
        return outs[0], outs[1], outs[2:5], outs[5:8], outs[8]

    def back_window(kept, gives, target, waiting):
        got = [links.across(array, target, 1 + i) for i, array in enumerate(gives)]
        ffn_packs, other = waiting
        if other is not None:
            got, other, ffn_packs = tie((got, other, ffn_packs))
            other = jnp.where(is_first, other[0], other[1])
            kept, other = tie((kept, other))
        own, one, two = call(
            combine_kernel, info, list(kept) + got,
            [shape((tokens, 2 * head), F32)] + [shape((tokens, 2 * head), BF)] * 2,
            section=target,
        )
        one, two = links.along(one, target, -1), links.along(two, target, -2)
        if other is None:
            one, ffn_packs = tie((one, ffn_packs))
        return (own, one, two), ffn_packs, other

    def back_project(window_grads, grad_query, grad_mixed, grad_branch, rows_ffn, rows_attn, s,
                     target):
        outs = call(
            project_back_kernel, info,
            list(window_grads) + [grad_query, s["qkv"], cosine, sine, s["x"], grad_mixed,
            grad_branch, s["attended"], s["blocks"], s["gains"], rows_ffn, rows_attn],
            [shape((tokens + GAIN_ROWS, wide + model + head + 256), BF)] * shards
            + [shape((tokens, model), BF)],
            [pltpu.VMEM((tokens, wide), BF), pltpu.VMEM((shards, GAIN_ROWS, 256), F32)]
            + qkv_scratch,
            section=target, pieces=s["pieces"],
        )
        return outs[:shards], outs[shards]

    def exchange(packs, target):
        return [packs[0]] + [links.across(packs[i], target, i) for i in range(1, shards)]

    total_width = 2 * hidden + 512

    def ffn_weights(packs, target):
        return call(
            functools.partial(ffn_weights_kernel, shard, model), info, list(packs),
            [shape((shard, 2 * hidden), BF), shape((shard, hidden), BF)],
            section=target,
        )

    def attn_weights(packs, ffn, target):
        return call(
            functools.partial(weights_kernel, shard, model), info, list(packs) + list(ffn),
            [shape((shard, total_width), BF)] * 2,
            section=target,
        )

    def backward(upstream, s, target, other=None):
        ffn_packs, grad_mixed, rows_ffn = back_ffn(upstream, s, target)
        grad_branch, grad_query, kept, gives, rows_attn = back_attend(grad_mixed, s, target)
        window_grads, ffn_packs, other = back_window(kept, gives, target, (ffn_packs, other))
        ffn_packs = exchange(ffn_packs, target)
        attn_packs, grad_in = back_project(
            window_grads, grad_query, grad_mixed, grad_branch, rows_ffn, rows_attn, s, target
        )
        return ffn_weights(ffn_packs, target), attn_packs, grad_in, other

    x_first = hidden_in.reshape(tokens, model)
    x_window, near = fetch(x_first, 0, neighbours(folded, 0))
    pieces = gather(folded, near, 0)
    token = pieces[3][:16, :128] + pieces[4][:16, :128]
    got, token = tie((x_window[3:], token))
    x_window = x_window[:3] + got
    token = links.cross(token, 0)
    result_a, saved_a = forward(x_first, pieces, 0, x_window)
    later, token = tie((folded, token))
    pieces = gather(later, neighbours(later, 1), 1)
    middle = links.cross(result_a, 0)
    result_b, saved_b = forward(middle, pieces, 1, token=token)

    ffn, attn_packs, grad_b, _ = backward(cotangent.reshape(tokens, model), saved_b, 1)
    upstream = links.cross(grad_b, 1)
    upstream, attn_packs = tie((upstream, attn_packs))
    b_first, b_second = attn_weights(exchange(attn_packs, 1), ffn, 1)
    upstream, b_first, b_second = tie((upstream, b_first, b_second))
    halves_b = (links.cross(b_first, 1), b_second)

    ffn, attn_packs, grad_a, half_b = backward(upstream, saved_a, 0, halves_b)
    part_b = lax.psum(half_b, "seq")
    attn_packs, part_b = tie((exchange(attn_packs, 0), part_b))
    a_first, a_second = attn_weights(attn_packs, ffn, 0)
    part_a = lax.psum(jnp.where(is_first, a_first, links.cross(a_second, 0)), "seq")
    theirs = links.swap(jnp.where(is_first, part_b, part_a))

    part = head // shards
    grads = call(
        finish_kernel, info, [part_a, part_b, theirs],
        [shape((1, shard, heads_width), F32), shape((1, shard, head), F32),
         shape((1, shard, head), F32), shape((1, head, model), F32),
         shape((1, shard, hidden), F32), shape((1, shard, hidden), F32),
         shape((1, quarter, model), F32)]
        + [shape((1, shard), F32)] * 4 + [shape((1, part), F32)] * 2,
    )
    g_query, g_key, g_value, g_out, g_gate, g_up, g_down = grads[:7]
    g_attn, g_post_attn, g_ffn, g_post_ffn, g_query_gain, g_key_gain = grads[7:]
    section_outputs = jnp.where(is_first, result_a, result_b).reshape(1, micro, rows, model)
    input_grads = jnp.where(is_first, grad_a, grad_b).reshape(1, micro, rows, model)
    return (
        section_outputs, input_grads, g_attn, g_query, g_key, g_value, g_query_gain, g_key_gain,
        g_out, g_post_attn, g_ffn, g_gate, g_up, g_down, g_post_ffn,
    )


def solution(mesh):
    rows = P(None, ("seq", "fsdp"), None)
    vector, matrix = P("section", "fsdp"), P("section", "fsdp", None)
    weights = (vector, matrix, matrix, matrix, vector, vector, matrix, vector, vector, matrix,
               matrix, matrix, vector)
    out_rows = P("section", None, ("seq", "fsdp"), None)
    return jax.shard_map(
        functools.partial(body, dict(mesh.shape)),
        mesh=mesh,
        in_specs=(rows, rows, P(None, ("seq", "fsdp"))) + weights,
        out_specs=(out_rows, out_rows) + weights,
        check_vma=False,
    )
```

```python
import functools

import jax
import jax.numpy as jnp
from jax import lax
from jax.experimental import pallas as pl
from jax.experimental.pallas import tpu as pltpu
from jax.sharding import PartitionSpec as P

WIN = 512
EPSILON = 1e-06
ROPE_BASE = 10000.0
NEG_LARGE = -1e30
AXES = ("section", "seq", "fsdp")
BF = jnp.bfloat16
F32 = jnp.float32
GAIN_ROWS = 16
INTERPRET = False


def mm(left, right):
    return lax.dot_general(left, right, (((1,), (0,)), ((), ())), preferred_element_type=F32)


def mm_nt(left, right):
    return lax.dot_general(left, right, (((1,), (1,)), ((), ())), preferred_element_type=F32)


def mm_tn(left, right):
    return lax.dot_general(left, right, (((0,), (0,)), ((), ())), preferred_element_type=F32)


def inverse_rms(values):
    return lax.rsqrt(jnp.mean(values * values, axis=-1, keepdims=True) + EPSILON)


def norm_back(values, scale, gain, grad):
    weighted = grad * gain
    inner = jnp.mean(values * weighted, axis=-1, keepdims=True)
    return scale * weighted - values * (scale * scale * scale * inner)


def gain_back(values, scale, grad):
    return jnp.sum(values * scale * grad, axis=0, keepdims=True)


def call(kernel, info, arrays, outs, scratch=(), section=None, pieces=(), far=False):
    smem = pl.BlockSpec(memory_space=pltpu.SMEM)
    vmem = pl.BlockSpec(memory_space=pltpu.VMEM)
    hbm = pl.BlockSpec(memory_space=pltpu.HBM)
    lead = len(pieces)

    def entry(info, *refs):
        def run():
            kernel(info, *((refs[:lead],) if lead else ()), *refs[lead:])

        if section is None:
            run()
        else:
            pl.when(info[2] == section)(run)

    return pl.pallas_call(
        entry,
        out_shape=outs,
        in_specs=[smem] + [hbm] * lead + [hbm if far else vmem] * len(arrays),
        out_specs=[vmem] * len(outs),
        scratch_shapes=list(scratch),
        compiler_params=pltpu.CompilerParams(vmem_limit_bytes=(58 if far else 32) * 1024 * 1024),
        cost_estimate=pl.CostEstimate(flops=1, bytes_accessed=1, transcendentals=0),
        interpret=INTERPRET,
    )(info, *pieces, *arrays)


def shape(dims, kind):
    return jax.ShapeDtypeStruct(tuple(dims), kind)


def slot(index, width):
    return pl.ds(pl.multiple_of(index * width, width), width)


def layout(model):
    unit = model // 5
    return unit * 32, unit * 40, unit * 56, unit * 68


def sources(pieces, start):
    split = pieces[0].shape[1]
    if start < split:
        return [(piece, start) for piece in pieces[:4]]
    return [(piece, start - split) for piece in pieces[4:]]


def gains_kernel(info, gathered, out, held, sems):
    count, rows, width = held.shape
    shard = out.shape[1] // count
    part = shard * 2 // 5
    copies = []
    for flip, (piece, start) in enumerate(sources(gathered, layout(out.shape[1])[3])):
        source = piece.at[pl.ds(0, rows), pl.ds(start, width)]
        copies.append(pltpu.make_async_copy(source, held.at[info[0] ^ flip], sems.at[flip]))
    for copy in copies:
        copy.start()
    for copy in copies:
        copy.wait()
    out[...] = jnp.zeros_like(out)
    for place in range(count):
        values = held[place].astype(F32)
        start = place * shard
        for row in range(4):
            out[row : row + 1, start : start + width] = values[2 * row : 2 * row + 1]
            out[row : row + 1, start + width : start + shard] = values[
                2 * row + 1 : 2 * row + 2, : shard - width
            ]
        for row in range(2):
            out[4 + row : 5 + row, place * part : (place + 1) * part] = values[
                8 + row : 9 + row, :part
            ]


def fold_kernel(info, gate, up, query, key, value, out_w, down_w, attn, post_attn, ffn, post_ffn,
                query_gain, key_gain, first, second, out_held, down_held, *rest):
    shard = gate.shape[1]
    vectors, sems = rest[:-1], rest[-1]
    copies = []

    def load(source, target):
        copy = pltpu.make_async_copy(source, target, sems.at[len(copies)])
        copy.start()
        copies.append(copy)

    load(out_w.at[0], out_held)
    load(down_w.at[0], down_held)
    for source, held in zip((attn, post_attn, ffn, post_ffn, query_gain, key_gain), vectors):
        load(source, held)
    hidden = gate.shape[2]
    load(gate.at[0], first.at[:, pl.ds(0, hidden)])
    load(up.at[0], first.at[:, pl.ds(hidden, hidden)])
    start = 4 * (out_held.shape[0] + down_held.shape[0])
    for ref in (query, key, value):
        load(ref.at[0], second.at[:, pl.ds(start, ref.shape[2])])
        start += ref.shape[2]
    wait_all(copies)
    second[:, start:] = jnp.zeros_like(second[:, start:])
    width = 128
    for row, ref in enumerate(vectors[:4]):
        second[2 * row : 2 * row + 1, start : start + width] = ref[:, :width]
        second[2 * row + 1 : 2 * row + 2, start : start + shard - width] = ref[:, width:]
    for row, ref in enumerate(vectors[4:]):
        second[8 + row : 9 + row, start : start + ref.shape[1]] = ref[...]
    start = 0
    for held in (out_held, down_held):
        rows = held.shape[0]
        for place in range(4):
            block = held[:, place * shard : (place + 1) * shard].astype(F32)
            second[:, start : start + rows] = block.T.astype(BF)
            start += rows


def load_turned(info, gathered, held, sems, start):
    width, shard = held.shape[1] // 4, held.shape[0] // 4
    copies = []
    for flip, (piece, column) in enumerate(sources(gathered, start)):
        for row in range(4):
            copy = pltpu.make_async_copy(
                piece.at[:, pl.ds(column + row * width, width)],
                held.at[pl.ds(row * shard, shard), slot(info[0] ^ flip, width)],
                sems.at[4 * flip + row],
            )
            copy.start()
            copies.append(copy)
    return copies


def load_rows(info, gathered, held, sems, start):
    shard, width = held.shape[0] // 4, held.shape[1]
    copies = []
    for flip, (piece, column) in enumerate(sources(gathered, start)):
        copy = pltpu.make_async_copy(
            piece.at[:, pl.ds(column, width)], held.at[slot(info[0] ^ flip, shard)], sems.at[flip]
        )
        copy.start()
        copies.append(copy)
    return copies


def wait_all(copies):
    for copy in copies:
        copy.wait()


def rope_store(target, rows, start, normal, cos, sin):
    half = cos.shape[1]
    one, two = normal[:, :half], normal[:, half:]
    target[rows, start : start + half] = (one * cos - two * sin).astype(BF)
    target[rows, start + half : start + 2 * half] = (two * cos + one * sin).astype(BF)


def cut(blocks, normed):
    shard = blocks.shape[2]
    for place in range(blocks.shape[0]):
        blocks[place] = normed[:, place * shard : (place + 1) * shard].astype(BF)


def project_window_kernel(micro, info, gathered, x, one, two, *refs):
    got, (gains, cosine, sine, wide_cos, wide_sin) = refs[:3], refs[3:8]
    blocks, qkv, query, window, weight, sems = refs[8:]
    copies = load_rows(info, gathered, weight, sems, layout(x.shape[1])[2])
    rows = x.shape[0] // micro
    head = window.shape[2] // 2
    heads_width = query.shape[1]

    def normed_of(values):
        return values * inverse_rms(values) * gains[0:1, :]

    normed = normed_of(x[...].astype(F32))
    cut(blocks, normed)
    normed = normed.astype(BF)
    wait_all(copies)
    total = mm(normed, weight[:, :heads_width])
    qkv[:, :heads_width] = total
    for start in range(0, heads_width, head):
        raw = total[:, start : start + head]
        normal = raw * inverse_rms(raw) * gains[4:5, :head]
        rope_store(query, slice(None), start, normal, cosine[...], sine[...])
    for m in range(micro):
        span = slice(m * rows, (m + 1) * rows)
        parts = [x[span], one[span], two[span]]
        for ref in got:
            parts += [ref[0, span], ref[1, span]]
        values = jnp.concatenate(parts, axis=0).astype(F32)
        total = mm(normed_of(values).astype(BF), weight[:, heads_width:])
        qkv[span, heads_width:] = total[:rows]
        raw = total[:, :head]
        normal = raw * inverse_rms(raw) * gains[5:6, :head]
        rope_store(window.at[m], slice(None), 0, normal, wide_cos[...], wide_sin[...])
        window[m, :, head:] = total[:, head:].astype(BF)


def finish_kernel(info, part_a, part_b, theirs, *outs):
    query, key, value, out, gate, up, down = outs[:7]
    vectors = outs[7:]
    shard, hidden = gate.shape[1], gate.shape[2]

    def emit(first, second):
        gate[0] = first[:, :hidden].astype(F32)
        up[0] = first[:, hidden : 2 * hidden].astype(F32)
        for row, ref in enumerate(vectors):
            ref[...] = first[:GAIN_ROWS, 2 * hidden : 2 * hidden + ref.shape[1]].astype(F32)[
                row : row + 1
            ]
        start = 0
        for ref in (query, key, value):
            ref[0] = second[:, start : start + ref.shape[2]].astype(F32)
            start += ref.shape[2]
        for ref in (out, down):
            rows = ref.shape[1]
            for place in range(4):
                block = second[:, start : start + rows].astype(F32)
                ref[0, :, place * shard : (place + 1) * shard] = block.T
                start += rows

    @pl.when(info[2] == 0)
    def _():
        emit(part_a, theirs)

    @pl.when(info[2] == 1)
    def _():
        emit(theirs, part_b)


def project_kernel(info, gathered, x, gains, cosine, sine, token, blocks, qkv, query, own, weight,
                   sems):
    copies = load_rows(info, gathered, weight, sems, layout(x.shape[1])[2])
    head = 2 * cosine.shape[1]
    residual = x[...].astype(F32)
    normed = residual * inverse_rms(residual) * gains[0:1, :]
    cut(blocks, normed)
    wait_all(copies)
    total = mm(normed.astype(BF), weight[...])
    qkv[...] = total
    heads = query.shape[1] // head
    for index in range(heads + 1):
        raw = total[:, index * head : (index + 1) * head]
        row = 4 if index < heads else 5
        normal = raw * inverse_rms(raw) * gains[row : row + 1, :head]
        target, start = (query, index * head) if index < heads else (own, 0)
        rope_store(target, slice(None), start, normal, cosine[...], sine[...])
    own[:, head:] = total[:, (heads + 1) * head :].astype(BF)


def select_kernel(info, own, one, two, *outs):
    for index, out in enumerate(outs):
        lower = (info[0] < (info[0] ^ (index + 1))).astype(F32)
        out[0] = one[...]
        mixed = own[...].astype(F32) * lower + two[...].astype(F32) * (1.0 - lower)
        out[1] = mixed.astype(BF)


def window_kernel(micro, info, own, one, two, *refs):
    got, window = refs[:3], refs[3]
    rows = own.shape[0] // micro
    for m in range(micro):
        span = slice(m * rows, (m + 1) * rows)
        parts = [own[span], one[span], two[span]]
        for ref in got:
            parts += [ref[0, span], ref[1, span]]
        for index, part in enumerate(parts):
            window[m, index * rows : (index + 1) * rows] = part


def attend_kernel(micro, info, gathered, query, x, gains, limit, *refs):
    out_w, sems = refs[-2:]
    model = x.shape[1]
    shard = model // 4
    copies = load_turned(info, gathered, out_w, sems, layout(model)[0])
    if len(refs) == 1 + 6 + 2:
        window = refs[0]
        outs = refs[1:-2]
    else:
        window = refs[6]
        outs = refs[7:-2]
        window_kernel(micro, info, *refs[:6], window)
    probs, attended, branch, mixed, blocks, ffn_in = outs
    rows = query.shape[0] // micro
    head = window.shape[2] // 2
    heads = query.shape[1] // head
    count = window.shape[1]
    column = lax.broadcasted_iota(jnp.int32, (rows, count), 1)
    distance = lax.broadcasted_iota(jnp.int32, (rows, count), 0) + info[3]
    for index in range(count // rows):
        inside = (column >= index * rows) & (column < (index + 1) * rows)
        distance = distance - jnp.where(inside, column - index * rows + info[4 + index], 0)
    for m in range(micro):
        span = slice(m * rows, (m + 1) * rows)
        allowed = (distance >= 0) & (distance <= limit[span])
        bias = jnp.where(allowed, 0.0, NEG_LARGE)
        bias = jnp.concatenate([bias] * heads, axis=0)
        stacked = jnp.concatenate(
            [query[span, h * head : (h + 1) * head] for h in range(heads)], axis=0
        )
        scores = mm_nt(stacked, window[m, :, :head]) * head ** (-0.5) + bias
        exponent = jnp.exp(scores - jnp.max(scores, axis=-1, keepdims=True))
        chance = exponent / jnp.sum(exponent, axis=-1, keepdims=True)
        probs[m] = chance
        result = mm(chance.astype(BF), window[m, :, head:]).astype(BF)
        for h in range(heads):
            attended[span, h * head : (h + 1) * head] = result[h * rows : (h + 1) * rows]
    for copy in copies:
        copy.wait()
    total = mm_nt(attended[...], out_w[...])
    branch[...] = total
    value = x[...].astype(F32) + total * inverse_rms(total) * gains[1:2, :]
    mixed[...] = value
    normed = value * inverse_rms(value) * gains[2:3, :]
    ffn_in[...] = normed.astype(BF)
    for place in range(4):
        blocks[place] = normed[:, place * shard : (place + 1) * shard].astype(BF)


def gelu_parts(gate):
    c = 0.7978845608028654
    inner = jnp.tanh(c * (gate + 0.044715 * gate * gate * gate))
    value = 0.5 * gate * (1.0 + inner)
    slope = 0.5 * (1.0 + inner) + 0.5 * gate * (1.0 - inner * inner) * c * (
        1.0 + 3 * 0.044715 * gate * gate
    )
    return value, slope


def ffn_kernel(info, gathered, ffn_in, mixed, gains, gate_up, activated, down, result,
               gate_up_w, down_w, column_sems, sems):
    hidden = activated.shape[1]
    width = 512
    columns = load_rows(info, gathered, gate_up_w, column_sems, 0)
    copies = load_turned(info, gathered, down_w, sems, layout(mixed.shape[1])[1])
    wait_all(columns)
    for start in range(0, hidden, width):
        both = []
        for base in (start, hidden + start):
            total = mm(ffn_in[...], gate_up_w[:, base : base + width])
            gate_up[:, base : base + width] = total
            both.append(total)
        value, _ = gelu_parts(both[0])
        activated[:, start : start + width] = (value * both[1]).astype(BF)
    for copy in copies:
        copy.wait()
    total = mm_nt(activated[...], down_w[...])
    down[...] = total
    result[...] = (mixed[...] + total * inverse_rms(total) * gains[3:4, :]).astype(BF)


def ffn_back_kernel(info, gathered, upstream, mixed, down, gate_up, activated, blocks, gains,
                    *refs):
    packs, grad_mixed, gain_rows = refs[:4], refs[4], refs[5]
    grad_gate_up, gate_up_w, down_w, column_sems, sems = refs[6:]
    hidden = activated.shape[1]
    model = mixed.shape[1]
    shard = blocks.shape[2]
    copies = load_turned(info, gathered, down_w, sems, layout(mixed.shape[1])[1])
    columns = load_rows(info, gathered, gate_up_w, column_sems, 0)
    top = upstream[...].astype(F32)
    raw = down[...]
    scale = inverse_rms(raw)
    grad_down = norm_back(raw, scale, gains[3:4, :], top).astype(BF)
    gain_rows[...] = jnp.zeros_like(gain_rows)
    gain_rows[3:4, :] = gain_back(raw, scale, top)
    act_at = 2 * hidden + model
    block_at = act_at + hidden // 4
    for flip, pack in enumerate(packs):
        pack[:, 2 * hidden : act_at] = grad_down
        pack[:, act_at:block_at] = activated[:, slot(info[0] ^ flip, hidden // 4)]
        pack[:, block_at:] = jnp.zeros_like(pack[:, block_at:])
        pack[:, block_at : block_at + shard] = blocks[info[0] ^ flip]
    for copy in copies:
        copy.wait()
    width = 512
    for start in range(0, hidden, width):
        value, slope = gelu_parts(gate_up[:, start : start + width])
        up = gate_up[:, hidden + start : hidden + start + width]
        grad = mm(grad_down, down_w[:, start : start + width])
        grad_gate_up[:, start : start + width] = (grad * up * slope).astype(BF)
        grad_gate_up[:, hidden + start : hidden + start + width] = (grad * value).astype(BF)
    for pack in packs:
        pack[:, : 2 * hidden] = grad_gate_up[...]
    for copy in columns:
        copy.wait()
    grad_in = mm_nt(grad_gate_up[...], gate_up_w[...])
    raw = mixed[...]
    scale = inverse_rms(raw)
    gain_rows[2:3, :] = gain_back(raw, scale, grad_in)
    grad_mixed[...] = top + norm_back(raw, scale, gains[2:3, :], grad_in)


def attend_back_kernel(micro, info, gathered, grad_mixed, branch, window, probs, query, gains,
                       *refs):
    grad_branch, grad_query, own, one, two = refs[:5]
    gives, gain_rows, grad_attended, out_w, sems = refs[5:8], refs[8], refs[9], refs[10], refs[11]
    model = branch.shape[1]
    copies = load_turned(info, gathered, out_w, sems, layout(model)[0])
    rows = own.shape[0] // micro
    head = own.shape[1] // 2
    heads = query.shape[1] // head
    factor = head ** (-0.5)
    raw = branch[...]
    scale = inverse_rms(raw)
    grad = grad_mixed[...]
    gain_rows[...] = jnp.zeros_like(gain_rows)
    gain_rows[1:2, :] = gain_back(raw, scale, grad)
    low = norm_back(raw, scale, gains[1:2, :], grad).astype(BF)
    grad_branch[...] = low
    for copy in copies:
        copy.wait()
    grad_attended[...] = mm(low, out_w[...]).astype(BF)
    for m in range(micro):
        span = slice(m * rows, (m + 1) * rows)
        chance = probs[m]
        keys, values = window[m, :, :head], window[m, :, head:]
        stacked = jnp.concatenate(
            [query[span, h * head : (h + 1) * head] for h in range(heads)], axis=0
        )
        upstream = jnp.concatenate(
            [grad_attended[span, h * head : (h + 1) * head] for h in range(heads)], axis=0
        )
        grad_values = mm_tn(chance.astype(BF), upstream)
        grad_chance = mm_nt(upstream, values)
        inner = jnp.sum(chance * grad_chance, axis=-1, keepdims=True)
        grad_scores = (chance * (grad_chance - inner)).astype(BF)
        grad_stacked = mm(grad_scores, keys) * factor
        grad_keys = mm_tn(grad_scores, stacked) * factor
        for h in range(heads):
            grad_query[span, h * head : (h + 1) * head] = grad_stacked[h * rows : (h + 1) * rows]
        for index, target in enumerate((own, one, two)):
            part = slice(index * rows, (index + 1) * rows)
            target[span, :head] = grad_keys[part]
            target[span, head:] = grad_values[part]
        for index, target in enumerate(gives):
            for side in range(2):
                start = (3 + 2 * index + side) * rows
                target[side, span, :head] = grad_keys[start : start + rows].astype(BF)
                target[side, span, head:] = grad_values[start : start + rows].astype(BF)


def combine_kernel(info, own, one, two, first, second, third, own_out, one_out, two_out):
    total_own, total_one, total_two = own[...], one[...], two[...]
    for index, got in enumerate((first, second, third)):
        lower = (info[0] < (info[0] ^ (index + 1))).astype(F32)
        total_one = total_one + got[0].astype(F32)
        side = got[1].astype(F32)
        total_own = total_own + side * lower
        total_two = total_two + side * (1.0 - lower)
    own_out[...] = total_own
    one_out[...] = total_one.astype(BF)
    two_out[...] = total_two.astype(BF)


def project_back_kernel(info, gathered, own, back_one, back_two, grad_query, qkv, cosine, sine, x, grad_mixed,
                        grad_branch, attended, blocks, gains, rows_ffn, rows_attn, *refs):
    packs, grad_in = refs[:4], refs[4]
    grad_qkv, gain_held, weight, sems = refs[5:]
    copies = load_rows(info, gathered, weight, sems, layout(x.shape[1])[2])
    tokens, model = x.shape
    shard = blocks.shape[2]
    half = cosine.shape[1]
    head = 2 * half
    heads = grad_query.shape[1] // head
    cos, sin = cosine[...], sine[...]
    grad_own = own[...] + back_one[...].astype(F32) + back_two[...].astype(F32)
    head_gains = [None, None]
    for index in range(heads + 1):
        if index < heads:
            grad = grad_query[:, index * head : (index + 1) * head]
        else:
            grad = grad_own[:, :head]
        one, two = grad[:, :half], grad[:, half:]
        grad = jnp.concatenate((one * cos + two * sin, two * cos - one * sin), axis=1)
        raw = qkv[:, index * head : (index + 1) * head]
        scale = inverse_rms(raw)
        kind = 0 if index < heads else 1
        term = gain_back(raw, scale, grad)
        head_gains[kind] = term if head_gains[kind] is None else head_gains[kind] + term
        back = norm_back(raw, scale, gains[4 + kind : 5 + kind, :head], grad)
        grad_qkv[:, index * head : (index + 1) * head] = back.astype(BF)
    grad_qkv[:, (heads + 1) * head :] = grad_own[:, head:].astype(BF)
    wait_all(copies)
    grad_normed = mm_nt(grad_qkv[...], weight[...])
    residual = x[...].astype(F32)
    scale = inverse_rms(residual)
    first_gain = gain_back(residual, scale, grad_normed)
    total = grad_mixed[...] + norm_back(residual, scale, gains[0:1, :], grad_normed)
    grad_in[...] = total.astype(BF)
    gain_held[...] = jnp.zeros_like(gain_held)
    part = head // 4
    four = (first_gain, rows_attn[1:2, :], rows_ffn[2:3, :], rows_ffn[3:4, :])
    for place in range(4):
        for row, values in enumerate(four):
            gain_held[place, row : row + 1, :shard] = values[
                :, place * shard : (place + 1) * shard
            ]
        for row, values in enumerate(head_gains):
            gain_held[place, 4 + row : 5 + row, :part] = values[
                :, place * part : (place + 1) * part
            ]
    wide = grad_qkv.shape[1]
    att_at = wide + model
    block_at = att_at + head
    for flip, pack in enumerate(packs):
        other = info[0] ^ flip
        pack[tokens:, :] = jnp.zeros_like(pack[tokens:, :])
        pack[tokens:, : gain_held.shape[2]] = gain_held[other].astype(BF)
        pack[:tokens, :wide] = grad_qkv[...]
        pack[:tokens, wide:att_at] = grad_branch[...]
        pack[:tokens, att_at:block_at] = attended[:, slot(other, head)]
        pack[:tokens, block_at:] = jnp.zeros_like(pack[:tokens, block_at:])
        pack[:tokens, block_at : block_at + shard] = blocks[other]


def over(packs, tokens, left, right, left_width, right_width):
    total = None
    for pack in packs:
        term = mm_tn(
            pack[:tokens, left : left + left_width], pack[:tokens, right : right + right_width]
        )
        total = term if total is None else total + term
    return total.astype(BF)


def ffn_weights_kernel(shard, model, info, *refs):
    packs, first, second = refs[:4], refs[4], refs[5]
    tokens = packs[0].shape[0]
    wide = first.shape[1]
    quarter = second.shape[1] // 4
    act_at = wide + model
    for start in range(0, wide, 1024):
        first[:, start : start + 1024] = over(
            packs, tokens, act_at + quarter, start, shard, 1024
        )
    for place in range(4):
        second[:, place * quarter : (place + 1) * quarter] = over(
            packs, tokens, wide + place * shard, act_at, shard, quarter
        )


def weights_kernel(shard, model, info, *refs):
    packs, gate_up, down, first, second = refs[:4], refs[4], refs[5], refs[6], refs[7]
    tokens = packs[0].shape[0] - GAIN_ROWS
    head = model // 5 * 2
    wide = packs[0].shape[1] - model - 2 * head
    hidden = gate_up.shape[1]
    first[:, :hidden] = gate_up[...]
    first[:, hidden:] = jnp.zeros_like(first[:, hidden:])
    gains = sum(pack[tokens:, :head].astype(F32) for pack in packs)
    first[:GAIN_ROWS, hidden : hidden + head] = gains.astype(BF)
    att_at = wide + model
    second[:, :wide] = over(packs, tokens, att_at + head, 0, shard, wide)
    for place in range(4):
        start = wide + place * head
        second[:, start : start + head] = over(
            packs, tokens, wide + place * shard, att_at, shard, head
        )
    second[:, wide + 4 * head :] = down[...]


class Links:
    def __init__(self, sizes):
        self.sizes = sizes

    def index(self, section, seq, fsdp):
        return (section * self.sizes["seq"] + seq) * self.sizes["fsdp"] + fsdp

    def send(self, array, section, place):
        pairs = []
        for z in range(self.sizes["seq"]):
            for f in range(self.sizes["fsdp"]):
                to_section, to_z, to_f = place(z, f)
                if 0 <= to_z < self.sizes["seq"]:
                    pairs.append((self.index(section, z, f), self.index(to_section, to_z, to_f)))
        return lax.ppermute(array, AXES, pairs)

    def along(self, array, section, by):
        return self.send(array, section, lambda z, f: (section, z + by, f))

    def across(self, array, section, flip):
        return self.send(array, section, lambda z, f: (section, z, f ^ flip))

    def cross(self, array, section):
        return self.send(array, section, lambda z, f: (1 - section, z, f))

    def both(self, array, flip):
        pairs = []
        for section in range(2):
            for z in range(self.sizes["seq"]):
                for f in range(self.sizes["fsdp"]):
                    pairs.append((self.index(section, z, f), self.index(section, z, f ^ flip)))
        return lax.ppermute(array, AXES, pairs)

    def swap(self, array):
        pairs = []
        for section in range(2):
            for z in range(self.sizes["seq"]):
                for f in range(self.sizes["fsdp"]):
                    pairs.append((self.index(section, z, f), self.index(1 - section, z, f)))
        return lax.ppermute(array, AXES, pairs)


def body(sizes, hidden_in, cotangent, positions, attn_gain, w_query, w_key, w_value, query_gain,
         key_gain, w_output, post_attn_gain, ffn_gain, w_gate, w_up, w_down, post_ffn_gain):
    section = lax.axis_index("section")
    seq = lax.axis_index("seq")
    fsdp = lax.axis_index("fsdp")
    is_first = section == 0
    micro, rows, model = hidden_in.shape
    tokens = micro * rows
    shard = w_query.shape[1]
    shards = sizes["fsdp"]
    heads_width, head = w_query.shape[2], w_key.shape[2]
    wide = heads_width + 2 * head
    hidden = w_gate.shape[2]
    quarter = hidden // shards
    assert shards == 4 and 2 * shards * rows == WIN and heads_width == shards * head
    links = Links(sizes)
    tie = lax.optimization_barrier
    info = jnp.stack([fsdp, seq, section]).astype(jnp.int32)

    folded = call(
        fold_kernel, info,
        [w_gate, w_up, w_query, w_key, w_value, w_output, w_down, attn_gain, post_attn_gain,
         ffn_gain, post_ffn_gain, query_gain, key_gain],
        [shape((shard, 2 * hidden), BF), shape((shard, heads_width + hidden + wide + 128), BF)],
        [pltpu.VMEM((head, model), BF), pltpu.VMEM((quarter, model), BF)]
        + [pltpu.VMEM((1, shard), BF)] * 4 + [pltpu.VMEM((1, query_gain.shape[1]), BF)] * 2
        + [pltpu.SemaphoreType.DMA((13,))],
        far=True,
    )

    def gather(arrays, target):
        first, second = arrays
        second_one = links.across(second, target, 1)
        first_two = links.across(first, target, 2)
        first_one = links.across(first, target, 1)
        second_two = links.across(second, target, 2)
        second_three = links.across(second_one, target, 2)
        first_three = links.across(first_two, target, 1)
        return [first, first_one, first_two, first_three,
                second, second_one, second_two, second_three]

    def gain_table(pieces, target):
        return call(
            gains_kernel, info, [], [shape((8, model), F32)],
            [pltpu.VMEM((shards, GAIN_ROWS, 128), BF), pltpu.SemaphoreType.DMA((shards,))],
            pieces=pieces, section=target,
        )[0]

    qkv_scratch = [pltpu.VMEM((model, wide), BF), pltpu.SemaphoreType.DMA((shards,))]
    out_scratch = [pltpu.VMEM((model, heads_width), BF), pltpu.SemaphoreType.DMA((16,))]
    ffn_scratch = [pltpu.VMEM((model, 2 * hidden), BF), pltpu.VMEM((model, hidden), BF),
                   pltpu.SemaphoreType.DMA((shards,)), pltpu.SemaphoreType.DMA((16,))]

    half = head // 2
    limit = jnp.minimum(positions.reshape(tokens, 1), WIN - 1)
    starts = [(seq - back) * shards + fsdp for back in range(3)]
    for flip in range(1, shards):
        other = fsdp ^ flip
        starts.append((seq - 1) * shards + other)
        starts.append(jnp.where(other < fsdp, seq, seq - 2) * shards + other)
    starts = jnp.stack(starts).astype(jnp.int32) * rows
    key_place = (starts[:, None] + jnp.arange(rows, dtype=jnp.int32)[None, :]).reshape(1, -1)
    info = jnp.concatenate((info, starts[:1], starts))
    span = key_place.shape[1]
    frequency = ROPE_BASE ** (-2.0 * jnp.arange(half, dtype=F32) / head)
    angles = key_place.reshape(span, 1).astype(F32) * frequency[None, :]
    wide_cos, wide_sin = jnp.cos(angles), jnp.sin(angles)
    cosine, sine = (jnp.tile(table[:rows], (micro, 1)) for table in (wide_cos, wide_sin))

    def fetch(own, target, waiting=None):
        one, two = links.along(own, target, 1), links.along(own, target, 2)
        if waiting is not None:
            one, two, waiting = tie((one, two, waiting))
        sent = call(
            select_kernel, info, [own, one, two], [shape((2,) + own.shape, BF)] * (shards - 1),
            section=target,
        )
        got = [links.across(array, target, 1 + i) for i, array in enumerate(sent)]
        return [own, one, two] + got, waiting

    def forward(x, pieces, target, x_window=None, token=None):
        gains = gain_table(pieces, target)
        sizes_of = [shape((shards, tokens, shard), BF), shape((tokens, wide), F32),
                    shape((tokens, heads_width), BF)]
        whole = shape((micro, span, 2 * head), BF)
        attend_outs = [
            shape((micro, shards * rows, span), F32), shape((tokens, heads_width), BF),
            shape((tokens, model), F32), shape((tokens, model), F32),
            shape((shards, tokens, shard), BF), shape((tokens, model), BF),
        ]
        if x_window is not None:
            blocks, qkv, query, window = call(
                functools.partial(project_window_kernel, micro), info,
                x_window + [gains, cosine, sine, wide_cos, wide_sin],
                sizes_of + [whole], qkv_scratch, section=target, pieces=pieces,
            )
            parts = [window]
        else:
            blocks, qkv, query, own = call(
                project_kernel, info, [x, gains, cosine, sine, token],
                sizes_of + [shape((tokens, 2 * head), BF)], qkv_scratch, section=target,
                pieces=pieces,
            )
            parts, _ = fetch(own, target)
            attend_outs = [whole] + attend_outs
        outs = call(
            functools.partial(attend_kernel, micro), info,
            [query, x, gains, limit] + parts, attend_outs, out_scratch, section=target,
            pieces=pieces,
        )
        if x_window is None:
            window, *outs = outs
        probs, attended, branch, mixed, ffn_blocks, ffn_in = outs
        gate_up, activated, down, result = call(
            ffn_kernel, info, [ffn_in, mixed, gains],
            [shape((tokens, 2 * hidden), F32), shape((tokens, hidden), BF),
             shape((tokens, model), F32), shape((tokens, model), BF)], ffn_scratch,
            section=target, pieces=pieces,
        )
        saved = dict(
            x=x, gains=gains, pieces=pieces, blocks=blocks, qkv=qkv, query=query, window=window, probs=probs,
            attended=attended, branch=branch, mixed=mixed, ffn_blocks=ffn_blocks, gate_up=gate_up,
            activated=activated, down=down,
        )
        return result, saved

    def back_ffn(upstream, s, target):
        outs = call(
            ffn_back_kernel, info,
            [upstream, s["mixed"], s["down"], s["gate_up"], s["activated"], s["ffn_blocks"],
             s["gains"]],
            [shape((tokens, 2 * hidden + model + quarter + 256), BF)] * shards
            + [shape((tokens, model), F32), shape((8, model), F32)],
            [pltpu.VMEM((tokens, 2 * hidden), BF)] + ffn_scratch,
            section=target, pieces=s["pieces"],
        )
        return outs[:shards], outs[shards], outs[shards + 1]

    def back_attend(grad_mixed, s, target):
        pair = [shape((tokens, 2 * head), F32)] * 3
        outs = call(
            functools.partial(attend_back_kernel, micro), info,
            [grad_mixed, s["branch"], s["window"], s["probs"], s["query"], s["gains"]],
            [shape((tokens, model), BF), shape((tokens, heads_width), F32)] + pair
            + [shape((2, tokens, 2 * head), BF)] * (shards - 1) + [shape((8, model), F32)],
            [pltpu.VMEM((tokens, heads_width), BF)] + out_scratch,
            section=target, pieces=s["pieces"],
        )
        return outs[0], outs[1], outs[2:5], outs[5:8], outs[8]

    def back_window(kept, gives, target, waiting):
        got = [links.across(array, target, 1 + i) for i, array in enumerate(gives)]
        ffn_packs, other = waiting
        if other is not None:
            got, other, ffn_packs = tie((got, other, ffn_packs))
            other = jnp.where(is_first, other[0], other[1])
            kept, other = tie((kept, other))
        own, one, two = call(
            combine_kernel, info, list(kept) + got,
            [shape((tokens, 2 * head), F32)] + [shape((tokens, 2 * head), BF)] * 2,
            section=target,
        )
        one, two = links.along(one, target, -1), links.along(two, target, -2)
        if other is None:
            one, ffn_packs = tie((one, ffn_packs))
        return (own, one, two), ffn_packs, other

    def back_project(window_grads, grad_query, grad_mixed, grad_branch, rows_ffn, rows_attn, s,
                     target):
        outs = call(
            project_back_kernel, info,
            list(window_grads) + [grad_query, s["qkv"], cosine, sine, s["x"], grad_mixed,
            grad_branch, s["attended"], s["blocks"], s["gains"], rows_ffn, rows_attn],
            [shape((tokens + GAIN_ROWS, wide + model + head + 256), BF)] * shards
            + [shape((tokens, model), BF)],
            [pltpu.VMEM((tokens, wide), BF), pltpu.VMEM((shards, GAIN_ROWS, 256), F32)]
            + qkv_scratch,
            section=target, pieces=s["pieces"],
        )
        return outs[:shards], outs[shards]

    def exchange(packs, target):
        return [packs[0]] + [links.across(packs[i], target, i) for i in range(1, shards)]

    total_width = 2 * hidden + 512

    def ffn_weights(packs, target):
        return call(
            functools.partial(ffn_weights_kernel, shard, model), info, list(packs),
            [shape((shard, 2 * hidden), BF), shape((shard, hidden), BF)],
            section=target,
        )

    def attn_weights(packs, ffn, target):
        return call(
            functools.partial(weights_kernel, shard, model), info, list(packs) + list(ffn),
            [shape((shard, total_width), BF)] * 2,
            section=target,
        )

    def backward(upstream, s, target, other=None):
        ffn_packs, grad_mixed, rows_ffn = back_ffn(upstream, s, target)
        grad_branch, grad_query, kept, gives, rows_attn = back_attend(grad_mixed, s, target)
        window_grads, ffn_packs, other = back_window(kept, gives, target, (ffn_packs, other))
        ffn_packs = exchange(ffn_packs, target)
        attn_packs, grad_in = back_project(
            window_grads, grad_query, grad_mixed, grad_branch, rows_ffn, rows_attn, s, target
        )
        return ffn_weights(ffn_packs, target), attn_packs, grad_in, other

    x_first = hidden_in.reshape(tokens, model)
    x_window, _ = fetch(x_first, 0)
    pieces = gather(folded, 0)
    token = links.cross(pieces[2][:16, :128] + pieces[5][:16, :128], 0)
    result_a, saved_a = forward(x_first, pieces, 0, x_window)
    later, token = tie((folded, token))
    pieces = gather(later, 1)
    middle = links.cross(result_a, 0)
    result_b, saved_b = forward(middle, pieces, 1, token=token)

    ffn, attn_packs, grad_b, _ = backward(cotangent.reshape(tokens, model), saved_b, 1)
    upstream = links.cross(grad_b, 1)
    upstream, attn_packs = tie((upstream, attn_packs))
    b_first, b_second = attn_weights(exchange(attn_packs, 1), ffn, 1)
    upstream, b_first, b_second = tie((upstream, b_first, b_second))
    halves_b = (links.cross(b_first, 1), b_second)

    ffn, attn_packs, grad_a, half_b = backward(upstream, saved_a, 0, halves_b)
    part_b = lax.psum(half_b, "seq")
    attn_packs, part_b = tie((exchange(attn_packs, 0), part_b))
    a_first, a_second = attn_weights(attn_packs, ffn, 0)
    part_a = lax.psum(jnp.where(is_first, a_first, links.cross(a_second, 0)), "seq")
    theirs = links.swap(jnp.where(is_first, part_b, part_a))

    part = head // shards
    grads = call(
        finish_kernel, info, [part_a, part_b, theirs],
        [shape((1, shard, heads_width), F32), shape((1, shard, head), F32),
         shape((1, shard, head), F32), shape((1, head, model), F32),
         shape((1, shard, hidden), F32), shape((1, shard, hidden), F32),
         shape((1, quarter, model), F32)]
        + [shape((1, shard), F32)] * 4 + [shape((1, part), F32)] * 2,
    )
    g_query, g_key, g_value, g_out, g_gate, g_up, g_down = grads[:7]
    g_attn, g_post_attn, g_ffn, g_post_ffn, g_query_gain, g_key_gain = grads[7:]
    section_outputs = jnp.where(is_first, result_a, result_b).reshape(1, micro, rows, model)
    input_grads = jnp.where(is_first, grad_a, grad_b).reshape(1, micro, rows, model)
    return (
        section_outputs, input_grads, g_attn, g_query, g_key, g_value, g_query_gain, g_key_gain,
        g_out, g_post_attn, g_ffn, g_gate, g_up, g_down, g_post_ffn,
    )


def solution(mesh):
    rows = P(None, ("seq", "fsdp"), None)
    vector, matrix = P("section", "fsdp"), P("section", "fsdp", None)
    weights = (vector, matrix, matrix, matrix, vector, vector, matrix, vector, vector, matrix,
               matrix, matrix, vector)
    out_rows = P("section", None, ("seq", "fsdp"), None)
    return jax.shard_map(
        functools.partial(body, dict(mesh.shape)),
        mesh=mesh,
        in_specs=(rows, rows, P(None, ("seq", "fsdp"))) + weights,
        out_specs=(out_rows, out_rows) + weights,
        check_vma=False,
    )
```

```python
import functools

import jax
import jax.numpy as jnp
from jax import lax
from jax.experimental import pallas as pl
from jax.experimental.pallas import tpu as pltpu
from jax.sharding import PartitionSpec as P

WIN = 512
EPSILON = 1e-06
ROPE_BASE = 10000.0
NEG_LARGE = -1e30
AXES = ("section", "seq", "fsdp")
BF = jnp.bfloat16
F32 = jnp.float32
GAIN_ROWS = 16
INTERPRET = False


def mm(left, right):
    return lax.dot_general(left, right, (((1,), (0,)), ((), ())), preferred_element_type=F32)


def mm_nt(left, right):
    return lax.dot_general(left, right, (((1,), (1,)), ((), ())), preferred_element_type=F32)


def mm_tn(left, right):
    return lax.dot_general(left, right, (((0,), (0,)), ((), ())), preferred_element_type=F32)


def inverse_rms(values):
    return lax.rsqrt(jnp.mean(values * values, axis=-1, keepdims=True) + EPSILON)


def norm_back(values, scale, gain, grad):
    weighted = grad * gain
    inner = jnp.mean(values * weighted, axis=-1, keepdims=True)
    return scale * weighted - values * (scale * scale * scale * inner)


def gain_back(values, scale, grad):
    return jnp.sum(values * scale * grad, axis=0, keepdims=True)


def call(kernel, info, arrays, outs, scratch=(), section=None, pieces=(), far=False):
    smem = pl.BlockSpec(memory_space=pltpu.SMEM)
    vmem = pl.BlockSpec(memory_space=pltpu.VMEM)
    hbm = pl.BlockSpec(memory_space=pltpu.HBM)
    lead = len(pieces)

    def entry(info, *refs):
        def run():
            kernel(info, *((refs[:lead],) if lead else ()), *refs[lead:])

        if section is None:
            run()
        else:
            pl.when(info[2] == section)(run)

    return pl.pallas_call(
        entry,
        out_shape=outs,
        in_specs=[smem] + [hbm] * lead + [hbm if far else vmem] * len(arrays),
        out_specs=[vmem] * len(outs),
        scratch_shapes=list(scratch),
        compiler_params=pltpu.CompilerParams(vmem_limit_bytes=(58 if far else 32) * 1024 * 1024),
        cost_estimate=pl.CostEstimate(flops=1, bytes_accessed=1, transcendentals=0),
        interpret=INTERPRET,
    )(info, *pieces, *arrays)


def shape(dims, kind):
    return jax.ShapeDtypeStruct(tuple(dims), kind)


def slot(index, width):
    return pl.ds(pl.multiple_of(index * width, width), width)


def layout(model):
    unit = model // 5
    return unit * 32, unit * 40, unit * 56, unit * 68


def sources(pieces, start):
    split = pieces[0].shape[1]
    if start < split:
        return [(piece, start) for piece in pieces[:4]]
    return [(piece, start - split) for piece in pieces[4:]]


def gains_kernel(info, gathered, out, held, sems):
    count, rows, width = held.shape
    shard = out.shape[1] // count
    part = shard * 2 // 5
    copies = []
    for flip, (piece, start) in enumerate(sources(gathered, layout(out.shape[1])[3])):
        source = piece.at[pl.ds(0, rows), pl.ds(start, width)]
        copies.append(pltpu.make_async_copy(source, held.at[info[0] ^ flip], sems.at[flip]))
    for copy in copies:
        copy.start()
    for copy in copies:
        copy.wait()
    out[...] = jnp.zeros_like(out)
    for place in range(count):
        values = held[place].astype(F32)
        start = place * shard
        for row in range(4):
            out[row : row + 1, start : start + width] = values[2 * row : 2 * row + 1]
            out[row : row + 1, start + width : start + shard] = values[
                2 * row + 1 : 2 * row + 2, : shard - width
            ]
        for row in range(2):
            out[4 + row : 5 + row, place * part : (place + 1) * part] = values[
                8 + row : 9 + row, :part
            ]


def fold_kernel(info, gate, up, query, key, value, out_w, down_w, attn, post_attn, ffn, post_ffn,
                query_gain, key_gain, first, second, out_held, down_held, *rest):
    shard = gate.shape[1]
    vectors, sems = rest[:-1], rest[-1]
    copies = []

    def load(source, target):
        copy = pltpu.make_async_copy(source, target, sems.at[len(copies)])
        copy.start()
        copies.append(copy)

    load(out_w.at[0], out_held)
    load(down_w.at[0], down_held)
    for source, held in zip((attn, post_attn, ffn, post_ffn, query_gain, key_gain), vectors):
        load(source, held)
    hidden = gate.shape[2]
    load(gate.at[0], first.at[:, pl.ds(0, hidden)])
    load(up.at[0], first.at[:, pl.ds(hidden, hidden)])
    start = 4 * (out_held.shape[0] + down_held.shape[0])
    for ref in (query, key, value):
        load(ref.at[0], second.at[:, pl.ds(start, ref.shape[2])])
        start += ref.shape[2]
    wait_all(copies)
    second[:, start:] = jnp.zeros_like(second[:, start:])
    width = 128
    for row, ref in enumerate(vectors[:4]):
        second[2 * row : 2 * row + 1, start : start + width] = ref[:, :width]
        second[2 * row + 1 : 2 * row + 2, start : start + shard - width] = ref[:, width:]
    for row, ref in enumerate(vectors[4:]):
        second[8 + row : 9 + row, start : start + ref.shape[1]] = ref[...]
    start = 0
    for held in (out_held, down_held):
        rows = held.shape[0]
        for place in range(4):
            block = held[:, place * shard : (place + 1) * shard].astype(F32)
            second[:, start : start + rows] = block.T.astype(BF)
            start += rows


def load_turned(info, gathered, held, sems, start):
    width, shard = held.shape[1] // 4, held.shape[0] // 4
    copies = []
    for flip, (piece, column) in enumerate(sources(gathered, start)):
        for row in range(4):
            copy = pltpu.make_async_copy(
                piece.at[:, pl.ds(column + row * width, width)],
                held.at[pl.ds(row * shard, shard), slot(info[0] ^ flip, width)],
                sems.at[4 * flip + row],
            )
            copy.start()
            copies.append(copy)
    return copies


def load_rows(info, gathered, held, sems, start):
    shard, width = held.shape[0] // 4, held.shape[1]
    copies = []
    for flip, (piece, column) in enumerate(sources(gathered, start)):
        copy = pltpu.make_async_copy(
            piece.at[:, pl.ds(column, width)], held.at[slot(info[0] ^ flip, shard)], sems.at[flip]
        )
        copy.start()
        copies.append(copy)
    return copies


def wait_all(copies):
    for copy in copies:
        copy.wait()


def rope_store(target, rows, start, normal, cos, sin):
    half = cos.shape[1]
    one, two = normal[:, :half], normal[:, half:]
    target[rows, start : start + half] = (one * cos - two * sin).astype(BF)
    target[rows, start + half : start + 2 * half] = (two * cos + one * sin).astype(BF)


def cut(blocks, normed):
    shard = blocks.shape[2]
    for place in range(blocks.shape[0]):
        blocks[place] = normed[:, place * shard : (place + 1) * shard].astype(BF)


def project_window_kernel(micro, info, gathered, x, one, two, *refs):
    got, (gains, cosine, sine, wide_cos, wide_sin) = refs[:3], refs[3:8]
    blocks, qkv, query, window, weight, sems = refs[8:]
    copies = load_rows(info, gathered, weight, sems, layout(x.shape[1])[2])
    rows = x.shape[0] // micro
    head = window.shape[2] // 2
    heads_width = query.shape[1]

    def normed_of(values):
        return values * inverse_rms(values) * gains[0:1, :]

    normed = normed_of(x[...].astype(F32))
    cut(blocks, normed)
    normed = normed.astype(BF)
    wait_all(copies)
    total = mm(normed, weight[:, :heads_width])
    qkv[:, :heads_width] = total
    for start in range(0, heads_width, head):
        raw = total[:, start : start + head]
        normal = raw * inverse_rms(raw) * gains[4:5, :head]
        rope_store(query, slice(None), start, normal, cosine[...], sine[...])
    for m in range(micro):
        span = slice(m * rows, (m + 1) * rows)
        parts = [x[span], one[span], two[span]]
        for ref in got:
            parts += [ref[0, span], ref[1, span]]
        values = jnp.concatenate(parts, axis=0).astype(F32)
        total = mm(normed_of(values).astype(BF), weight[:, heads_width:])
        qkv[span, heads_width:] = total[:rows]
        raw = total[:, :head]
        normal = raw * inverse_rms(raw) * gains[5:6, :head]
        rope_store(window.at[m], slice(None), 0, normal, wide_cos[...], wide_sin[...])
        window[m, :, head:] = total[:, head:].astype(BF)


def finish_kernel(info, part_a, part_b, theirs, *outs):
    query, key, value, out, gate, up, down = outs[:7]
    vectors = outs[7:]
    shard, hidden = gate.shape[1], gate.shape[2]

    def emit(first, second):
        gate[0] = first[:, :hidden].astype(F32)
        up[0] = first[:, hidden : 2 * hidden].astype(F32)
        for row, ref in enumerate(vectors):
            ref[...] = first[:GAIN_ROWS, 2 * hidden : 2 * hidden + ref.shape[1]].astype(F32)[
                row : row + 1
            ]
        start = 0
        for ref in (query, key, value):
            ref[0] = second[:, start : start + ref.shape[2]].astype(F32)
            start += ref.shape[2]
        for ref in (out, down):
            rows = ref.shape[1]
            for place in range(4):
                block = second[:, start : start + rows].astype(F32)
                ref[0, :, place * shard : (place + 1) * shard] = block.T
                start += rows

    @pl.when(info[2] == 0)
    def _():
        emit(part_a, theirs)

    @pl.when(info[2] == 1)
    def _():
        emit(theirs, part_b)


def project_kernel(info, gathered, x, gains, cosine, sine, blocks, qkv, query, own, weight, sems):
    copies = load_rows(info, gathered, weight, sems, layout(x.shape[1])[2])
    head = 2 * cosine.shape[1]
    residual = x[...].astype(F32)
    normed = residual * inverse_rms(residual) * gains[0:1, :]
    cut(blocks, normed)
    wait_all(copies)
    total = mm(normed.astype(BF), weight[...])
    qkv[...] = total
    heads = query.shape[1] // head
    for index in range(heads + 1):
        raw = total[:, index * head : (index + 1) * head]
        row = 4 if index < heads else 5
        normal = raw * inverse_rms(raw) * gains[row : row + 1, :head]
        target, start = (query, index * head) if index < heads else (own, 0)
        rope_store(target, slice(None), start, normal, cosine[...], sine[...])
    own[:, head:] = total[:, (heads + 1) * head :].astype(BF)


def select_kernel(info, own, one, two, *outs):
    for index, out in enumerate(outs):
        lower = (info[0] < (info[0] ^ (index + 1))).astype(F32)
        out[0] = one[...]
        mixed = own[...].astype(F32) * lower + two[...].astype(F32) * (1.0 - lower)
        out[1] = mixed.astype(BF)


def window_kernel(micro, info, own, one, two, *refs):
    got, window = refs[:3], refs[3]
    rows = own.shape[0] // micro
    for m in range(micro):
        span = slice(m * rows, (m + 1) * rows)
        parts = [own[span], one[span], two[span]]
        for ref in got:
            parts += [ref[0, span], ref[1, span]]
        for index, part in enumerate(parts):
            window[m, index * rows : (index + 1) * rows] = part


def attend_kernel(micro, info, gathered, query, x, gains, limit, *refs):
    out_w, sems = refs[-2:]
    model = x.shape[1]
    shard = model // 4
    copies = load_turned(info, gathered, out_w, sems, layout(model)[0])
    if len(refs) == 1 + 6 + 2:
        window = refs[0]
        outs = refs[1:-2]
    else:
        window = refs[6]
        outs = refs[7:-2]
        window_kernel(micro, info, *refs[:6], window)
    probs, attended, branch, mixed, blocks, ffn_in = outs
    rows = query.shape[0] // micro
    head = window.shape[2] // 2
    heads = query.shape[1] // head
    count = window.shape[1]
    column = lax.broadcasted_iota(jnp.int32, (rows, count), 1)
    distance = lax.broadcasted_iota(jnp.int32, (rows, count), 0) + info[3]
    for index in range(count // rows):
        inside = (column >= index * rows) & (column < (index + 1) * rows)
        distance = distance - jnp.where(inside, column - index * rows + info[4 + index], 0)
    for m in range(micro):
        span = slice(m * rows, (m + 1) * rows)
        allowed = (distance >= 0) & (distance <= limit[span])
        bias = jnp.where(allowed, 0.0, NEG_LARGE)
        bias = jnp.concatenate([bias] * heads, axis=0)
        stacked = jnp.concatenate(
            [query[span, h * head : (h + 1) * head] for h in range(heads)], axis=0
        )
        scores = mm_nt(stacked, window[m, :, :head]) * head ** (-0.5) + bias
        exponent = jnp.exp(scores - jnp.max(scores, axis=-1, keepdims=True))
        chance = exponent / jnp.sum(exponent, axis=-1, keepdims=True)
        probs[m] = chance
        result = mm(chance.astype(BF), window[m, :, head:]).astype(BF)
        for h in range(heads):
            attended[span, h * head : (h + 1) * head] = result[h * rows : (h + 1) * rows]
    for copy in copies:
        copy.wait()
    total = mm_nt(attended[...], out_w[...])
    branch[...] = total
    value = x[...].astype(F32) + total * inverse_rms(total) * gains[1:2, :]
    mixed[...] = value
    normed = value * inverse_rms(value) * gains[2:3, :]
    ffn_in[...] = normed.astype(BF)
    for place in range(4):
        blocks[place] = normed[:, place * shard : (place + 1) * shard].astype(BF)


def gelu_parts(gate):
    c = 0.7978845608028654
    inner = jnp.tanh(c * (gate + 0.044715 * gate * gate * gate))
    value = 0.5 * gate * (1.0 + inner)
    slope = 0.5 * (1.0 + inner) + 0.5 * gate * (1.0 - inner * inner) * c * (
        1.0 + 3 * 0.044715 * gate * gate
    )
    return value, slope


def ffn_kernel(info, gathered, ffn_in, mixed, gains, gate_up, activated, down, result,
               gate_up_w, down_w, column_sems, sems):
    hidden = activated.shape[1]
    width = 512
    columns = load_rows(info, gathered, gate_up_w, column_sems, 0)
    copies = load_turned(info, gathered, down_w, sems, layout(mixed.shape[1])[1])
    wait_all(columns)
    for start in range(0, hidden, width):
        both = []
        for base in (start, hidden + start):
            total = mm(ffn_in[...], gate_up_w[:, base : base + width])
            gate_up[:, base : base + width] = total
            both.append(total)
        value, _ = gelu_parts(both[0])
        activated[:, start : start + width] = (value * both[1]).astype(BF)
    for copy in copies:
        copy.wait()
    total = mm_nt(activated[...], down_w[...])
    down[...] = total
    result[...] = (mixed[...] + total * inverse_rms(total) * gains[3:4, :]).astype(BF)


def ffn_back_kernel(info, gathered, upstream, mixed, down, gate_up, activated, blocks, gains,
                    *refs):
    packs, grad_mixed, gain_rows = refs[:4], refs[4], refs[5]
    grad_gate_up, gate_up_w, down_w, column_sems, sems = refs[6:]
    hidden = activated.shape[1]
    model = mixed.shape[1]
    shard = blocks.shape[2]
    copies = load_turned(info, gathered, down_w, sems, layout(mixed.shape[1])[1])
    columns = load_rows(info, gathered, gate_up_w, column_sems, 0)
    top = upstream[...].astype(F32)
    raw = down[...]
    scale = inverse_rms(raw)
    grad_down = norm_back(raw, scale, gains[3:4, :], top).astype(BF)
    gain_rows[...] = jnp.zeros_like(gain_rows)
    gain_rows[3:4, :] = gain_back(raw, scale, top)
    act_at = 2 * hidden + model
    block_at = act_at + hidden // 4
    for flip, pack in enumerate(packs):
        pack[:, 2 * hidden : act_at] = grad_down
        pack[:, act_at:block_at] = activated[:, slot(info[0] ^ flip, hidden // 4)]
        pack[:, block_at:] = jnp.zeros_like(pack[:, block_at:])
        pack[:, block_at : block_at + shard] = blocks[info[0] ^ flip]
    for copy in copies:
        copy.wait()
    width = 512
    for start in range(0, hidden, width):
        value, slope = gelu_parts(gate_up[:, start : start + width])
        up = gate_up[:, hidden + start : hidden + start + width]
        grad = mm(grad_down, down_w[:, start : start + width])
        grad_gate_up[:, start : start + width] = (grad * up * slope).astype(BF)
        grad_gate_up[:, hidden + start : hidden + start + width] = (grad * value).astype(BF)
    for pack in packs:
        pack[:, : 2 * hidden] = grad_gate_up[...]
    for copy in columns:
        copy.wait()
    grad_in = mm_nt(grad_gate_up[...], gate_up_w[...])
    raw = mixed[...]
    scale = inverse_rms(raw)
    gain_rows[2:3, :] = gain_back(raw, scale, grad_in)
    grad_mixed[...] = top + norm_back(raw, scale, gains[2:3, :], grad_in)


def attend_back_kernel(micro, info, gathered, grad_mixed, branch, window, probs, query, gains,
                       *refs):
    grad_branch, grad_query, own, one, two = refs[:5]
    gives, gain_rows, grad_attended, out_w, sems = refs[5:8], refs[8], refs[9], refs[10], refs[11]
    model = branch.shape[1]
    copies = load_turned(info, gathered, out_w, sems, layout(model)[0])
    rows = own.shape[0] // micro
    head = own.shape[1] // 2
    heads = query.shape[1] // head
    factor = head ** (-0.5)
    raw = branch[...]
    scale = inverse_rms(raw)
    grad = grad_mixed[...]
    gain_rows[...] = jnp.zeros_like(gain_rows)
    gain_rows[1:2, :] = gain_back(raw, scale, grad)
    low = norm_back(raw, scale, gains[1:2, :], grad).astype(BF)
    grad_branch[...] = low
    for copy in copies:
        copy.wait()
    grad_attended[...] = mm(low, out_w[...]).astype(BF)
    for m in range(micro):
        span = slice(m * rows, (m + 1) * rows)
        chance = probs[m]
        keys, values = window[m, :, :head], window[m, :, head:]
        stacked = jnp.concatenate(
            [query[span, h * head : (h + 1) * head] for h in range(heads)], axis=0
        )
        upstream = jnp.concatenate(
            [grad_attended[span, h * head : (h + 1) * head] for h in range(heads)], axis=0
        )
        grad_values = mm_tn(chance.astype(BF), upstream)
        grad_chance = mm_nt(upstream, values)
        inner = jnp.sum(chance * grad_chance, axis=-1, keepdims=True)
        grad_scores = (chance * (grad_chance - inner)).astype(BF)
        grad_stacked = mm(grad_scores, keys) * factor
        grad_keys = mm_tn(grad_scores, stacked) * factor
        for h in range(heads):
            grad_query[span, h * head : (h + 1) * head] = grad_stacked[h * rows : (h + 1) * rows]
        for index, target in enumerate((own, one, two)):
            part = slice(index * rows, (index + 1) * rows)
            target[span, :head] = grad_keys[part]
            target[span, head:] = grad_values[part]
        for index, target in enumerate(gives):
            for side in range(2):
                start = (3 + 2 * index + side) * rows
                target[side, span, :head] = grad_keys[start : start + rows].astype(BF)
                target[side, span, head:] = grad_values[start : start + rows].astype(BF)


def combine_kernel(info, own, one, two, first, second, third, own_out, one_out, two_out):
    total_own, total_one, total_two = own[...], one[...], two[...]
    for index, got in enumerate((first, second, third)):
        lower = (info[0] < (info[0] ^ (index + 1))).astype(F32)
        total_one = total_one + got[0].astype(F32)
        side = got[1].astype(F32)
        total_own = total_own + side * lower
        total_two = total_two + side * (1.0 - lower)
    own_out[...] = total_own
    one_out[...] = total_one.astype(BF)
    two_out[...] = total_two.astype(BF)


def project_back_kernel(info, gathered, own, back_one, back_two, grad_query, qkv, cosine, sine, x, grad_mixed,
                        grad_branch, attended, blocks, gains, rows_ffn, rows_attn, *refs):
    packs, grad_in = refs[:4], refs[4]
    grad_qkv, gain_held, weight, sems = refs[5:]
    copies = load_rows(info, gathered, weight, sems, layout(x.shape[1])[2])
    tokens, model = x.shape
    shard = blocks.shape[2]
    half = cosine.shape[1]
    head = 2 * half
    heads = grad_query.shape[1] // head
    cos, sin = cosine[...], sine[...]
    grad_own = own[...] + back_one[...].astype(F32) + back_two[...].astype(F32)
    head_gains = [None, None]
    for index in range(heads + 1):
        if index < heads:
            grad = grad_query[:, index * head : (index + 1) * head]
        else:
            grad = grad_own[:, :head]
        one, two = grad[:, :half], grad[:, half:]
        grad = jnp.concatenate((one * cos + two * sin, two * cos - one * sin), axis=1)
        raw = qkv[:, index * head : (index + 1) * head]
        scale = inverse_rms(raw)
        kind = 0 if index < heads else 1
        term = gain_back(raw, scale, grad)
        head_gains[kind] = term if head_gains[kind] is None else head_gains[kind] + term
        back = norm_back(raw, scale, gains[4 + kind : 5 + kind, :head], grad)
        grad_qkv[:, index * head : (index + 1) * head] = back.astype(BF)
    grad_qkv[:, (heads + 1) * head :] = grad_own[:, head:].astype(BF)
    wait_all(copies)
    grad_normed = mm_nt(grad_qkv[...], weight[...])
    residual = x[...].astype(F32)
    scale = inverse_rms(residual)
    first_gain = gain_back(residual, scale, grad_normed)
    total = grad_mixed[...] + norm_back(residual, scale, gains[0:1, :], grad_normed)
    grad_in[...] = total.astype(BF)
    gain_held[...] = jnp.zeros_like(gain_held)
    part = head // 4
    four = (first_gain, rows_attn[1:2, :], rows_ffn[2:3, :], rows_ffn[3:4, :])
    for place in range(4):
        for row, values in enumerate(four):
            gain_held[place, row : row + 1, :shard] = values[
                :, place * shard : (place + 1) * shard
            ]
        for row, values in enumerate(head_gains):
            gain_held[place, 4 + row : 5 + row, :part] = values[
                :, place * part : (place + 1) * part
            ]
    wide = grad_qkv.shape[1]
    att_at = wide + model
    block_at = att_at + head
    for flip, pack in enumerate(packs):
        other = info[0] ^ flip
        pack[tokens:, :] = jnp.zeros_like(pack[tokens:, :])
        pack[tokens:, : gain_held.shape[2]] = gain_held[other].astype(BF)
        pack[:tokens, :wide] = grad_qkv[...]
        pack[:tokens, wide:att_at] = grad_branch[...]
        pack[:tokens, att_at:block_at] = attended[:, slot(other, head)]
        pack[:tokens, block_at:] = jnp.zeros_like(pack[:tokens, block_at:])
        pack[:tokens, block_at : block_at + shard] = blocks[other]


def over(packs, tokens, left, right, left_width, right_width):
    total = None
    for pack in packs:
        term = mm_tn(
            pack[:tokens, left : left + left_width], pack[:tokens, right : right + right_width]
        )
        total = term if total is None else total + term
    return total.astype(BF)


def ffn_weights_kernel(shard, model, info, *refs):
    packs, first, second = refs[:4], refs[4], refs[5]
    tokens = packs[0].shape[0]
    wide = first.shape[1]
    quarter = second.shape[1] // 4
    act_at = wide + model
    for start in range(0, wide, 1024):
        first[:, start : start + 1024] = over(
            packs, tokens, act_at + quarter, start, shard, 1024
        )
    for place in range(4):
        second[:, place * quarter : (place + 1) * quarter] = over(
            packs, tokens, wide + place * shard, act_at, shard, quarter
        )


def weights_kernel(shard, model, info, *refs):
    packs, gate_up, down, first, second = refs[:4], refs[4], refs[5], refs[6], refs[7]
    tokens = packs[0].shape[0] - GAIN_ROWS
    head = model // 5 * 2
    wide = packs[0].shape[1] - model - 2 * head
    hidden = gate_up.shape[1]
    first[:, :hidden] = gate_up[...]
    first[:, hidden:] = jnp.zeros_like(first[:, hidden:])
    gains = sum(pack[tokens:, :head].astype(F32) for pack in packs)
    first[:GAIN_ROWS, hidden : hidden + head] = gains.astype(BF)
    att_at = wide + model
    second[:, :wide] = over(packs, tokens, att_at + head, 0, shard, wide)
    for place in range(4):
        start = wide + place * head
        second[:, start : start + head] = over(
            packs, tokens, wide + place * shard, att_at, shard, head
        )
    second[:, wide + 4 * head :] = down[...]


class Links:
    def __init__(self, sizes):
        self.sizes = sizes

    def index(self, section, seq, fsdp):
        return (section * self.sizes["seq"] + seq) * self.sizes["fsdp"] + fsdp

    def send(self, array, section, place):
        pairs = []
        for z in range(self.sizes["seq"]):
            for f in range(self.sizes["fsdp"]):
                to_section, to_z, to_f = place(z, f)
                if 0 <= to_z < self.sizes["seq"]:
                    pairs.append((self.index(section, z, f), self.index(to_section, to_z, to_f)))
        return lax.ppermute(array, AXES, pairs)

    def along(self, array, section, by):
        return self.send(array, section, lambda z, f: (section, z + by, f))

    def across(self, array, section, flip):
        return self.send(array, section, lambda z, f: (section, z, f ^ flip))

    def cross(self, array, section):
        return self.send(array, section, lambda z, f: (1 - section, z, f))

    def both(self, array, flip):
        pairs = []
        for section in range(2):
            for z in range(self.sizes["seq"]):
                for f in range(self.sizes["fsdp"]):
                    pairs.append((self.index(section, z, f), self.index(section, z, f ^ flip)))
        return lax.ppermute(array, AXES, pairs)

    def swap(self, array):
        pairs = []
        for section in range(2):
            for z in range(self.sizes["seq"]):
                for f in range(self.sizes["fsdp"]):
                    pairs.append((self.index(section, z, f), self.index(1 - section, z, f)))
        return lax.ppermute(array, AXES, pairs)


def body(sizes, hidden_in, cotangent, positions, attn_gain, w_query, w_key, w_value, query_gain,
         key_gain, w_output, post_attn_gain, ffn_gain, w_gate, w_up, w_down, post_ffn_gain):
    section = lax.axis_index("section")
    seq = lax.axis_index("seq")
    fsdp = lax.axis_index("fsdp")
    is_first = section == 0
    micro, rows, model = hidden_in.shape
    tokens = micro * rows
    shard = w_query.shape[1]
    shards = sizes["fsdp"]
    heads_width, head = w_query.shape[2], w_key.shape[2]
    wide = heads_width + 2 * head
    hidden = w_gate.shape[2]
    quarter = hidden // shards
    assert shards == 4 and 2 * shards * rows == WIN and heads_width == shards * head
    links = Links(sizes)
    tie = lax.optimization_barrier
    info = jnp.stack([fsdp, seq, section]).astype(jnp.int32)

    folded = call(
        fold_kernel, info,
        [w_gate, w_up, w_query, w_key, w_value, w_output, w_down, attn_gain, post_attn_gain,
         ffn_gain, post_ffn_gain, query_gain, key_gain],
        [shape((shard, 2 * hidden), BF), shape((shard, heads_width + hidden + wide + 128), BF)],
        [pltpu.VMEM((head, model), BF), pltpu.VMEM((quarter, model), BF)]
        + [pltpu.VMEM((1, shard), BF)] * 4 + [pltpu.VMEM((1, query_gain.shape[1]), BF)] * 2
        + [pltpu.SemaphoreType.DMA((13,))],
        far=True,
    )

    def gather(arrays):
        first, second = arrays
        second_one, first_two = links.both(second, 1), links.both(first, 2)
        first_one, second_two = links.both(first, 1), links.both(second, 2)
        second_three, first_three = links.both(second_one, 2), links.both(first_two, 1)
        return [first, first_one, first_two, first_three,
                second, second_one, second_two, second_three]

    def gain_table(pieces, target):
        return call(
            gains_kernel, info, [], [shape((8, model), F32)],
            [pltpu.VMEM((shards, GAIN_ROWS, 128), BF), pltpu.SemaphoreType.DMA((shards,))],
            pieces=pieces, section=target,
        )[0]

    qkv_scratch = [pltpu.VMEM((model, wide), BF), pltpu.SemaphoreType.DMA((shards,))]
    out_scratch = [pltpu.VMEM((model, heads_width), BF), pltpu.SemaphoreType.DMA((16,))]
    ffn_scratch = [pltpu.VMEM((model, 2 * hidden), BF), pltpu.VMEM((model, hidden), BF),
                   pltpu.SemaphoreType.DMA((shards,)), pltpu.SemaphoreType.DMA((16,))]

    half = head // 2
    limit = jnp.minimum(positions.reshape(tokens, 1), WIN - 1)
    starts = [(seq - back) * shards + fsdp for back in range(3)]
    for flip in range(1, shards):
        other = fsdp ^ flip
        starts.append((seq - 1) * shards + other)
        starts.append(jnp.where(other < fsdp, seq, seq - 2) * shards + other)
    starts = jnp.stack(starts).astype(jnp.int32) * rows
    key_place = (starts[:, None] + jnp.arange(rows, dtype=jnp.int32)[None, :]).reshape(1, -1)
    info = jnp.concatenate((info, starts[:1], starts))
    span = key_place.shape[1]
    frequency = ROPE_BASE ** (-2.0 * jnp.arange(half, dtype=F32) / head)
    angles = key_place.reshape(span, 1).astype(F32) * frequency[None, :]
    wide_cos, wide_sin = jnp.cos(angles), jnp.sin(angles)
    cosine, sine = (jnp.tile(table[:rows], (micro, 1)) for table in (wide_cos, wide_sin))

    def fetch(own, target, waiting=None):
        one, two = links.along(own, target, 1), links.along(own, target, 2)
        sent = call(
            select_kernel, info, [own, one, two], [shape((2,) + own.shape, BF)] * (shards - 1),
            section=target,
        )
        if waiting is not None:
            sent, waiting = tie((list(sent), waiting))
        got = [links.across(array, target, 1 + i) for i, array in enumerate(sent)]
        return [own, one, two] + got, waiting

    def forward(x, pieces, target, x_window=None):
        sizes_of = [shape((shards, tokens, shard), BF), shape((tokens, wide), F32),
                    shape((tokens, heads_width), BF)]
        whole = shape((micro, span, 2 * head), BF)
        attend_outs = [
            shape((micro, shards * rows, span), F32), shape((tokens, heads_width), BF),
            shape((tokens, model), F32), shape((tokens, model), F32),
            shape((shards, tokens, shard), BF), shape((tokens, model), BF),
        ]
        if x_window is not None:
            blocks, qkv, query, window = call(
                functools.partial(project_window_kernel, micro), info,
                x_window + [gains, cosine, sine, wide_cos, wide_sin],
                sizes_of + [whole], qkv_scratch, section=target, pieces=pieces,
            )
            parts = [window]
        else:
            blocks, qkv, query, own = call(
                project_kernel, info, [x, gains, cosine, sine],
                sizes_of + [shape((tokens, 2 * head), BF)], qkv_scratch, section=target,
                pieces=pieces,
            )
            parts, _ = fetch(own, target)
            attend_outs = [whole] + attend_outs
        outs = call(
            functools.partial(attend_kernel, micro), info,
            [query, x, gains, limit] + parts, attend_outs, out_scratch, section=target,
            pieces=pieces,
        )
        if x_window is None:
            window, *outs = outs
        probs, attended, branch, mixed, ffn_blocks, ffn_in = outs
        gate_up, activated, down, result = call(
            ffn_kernel, info, [ffn_in, mixed, gains],
            [shape((tokens, 2 * hidden), F32), shape((tokens, hidden), BF),
             shape((tokens, model), F32), shape((tokens, model), BF)], ffn_scratch,
            section=target, pieces=pieces,
        )
        saved = dict(
            x=x, gains=gains, pieces=pieces, blocks=blocks, qkv=qkv, query=query, window=window, probs=probs,
            attended=attended, branch=branch, mixed=mixed, ffn_blocks=ffn_blocks, gate_up=gate_up,
            activated=activated, down=down,
        )
        return result, saved

    def back_ffn(upstream, s, target):
        outs = call(
            ffn_back_kernel, info,
            [upstream, s["mixed"], s["down"], s["gate_up"], s["activated"], s["ffn_blocks"],
             s["gains"]],
            [shape((tokens, 2 * hidden + model + quarter + 256), BF)] * shards
            + [shape((tokens, model), F32), shape((8, model), F32)],
            [pltpu.VMEM((tokens, 2 * hidden), BF)] + ffn_scratch,
            section=target, pieces=s["pieces"],
        )
        return outs[:shards], outs[shards], outs[shards + 1]

    def back_attend(grad_mixed, s, target):
        pair = [shape((tokens, 2 * head), F32)] * 3
        outs = call(
            functools.partial(attend_back_kernel, micro), info,
            [grad_mixed, s["branch"], s["window"], s["probs"], s["query"], s["gains"]],
            [shape((tokens, model), BF), shape((tokens, heads_width), F32)] + pair
            + [shape((2, tokens, 2 * head), BF)] * (shards - 1) + [shape((8, model), F32)],
            [pltpu.VMEM((tokens, heads_width), BF)] + out_scratch,
            section=target, pieces=s["pieces"],
        )
        return outs[0], outs[1], outs[2:5], outs[5:8], outs[8]

    def back_window(kept, gives, target, waiting):
        got = [links.across(array, target, 1 + i) for i, array in enumerate(gives)]
        ffn_packs, other = waiting
        if other is not None:
            got, other, ffn_packs = tie((got, other, ffn_packs))
            other = jnp.where(is_first, other[0], other[1])
            kept, other = tie((kept, other))
        own, one, two = call(
            combine_kernel, info, list(kept) + got,
            [shape((tokens, 2 * head), F32)] + [shape((tokens, 2 * head), BF)] * 2,
            section=target,
        )
        one, two = links.along(one, target, -1), links.along(two, target, -2)
        if other is None:
            one, ffn_packs = tie((one, ffn_packs))
        return (own, one, two), ffn_packs, other

    def back_project(window_grads, grad_query, grad_mixed, grad_branch, rows_ffn, rows_attn, s,
                     target):
        outs = call(
            project_back_kernel, info,
            list(window_grads) + [grad_query, s["qkv"], cosine, sine, s["x"], grad_mixed,
            grad_branch, s["attended"], s["blocks"], s["gains"], rows_ffn, rows_attn],
            [shape((tokens + GAIN_ROWS, wide + model + head + 256), BF)] * shards
            + [shape((tokens, model), BF)],
            [pltpu.VMEM((tokens, wide), BF), pltpu.VMEM((shards, GAIN_ROWS, 256), F32)]
            + qkv_scratch,
            section=target, pieces=s["pieces"],
        )
        return outs[:shards], outs[shards]

    def exchange(packs, target):
        return [packs[0]] + [links.across(packs[i], target, i) for i in range(1, shards)]

    total_width = 2 * hidden + 512

    def ffn_weights(packs, target):
        return call(
            functools.partial(ffn_weights_kernel, shard, model), info, list(packs),
            [shape((shard, 2 * hidden), BF), shape((shard, hidden), BF)],
            section=target,
        )

    def attn_weights(packs, ffn, target):
        return call(
            functools.partial(weights_kernel, shard, model), info, list(packs) + list(ffn),
            [shape((shard, total_width), BF)] * 2,
            section=target,
        )

    def backward(upstream, s, target, other=None):
        ffn_packs, grad_mixed, rows_ffn = back_ffn(upstream, s, target)
        grad_branch, grad_query, kept, gives, rows_attn = back_attend(grad_mixed, s, target)
        window_grads, ffn_packs, other = back_window(kept, gives, target, (ffn_packs, other))
        ffn_packs = exchange(ffn_packs, target)
        attn_packs, grad_in = back_project(
            window_grads, grad_query, grad_mixed, grad_branch, rows_ffn, rows_attn, s, target
        )
        return ffn_weights(ffn_packs, target), attn_packs, grad_in, other

    x_first = hidden_in.reshape(tokens, model)
    pieces = gather(folded)
    x_window, pieces[5] = fetch(x_first, 0, pieces[5])
    gains = gain_table(pieces, None)
    result_a, saved_a = forward(x_first, pieces, 0, x_window)
    middle = links.cross(result_a, 0)
    result_b, saved_b = forward(middle, pieces, 1)

    ffn, attn_packs, grad_b, _ = backward(cotangent.reshape(tokens, model), saved_b, 1)
    upstream = links.cross(grad_b, 1)
    upstream, attn_packs = tie((upstream, attn_packs))
    b_first, b_second = attn_weights(exchange(attn_packs, 1), ffn, 1)
    upstream, b_first, b_second = tie((upstream, b_first, b_second))
    halves_b = (links.cross(b_first, 1), b_second)

    ffn, attn_packs, grad_a, half_b = backward(upstream, saved_a, 0, halves_b)
    part_b = lax.psum(half_b, "seq")
    attn_packs, part_b = tie((exchange(attn_packs, 0), part_b))
    a_first, a_second = attn_weights(attn_packs, ffn, 0)
    part_a = lax.psum(jnp.where(is_first, a_first, links.cross(a_second, 0)), "seq")
    theirs = links.swap(jnp.where(is_first, part_b, part_a))

    part = head // shards
    grads = call(
        finish_kernel, info, [part_a, part_b, theirs],
        [shape((1, shard, heads_width), F32), shape((1, shard, head), F32),
         shape((1, shard, head), F32), shape((1, head, model), F32),
         shape((1, shard, hidden), F32), shape((1, shard, hidden), F32),
         shape((1, quarter, model), F32)]
        + [shape((1, shard), F32)] * 4 + [shape((1, part), F32)] * 2,
    )
    g_query, g_key, g_value, g_out, g_gate, g_up, g_down = grads[:7]
    g_attn, g_post_attn, g_ffn, g_post_ffn, g_query_gain, g_key_gain = grads[7:]
    section_outputs = jnp.where(is_first, result_a, result_b).reshape(1, micro, rows, model)
    input_grads = jnp.where(is_first, grad_a, grad_b).reshape(1, micro, rows, model)
    return (
        section_outputs, input_grads, g_attn, g_query, g_key, g_value, g_query_gain, g_key_gain,
        g_out, g_post_attn, g_ffn, g_gate, g_up, g_down, g_post_ffn,
    )


def solution(mesh):
    rows = P(None, ("seq", "fsdp"), None)
    vector, matrix = P("section", "fsdp"), P("section", "fsdp", None)
    weights = (vector, matrix, matrix, matrix, vector, vector, matrix, vector, vector, matrix,
               matrix, matrix, vector)
    out_rows = P("section", None, ("seq", "fsdp"), None)
    return jax.shard_map(
        functools.partial(body, dict(mesh.shape)),
        mesh=mesh,
        in_specs=(rows, rows, P(None, ("seq", "fsdp"))) + weights,
        out_specs=(out_rows, out_rows) + weights,
        check_vma=False,
    )
```

```python
import functools

import jax
import jax.numpy as jnp
from jax import lax
from jax.experimental import pallas as pl
from jax.experimental.pallas import tpu as pltpu
from jax.sharding import PartitionSpec as P

WIN = 512
EPSILON = 1e-06
ROPE_BASE = 10000.0
NEG_LARGE = -1e30
AXES = ("section", "seq", "fsdp")
BF = jnp.bfloat16
F32 = jnp.float32
GAIN_ROWS = 16
INTERPRET = False


def mm(left, right):
    return lax.dot_general(left, right, (((1,), (0,)), ((), ())), preferred_element_type=F32)


def mm_nt(left, right):
    return lax.dot_general(left, right, (((1,), (1,)), ((), ())), preferred_element_type=F32)


def mm_tn(left, right):
    return lax.dot_general(left, right, (((0,), (0,)), ((), ())), preferred_element_type=F32)


def inverse_rms(values):
    return lax.rsqrt(jnp.mean(values * values, axis=-1, keepdims=True) + EPSILON)


def norm_back(values, scale, gain, grad):
    weighted = grad * gain
    inner = jnp.mean(values * weighted, axis=-1, keepdims=True)
    return scale * weighted - values * (scale * scale * scale * inner)


def gain_back(values, scale, grad):
    return jnp.sum(values * scale * grad, axis=0, keepdims=True)


def call(kernel, info, arrays, outs, scratch=(), section=None, pieces=(), far=False):
    smem = pl.BlockSpec(memory_space=pltpu.SMEM)
    vmem = pl.BlockSpec(memory_space=pltpu.VMEM)
    hbm = pl.BlockSpec(memory_space=pltpu.HBM)
    lead = len(pieces)

    def entry(info, *refs):
        def run():
            kernel(info, *((refs[:lead],) if lead else ()), *refs[lead:])

        if section is None:
            run()
        else:
            pl.when(info[2] == section)(run)

    return pl.pallas_call(
        entry,
        out_shape=outs,
        in_specs=[smem] + [hbm] * lead + [hbm if far else vmem] * len(arrays),
        out_specs=[vmem] * len(outs),
        scratch_shapes=list(scratch),
        compiler_params=pltpu.CompilerParams(vmem_limit_bytes=(58 if far else 32) * 1024 * 1024),
        cost_estimate=pl.CostEstimate(flops=1, bytes_accessed=1, transcendentals=0),
        interpret=INTERPRET,
    )(info, *pieces, *arrays)


def shape(dims, kind):
    return jax.ShapeDtypeStruct(tuple(dims), kind)


def slot(index, width):
    return pl.ds(pl.multiple_of(index * width, width), width)


def layout(model):
    unit = model // 5
    return unit * 32, unit * 40, unit * 56, unit * 68


def sources(pieces, start):
    split = pieces[0].shape[1]
    if start < split:
        return [(piece, start) for piece in pieces[:4]]
    return [(piece, start - split) for piece in pieces[4:]]


def gains_kernel(info, gathered, out, held, sems):
    count, rows, width = held.shape
    shard = out.shape[1] // count
    part = shard * 2 // 5
    copies = []
    for flip, (piece, start) in enumerate(sources(gathered, layout(out.shape[1])[3])):
        source = piece.at[pl.ds(0, rows), pl.ds(start, width)]
        copies.append(pltpu.make_async_copy(source, held.at[info[0] ^ flip], sems.at[flip]))
    for copy in copies:
        copy.start()
    for copy in copies:
        copy.wait()
    out[...] = jnp.zeros_like(out)
    for place in range(count):
        values = held[place].astype(F32)
        start = place * shard
        for row in range(4):
            out[row : row + 1, start : start + width] = values[2 * row : 2 * row + 1]
            out[row : row + 1, start + width : start + shard] = values[
                2 * row + 1 : 2 * row + 2, : shard - width
            ]
        for row in range(2):
            out[4 + row : 5 + row, place * part : (place + 1) * part] = values[
                8 + row : 9 + row, :part
            ]


def fold_kernel(info, gate, up, query, key, value, out_w, down_w, attn, post_attn, ffn, post_ffn,
                query_gain, key_gain, first, second, out_held, down_held, *rest):
    shard = gate.shape[1]
    vectors, sems = rest[:-1], rest[-1]
    copies = []

    def load(source, target):
        copy = pltpu.make_async_copy(source, target, sems.at[len(copies)])
        copy.start()
        copies.append(copy)

    load(out_w.at[0], out_held)
    load(down_w.at[0], down_held)
    for source, held in zip((attn, post_attn, ffn, post_ffn, query_gain, key_gain), vectors):
        load(source, held)
    hidden = gate.shape[2]
    load(gate.at[0], first.at[:, pl.ds(0, hidden)])
    load(up.at[0], first.at[:, pl.ds(hidden, hidden)])
    start = 4 * (out_held.shape[0] + down_held.shape[0])
    for ref in (query, key, value):
        load(ref.at[0], second.at[:, pl.ds(start, ref.shape[2])])
        start += ref.shape[2]
    wait_all(copies)
    second[:, start:] = jnp.zeros_like(second[:, start:])
    width = 128
    for row, ref in enumerate(vectors[:4]):
        second[2 * row : 2 * row + 1, start : start + width] = ref[:, :width]
        second[2 * row + 1 : 2 * row + 2, start : start + shard - width] = ref[:, width:]
    for row, ref in enumerate(vectors[4:]):
        second[8 + row : 9 + row, start : start + ref.shape[1]] = ref[...]
    start = 0
    for held in (out_held, down_held):
        rows = held.shape[0]
        for place in range(4):
            block = held[:, place * shard : (place + 1) * shard].astype(F32)
            second[:, start : start + rows] = block.T.astype(BF)
            start += rows


def load_turned(info, gathered, held, sems, start):
    width, shard = held.shape[1] // 4, held.shape[0] // 4
    copies = []
    for flip, (piece, column) in enumerate(sources(gathered, start)):
        for row in range(4):
            copy = pltpu.make_async_copy(
                piece.at[:, pl.ds(column + row * width, width)],
                held.at[pl.ds(row * shard, shard), slot(info[0] ^ flip, width)],
                sems.at[4 * flip + row],
            )
            copy.start()
            copies.append(copy)
    return copies


def load_rows(info, gathered, held, sems, start):
    shard, width = held.shape[0] // 4, held.shape[1]
    copies = []
    for flip, (piece, column) in enumerate(sources(gathered, start)):
        copy = pltpu.make_async_copy(
            piece.at[:, pl.ds(column, width)], held.at[slot(info[0] ^ flip, shard)], sems.at[flip]
        )
        copy.start()
        copies.append(copy)
    return copies


def wait_all(copies):
    for copy in copies:
        copy.wait()


def rope_store(target, rows, start, normal, cos, sin):
    half = cos.shape[1]
    one, two = normal[:, :half], normal[:, half:]
    target[rows, start : start + half] = (one * cos - two * sin).astype(BF)
    target[rows, start + half : start + 2 * half] = (two * cos + one * sin).astype(BF)


def cut(blocks, normed):
    shard = blocks.shape[2]
    for place in range(blocks.shape[0]):
        blocks[place] = normed[:, place * shard : (place + 1) * shard].astype(BF)


def project_window_kernel(micro, info, gathered, x, one, two, *refs):
    got, (gains, cosine, sine, wide_cos, wide_sin) = refs[:3], refs[3:8]
    blocks, qkv, query, window, weight, sems = refs[8:]
    copies = load_rows(info, gathered, weight, sems, layout(x.shape[1])[2])
    rows = x.shape[0] // micro
    head = window.shape[2] // 2
    heads_width = query.shape[1]

    def normed_of(values):
        return values * inverse_rms(values) * gains[0:1, :]

    normed = normed_of(x[...].astype(F32))
    cut(blocks, normed)
    normed = normed.astype(BF)
    wait_all(copies)
    total = mm(normed, weight[:, :heads_width])
    qkv[:, :heads_width] = total
    for start in range(0, heads_width, head):
        raw = total[:, start : start + head]
        normal = raw * inverse_rms(raw) * gains[4:5, :head]
        rope_store(query, slice(None), start, normal, cosine[...], sine[...])
    for m in range(micro):
        span = slice(m * rows, (m + 1) * rows)
        parts = [x[span], one[span], two[span]]
        for ref in got:
            parts += [ref[0, span], ref[1, span]]
        values = jnp.concatenate(parts, axis=0).astype(F32)
        total = mm(normed_of(values).astype(BF), weight[:, heads_width:])
        qkv[span, heads_width:] = total[:rows]
        raw = total[:, :head]
        normal = raw * inverse_rms(raw) * gains[5:6, :head]
        rope_store(window.at[m], slice(None), 0, normal, wide_cos[...], wide_sin[...])
        window[m, :, head:] = total[:, head:].astype(BF)


def finish_kernel(info, part_a, part_b, theirs, *outs):
    query, key, value, out, gate, up, down = outs[:7]
    vectors = outs[7:]
    shard, hidden = gate.shape[1], gate.shape[2]

    def emit(first, second):
        gate[0] = first[:, :hidden].astype(F32)
        up[0] = first[:, hidden : 2 * hidden].astype(F32)
        for row, ref in enumerate(vectors):
            ref[...] = first[:GAIN_ROWS, 2 * hidden : 2 * hidden + ref.shape[1]].astype(F32)[
                row : row + 1
            ]
        start = 0
        for ref in (query, key, value):
            ref[0] = second[:, start : start + ref.shape[2]].astype(F32)
            start += ref.shape[2]
        for ref in (out, down):
            rows = ref.shape[1]
            for place in range(4):
                block = second[:, start : start + rows].astype(F32)
                ref[0, :, place * shard : (place + 1) * shard] = block.T
                start += rows

    @pl.when(info[2] == 0)
    def _():
        emit(part_a, theirs)

    @pl.when(info[2] == 1)
    def _():
        emit(theirs, part_b)


def project_kernel(info, gathered, x, gains, cosine, sine, blocks, qkv, query, own, weight, sems):
    copies = load_rows(info, gathered, weight, sems, layout(x.shape[1])[2])
    head = 2 * cosine.shape[1]
    residual = x[...].astype(F32)
    normed = residual * inverse_rms(residual) * gains[0:1, :]
    cut(blocks, normed)
    wait_all(copies)
    total = mm(normed.astype(BF), weight[...])
    qkv[...] = total
    heads = query.shape[1] // head
    for index in range(heads + 1):
        raw = total[:, index * head : (index + 1) * head]
        row = 4 if index < heads else 5
        normal = raw * inverse_rms(raw) * gains[row : row + 1, :head]
        target, start = (query, index * head) if index < heads else (own, 0)
        rope_store(target, slice(None), start, normal, cosine[...], sine[...])
    own[:, head:] = total[:, (heads + 1) * head :].astype(BF)


def select_kernel(info, own, one, two, *outs):
    for index, out in enumerate(outs):
        lower = (info[0] < (info[0] ^ (index + 1))).astype(F32)
        out[0] = one[...]
        mixed = own[...].astype(F32) * lower + two[...].astype(F32) * (1.0 - lower)
        out[1] = mixed.astype(BF)


def window_kernel(micro, info, own, one, two, *refs):
    got, window = refs[:3], refs[3]
    rows = own.shape[0] // micro
    for m in range(micro):
        span = slice(m * rows, (m + 1) * rows)
        parts = [own[span], one[span], two[span]]
        for ref in got:
            parts += [ref[0, span], ref[1, span]]
        for index, part in enumerate(parts):
            window[m, index * rows : (index + 1) * rows] = part


def attend_kernel(micro, info, gathered, query, x, gains, limit, *refs):
    out_w, sems = refs[-2:]
    model = x.shape[1]
    shard = model // 4
    copies = load_turned(info, gathered, out_w, sems, layout(model)[0])
    if len(refs) == 1 + 6 + 2:
        window = refs[0]
        outs = refs[1:-2]
    else:
        window = refs[6]
        outs = refs[7:-2]
        window_kernel(micro, info, *refs[:6], window)
    probs, attended, branch, mixed, blocks, ffn_in = outs
    rows = query.shape[0] // micro
    head = window.shape[2] // 2
    heads = query.shape[1] // head
    count = window.shape[1]
    column = lax.broadcasted_iota(jnp.int32, (rows, count), 1)
    distance = lax.broadcasted_iota(jnp.int32, (rows, count), 0) + info[3]
    for index in range(count // rows):
        inside = (column >= index * rows) & (column < (index + 1) * rows)
        distance = distance - jnp.where(inside, column - index * rows + info[4 + index], 0)
    for m in range(micro):
        span = slice(m * rows, (m + 1) * rows)
        allowed = (distance >= 0) & (distance <= limit[span])
        bias = jnp.where(allowed, 0.0, NEG_LARGE)
        bias = jnp.concatenate([bias] * heads, axis=0)
        stacked = jnp.concatenate(
            [query[span, h * head : (h + 1) * head] for h in range(heads)], axis=0
        )
        scores = mm_nt(stacked, window[m, :, :head]) * head ** (-0.5) + bias
        exponent = jnp.exp(scores - jnp.max(scores, axis=-1, keepdims=True))
        chance = exponent / jnp.sum(exponent, axis=-1, keepdims=True)
        probs[m] = chance
        result = mm(chance.astype(BF), window[m, :, head:]).astype(BF)
        for h in range(heads):
            attended[span, h * head : (h + 1) * head] = result[h * rows : (h + 1) * rows]
    for copy in copies:
        copy.wait()
    total = mm_nt(attended[...], out_w[...])
    branch[...] = total
    value = x[...].astype(F32) + total * inverse_rms(total) * gains[1:2, :]
    mixed[...] = value
    normed = value * inverse_rms(value) * gains[2:3, :]
    ffn_in[...] = normed.astype(BF)
    for place in range(4):
        blocks[place] = normed[:, place * shard : (place + 1) * shard].astype(BF)


def gelu_parts(gate):
    c = 0.7978845608028654
    inner = jnp.tanh(c * (gate + 0.044715 * gate * gate * gate))
    value = 0.5 * gate * (1.0 + inner)
    slope = 0.5 * (1.0 + inner) + 0.5 * gate * (1.0 - inner * inner) * c * (
        1.0 + 3 * 0.044715 * gate * gate
    )
    return value, slope


def ffn_kernel(info, gathered, ffn_in, mixed, gains, gate_up, activated, down, result,
               gate_up_w, down_w, column_sems, sems):
    hidden = activated.shape[1]
    width = 512
    columns = load_rows(info, gathered, gate_up_w, column_sems, 0)
    copies = load_turned(info, gathered, down_w, sems, layout(mixed.shape[1])[1])
    wait_all(columns)
    for start in range(0, hidden, width):
        both = []
        for base in (start, hidden + start):
            total = mm(ffn_in[...], gate_up_w[:, base : base + width])
            gate_up[:, base : base + width] = total
            both.append(total)
        value, _ = gelu_parts(both[0])
        activated[:, start : start + width] = (value * both[1]).astype(BF)
    for copy in copies:
        copy.wait()
    total = mm_nt(activated[...], down_w[...])
    down[...] = total
    result[...] = (mixed[...] + total * inverse_rms(total) * gains[3:4, :]).astype(BF)


def ffn_back_kernel(info, gathered, upstream, mixed, down, gate_up, activated, blocks, gains,
                    *refs):
    packs, grad_mixed, gain_rows = refs[:4], refs[4], refs[5]
    grad_gate_up, gate_up_w, down_w, column_sems, sems = refs[6:]
    hidden = activated.shape[1]
    model = mixed.shape[1]
    shard = blocks.shape[2]
    copies = load_turned(info, gathered, down_w, sems, layout(mixed.shape[1])[1])
    columns = load_rows(info, gathered, gate_up_w, column_sems, 0)
    top = upstream[...].astype(F32)
    raw = down[...]
    scale = inverse_rms(raw)
    grad_down = norm_back(raw, scale, gains[3:4, :], top).astype(BF)
    gain_rows[...] = jnp.zeros_like(gain_rows)
    gain_rows[3:4, :] = gain_back(raw, scale, top)
    act_at = 2 * hidden + model
    block_at = act_at + hidden // 4
    for flip, pack in enumerate(packs):
        pack[:, 2 * hidden : act_at] = grad_down
        pack[:, act_at:block_at] = activated[:, slot(info[0] ^ flip, hidden // 4)]
        pack[:, block_at:] = jnp.zeros_like(pack[:, block_at:])
        pack[:, block_at : block_at + shard] = blocks[info[0] ^ flip]
    for copy in copies:
        copy.wait()
    width = 512
    for start in range(0, hidden, width):
        value, slope = gelu_parts(gate_up[:, start : start + width])
        up = gate_up[:, hidden + start : hidden + start + width]
        grad = mm(grad_down, down_w[:, start : start + width])
        grad_gate_up[:, start : start + width] = (grad * up * slope).astype(BF)
        grad_gate_up[:, hidden + start : hidden + start + width] = (grad * value).astype(BF)
    for pack in packs:
        pack[:, : 2 * hidden] = grad_gate_up[...]
    for copy in columns:
        copy.wait()
    grad_in = mm_nt(grad_gate_up[...], gate_up_w[...])
    raw = mixed[...]
    scale = inverse_rms(raw)
    gain_rows[2:3, :] = gain_back(raw, scale, grad_in)
    grad_mixed[...] = top + norm_back(raw, scale, gains[2:3, :], grad_in)


def attend_back_kernel(micro, info, gathered, grad_mixed, branch, window, probs, query, gains,
                       *refs):
    grad_branch, grad_query, own, one, two = refs[:5]
    gives, gain_rows, grad_attended, out_w, sems = refs[5:8], refs[8], refs[9], refs[10], refs[11]
    model = branch.shape[1]
    copies = load_turned(info, gathered, out_w, sems, layout(model)[0])
    rows = own.shape[0] // micro
    head = own.shape[1] // 2
    heads = query.shape[1] // head
    factor = head ** (-0.5)
    raw = branch[...]
    scale = inverse_rms(raw)
    grad = grad_mixed[...]
    gain_rows[...] = jnp.zeros_like(gain_rows)
    gain_rows[1:2, :] = gain_back(raw, scale, grad)
    low = norm_back(raw, scale, gains[1:2, :], grad).astype(BF)
    grad_branch[...] = low
    for copy in copies:
        copy.wait()
    grad_attended[...] = mm(low, out_w[...]).astype(BF)
    for m in range(micro):
        span = slice(m * rows, (m + 1) * rows)
        chance = probs[m]
        keys, values = window[m, :, :head], window[m, :, head:]
        stacked = jnp.concatenate(
            [query[span, h * head : (h + 1) * head] for h in range(heads)], axis=0
        )
        upstream = jnp.concatenate(
            [grad_attended[span, h * head : (h + 1) * head] for h in range(heads)], axis=0
        )
        grad_values = mm_tn(chance.astype(BF), upstream)
        grad_chance = mm_nt(upstream, values)
        inner = jnp.sum(chance * grad_chance, axis=-1, keepdims=True)
        grad_scores = (chance * (grad_chance - inner)).astype(BF)
        grad_stacked = mm(grad_scores, keys) * factor
        grad_keys = mm_tn(grad_scores, stacked) * factor
        for h in range(heads):
            grad_query[span, h * head : (h + 1) * head] = grad_stacked[h * rows : (h + 1) * rows]
        for index, target in enumerate((own, one, two)):
            part = slice(index * rows, (index + 1) * rows)
            target[span, :head] = grad_keys[part]
            target[span, head:] = grad_values[part]
        for index, target in enumerate(gives):
            for side in range(2):
                start = (3 + 2 * index + side) * rows
                target[side, span, :head] = grad_keys[start : start + rows].astype(BF)
                target[side, span, head:] = grad_values[start : start + rows].astype(BF)


def combine_kernel(info, own, one, two, first, second, third, own_out, one_out, two_out):
    total_own, total_one, total_two = own[...], one[...], two[...]
    for index, got in enumerate((first, second, third)):
        lower = (info[0] < (info[0] ^ (index + 1))).astype(F32)
        total_one = total_one + got[0].astype(F32)
        side = got[1].astype(F32)
        total_own = total_own + side * lower
        total_two = total_two + side * (1.0 - lower)
    own_out[...] = total_own
    one_out[...] = total_one.astype(BF)
    two_out[...] = total_two.astype(BF)


def project_back_kernel(info, gathered, own, back_one, back_two, grad_query, qkv, cosine, sine, x, grad_mixed,
                        grad_branch, attended, blocks, gains, rows_ffn, rows_attn, *refs):
    packs, grad_in = refs[:4], refs[4]
    grad_qkv, gain_held, weight, sems = refs[5:]
    copies = load_rows(info, gathered, weight, sems, layout(x.shape[1])[2])
    tokens, model = x.shape
    shard = blocks.shape[2]
    half = cosine.shape[1]
    head = 2 * half
    heads = grad_query.shape[1] // head
    cos, sin = cosine[...], sine[...]
    grad_own = own[...] + back_one[...].astype(F32) + back_two[...].astype(F32)
    head_gains = [None, None]
    for index in range(heads + 1):
        if index < heads:
            grad = grad_query[:, index * head : (index + 1) * head]
        else:
            grad = grad_own[:, :head]
        one, two = grad[:, :half], grad[:, half:]
        grad = jnp.concatenate((one * cos + two * sin, two * cos - one * sin), axis=1)
        raw = qkv[:, index * head : (index + 1) * head]
        scale = inverse_rms(raw)
        kind = 0 if index < heads else 1
        term = gain_back(raw, scale, grad)
        head_gains[kind] = term if head_gains[kind] is None else head_gains[kind] + term
        back = norm_back(raw, scale, gains[4 + kind : 5 + kind, :head], grad)
        grad_qkv[:, index * head : (index + 1) * head] = back.astype(BF)
    grad_qkv[:, (heads + 1) * head :] = grad_own[:, head:].astype(BF)
    wait_all(copies)
    grad_normed = mm_nt(grad_qkv[...], weight[...])
    residual = x[...].astype(F32)
    scale = inverse_rms(residual)
    first_gain = gain_back(residual, scale, grad_normed)
    total = grad_mixed[...] + norm_back(residual, scale, gains[0:1, :], grad_normed)
    grad_in[...] = total.astype(BF)
    gain_held[...] = jnp.zeros_like(gain_held)
    part = head // 4
    four = (first_gain, rows_attn[1:2, :], rows_ffn[2:3, :], rows_ffn[3:4, :])
    for place in range(4):
        for row, values in enumerate(four):
            gain_held[place, row : row + 1, :shard] = values[
                :, place * shard : (place + 1) * shard
            ]
        for row, values in enumerate(head_gains):
            gain_held[place, 4 + row : 5 + row, :part] = values[
                :, place * part : (place + 1) * part
            ]
    wide = grad_qkv.shape[1]
    att_at = wide + model
    block_at = att_at + head
    for flip, pack in enumerate(packs):
        other = info[0] ^ flip
        pack[tokens:, :] = jnp.zeros_like(pack[tokens:, :])
        pack[tokens:, : gain_held.shape[2]] = gain_held[other].astype(BF)
        pack[:tokens, :wide] = grad_qkv[...]
        pack[:tokens, wide:att_at] = grad_branch[...]
        pack[:tokens, att_at:block_at] = attended[:, slot(other, head)]
        pack[:tokens, block_at:] = jnp.zeros_like(pack[:tokens, block_at:])
        pack[:tokens, block_at : block_at + shard] = blocks[other]


def over(packs, tokens, left, right, left_width, right_width):
    total = None
    for pack in packs:
        term = mm_tn(
            pack[:tokens, left : left + left_width], pack[:tokens, right : right + right_width]
        )
        total = term if total is None else total + term
    return total.astype(BF)


def ffn_weights_kernel(shard, model, info, *refs):
    packs, first, second = refs[:4], refs[4], refs[5]
    tokens = packs[0].shape[0]
    wide = first.shape[1]
    quarter = second.shape[1] // 4
    act_at = wide + model
    for start in range(0, wide, 1024):
        first[:, start : start + 1024] = over(
            packs, tokens, act_at + quarter, start, shard, 1024
        )
    for place in range(4):
        second[:, place * quarter : (place + 1) * quarter] = over(
            packs, tokens, wide + place * shard, act_at, shard, quarter
        )


def weights_kernel(shard, model, info, *refs):
    packs, gate_up, down, first, second = refs[:4], refs[4], refs[5], refs[6], refs[7]
    tokens = packs[0].shape[0] - GAIN_ROWS
    head = model // 5 * 2
    wide = packs[0].shape[1] - model - 2 * head
    hidden = gate_up.shape[1]
    first[:, :hidden] = gate_up[...]
    first[:, hidden:] = jnp.zeros_like(first[:, hidden:])
    gains = sum(pack[tokens:, :head].astype(F32) for pack in packs)
    first[:GAIN_ROWS, hidden : hidden + head] = gains.astype(BF)
    att_at = wide + model
    second[:, :wide] = over(packs, tokens, att_at + head, 0, shard, wide)
    for place in range(4):
        start = wide + place * head
        second[:, start : start + head] = over(
            packs, tokens, wide + place * shard, att_at, shard, head
        )
    second[:, wide + 4 * head :] = down[...]


class Links:
    def __init__(self, sizes):
        self.sizes = sizes

    def index(self, section, seq, fsdp):
        return (section * self.sizes["seq"] + seq) * self.sizes["fsdp"] + fsdp

    def send(self, array, section, place):
        pairs = []
        for z in range(self.sizes["seq"]):
            for f in range(self.sizes["fsdp"]):
                to_section, to_z, to_f = place(z, f)
                if 0 <= to_z < self.sizes["seq"]:
                    pairs.append((self.index(section, z, f), self.index(to_section, to_z, to_f)))
        return lax.ppermute(array, AXES, pairs)

    def along(self, array, section, by):
        return self.send(array, section, lambda z, f: (section, z + by, f))

    def across(self, array, section, flip):
        return self.send(array, section, lambda z, f: (section, z, f ^ flip))

    def cross(self, array, section):
        return self.send(array, section, lambda z, f: (1 - section, z, f))

    def both(self, array, flip):
        pairs = []
        for section in range(2):
            for z in range(self.sizes["seq"]):
                for f in range(self.sizes["fsdp"]):
                    pairs.append((self.index(section, z, f), self.index(section, z, f ^ flip)))
        return lax.ppermute(array, AXES, pairs)

    def swap(self, array):
        pairs = []
        for section in range(2):
            for z in range(self.sizes["seq"]):
                for f in range(self.sizes["fsdp"]):
                    pairs.append((self.index(section, z, f), self.index(1 - section, z, f)))
        return lax.ppermute(array, AXES, pairs)


def body(sizes, hidden_in, cotangent, positions, attn_gain, w_query, w_key, w_value, query_gain,
         key_gain, w_output, post_attn_gain, ffn_gain, w_gate, w_up, w_down, post_ffn_gain):
    section = lax.axis_index("section")
    seq = lax.axis_index("seq")
    fsdp = lax.axis_index("fsdp")
    is_first = section == 0
    micro, rows, model = hidden_in.shape
    tokens = micro * rows
    shard = w_query.shape[1]
    shards = sizes["fsdp"]
    heads_width, head = w_query.shape[2], w_key.shape[2]
    wide = heads_width + 2 * head
    hidden = w_gate.shape[2]
    quarter = hidden // shards
    assert shards == 4 and 2 * shards * rows == WIN and heads_width == shards * head
    links = Links(sizes)
    tie = lax.optimization_barrier
    info = jnp.stack([fsdp, seq, section]).astype(jnp.int32)

    folded = call(
        fold_kernel, info,
        [w_gate, w_up, w_query, w_key, w_value, w_output, w_down, attn_gain, post_attn_gain,
         ffn_gain, post_ffn_gain, query_gain, key_gain],
        [shape((shard, 2 * hidden), BF), shape((shard, heads_width + hidden + wide + 128), BF)],
        [pltpu.VMEM((head, model), BF), pltpu.VMEM((quarter, model), BF)]
        + [pltpu.VMEM((1, shard), BF)] * 4 + [pltpu.VMEM((1, query_gain.shape[1]), BF)] * 2
        + [pltpu.SemaphoreType.DMA((13,))],
        far=True,
    )

    def gather(arrays):
        first, second = arrays
        second_one, first_two = links.both(second, 1), links.both(first, 2)
        first_one, second_two = links.both(first, 1), links.both(second, 2)
        second_three, first_three = links.both(second_one, 2), links.both(first_two, 1)
        return [first, first_one, first_two, first_three,
                second, second_one, second_two, second_three]

    def gain_table(pieces, target):
        return call(
            gains_kernel, info, [], [shape((8, model), F32)],
            [pltpu.VMEM((shards, GAIN_ROWS, 128), BF), pltpu.SemaphoreType.DMA((shards,))],
            pieces=pieces, section=target,
        )[0]

    qkv_scratch = [pltpu.VMEM((model, wide), BF), pltpu.SemaphoreType.DMA((shards,))]
    out_scratch = [pltpu.VMEM((model, heads_width), BF), pltpu.SemaphoreType.DMA((16,))]
    ffn_scratch = [pltpu.VMEM((model, 2 * hidden), BF), pltpu.VMEM((model, hidden), BF),
                   pltpu.SemaphoreType.DMA((shards,)), pltpu.SemaphoreType.DMA((16,))]

    half = head // 2
    limit = jnp.minimum(positions.reshape(tokens, 1), WIN - 1)
    starts = [(seq - back) * shards + fsdp for back in range(3)]
    for flip in range(1, shards):
        other = fsdp ^ flip
        starts.append((seq - 1) * shards + other)
        starts.append(jnp.where(other < fsdp, seq, seq - 2) * shards + other)
    starts = jnp.stack(starts).astype(jnp.int32) * rows
    key_place = (starts[:, None] + jnp.arange(rows, dtype=jnp.int32)[None, :]).reshape(1, -1)
    info = jnp.concatenate((info, starts[:1], starts))
    span = key_place.shape[1]
    frequency = ROPE_BASE ** (-2.0 * jnp.arange(half, dtype=F32) / head)
    angles = key_place.reshape(span, 1).astype(F32) * frequency[None, :]
    wide_cos, wide_sin = jnp.cos(angles), jnp.sin(angles)
    cosine, sine = (jnp.tile(table[:rows], (micro, 1)) for table in (wide_cos, wide_sin))

    def fetch(own, target, waiting=None):
        one, two = links.along(own, target, 1), links.along(own, target, 2)
        sent = call(
            select_kernel, info, [own, one, two], [shape((2,) + own.shape, BF)] * (shards - 1),
            section=target,
        )
        if waiting is not None:
            sent, waiting = tie((list(sent), waiting))
        got = [links.across(array, target, 1 + i) for i, array in enumerate(sent)]
        return [own, one, two] + got, waiting

    def forward(x, pieces, target, x_window=None):
        sizes_of = [shape((shards, tokens, shard), BF), shape((tokens, wide), F32),
                    shape((tokens, heads_width), BF)]
        whole = shape((micro, span, 2 * head), BF)
        attend_outs = [
            shape((micro, shards * rows, span), F32), shape((tokens, heads_width), BF),
            shape((tokens, model), F32), shape((tokens, model), F32),
            shape((shards, tokens, shard), BF), shape((tokens, model), BF),
        ]
        if x_window is not None:
            blocks, qkv, query, window = call(
                functools.partial(project_window_kernel, micro), info,
                x_window + [gains, cosine, sine, wide_cos, wide_sin],
                sizes_of + [whole], qkv_scratch, section=target, pieces=pieces,
            )
            parts = [window]
        else:
            blocks, qkv, query, own = call(
                project_kernel, info, [x, gains, cosine, sine],
                sizes_of + [shape((tokens, 2 * head), BF)], qkv_scratch, section=target,
                pieces=pieces,
            )
            parts, _ = fetch(own, target)
            attend_outs = [whole] + attend_outs
        outs = call(
            functools.partial(attend_kernel, micro), info,
            [query, x, gains, limit] + parts, attend_outs, out_scratch, section=target,
            pieces=pieces,
        )
        if x_window is None:
            window, *outs = outs
        probs, attended, branch, mixed, ffn_blocks, ffn_in = outs
        gate_up, activated, down, result = call(
            ffn_kernel, info, [ffn_in, mixed, gains],
            [shape((tokens, 2 * hidden), F32), shape((tokens, hidden), BF),
             shape((tokens, model), F32), shape((tokens, model), BF)], ffn_scratch,
            section=target, pieces=pieces,
        )
        saved = dict(
            x=x, gains=gains, pieces=pieces, blocks=blocks, qkv=qkv, query=query, window=window, probs=probs,
            attended=attended, branch=branch, mixed=mixed, ffn_blocks=ffn_blocks, gate_up=gate_up,
            activated=activated, down=down,
        )
        return result, saved

    def back_ffn(upstream, s, target):
        outs = call(
            ffn_back_kernel, info,
            [upstream, s["mixed"], s["down"], s["gate_up"], s["activated"], s["ffn_blocks"],
             s["gains"]],
            [shape((tokens, 2 * hidden + model + quarter + 256), BF)] * shards
            + [shape((tokens, model), F32), shape((8, model), F32)],
            [pltpu.VMEM((tokens, 2 * hidden), BF)] + ffn_scratch,
            section=target, pieces=s["pieces"],
        )
        return outs[:shards], outs[shards], outs[shards + 1]

    def back_attend(grad_mixed, s, target):
        pair = [shape((tokens, 2 * head), F32)] * 3
        outs = call(
            functools.partial(attend_back_kernel, micro), info,
            [grad_mixed, s["branch"], s["window"], s["probs"], s["query"], s["gains"]],
            [shape((tokens, model), BF), shape((tokens, heads_width), F32)] + pair
            + [shape((2, tokens, 2 * head), BF)] * (shards - 1) + [shape((8, model), F32)],
            [pltpu.VMEM((tokens, heads_width), BF)] + out_scratch,
            section=target, pieces=s["pieces"],
        )
        return outs[0], outs[1], outs[2:5], outs[5:8], outs[8]

    def back_window(kept, gives, target, waiting):
        got = [links.across(array, target, 1 + i) for i, array in enumerate(gives)]
        ffn_packs, other = waiting
        if other is not None:
            got, other = tie((got, other))
            other = jnp.where(is_first, other[0], other[1])
            kept, other, ffn_packs = tie((kept, other, ffn_packs))
        own, one, two = call(
            combine_kernel, info, list(kept) + got,
            [shape((tokens, 2 * head), F32)] + [shape((tokens, 2 * head), BF)] * 2,
            section=target,
        )
        one, two = links.along(one, target, -1), links.along(two, target, -2)
        if other is None:
            one, ffn_packs = tie((one, ffn_packs))
        return (own, one, two), ffn_packs, other

    def back_project(window_grads, grad_query, grad_mixed, grad_branch, rows_ffn, rows_attn, s,
                     target):
        outs = call(
            project_back_kernel, info,
            list(window_grads) + [grad_query, s["qkv"], cosine, sine, s["x"], grad_mixed,
            grad_branch, s["attended"], s["blocks"], s["gains"], rows_ffn, rows_attn],
            [shape((tokens + GAIN_ROWS, wide + model + head + 256), BF)] * shards
            + [shape((tokens, model), BF)],
            [pltpu.VMEM((tokens, wide), BF), pltpu.VMEM((shards, GAIN_ROWS, 256), F32)]
            + qkv_scratch,
            section=target, pieces=s["pieces"],
        )
        return outs[:shards], outs[shards]

    def exchange(packs, target):
        return [packs[0]] + [links.across(packs[i], target, i) for i in range(1, shards)]

    total_width = 2 * hidden + 512

    def ffn_weights(packs, target):
        return call(
            functools.partial(ffn_weights_kernel, shard, model), info, list(packs),
            [shape((shard, 2 * hidden), BF), shape((shard, hidden), BF)],
            section=target,
        )

    def attn_weights(packs, ffn, target):
        return call(
            functools.partial(weights_kernel, shard, model), info, list(packs) + list(ffn),
            [shape((shard, total_width), BF)] * 2,
            section=target,
        )

    def backward(upstream, s, target, other=None):
        ffn_packs, grad_mixed, rows_ffn = back_ffn(upstream, s, target)
        grad_branch, grad_query, kept, gives, rows_attn = back_attend(grad_mixed, s, target)
        window_grads, ffn_packs, other = back_window(kept, gives, target, (ffn_packs, other))
        ffn_packs = exchange(ffn_packs, target)
        attn_packs, grad_in = back_project(
            window_grads, grad_query, grad_mixed, grad_branch, rows_ffn, rows_attn, s, target
        )
        return ffn_weights(ffn_packs, target), attn_packs, grad_in, other

    x_first = hidden_in.reshape(tokens, model)
    pieces = gather(folded)
    x_window, pieces[5] = fetch(x_first, 0, pieces[5])
    gains = gain_table(pieces, None)
    result_a, saved_a = forward(x_first, pieces, 0, x_window)
    middle = links.cross(result_a, 0)
    result_b, saved_b = forward(middle, pieces, 1)

    ffn, attn_packs, grad_b, _ = backward(cotangent.reshape(tokens, model), saved_b, 1)
    upstream = links.cross(grad_b, 1)
    upstream, attn_packs = tie((upstream, attn_packs))
    b_first, b_second = attn_weights(exchange(attn_packs, 1), ffn, 1)
    upstream, b_first, b_second = tie((upstream, b_first, b_second))
    halves_b = (links.cross(b_first, 1), b_second)

    ffn, attn_packs, grad_a, half_b = backward(upstream, saved_a, 0, halves_b)
    part_b = lax.psum(half_b, "seq")
    a_first, a_second = attn_weights(exchange(attn_packs, 0), ffn, 0)
    a_second, part_b = tie((a_second, part_b))
    part_a = lax.psum(jnp.where(is_first, a_first, links.cross(a_second, 0)), "seq")
    theirs = links.swap(jnp.where(is_first, part_b, part_a))

    part = head // shards
    grads = call(
        finish_kernel, info, [part_a, part_b, theirs],
        [shape((1, shard, heads_width), F32), shape((1, shard, head), F32),
         shape((1, shard, head), F32), shape((1, head, model), F32),
         shape((1, shard, hidden), F32), shape((1, shard, hidden), F32),
         shape((1, quarter, model), F32)]
        + [shape((1, shard), F32)] * 4 + [shape((1, part), F32)] * 2,
    )
    g_query, g_key, g_value, g_out, g_gate, g_up, g_down = grads[:7]
    g_attn, g_post_attn, g_ffn, g_post_ffn, g_query_gain, g_key_gain = grads[7:]
    section_outputs = jnp.where(is_first, result_a, result_b).reshape(1, micro, rows, model)
    input_grads = jnp.where(is_first, grad_a, grad_b).reshape(1, micro, rows, model)
    return (
        section_outputs, input_grads, g_attn, g_query, g_key, g_value, g_query_gain, g_key_gain,
        g_out, g_post_attn, g_ffn, g_gate, g_up, g_down, g_post_ffn,
    )


def solution(mesh):
    rows = P(None, ("seq", "fsdp"), None)
    vector, matrix = P("section", "fsdp"), P("section", "fsdp", None)
    weights = (vector, matrix, matrix, matrix, vector, vector, matrix, vector, vector, matrix,
               matrix, matrix, vector)
    out_rows = P("section", None, ("seq", "fsdp"), None)
    return jax.shard_map(
        functools.partial(body, dict(mesh.shape)),
        mesh=mesh,
        in_specs=(rows, rows, P(None, ("seq", "fsdp"))) + weights,
        out_specs=(out_rows, out_rows) + weights,
        check_vma=False,
    )
```

```python
import functools

import jax
import jax.numpy as jnp
from jax import lax
from jax.experimental import pallas as pl
from jax.experimental.pallas import tpu as pltpu
from jax.sharding import PartitionSpec as P

WIN = 512
EPSILON = 1e-06
ROPE_BASE = 10000.0
NEG_LARGE = -1e30
AXES = ("section", "seq", "fsdp")
BF = jnp.bfloat16
F32 = jnp.float32
GAIN_ROWS = 16
INTERPRET = False


def mm(left, right):
    return lax.dot_general(left, right, (((1,), (0,)), ((), ())), preferred_element_type=F32)


def mm_nt(left, right):
    return lax.dot_general(left, right, (((1,), (1,)), ((), ())), preferred_element_type=F32)


def mm_tn(left, right):
    return lax.dot_general(left, right, (((0,), (0,)), ((), ())), preferred_element_type=F32)


def inverse_rms(values):
    return lax.rsqrt(jnp.mean(values * values, axis=-1, keepdims=True) + EPSILON)


def norm_back(values, scale, gain, grad):
    weighted = grad * gain
    inner = jnp.mean(values * weighted, axis=-1, keepdims=True)
    return scale * weighted - values * (scale * scale * scale * inner)


def gain_back(values, scale, grad):
    return jnp.sum(values * scale * grad, axis=0, keepdims=True)


def call(kernel, info, arrays, outs, scratch=(), section=None, pieces=(), far=False):
    smem = pl.BlockSpec(memory_space=pltpu.SMEM)
    vmem = pl.BlockSpec(memory_space=pltpu.VMEM)
    hbm = pl.BlockSpec(memory_space=pltpu.HBM)
    lead = len(pieces)

    def entry(info, *refs):
        def run():
            kernel(info, *((refs[:lead],) if lead else ()), *refs[lead:])

        if section is None:
            run()
        else:
            pl.when(info[2] == section)(run)

    return pl.pallas_call(
        entry,
        out_shape=outs,
        in_specs=[smem] + [hbm] * lead + [hbm if far else vmem] * len(arrays),
        out_specs=[vmem] * len(outs),
        scratch_shapes=list(scratch),
        compiler_params=pltpu.CompilerParams(vmem_limit_bytes=(58 if far else 32) * 1024 * 1024),
        cost_estimate=pl.CostEstimate(flops=1, bytes_accessed=1, transcendentals=0),
        interpret=INTERPRET,
    )(info, *pieces, *arrays)


def shape(dims, kind):
    return jax.ShapeDtypeStruct(tuple(dims), kind)


def slot(index, width):
    return pl.ds(pl.multiple_of(index * width, width), width)


def layout(model):
    unit = model // 5
    return unit * 32, unit * 40, unit * 56, unit * 68


def sources(pieces, start):
    split = pieces[0].shape[1]
    if start < split:
        return [(piece, start) for piece in pieces[:4]]
    return [(piece, start - split) for piece in pieces[4:]]


def gains_kernel(info, gathered, out, held, sems):
    count, rows, width = held.shape
    shard = out.shape[1] // count
    part = shard * 2 // 5
    copies = []
    for flip, (piece, start) in enumerate(sources(gathered, layout(out.shape[1])[3])):
        source = piece.at[pl.ds(0, rows), pl.ds(start, width)]
        copies.append(pltpu.make_async_copy(source, held.at[info[0] ^ flip], sems.at[flip]))
    for copy in copies:
        copy.start()
    for copy in copies:
        copy.wait()
    out[...] = jnp.zeros_like(out)
    for place in range(count):
        values = held[place].astype(F32)
        start = place * shard
        for row in range(4):
            out[row : row + 1, start : start + width] = values[2 * row : 2 * row + 1]
            out[row : row + 1, start + width : start + shard] = values[
                2 * row + 1 : 2 * row + 2, : shard - width
            ]
        for row in range(2):
            out[4 + row : 5 + row, place * part : (place + 1) * part] = values[
                8 + row : 9 + row, :part
            ]


def fold_kernel(info, gate, up, query, key, value, out_w, down_w, attn, post_attn, ffn, post_ffn,
                query_gain, key_gain, first, second, out_held, down_held, *rest):
    shard = gate.shape[1]
    vectors, sems = rest[:-1], rest[-1]
    copies = []

    def load(source, target):
        copy = pltpu.make_async_copy(source, target, sems.at[len(copies)])
        copy.start()
        copies.append(copy)

    load(out_w.at[0], out_held)
    load(down_w.at[0], down_held)
    for source, held in zip((attn, post_attn, ffn, post_ffn, query_gain, key_gain), vectors):
        load(source, held)
    hidden = gate.shape[2]
    load(gate.at[0], first.at[:, pl.ds(0, hidden)])
    load(up.at[0], first.at[:, pl.ds(hidden, hidden)])
    start = 4 * (out_held.shape[0] + down_held.shape[0])
    for ref in (query, key, value):
        load(ref.at[0], second.at[:, pl.ds(start, ref.shape[2])])
        start += ref.shape[2]
    wait_all(copies)
    second[:, start:] = jnp.zeros_like(second[:, start:])
    width = 128
    for row, ref in enumerate(vectors[:4]):
        second[2 * row : 2 * row + 1, start : start + width] = ref[:, :width]
        second[2 * row + 1 : 2 * row + 2, start : start + shard - width] = ref[:, width:]
    for row, ref in enumerate(vectors[4:]):
        second[8 + row : 9 + row, start : start + ref.shape[1]] = ref[...]
    start = 0
    for held in (out_held, down_held):
        rows = held.shape[0]
        for place in range(4):
            block = held[:, place * shard : (place + 1) * shard].astype(F32)
            second[:, start : start + rows] = block.T.astype(BF)
            start += rows


def load_turned(info, gathered, held, sems, start):
    width, shard = held.shape[1] // 4, held.shape[0] // 4
    copies = []
    for flip, (piece, column) in enumerate(sources(gathered, start)):
        for row in range(4):
            copy = pltpu.make_async_copy(
                piece.at[:, pl.ds(column + row * width, width)],
                held.at[pl.ds(row * shard, shard), slot(info[0] ^ flip, width)],
                sems.at[4 * flip + row],
            )
            copy.start()
            copies.append(copy)
    return copies


def load_rows(info, gathered, held, sems, start):
    shard, width = held.shape[0] // 4, held.shape[1]
    copies = []
    for flip, (piece, column) in enumerate(sources(gathered, start)):
        copy = pltpu.make_async_copy(
            piece.at[:, pl.ds(column, width)], held.at[slot(info[0] ^ flip, shard)], sems.at[flip]
        )
        copy.start()
        copies.append(copy)
    return copies


def wait_all(copies):
    for copy in copies:
        copy.wait()


def rope_store(target, rows, start, normal, cos, sin):
    half = cos.shape[1]
    one, two = normal[:, :half], normal[:, half:]
    target[rows, start : start + half] = (one * cos - two * sin).astype(BF)
    target[rows, start + half : start + 2 * half] = (two * cos + one * sin).astype(BF)


def cut(blocks, normed):
    shard = blocks.shape[2]
    for place in range(blocks.shape[0]):
        blocks[place] = normed[:, place * shard : (place + 1) * shard].astype(BF)


def project_window_kernel(micro, info, gathered, x, one, two, *refs):
    got, (gains, cosine, sine, wide_cos, wide_sin) = refs[:3], refs[3:8]
    blocks, qkv, query, window, weight, sems = refs[8:]
    copies = load_rows(info, gathered, weight, sems, layout(x.shape[1])[2])
    rows = x.shape[0] // micro
    head = window.shape[2] // 2
    heads_width = query.shape[1]

    def normed_of(values):
        return values * inverse_rms(values) * gains[0:1, :]

    normed = normed_of(x[...].astype(F32))
    cut(blocks, normed)
    normed = normed.astype(BF)
    wait_all(copies)
    total = mm(normed, weight[:, :heads_width])
    qkv[:, :heads_width] = total
    for start in range(0, heads_width, head):
        raw = total[:, start : start + head]
        normal = raw * inverse_rms(raw) * gains[4:5, :head]
        rope_store(query, slice(None), start, normal, cosine[...], sine[...])
    for m in range(micro):
        span = slice(m * rows, (m + 1) * rows)
        parts = [x[span], one[span], two[span]]
        for ref in got:
            parts += [ref[0, span], ref[1, span]]
        values = jnp.concatenate(parts, axis=0).astype(F32)
        total = mm(normed_of(values).astype(BF), weight[:, heads_width:])
        qkv[span, heads_width:] = total[:rows]
        raw = total[:, :head]
        normal = raw * inverse_rms(raw) * gains[5:6, :head]
        rope_store(window.at[m], slice(None), 0, normal, wide_cos[...], wide_sin[...])
        window[m, :, head:] = total[:, head:].astype(BF)


def finish_kernel(info, part_a, part_b, theirs_a, theirs_b, *outs):
    query, key, value, out, gate, up, down = outs[:7]
    vectors = outs[7:]
    shard, hidden = gate.shape[1], gate.shape[2]

    def emit(first, second):
        gate[0] = first[:, :hidden].astype(F32)
        up[0] = first[:, hidden : 2 * hidden].astype(F32)
        for row, ref in enumerate(vectors):
            ref[...] = first[:GAIN_ROWS, 2 * hidden : 2 * hidden + ref.shape[1]].astype(F32)[
                row : row + 1
            ]
        start = 0
        for ref in (query, key, value):
            ref[0] = second[:, start : start + ref.shape[2]].astype(F32)
            start += ref.shape[2]
        for ref in (out, down):
            rows = ref.shape[1]
            for place in range(4):
                block = second[:, start : start + rows].astype(F32)
                ref[0, :, place * shard : (place + 1) * shard] = block.T
                start += rows

    @pl.when(info[2] == 0)
    def _():
        emit(part_a, theirs_a)

    @pl.when(info[2] == 1)
    def _():
        emit(theirs_b, part_b)


def project_kernel(info, gathered, x, gains, cosine, sine, blocks, qkv, query, own, weight, sems):
    copies = load_rows(info, gathered, weight, sems, layout(x.shape[1])[2])
    head = 2 * cosine.shape[1]
    residual = x[...].astype(F32)
    normed = residual * inverse_rms(residual) * gains[0:1, :]
    cut(blocks, normed)
    wait_all(copies)
    total = mm(normed.astype(BF), weight[...])
    qkv[...] = total
    heads = query.shape[1] // head
    for index in range(heads + 1):
        raw = total[:, index * head : (index + 1) * head]
        row = 4 if index < heads else 5
        normal = raw * inverse_rms(raw) * gains[row : row + 1, :head]
        target, start = (query, index * head) if index < heads else (own, 0)
        rope_store(target, slice(None), start, normal, cosine[...], sine[...])
    own[:, head:] = total[:, (heads + 1) * head :].astype(BF)


def select_kernel(info, own, one, two, *outs):
    for index, out in enumerate(outs):
        lower = (info[0] < (info[0] ^ (index + 1))).astype(F32)
        out[0] = one[...]
        mixed = own[...].astype(F32) * lower + two[...].astype(F32) * (1.0 - lower)
        out[1] = mixed.astype(BF)


def window_kernel(micro, info, own, one, two, *refs):
    got, window = refs[:3], refs[3]
    rows = own.shape[0] // micro
    for m in range(micro):
        span = slice(m * rows, (m + 1) * rows)
        parts = [own[span], one[span], two[span]]
        for ref in got:
            parts += [ref[0, span], ref[1, span]]
        for index, part in enumerate(parts):
            window[m, index * rows : (index + 1) * rows] = part


def attend_kernel(micro, info, gathered, query, x, gains, limit, *refs):
    out_w, sems = refs[-2:]
    model = x.shape[1]
    shard = model // 4
    copies = load_turned(info, gathered, out_w, sems, layout(model)[0])
    if len(refs) == 1 + 6 + 2:
        window = refs[0]
        outs = refs[1:-2]
    else:
        window = refs[6]
        outs = refs[7:-2]
        window_kernel(micro, info, *refs[:6], window)
    probs, attended, branch, mixed, blocks, ffn_in = outs
    rows = query.shape[0] // micro
    head = window.shape[2] // 2
    heads = query.shape[1] // head
    count = window.shape[1]
    column = lax.broadcasted_iota(jnp.int32, (rows, count), 1)
    distance = lax.broadcasted_iota(jnp.int32, (rows, count), 0) + info[3]
    for index in range(count // rows):
        inside = (column >= index * rows) & (column < (index + 1) * rows)
        distance = distance - jnp.where(inside, column - index * rows + info[4 + index], 0)
    for m in range(micro):
        span = slice(m * rows, (m + 1) * rows)
        allowed = (distance >= 0) & (distance <= limit[span])
        bias = jnp.where(allowed, 0.0, NEG_LARGE)
        bias = jnp.concatenate([bias] * heads, axis=0)
        stacked = jnp.concatenate(
            [query[span, h * head : (h + 1) * head] for h in range(heads)], axis=0
        )
        scores = mm_nt(stacked, window[m, :, :head]) * head ** (-0.5) + bias
        exponent = jnp.exp(scores - jnp.max(scores, axis=-1, keepdims=True))
        chance = exponent / jnp.sum(exponent, axis=-1, keepdims=True)
        probs[m] = chance
        result = mm(chance.astype(BF), window[m, :, head:]).astype(BF)
        for h in range(heads):
            attended[span, h * head : (h + 1) * head] = result[h * rows : (h + 1) * rows]
    for copy in copies:
        copy.wait()
    total = mm_nt(attended[...], out_w[...])
    branch[...] = total
    value = x[...].astype(F32) + total * inverse_rms(total) * gains[1:2, :]
    mixed[...] = value
    normed = value * inverse_rms(value) * gains[2:3, :]
    ffn_in[...] = normed.astype(BF)
    for place in range(4):
        blocks[place] = normed[:, place * shard : (place + 1) * shard].astype(BF)


def gelu_parts(gate):
    c = 0.7978845608028654
    inner = jnp.tanh(c * (gate + 0.044715 * gate * gate * gate))
    value = 0.5 * gate * (1.0 + inner)
    slope = 0.5 * (1.0 + inner) + 0.5 * gate * (1.0 - inner * inner) * c * (
        1.0 + 3 * 0.044715 * gate * gate
    )
    return value, slope


def ffn_kernel(info, gathered, ffn_in, mixed, gains, gate_up, activated, down, result,
               gate_up_w, down_w, column_sems, sems):
    hidden = activated.shape[1]
    width = 512
    columns = load_rows(info, gathered, gate_up_w, column_sems, 0)
    copies = load_turned(info, gathered, down_w, sems, layout(mixed.shape[1])[1])
    wait_all(columns)
    for start in range(0, hidden, width):
        both = []
        for base in (start, hidden + start):
            total = mm(ffn_in[...], gate_up_w[:, base : base + width])
            gate_up[:, base : base + width] = total
            both.append(total)
        value, _ = gelu_parts(both[0])
        activated[:, start : start + width] = (value * both[1]).astype(BF)
    for copy in copies:
        copy.wait()
    total = mm_nt(activated[...], down_w[...])
    down[...] = total
    result[...] = (mixed[...] + total * inverse_rms(total) * gains[3:4, :]).astype(BF)


def ffn_back_kernel(info, gathered, upstream, mixed, down, gate_up, activated, blocks, gains,
                    *refs):
    packs, grad_mixed, gain_rows = refs[:4], refs[4], refs[5]
    grad_gate_up, gate_up_w, down_w, column_sems, sems = refs[6:]
    hidden = activated.shape[1]
    model = mixed.shape[1]
    shard = blocks.shape[2]
    copies = load_turned(info, gathered, down_w, sems, layout(mixed.shape[1])[1])
    columns = load_rows(info, gathered, gate_up_w, column_sems, 0)
    top = upstream[...].astype(F32)
    raw = down[...]
    scale = inverse_rms(raw)
    grad_down = norm_back(raw, scale, gains[3:4, :], top).astype(BF)
    gain_rows[...] = jnp.zeros_like(gain_rows)
    gain_rows[3:4, :] = gain_back(raw, scale, top)
    act_at = 2 * hidden + model
    block_at = act_at + hidden // 4
    for flip, pack in enumerate(packs):
        pack[:, 2 * hidden : act_at] = grad_down
        pack[:, act_at:block_at] = activated[:, slot(info[0] ^ flip, hidden // 4)]
        pack[:, block_at:] = jnp.zeros_like(pack[:, block_at:])
        pack[:, block_at : block_at + shard] = blocks[info[0] ^ flip]
    for copy in copies:
        copy.wait()
    width = 512
    for start in range(0, hidden, width):
        value, slope = gelu_parts(gate_up[:, start : start + width])
        up = gate_up[:, hidden + start : hidden + start + width]
        grad = mm(grad_down, down_w[:, start : start + width])
        grad_gate_up[:, start : start + width] = (grad * up * slope).astype(BF)
        grad_gate_up[:, hidden + start : hidden + start + width] = (grad * value).astype(BF)
    for pack in packs:
        pack[:, : 2 * hidden] = grad_gate_up[...]
    for copy in columns:
        copy.wait()
    grad_in = mm_nt(grad_gate_up[...], gate_up_w[...])
    raw = mixed[...]
    scale = inverse_rms(raw)
    gain_rows[2:3, :] = gain_back(raw, scale, grad_in)
    grad_mixed[...] = top + norm_back(raw, scale, gains[2:3, :], grad_in)


def attend_back_kernel(micro, info, gathered, grad_mixed, branch, window, probs, query, gains,
                       *refs):
    grad_branch, grad_query, own, one, two = refs[:5]
    gives, gain_rows, grad_attended, out_w, sems = refs[5:8], refs[8], refs[9], refs[10], refs[11]
    model = branch.shape[1]
    copies = load_turned(info, gathered, out_w, sems, layout(model)[0])
    rows = own.shape[0] // micro
    head = own.shape[1] // 2
    heads = query.shape[1] // head
    factor = head ** (-0.5)
    raw = branch[...]
    scale = inverse_rms(raw)
    grad = grad_mixed[...]
    gain_rows[...] = jnp.zeros_like(gain_rows)
    gain_rows[1:2, :] = gain_back(raw, scale, grad)
    low = norm_back(raw, scale, gains[1:2, :], grad).astype(BF)
    grad_branch[...] = low
    for copy in copies:
        copy.wait()
    grad_attended[...] = mm(low, out_w[...]).astype(BF)
    for m in range(micro):
        span = slice(m * rows, (m + 1) * rows)
        chance = probs[m]
        keys, values = window[m, :, :head], window[m, :, head:]
        stacked = jnp.concatenate(
            [query[span, h * head : (h + 1) * head] for h in range(heads)], axis=0
        )
        upstream = jnp.concatenate(
            [grad_attended[span, h * head : (h + 1) * head] for h in range(heads)], axis=0
        )
        grad_values = mm_tn(chance.astype(BF), upstream)
        grad_chance = mm_nt(upstream, values)
        inner = jnp.sum(chance * grad_chance, axis=-1, keepdims=True)
        grad_scores = (chance * (grad_chance - inner)).astype(BF)
        grad_stacked = mm(grad_scores, keys) * factor
        grad_keys = mm_tn(grad_scores, stacked) * factor
        for h in range(heads):
            grad_query[span, h * head : (h + 1) * head] = grad_stacked[h * rows : (h + 1) * rows]
        for index, target in enumerate((own, one, two)):
            part = slice(index * rows, (index + 1) * rows)
            target[span, :head] = grad_keys[part]
            target[span, head:] = grad_values[part]
        for index, target in enumerate(gives):
            for side in range(2):
                start = (3 + 2 * index + side) * rows
                target[side, span, :head] = grad_keys[start : start + rows].astype(BF)
                target[side, span, head:] = grad_values[start : start + rows].astype(BF)


def combine_kernel(info, own, one, two, first, second, third, own_out, one_out, two_out):
    total_own, total_one, total_two = own[...], one[...], two[...]
    for index, got in enumerate((first, second, third)):
        lower = (info[0] < (info[0] ^ (index + 1))).astype(F32)
        total_one = total_one + got[0].astype(F32)
        side = got[1].astype(F32)
        total_own = total_own + side * lower
        total_two = total_two + side * (1.0 - lower)
    own_out[...] = total_own
    one_out[...] = total_one.astype(BF)
    two_out[...] = total_two.astype(BF)


def project_back_kernel(info, gathered, own, back_one, back_two, grad_query, qkv, cosine, sine, x, grad_mixed,
                        grad_branch, attended, blocks, gains, rows_ffn, rows_attn, *refs):
    packs, grad_in = refs[:4], refs[4]
    grad_qkv, gain_held, weight, sems = refs[5:]
    copies = load_rows(info, gathered, weight, sems, layout(x.shape[1])[2])
    tokens, model = x.shape
    shard = blocks.shape[2]
    half = cosine.shape[1]
    head = 2 * half
    heads = grad_query.shape[1] // head
    cos, sin = cosine[...], sine[...]
    grad_own = own[...] + back_one[...].astype(F32) + back_two[...].astype(F32)
    head_gains = [None, None]
    for index in range(heads + 1):
        if index < heads:
            grad = grad_query[:, index * head : (index + 1) * head]
        else:
            grad = grad_own[:, :head]
        one, two = grad[:, :half], grad[:, half:]
        grad = jnp.concatenate((one * cos + two * sin, two * cos - one * sin), axis=1)
        raw = qkv[:, index * head : (index + 1) * head]
        scale = inverse_rms(raw)
        kind = 0 if index < heads else 1
        term = gain_back(raw, scale, grad)
        head_gains[kind] = term if head_gains[kind] is None else head_gains[kind] + term
        back = norm_back(raw, scale, gains[4 + kind : 5 + kind, :head], grad)
        grad_qkv[:, index * head : (index + 1) * head] = back.astype(BF)
    grad_qkv[:, (heads + 1) * head :] = grad_own[:, head:].astype(BF)
    wait_all(copies)
    grad_normed = mm_nt(grad_qkv[...], weight[...])
    residual = x[...].astype(F32)
    scale = inverse_rms(residual)
    first_gain = gain_back(residual, scale, grad_normed)
    total = grad_mixed[...] + norm_back(residual, scale, gains[0:1, :], grad_normed)
    grad_in[...] = total.astype(BF)
    gain_held[...] = jnp.zeros_like(gain_held)
    part = head // 4
    four = (first_gain, rows_attn[1:2, :], rows_ffn[2:3, :], rows_ffn[3:4, :])
    for place in range(4):
        for row, values in enumerate(four):
            gain_held[place, row : row + 1, :shard] = values[
                :, place * shard : (place + 1) * shard
            ]
        for row, values in enumerate(head_gains):
            gain_held[place, 4 + row : 5 + row, :part] = values[
                :, place * part : (place + 1) * part
            ]
    wide = grad_qkv.shape[1]
    att_at = wide + model
    block_at = att_at + head
    for flip, pack in enumerate(packs):
        other = info[0] ^ flip
        pack[tokens:, :] = jnp.zeros_like(pack[tokens:, :])
        pack[tokens:, : gain_held.shape[2]] = gain_held[other].astype(BF)
        pack[:tokens, :wide] = grad_qkv[...]
        pack[:tokens, wide:att_at] = grad_branch[...]
        pack[:tokens, att_at:block_at] = attended[:, slot(other, head)]
        pack[:tokens, block_at:] = jnp.zeros_like(pack[:tokens, block_at:])
        pack[:tokens, block_at : block_at + shard] = blocks[other]


def over(packs, tokens, left, right, left_width, right_width):
    total = None
    for pack in packs:
        term = mm_tn(
            pack[:tokens, left : left + left_width], pack[:tokens, right : right + right_width]
        )
        total = term if total is None else total + term
    return total.astype(BF)


def ffn_weights_kernel(shard, model, info, *refs):
    packs, first, second = refs[:4], refs[4], refs[5]
    tokens = packs[0].shape[0]
    wide = first.shape[1]
    quarter = second.shape[1] // 4
    act_at = wide + model
    for start in range(0, wide, 1024):
        first[:, start : start + 1024] = over(
            packs, tokens, act_at + quarter, start, shard, 1024
        )
    for place in range(4):
        second[:, place * quarter : (place + 1) * quarter] = over(
            packs, tokens, wide + place * shard, act_at, shard, quarter
        )


def weights_kernel(shard, model, info, *refs):
    packs, gate_up, down, first, second = refs[:4], refs[4], refs[5], refs[6], refs[7]
    tokens = packs[0].shape[0] - GAIN_ROWS
    head = model // 5 * 2
    wide = packs[0].shape[1] - model - 2 * head
    hidden = gate_up.shape[1]
    first[:, :hidden] = gate_up[...]
    first[:, hidden:] = jnp.zeros_like(first[:, hidden:])
    gains = sum(pack[tokens:, :head].astype(F32) for pack in packs)
    first[:GAIN_ROWS, hidden : hidden + head] = gains.astype(BF)
    att_at = wide + model
    second[:, :wide] = over(packs, tokens, att_at + head, 0, shard, wide)
    for place in range(4):
        start = wide + place * head
        second[:, start : start + head] = over(
            packs, tokens, wide + place * shard, att_at, shard, head
        )
    second[:, wide + 4 * head :] = down[...]


class Links:
    def __init__(self, sizes):
        self.sizes = sizes

    def index(self, section, seq, fsdp):
        return (section * self.sizes["seq"] + seq) * self.sizes["fsdp"] + fsdp

    def send(self, array, section, place):
        pairs = []
        for z in range(self.sizes["seq"]):
            for f in range(self.sizes["fsdp"]):
                to_section, to_z, to_f = place(z, f)
                if 0 <= to_z < self.sizes["seq"]:
                    pairs.append((self.index(section, z, f), self.index(to_section, to_z, to_f)))
        return lax.ppermute(array, AXES, pairs)

    def along(self, array, section, by):
        return self.send(array, section, lambda z, f: (section, z + by, f))

    def across(self, array, section, flip):
        return self.send(array, section, lambda z, f: (section, z, f ^ flip))

    def cross(self, array, section):
        return self.send(array, section, lambda z, f: (1 - section, z, f))

    def both(self, array, flip):
        pairs = []
        for section in range(2):
            for z in range(self.sizes["seq"]):
                for f in range(self.sizes["fsdp"]):
                    pairs.append((self.index(section, z, f), self.index(section, z, f ^ flip)))
        return lax.ppermute(array, AXES, pairs)

    def swap(self, array):
        pairs = []
        for section in range(2):
            for z in range(self.sizes["seq"]):
                for f in range(self.sizes["fsdp"]):
                    pairs.append((self.index(section, z, f), self.index(1 - section, z, f)))
        return lax.ppermute(array, AXES, pairs)


def body(sizes, hidden_in, cotangent, positions, attn_gain, w_query, w_key, w_value, query_gain,
         key_gain, w_output, post_attn_gain, ffn_gain, w_gate, w_up, w_down, post_ffn_gain):
    section = lax.axis_index("section")
    seq = lax.axis_index("seq")
    fsdp = lax.axis_index("fsdp")
    is_first = section == 0
    micro, rows, model = hidden_in.shape
    tokens = micro * rows
    shard = w_query.shape[1]
    shards = sizes["fsdp"]
    heads_width, head = w_query.shape[2], w_key.shape[2]
    wide = heads_width + 2 * head
    hidden = w_gate.shape[2]
    quarter = hidden // shards
    assert shards == 4 and 2 * shards * rows == WIN and heads_width == shards * head
    links = Links(sizes)
    tie = lax.optimization_barrier
    info = jnp.stack([fsdp, seq, section]).astype(jnp.int32)

    folded = call(
        fold_kernel, info,
        [w_gate, w_up, w_query, w_key, w_value, w_output, w_down, attn_gain, post_attn_gain,
         ffn_gain, post_ffn_gain, query_gain, key_gain],
        [shape((shard, 2 * hidden), BF), shape((shard, heads_width + hidden + wide + 128), BF)],
        [pltpu.VMEM((head, model), BF), pltpu.VMEM((quarter, model), BF)]
        + [pltpu.VMEM((1, shard), BF)] * 4 + [pltpu.VMEM((1, query_gain.shape[1]), BF)] * 2
        + [pltpu.SemaphoreType.DMA((13,))],
        far=True,
    )

    def gather(arrays):
        first, second = arrays
        second_one, first_two = links.both(second, 1), links.both(first, 2)
        first_one, second_two = links.both(first, 1), links.both(second, 2)
        second_three, first_three = links.both(second_one, 2), links.both(first_two, 1)
        return [first, first_one, first_two, first_three,
                second, second_one, second_two, second_three]

    def gain_table(pieces, target):
        return call(
            gains_kernel, info, [], [shape((8, model), F32)],
            [pltpu.VMEM((shards, GAIN_ROWS, 128), BF), pltpu.SemaphoreType.DMA((shards,))],
            pieces=pieces, section=target,
        )[0]

    qkv_scratch = [pltpu.VMEM((model, wide), BF), pltpu.SemaphoreType.DMA((shards,))]
    out_scratch = [pltpu.VMEM((model, heads_width), BF), pltpu.SemaphoreType.DMA((16,))]
    ffn_scratch = [pltpu.VMEM((model, 2 * hidden), BF), pltpu.VMEM((model, hidden), BF),
                   pltpu.SemaphoreType.DMA((shards,)), pltpu.SemaphoreType.DMA((16,))]

    half = head // 2
    limit = jnp.minimum(positions.reshape(tokens, 1), WIN - 1)
    starts = [(seq - back) * shards + fsdp for back in range(3)]
    for flip in range(1, shards):
        other = fsdp ^ flip
        starts.append((seq - 1) * shards + other)
        starts.append(jnp.where(other < fsdp, seq, seq - 2) * shards + other)
    starts = jnp.stack(starts).astype(jnp.int32) * rows
    key_place = (starts[:, None] + jnp.arange(rows, dtype=jnp.int32)[None, :]).reshape(1, -1)
    info = jnp.concatenate((info, starts[:1], starts))
    span = key_place.shape[1]
    frequency = ROPE_BASE ** (-2.0 * jnp.arange(half, dtype=F32) / head)
    angles = key_place.reshape(span, 1).astype(F32) * frequency[None, :]
    wide_cos, wide_sin = jnp.cos(angles), jnp.sin(angles)
    cosine, sine = (jnp.tile(table[:rows], (micro, 1)) for table in (wide_cos, wide_sin))

    def fetch(own, target, waiting=None):
        one, two = links.along(own, target, 1), links.along(own, target, 2)
        sent = call(
            select_kernel, info, [own, one, two], [shape((2,) + own.shape, BF)] * (shards - 1),
            section=target,
        )
        if waiting is not None:
            sent, waiting = tie((list(sent), waiting))
        got = [links.across(array, target, 1 + i) for i, array in enumerate(sent)]
        return [own, one, two] + got, waiting

    def forward(x, pieces, target, x_window=None):
        sizes_of = [shape((shards, tokens, shard), BF), shape((tokens, wide), F32),
                    shape((tokens, heads_width), BF)]
        whole = shape((micro, span, 2 * head), BF)
        attend_outs = [
            shape((micro, shards * rows, span), F32), shape((tokens, heads_width), BF),
            shape((tokens, model), F32), shape((tokens, model), F32),
            shape((shards, tokens, shard), BF), shape((tokens, model), BF),
        ]
        if x_window is not None:
            blocks, qkv, query, window = call(
                functools.partial(project_window_kernel, micro), info,
                x_window + [gains, cosine, sine, wide_cos, wide_sin],
                sizes_of + [whole], qkv_scratch, section=target, pieces=pieces,
            )
            parts = [window]
        else:
            blocks, qkv, query, own = call(
                project_kernel, info, [x, gains, cosine, sine],
                sizes_of + [shape((tokens, 2 * head), BF)], qkv_scratch, section=target,
                pieces=pieces,
            )
            parts, _ = fetch(own, target)
            attend_outs = [whole] + attend_outs
        outs = call(
            functools.partial(attend_kernel, micro), info,
            [query, x, gains, limit] + parts, attend_outs, out_scratch, section=target,
            pieces=pieces,
        )
        if x_window is None:
            window, *outs = outs
        probs, attended, branch, mixed, ffn_blocks, ffn_in = outs
        gate_up, activated, down, result = call(
            ffn_kernel, info, [ffn_in, mixed, gains],
            [shape((tokens, 2 * hidden), F32), shape((tokens, hidden), BF),
             shape((tokens, model), F32), shape((tokens, model), BF)], ffn_scratch,
            section=target, pieces=pieces,
        )
        saved = dict(
            x=x, gains=gains, pieces=pieces, blocks=blocks, qkv=qkv, query=query, window=window, probs=probs,
            attended=attended, branch=branch, mixed=mixed, ffn_blocks=ffn_blocks, gate_up=gate_up,
            activated=activated, down=down,
        )
        return result, saved

    def back_ffn(upstream, s, target):
        outs = call(
            ffn_back_kernel, info,
            [upstream, s["mixed"], s["down"], s["gate_up"], s["activated"], s["ffn_blocks"],
             s["gains"]],
            [shape((tokens, 2 * hidden + model + quarter + 256), BF)] * shards
            + [shape((tokens, model), F32), shape((8, model), F32)],
            [pltpu.VMEM((tokens, 2 * hidden), BF)] + ffn_scratch,
            section=target, pieces=s["pieces"],
        )
        return outs[:shards], outs[shards], outs[shards + 1]

    def back_attend(grad_mixed, s, target):
        pair = [shape((tokens, 2 * head), F32)] * 3
        outs = call(
            functools.partial(attend_back_kernel, micro), info,
            [grad_mixed, s["branch"], s["window"], s["probs"], s["query"], s["gains"]],
            [shape((tokens, model), BF), shape((tokens, heads_width), F32)] + pair
            + [shape((2, tokens, 2 * head), BF)] * (shards - 1) + [shape((8, model), F32)],
            [pltpu.VMEM((tokens, heads_width), BF)] + out_scratch,
            section=target, pieces=s["pieces"],
        )
        return outs[0], outs[1], outs[2:5], outs[5:8], outs[8]

    def back_window(kept, gives, target, waiting):
        got = [links.across(array, target, 1 + i) for i, array in enumerate(gives)]
        ffn_packs, other = waiting
        if other is not None:
            got, other = tie((got, other))
            other = jnp.where(is_first, other[0], other[1])
            kept, other, ffn_packs = tie((kept, other, ffn_packs))
        own, one, two = call(
            combine_kernel, info, list(kept) + got,
            [shape((tokens, 2 * head), F32)] + [shape((tokens, 2 * head), BF)] * 2,
            section=target,
        )
        one, two = links.along(one, target, -1), links.along(two, target, -2)
        if other is None:
            one, ffn_packs = tie((one, ffn_packs))
        return (own, one, two), ffn_packs, other

    def back_project(window_grads, grad_query, grad_mixed, grad_branch, rows_ffn, rows_attn, s,
                     target):
        outs = call(
            project_back_kernel, info,
            list(window_grads) + [grad_query, s["qkv"], cosine, sine, s["x"], grad_mixed,
            grad_branch, s["attended"], s["blocks"], s["gains"], rows_ffn, rows_attn],
            [shape((tokens + GAIN_ROWS, wide + model + head + 256), BF)] * shards
            + [shape((tokens, model), BF)],
            [pltpu.VMEM((tokens, wide), BF), pltpu.VMEM((shards, GAIN_ROWS, 256), F32)]
            + qkv_scratch,
            section=target, pieces=s["pieces"],
        )
        return outs[:shards], outs[shards]

    def exchange(packs, target):
        return [packs[0]] + [links.across(packs[i], target, i) for i in range(1, shards)]

    total_width = 2 * hidden + 512

    def ffn_weights(packs, target):
        return call(
            functools.partial(ffn_weights_kernel, shard, model), info, list(packs),
            [shape((shard, 2 * hidden), BF), shape((shard, hidden), BF)],
            section=target,
        )

    def attn_weights(packs, ffn, target):
        return call(
            functools.partial(weights_kernel, shard, model), info, list(packs) + list(ffn),
            [shape((shard, total_width), BF)] * 2,
            section=target,
        )

    def backward(upstream, s, target, other=None):
        ffn_packs, grad_mixed, rows_ffn = back_ffn(upstream, s, target)
        grad_branch, grad_query, kept, gives, rows_attn = back_attend(grad_mixed, s, target)
        window_grads, ffn_packs, other = back_window(kept, gives, target, (ffn_packs, other))
        ffn_packs = exchange(ffn_packs, target)
        attn_packs, grad_in = back_project(
            window_grads, grad_query, grad_mixed, grad_branch, rows_ffn, rows_attn, s, target
        )
        return ffn_weights(ffn_packs, target), attn_packs, grad_in, other

    x_first = hidden_in.reshape(tokens, model)
    pieces = gather(folded)
    x_window, pieces[5] = fetch(x_first, 0, pieces[5])
    gains = gain_table(pieces, None)
    result_a, saved_a = forward(x_first, pieces, 0, x_window)
    middle = links.cross(result_a, 0)
    result_b, saved_b = forward(middle, pieces, 1)

    ffn, attn_packs, grad_b, _ = backward(cotangent.reshape(tokens, model), saved_b, 1)
    upstream = links.cross(grad_b, 1)
    upstream, attn_packs = tie((upstream, attn_packs))
    b_first, b_second = attn_weights(exchange(attn_packs, 1), ffn, 1)
    upstream, b_first, b_second = tie((upstream, b_first, b_second))
    halves_b = (links.cross(b_first, 1), b_second)

    ffn, attn_packs, grad_a, half_b = backward(upstream, saved_a, 0, halves_b)
    part_b = lax.psum(half_b, "seq")
    a_first, a_second = attn_weights(exchange(attn_packs, 0), ffn, 0)
    a_second, part_b = tie((a_second, part_b))
    part_a = lax.psum(jnp.where(is_first, a_first, links.cross(a_second, 0)), "seq")
    theirs_b, theirs_a = links.cross(part_b, 0), links.cross(part_a, 1)

    part = head // shards
    grads = call(
        finish_kernel, info, [part_a, part_b, theirs_a, theirs_b],
        [shape((1, shard, heads_width), F32), shape((1, shard, head), F32),
         shape((1, shard, head), F32), shape((1, head, model), F32),
         shape((1, shard, hidden), F32), shape((1, shard, hidden), F32),
         shape((1, quarter, model), F32)]
        + [shape((1, shard), F32)] * 4 + [shape((1, part), F32)] * 2,
    )
    g_query, g_key, g_value, g_out, g_gate, g_up, g_down = grads[:7]
    g_attn, g_post_attn, g_ffn, g_post_ffn, g_query_gain, g_key_gain = grads[7:]
    section_outputs = jnp.where(is_first, result_a, result_b).reshape(1, micro, rows, model)
    input_grads = jnp.where(is_first, grad_a, grad_b).reshape(1, micro, rows, model)
    return (
        section_outputs, input_grads, g_attn, g_query, g_key, g_value, g_query_gain, g_key_gain,
        g_out, g_post_attn, g_ffn, g_gate, g_up, g_down, g_post_ffn,
    )


def solution(mesh):
    rows = P(None, ("seq", "fsdp"), None)
    vector, matrix = P("section", "fsdp"), P("section", "fsdp", None)
    weights = (vector, matrix, matrix, matrix, vector, vector, matrix, vector, vector, matrix,
               matrix, matrix, vector)
    out_rows = P("section", None, ("seq", "fsdp"), None)
    return jax.shard_map(
        functools.partial(body, dict(mesh.shape)),
        mesh=mesh,
        in_specs=(rows, rows, P(None, ("seq", "fsdp"))) + weights,
        out_specs=(out_rows, out_rows) + weights,
        check_vma=False,
    )
```

```python
import functools

import jax
import jax.numpy as jnp
from jax import lax
from jax.experimental import pallas as pl
from jax.experimental.pallas import tpu as pltpu
from jax.sharding import PartitionSpec as P

WIN = 512
EPSILON = 1e-06
ROPE_BASE = 10000.0
NEG_LARGE = -1e30
AXES = ("section", "seq", "fsdp")
BF = jnp.bfloat16
F32 = jnp.float32
GAIN_ROWS = 16
INTERPRET = False


def mm(left, right):
    return lax.dot_general(left, right, (((1,), (0,)), ((), ())), preferred_element_type=F32)


def mm_nt(left, right):
    return lax.dot_general(left, right, (((1,), (1,)), ((), ())), preferred_element_type=F32)


def mm_tn(left, right):
    return lax.dot_general(left, right, (((0,), (0,)), ((), ())), preferred_element_type=F32)


def inverse_rms(values):
    return lax.rsqrt(jnp.mean(values * values, axis=-1, keepdims=True) + EPSILON)


def norm_back(values, scale, gain, grad):
    weighted = grad * gain
    inner = jnp.mean(values * weighted, axis=-1, keepdims=True)
    return scale * weighted - values * (scale * scale * scale * inner)


def gain_back(values, scale, grad):
    return jnp.sum(values * scale * grad, axis=0, keepdims=True)


def call(kernel, info, arrays, outs, scratch=(), section=None, pieces=(), far=False):
    smem = pl.BlockSpec(memory_space=pltpu.SMEM)
    vmem = pl.BlockSpec(memory_space=pltpu.VMEM)
    hbm = pl.BlockSpec(memory_space=pltpu.HBM)
    lead = len(pieces)

    def entry(info, *refs):
        def run():
            kernel(info, *((refs[:lead],) if lead else ()), *refs[lead:])

        if section is None:
            run()
        else:
            pl.when(info[2] == section)(run)

    return pl.pallas_call(
        entry,
        out_shape=outs,
        in_specs=[smem] + [hbm] * lead + [hbm if far else vmem] * len(arrays),
        out_specs=[vmem] * len(outs),
        scratch_shapes=list(scratch),
        compiler_params=pltpu.CompilerParams(vmem_limit_bytes=(58 if far else 24) * 1024 * 1024),
        cost_estimate=pl.CostEstimate(flops=1, bytes_accessed=1, transcendentals=0),
        interpret=INTERPRET,
    )(info, *pieces, *arrays)


def shape(dims, kind):
    return jax.ShapeDtypeStruct(tuple(dims), kind)


def slot(index, width):
    return pl.ds(pl.multiple_of(index * width, width), width)


def layout(model):
    unit = model // 5
    return unit * 32, unit * 40, unit * 56, unit * 68


def sources(pieces, start):
    split = pieces[0].shape[1]
    if start < split:
        return [(piece, start) for piece in pieces[:4]]
    return [(piece, start - split) for piece in pieces[4:]]


def gains_kernel(info, gathered, out, held, sems):
    count, rows, width = held.shape
    shard = out.shape[1] // count
    part = shard * 2 // 5
    copies = []
    for flip, (piece, start) in enumerate(sources(gathered, layout(out.shape[1])[3])):
        source = piece.at[pl.ds(0, rows), pl.ds(start, width)]
        copies.append(pltpu.make_async_copy(source, held.at[info[0] ^ flip], sems.at[flip]))
    for copy in copies:
        copy.start()
    for copy in copies:
        copy.wait()
    out[...] = jnp.zeros_like(out)
    for place in range(count):
        values = held[place].astype(F32)
        start = place * shard
        for row in range(4):
            out[row : row + 1, start : start + width] = values[2 * row : 2 * row + 1]
            out[row : row + 1, start + width : start + shard] = values[
                2 * row + 1 : 2 * row + 2, : shard - width
            ]
        for row in range(2):
            out[4 + row : 5 + row, place * part : (place + 1) * part] = values[
                8 + row : 9 + row, :part
            ]


def fold_kernel(info, gate, up, query, key, value, out_w, down_w, attn, post_attn, ffn, post_ffn,
                query_gain, key_gain, first, second, out_held, down_held, *rest):
    shard = gate.shape[1]
    vectors, sems = rest[:-1], rest[-1]
    copies = []

    def load(source, target):
        copy = pltpu.make_async_copy(source, target, sems.at[len(copies)])
        copy.start()
        copies.append(copy)

    load(out_w.at[0], out_held)
    load(down_w.at[0], down_held)
    for source, held in zip((attn, post_attn, ffn, post_ffn, query_gain, key_gain), vectors):
        load(source, held)
    hidden = gate.shape[2]
    load(gate.at[0], first.at[:, pl.ds(0, hidden)])
    load(up.at[0], first.at[:, pl.ds(hidden, hidden)])
    start = 4 * (out_held.shape[0] + down_held.shape[0])
    for ref in (query, key, value):
        load(ref.at[0], second.at[:, pl.ds(start, ref.shape[2])])
        start += ref.shape[2]
    wait_all(copies)
    second[:, start:] = jnp.zeros_like(second[:, start:])
    width = 128
    for row, ref in enumerate(vectors[:4]):
        second[2 * row : 2 * row + 1, start : start + width] = ref[:, :width]
        second[2 * row + 1 : 2 * row + 2, start : start + shard - width] = ref[:, width:]
    for row, ref in enumerate(vectors[4:]):
        second[8 + row : 9 + row, start : start + ref.shape[1]] = ref[...]
    start = 0
    for held in (out_held, down_held):
        rows = held.shape[0]
        for place in range(4):
            block = held[:, place * shard : (place + 1) * shard].astype(F32)
            second[:, start : start + rows] = block.T.astype(BF)
            start += rows


def load_turned(info, gathered, held, sems, start):
    width, shard = held.shape[1] // 4, held.shape[0] // 4
    copies = []
    for flip, (piece, column) in enumerate(sources(gathered, start)):
        for row in range(4):
            copy = pltpu.make_async_copy(
                piece.at[:, pl.ds(column + row * width, width)],
                held.at[pl.ds(row * shard, shard), slot(info[0] ^ flip, width)],
                sems.at[4 * flip + row],
            )
            copy.start()
            copies.append(copy)
    return copies


def load_rows(info, gathered, held, sems, start):
    shard, width = held.shape[0] // 4, held.shape[1]
    copies = []
    for flip, (piece, column) in enumerate(sources(gathered, start)):
        copy = pltpu.make_async_copy(
            piece.at[:, pl.ds(column, width)], held.at[slot(info[0] ^ flip, shard)], sems.at[flip]
        )
        copy.start()
        copies.append(copy)
    return copies


def wait_all(copies):
    for copy in copies:
        copy.wait()


def rope_store(target, rows, start, normal, cos, sin):
    half = cos.shape[1]
    one, two = normal[:, :half], normal[:, half:]
    target[rows, start : start + half] = (one * cos - two * sin).astype(BF)
    target[rows, start + half : start + 2 * half] = (two * cos + one * sin).astype(BF)


def cut(blocks, normed):
    shard = blocks.shape[2]
    for place in range(blocks.shape[0]):
        blocks[place] = normed[:, place * shard : (place + 1) * shard].astype(BF)


def project_window_kernel(micro, info, gathered, x, one, two, *refs):
    got, (gains, cosine, sine, wide_cos, wide_sin) = refs[:3], refs[3:8]
    blocks, qkv, query, window, weight, sems = refs[8:]
    copies = load_rows(info, gathered, weight, sems, layout(x.shape[1])[2])
    rows = x.shape[0] // micro
    head = window.shape[2] // 2
    heads_width = query.shape[1]

    def normed_of(values):
        return values * inverse_rms(values) * gains[0:1, :]

    normed = normed_of(x[...].astype(F32))
    cut(blocks, normed)
    normed = normed.astype(BF)
    wait_all(copies)
    total = mm(normed, weight[:, :heads_width])
    qkv[:, :heads_width] = total
    for start in range(0, heads_width, head):
        raw = total[:, start : start + head]
        normal = raw * inverse_rms(raw) * gains[4:5, :head]
        rope_store(query, slice(None), start, normal, cosine[...], sine[...])
    for m in range(micro):
        span = slice(m * rows, (m + 1) * rows)
        parts = [x[span], one[span], two[span]]
        for ref in got:
            parts += [ref[0, span], ref[1, span]]
        values = jnp.concatenate(parts, axis=0).astype(F32)
        total = mm(normed_of(values).astype(BF), weight[:, heads_width:])
        qkv[span, heads_width:] = total[:rows]
        raw = total[:, :head]
        normal = raw * inverse_rms(raw) * gains[5:6, :head]
        rope_store(window.at[m], slice(None), 0, normal, wide_cos[...], wide_sin[...])
        window[m, :, head:] = total[:, head:].astype(BF)


def finish_kernel(info, part_a, part_b, theirs, *outs):
    query, key, value, out, gate, up, down = outs[:7]
    vectors = outs[7:]
    shard, hidden = gate.shape[1], gate.shape[2]

    def emit(first, second):
        gate[0] = first[:, :hidden].astype(F32)
        up[0] = first[:, hidden : 2 * hidden].astype(F32)
        for row, ref in enumerate(vectors):
            ref[...] = first[:GAIN_ROWS, 2 * hidden : 2 * hidden + ref.shape[1]].astype(F32)[
                row : row + 1
            ]
        start = 0
        for ref in (query, key, value):
            ref[0] = second[:, start : start + ref.shape[2]].astype(F32)
            start += ref.shape[2]
        for ref in (out, down):
            rows = ref.shape[1]
            for place in range(4):
                block = second[:, start : start + rows].astype(F32)
                ref[0, :, place * shard : (place + 1) * shard] = block.T
                start += rows

    @pl.when(info[2] == 0)
    def _():
        emit(part_a, theirs)

    @pl.when(info[2] == 1)
    def _():
        emit(theirs, part_b)


def project_kernel(info, gathered, x, gains, cosine, sine, blocks, qkv, query, own, weight, sems):
    copies = load_rows(info, gathered, weight, sems, layout(x.shape[1])[2])
    head = 2 * cosine.shape[1]
    residual = x[...].astype(F32)
    normed = residual * inverse_rms(residual) * gains[0:1, :]
    cut(blocks, normed)
    wait_all(copies)
    total = mm(normed.astype(BF), weight[...])
    qkv[...] = total
    heads = query.shape[1] // head
    for index in range(heads + 1):
        raw = total[:, index * head : (index + 1) * head]
        row = 4 if index < heads else 5
        normal = raw * inverse_rms(raw) * gains[row : row + 1, :head]
        target, start = (query, index * head) if index < heads else (own, 0)
        rope_store(target, slice(None), start, normal, cosine[...], sine[...])
    own[:, head:] = total[:, (heads + 1) * head :].astype(BF)


def select_kernel(info, own, one, two, *outs):
    for index, out in enumerate(outs):
        lower = (info[0] < (info[0] ^ (index + 1))).astype(F32)
        out[0] = one[...]
        mixed = own[...].astype(F32) * lower + two[...].astype(F32) * (1.0 - lower)
        out[1] = mixed.astype(BF)


def window_kernel(micro, info, own, one, two, *refs):
    got, window = refs[:3], refs[3]
    rows = own.shape[0] // micro
    for m in range(micro):
        span = slice(m * rows, (m + 1) * rows)
        parts = [own[span], one[span], two[span]]
        for ref in got:
            parts += [ref[0, span], ref[1, span]]
        for index, part in enumerate(parts):
            window[m, index * rows : (index + 1) * rows] = part


def attend_kernel(micro, info, gathered, query, x, gains, limit, *refs):
    out_w, sems = refs[-2:]
    model = x.shape[1]
    shard = model // 4
    copies = load_turned(info, gathered, out_w, sems, layout(model)[0])
    if len(refs) == 1 + 6 + 2:
        window = refs[0]
        outs = refs[1:-2]
    else:
        window = refs[6]
        outs = refs[7:-2]
        window_kernel(micro, info, *refs[:6], window)
    probs, attended, branch, mixed, blocks, ffn_in = outs
    rows = query.shape[0] // micro
    head = window.shape[2] // 2
    heads = query.shape[1] // head
    count = window.shape[1]
    column = lax.broadcasted_iota(jnp.int32, (rows, count), 1)
    distance = lax.broadcasted_iota(jnp.int32, (rows, count), 0) + info[3]
    for index in range(count // rows):
        inside = (column >= index * rows) & (column < (index + 1) * rows)
        distance = distance - jnp.where(inside, column - index * rows + info[4 + index], 0)
    for m in range(micro):
        span = slice(m * rows, (m + 1) * rows)
        allowed = (distance >= 0) & (distance <= limit[span])
        bias = jnp.where(allowed, 0.0, NEG_LARGE)
        bias = jnp.concatenate([bias] * heads, axis=0)
        stacked = jnp.concatenate(
            [query[span, h * head : (h + 1) * head] for h in range(heads)], axis=0
        )
        scores = mm_nt(stacked, window[m, :, :head]) * head ** (-0.5) + bias
        exponent = jnp.exp(scores - jnp.max(scores, axis=-1, keepdims=True))
        chance = exponent / jnp.sum(exponent, axis=-1, keepdims=True)
        probs[m] = chance
        result = mm(chance.astype(BF), window[m, :, head:]).astype(BF)
        for h in range(heads):
            attended[span, h * head : (h + 1) * head] = result[h * rows : (h + 1) * rows]
    for copy in copies:
        copy.wait()
    total = mm_nt(attended[...], out_w[...])
    branch[...] = total
    value = x[...].astype(F32) + total * inverse_rms(total) * gains[1:2, :]
    mixed[...] = value
    normed = value * inverse_rms(value) * gains[2:3, :]
    ffn_in[...] = normed.astype(BF)
    for place in range(4):
        blocks[place] = normed[:, place * shard : (place + 1) * shard].astype(BF)


def gelu_parts(gate):
    c = 0.7978845608028654
    inner = jnp.tanh(c * (gate + 0.044715 * gate * gate * gate))
    value = 0.5 * gate * (1.0 + inner)
    slope = 0.5 * (1.0 + inner) + 0.5 * gate * (1.0 - inner * inner) * c * (
        1.0 + 3 * 0.044715 * gate * gate
    )
    return value, slope


def ffn_kernel(info, gathered, ffn_in, mixed, gains, gate_up, activated, down, result,
               gate_up_w, down_w, column_sems, sems):
    hidden = activated.shape[1]
    width = 512
    columns = load_rows(info, gathered, gate_up_w, column_sems, 0)
    copies = load_turned(info, gathered, down_w, sems, layout(mixed.shape[1])[1])
    wait_all(columns)
    for start in range(0, hidden, width):
        both = []
        for base in (start, hidden + start):
            total = mm(ffn_in[...], gate_up_w[:, base : base + width])
            gate_up[:, base : base + width] = total
            both.append(total)
        value, _ = gelu_parts(both[0])
        activated[:, start : start + width] = (value * both[1]).astype(BF)
    for copy in copies:
        copy.wait()
    total = mm_nt(activated[...], down_w[...])
    down[...] = total
    result[...] = (mixed[...] + total * inverse_rms(total) * gains[3:4, :]).astype(BF)


def ffn_back_kernel(info, gathered, upstream, mixed, down, gate_up, activated, blocks, gains,
                    *refs):
    packs, grad_mixed, gain_rows = refs[:4], refs[4], refs[5]
    grad_gate_up, gate_up_w, down_w, column_sems, sems = refs[6:]
    hidden = activated.shape[1]
    model = mixed.shape[1]
    shard = blocks.shape[2]
    copies = load_turned(info, gathered, down_w, sems, layout(mixed.shape[1])[1])
    columns = load_rows(info, gathered, gate_up_w, column_sems, 0)
    top = upstream[...].astype(F32)
    raw = down[...]
    scale = inverse_rms(raw)
    grad_down = norm_back(raw, scale, gains[3:4, :], top).astype(BF)
    gain_rows[...] = jnp.zeros_like(gain_rows)
    gain_rows[3:4, :] = gain_back(raw, scale, top)
    act_at = 2 * hidden + model
    block_at = act_at + hidden // 4
    for flip, pack in enumerate(packs):
        pack[:, 2 * hidden : act_at] = grad_down
        pack[:, act_at:block_at] = activated[:, slot(info[0] ^ flip, hidden // 4)]
        pack[:, block_at:] = jnp.zeros_like(pack[:, block_at:])
        pack[:, block_at : block_at + shard] = blocks[info[0] ^ flip]
    for copy in copies:
        copy.wait()
    width = 512
    for start in range(0, hidden, width):
        value, slope = gelu_parts(gate_up[:, start : start + width])
        up = gate_up[:, hidden + start : hidden + start + width]
        grad = mm(grad_down, down_w[:, start : start + width])
        grad_gate_up[:, start : start + width] = (grad * up * slope).astype(BF)
        grad_gate_up[:, hidden + start : hidden + start + width] = (grad * value).astype(BF)
    for pack in packs:
        pack[:, : 2 * hidden] = grad_gate_up[...]
    for copy in columns:
        copy.wait()
    grad_in = mm_nt(grad_gate_up[...], gate_up_w[...])
    raw = mixed[...]
    scale = inverse_rms(raw)
    gain_rows[2:3, :] = gain_back(raw, scale, grad_in)
    grad_mixed[...] = top + norm_back(raw, scale, gains[2:3, :], grad_in)


def attend_back_kernel(micro, info, gathered, grad_mixed, branch, window, probs, query, gains,
                       *refs):
    grad_branch, grad_query, own, one, two = refs[:5]
    gives, gain_rows, grad_attended, out_w, sems = refs[5:8], refs[8], refs[9], refs[10], refs[11]
    model = branch.shape[1]
    copies = load_turned(info, gathered, out_w, sems, layout(model)[0])
    rows = own.shape[0] // micro
    head = own.shape[1] // 2
    heads = query.shape[1] // head
    factor = head ** (-0.5)
    raw = branch[...]
    scale = inverse_rms(raw)
    grad = grad_mixed[...]
    gain_rows[...] = jnp.zeros_like(gain_rows)
    gain_rows[1:2, :] = gain_back(raw, scale, grad)
    low = norm_back(raw, scale, gains[1:2, :], grad).astype(BF)
    grad_branch[...] = low
    for copy in copies:
        copy.wait()
    grad_attended[...] = mm(low, out_w[...]).astype(BF)
    for m in range(micro):
        span = slice(m * rows, (m + 1) * rows)
        chance = probs[m]
        keys, values = window[m, :, :head], window[m, :, head:]
        stacked = jnp.concatenate(
            [query[span, h * head : (h + 1) * head] for h in range(heads)], axis=0
        )
        upstream = jnp.concatenate(
            [grad_attended[span, h * head : (h + 1) * head] for h in range(heads)], axis=0
        )
        grad_values = mm_tn(chance.astype(BF), upstream)
        grad_chance = mm_nt(upstream, values)
        inner = jnp.sum(chance * grad_chance, axis=-1, keepdims=True)
        grad_scores = (chance * (grad_chance - inner)).astype(BF)
        grad_stacked = mm(grad_scores, keys) * factor
        grad_keys = mm_tn(grad_scores, stacked) * factor
        for h in range(heads):
            grad_query[span, h * head : (h + 1) * head] = grad_stacked[h * rows : (h + 1) * rows]
        for index, target in enumerate((own, one, two)):
            part = slice(index * rows, (index + 1) * rows)
            target[span, :head] = grad_keys[part]
            target[span, head:] = grad_values[part]
        for index, target in enumerate(gives):
            for side in range(2):
                start = (3 + 2 * index + side) * rows
                target[side, span, :head] = grad_keys[start : start + rows].astype(BF)
                target[side, span, head:] = grad_values[start : start + rows].astype(BF)


def combine_kernel(info, own, one, two, first, second, third, own_out, one_out, two_out):
    total_own, total_one, total_two = own[...], one[...], two[...]
    for index, got in enumerate((first, second, third)):
        lower = (info[0] < (info[0] ^ (index + 1))).astype(F32)
        total_one = total_one + got[0].astype(F32)
        side = got[1].astype(F32)
        total_own = total_own + side * lower
        total_two = total_two + side * (1.0 - lower)
    own_out[...] = total_own
    one_out[...] = total_one.astype(BF)
    two_out[...] = total_two.astype(BF)


def project_back_kernel(info, gathered, own, back_one, back_two, grad_query, qkv, cosine, sine, x, grad_mixed,
                        grad_branch, attended, blocks, gains, rows_ffn, rows_attn, *refs):
    packs, grad_in = refs[:4], refs[4]
    grad_qkv, gain_held, weight, sems = refs[5:]
    copies = load_rows(info, gathered, weight, sems, layout(x.shape[1])[2])
    tokens, model = x.shape
    shard = blocks.shape[2]
    half = cosine.shape[1]
    head = 2 * half
    heads = grad_query.shape[1] // head
    cos, sin = cosine[...], sine[...]
    grad_own = own[...] + back_one[...].astype(F32) + back_two[...].astype(F32)
    head_gains = [None, None]
    for index in range(heads + 1):
        if index < heads:
            grad = grad_query[:, index * head : (index + 1) * head]
        else:
            grad = grad_own[:, :head]
        one, two = grad[:, :half], grad[:, half:]
        grad = jnp.concatenate((one * cos + two * sin, two * cos - one * sin), axis=1)
        raw = qkv[:, index * head : (index + 1) * head]
        scale = inverse_rms(raw)
        kind = 0 if index < heads else 1
        term = gain_back(raw, scale, grad)
        head_gains[kind] = term if head_gains[kind] is None else head_gains[kind] + term
        back = norm_back(raw, scale, gains[4 + kind : 5 + kind, :head], grad)
        grad_qkv[:, index * head : (index + 1) * head] = back.astype(BF)
    grad_qkv[:, (heads + 1) * head :] = grad_own[:, head:].astype(BF)
    wait_all(copies)
    grad_normed = mm_nt(grad_qkv[...], weight[...])
    residual = x[...].astype(F32)
    scale = inverse_rms(residual)
    first_gain = gain_back(residual, scale, grad_normed)
    total = grad_mixed[...] + norm_back(residual, scale, gains[0:1, :], grad_normed)
    grad_in[...] = total.astype(BF)
    gain_held[...] = jnp.zeros_like(gain_held)
    part = head // 4
    four = (first_gain, rows_attn[1:2, :], rows_ffn[2:3, :], rows_ffn[3:4, :])
    for place in range(4):
        for row, values in enumerate(four):
            gain_held[place, row : row + 1, :shard] = values[
                :, place * shard : (place + 1) * shard
            ]
        for row, values in enumerate(head_gains):
            gain_held[place, 4 + row : 5 + row, :part] = values[
                :, place * part : (place + 1) * part
            ]
    wide = grad_qkv.shape[1]
    att_at = wide + model
    block_at = att_at + head
    for flip, pack in enumerate(packs):
        other = info[0] ^ flip
        pack[tokens:, :] = jnp.zeros_like(pack[tokens:, :])
        pack[tokens:, : gain_held.shape[2]] = gain_held[other].astype(BF)
        pack[:tokens, :wide] = grad_qkv[...]
        pack[:tokens, wide:att_at] = grad_branch[...]
        pack[:tokens, att_at:block_at] = attended[:, slot(other, head)]
        pack[:tokens, block_at:] = jnp.zeros_like(pack[:tokens, block_at:])
        pack[:tokens, block_at : block_at + shard] = blocks[other]


def over(packs, tokens, left, right, left_width, right_width):
    total = None
    for pack in packs:
        term = mm_tn(
            pack[:tokens, left : left + left_width], pack[:tokens, right : right + right_width]
        )
        total = term if total is None else total + term
    return total.astype(BF)


def ffn_weights_kernel(shard, model, info, *refs):
    packs, first, second = refs[:4], refs[4], refs[5]
    tokens = packs[0].shape[0]
    wide = first.shape[1]
    quarter = second.shape[1] // 4
    act_at = wide + model
    for start in range(0, wide, 1024):
        first[:, start : start + 1024] = over(
            packs, tokens, act_at + quarter, start, shard, 1024
        )
    for place in range(4):
        second[:, place * quarter : (place + 1) * quarter] = over(
            packs, tokens, wide + place * shard, act_at, shard, quarter
        )


def weights_kernel(shard, model, info, *refs):
    packs, gate_up, down, first, second = refs[:4], refs[4], refs[5], refs[6], refs[7]
    tokens = packs[0].shape[0] - GAIN_ROWS
    head = model // 5 * 2
    wide = packs[0].shape[1] - model - 2 * head
    hidden = gate_up.shape[1]
    first[:, :hidden] = gate_up[...]
    first[:, hidden:] = jnp.zeros_like(first[:, hidden:])
    gains = sum(pack[tokens:, :head].astype(F32) for pack in packs)
    first[:GAIN_ROWS, hidden : hidden + head] = gains.astype(BF)
    att_at = wide + model
    second[:, :wide] = over(packs, tokens, att_at + head, 0, shard, wide)
    for place in range(4):
        start = wide + place * head
        second[:, start : start + head] = over(
            packs, tokens, wide + place * shard, att_at, shard, head
        )
    second[:, wide + 4 * head :] = down[...]


class Links:
    def __init__(self, sizes):
        self.sizes = sizes

    def index(self, section, seq, fsdp):
        return (section * self.sizes["seq"] + seq) * self.sizes["fsdp"] + fsdp

    def send(self, array, section, place):
        pairs = []
        for z in range(self.sizes["seq"]):
            for f in range(self.sizes["fsdp"]):
                to_section, to_z, to_f = place(z, f)
                if 0 <= to_z < self.sizes["seq"]:
                    pairs.append((self.index(section, z, f), self.index(to_section, to_z, to_f)))
        return lax.ppermute(array, AXES, pairs)

    def along(self, array, section, by):
        return self.send(array, section, lambda z, f: (section, z + by, f))

    def across(self, array, section, flip):
        return self.send(array, section, lambda z, f: (section, z, f ^ flip))

    def cross(self, array, section):
        return self.send(array, section, lambda z, f: (1 - section, z, f))

    def both(self, array, flip):
        pairs = []
        for section in range(2):
            for z in range(self.sizes["seq"]):
                for f in range(self.sizes["fsdp"]):
                    pairs.append((self.index(section, z, f), self.index(section, z, f ^ flip)))
        return lax.ppermute(array, AXES, pairs)

    def swap(self, array):
        pairs = []
        for section in range(2):
            for z in range(self.sizes["seq"]):
                for f in range(self.sizes["fsdp"]):
                    pairs.append((self.index(section, z, f), self.index(1 - section, z, f)))
        return lax.ppermute(array, AXES, pairs)


def body(sizes, hidden_in, cotangent, positions, attn_gain, w_query, w_key, w_value, query_gain,
         key_gain, w_output, post_attn_gain, ffn_gain, w_gate, w_up, w_down, post_ffn_gain):
    section = lax.axis_index("section")
    seq = lax.axis_index("seq")
    fsdp = lax.axis_index("fsdp")
    is_first = section == 0
    micro, rows, model = hidden_in.shape
    tokens = micro * rows
    shard = w_query.shape[1]
    shards = sizes["fsdp"]
    heads_width, head = w_query.shape[2], w_key.shape[2]
    wide = heads_width + 2 * head
    hidden = w_gate.shape[2]
    quarter = hidden // shards
    assert shards == 4 and 2 * shards * rows == WIN and heads_width == shards * head
    links = Links(sizes)
    tie = lax.optimization_barrier
    info = jnp.stack([fsdp, seq, section]).astype(jnp.int32)

    folded = call(
        fold_kernel, info,
        [w_gate, w_up, w_query, w_key, w_value, w_output, w_down, attn_gain, post_attn_gain,
         ffn_gain, post_ffn_gain, query_gain, key_gain],
        [shape((shard, 2 * hidden), BF), shape((shard, heads_width + hidden + wide + 128), BF)],
        [pltpu.VMEM((head, model), BF), pltpu.VMEM((quarter, model), BF)]
        + [pltpu.VMEM((1, shard), BF)] * 4 + [pltpu.VMEM((1, query_gain.shape[1]), BF)] * 2
        + [pltpu.SemaphoreType.DMA((13,))],
        far=True,
    )

    def gather(arrays):
        first, second = arrays
        second_one, first_two = links.both(second, 1), links.both(first, 2)
        first_one, second_two = links.both(first, 1), links.both(second, 2)
        second_three, first_three = links.both(second_one, 2), links.both(first_two, 1)
        return [first, first_one, first_two, first_three,
                second, second_one, second_two, second_three]

    def gain_table(pieces, target):
        return call(
            gains_kernel, info, [], [shape((8, model), F32)],
            [pltpu.VMEM((shards, GAIN_ROWS, 128), BF), pltpu.SemaphoreType.DMA((shards,))],
            pieces=pieces, section=target,
        )[0]

    qkv_scratch = [pltpu.VMEM((model, wide), BF), pltpu.SemaphoreType.DMA((shards,))]
    out_scratch = [pltpu.VMEM((model, heads_width), BF), pltpu.SemaphoreType.DMA((16,))]
    ffn_scratch = [pltpu.VMEM((model, 2 * hidden), BF), pltpu.VMEM((model, hidden), BF),
                   pltpu.SemaphoreType.DMA((shards,)), pltpu.SemaphoreType.DMA((16,))]

    half = head // 2
    limit = jnp.minimum(positions.reshape(tokens, 1), WIN - 1)
    starts = [(seq - back) * shards + fsdp for back in range(3)]
    for flip in range(1, shards):
        other = fsdp ^ flip
        starts.append((seq - 1) * shards + other)
        starts.append(jnp.where(other < fsdp, seq, seq - 2) * shards + other)
    starts = jnp.stack(starts).astype(jnp.int32) * rows
    key_place = (starts[:, None] + jnp.arange(rows, dtype=jnp.int32)[None, :]).reshape(1, -1)
    info = jnp.concatenate((info, starts[:1], starts))
    span = key_place.shape[1]
    frequency = ROPE_BASE ** (-2.0 * jnp.arange(half, dtype=F32) / head)
    angles = key_place.reshape(span, 1).astype(F32) * frequency[None, :]
    wide_cos, wide_sin = jnp.cos(angles), jnp.sin(angles)
    cosine, sine = (jnp.tile(table[:rows], (micro, 1)) for table in (wide_cos, wide_sin))

    def fetch(own, target, waiting=None):
        one, two = links.along(own, target, 1), links.along(own, target, 2)
        sent = call(
            select_kernel, info, [own, one, two], [shape((2,) + own.shape, BF)] * (shards - 1),
            section=target,
        )
        if waiting is not None:
            sent, waiting = tie((list(sent), waiting))
        got = [links.across(array, target, 1 + i) for i, array in enumerate(sent)]
        return [own, one, two] + got, waiting

    def forward(x, pieces, target, x_window=None):
        sizes_of = [shape((shards, tokens, shard), BF), shape((tokens, wide), F32),
                    shape((tokens, heads_width), BF)]
        whole = shape((micro, span, 2 * head), BF)
        attend_outs = [
            shape((micro, shards * rows, span), F32), shape((tokens, heads_width), BF),
            shape((tokens, model), F32), shape((tokens, model), F32),
            shape((shards, tokens, shard), BF), shape((tokens, model), BF),
        ]
        if x_window is not None:
            blocks, qkv, query, window = call(
                functools.partial(project_window_kernel, micro), info,
                x_window + [gains, cosine, sine, wide_cos, wide_sin],
                sizes_of + [whole], qkv_scratch, section=target, pieces=pieces,
            )
            parts = [window]
        else:
            blocks, qkv, query, own = call(
                project_kernel, info, [x, gains, cosine, sine],
                sizes_of + [shape((tokens, 2 * head), BF)], qkv_scratch, section=target,
                pieces=pieces,
            )
            parts, _ = fetch(own, target)
            attend_outs = [whole] + attend_outs
        outs = call(
            functools.partial(attend_kernel, micro), info,
            [query, x, gains, limit] + parts, attend_outs, out_scratch, section=target,
            pieces=pieces,
        )
        if x_window is None:
            window, *outs = outs
        probs, attended, branch, mixed, ffn_blocks, ffn_in = outs
        gate_up, activated, down, result = call(
            ffn_kernel, info, [ffn_in, mixed, gains],
            [shape((tokens, 2 * hidden), F32), shape((tokens, hidden), BF),
             shape((tokens, model), F32), shape((tokens, model), BF)], ffn_scratch,
            section=target, pieces=pieces,
        )
        saved = dict(
            x=x, gains=gains, pieces=pieces, blocks=blocks, qkv=qkv, query=query, window=window, probs=probs,
            attended=attended, branch=branch, mixed=mixed, ffn_blocks=ffn_blocks, gate_up=gate_up,
            activated=activated, down=down,
        )
        return result, saved

    def back_ffn(upstream, s, target):
        outs = call(
            ffn_back_kernel, info,
            [upstream, s["mixed"], s["down"], s["gate_up"], s["activated"], s["ffn_blocks"],
             s["gains"]],
            [shape((tokens, 2 * hidden + model + quarter + 256), BF)] * shards
            + [shape((tokens, model), F32), shape((8, model), F32)],
            [pltpu.VMEM((tokens, 2 * hidden), BF)] + ffn_scratch,
            section=target, pieces=s["pieces"],
        )
        return outs[:shards], outs[shards], outs[shards + 1]

    def back_attend(grad_mixed, s, target):
        pair = [shape((tokens, 2 * head), F32)] * 3
        outs = call(
            functools.partial(attend_back_kernel, micro), info,
            [grad_mixed, s["branch"], s["window"], s["probs"], s["query"], s["gains"]],
            [shape((tokens, model), BF), shape((tokens, heads_width), F32)] + pair
            + [shape((2, tokens, 2 * head), BF)] * (shards - 1) + [shape((8, model), F32)],
            [pltpu.VMEM((tokens, heads_width), BF)] + out_scratch,
            section=target, pieces=s["pieces"],
        )
        return outs[0], outs[1], outs[2:5], outs[5:8], outs[8]

    def back_window(kept, gives, target, waiting):
        got = [links.across(array, target, 1 + i) for i, array in enumerate(gives)]
        ffn_packs, other = waiting
        if other is not None:
            got, other = tie((got, other))
            other = jnp.where(is_first, other[0], other[1])
            kept, other, ffn_packs = tie((kept, other, ffn_packs))
        own, one, two = call(
            combine_kernel, info, list(kept) + got,
            [shape((tokens, 2 * head), F32)] + [shape((tokens, 2 * head), BF)] * 2,
            section=target,
        )
        one, two = links.along(one, target, -1), links.along(two, target, -2)
        if other is None:
            one, ffn_packs = tie((one, ffn_packs))
        return (own, one, two), ffn_packs, other

    def back_project(window_grads, grad_query, grad_mixed, grad_branch, rows_ffn, rows_attn, s,
                     target):
        outs = call(
            project_back_kernel, info,
            list(window_grads) + [grad_query, s["qkv"], cosine, sine, s["x"], grad_mixed,
            grad_branch, s["attended"], s["blocks"], s["gains"], rows_ffn, rows_attn],
            [shape((tokens + GAIN_ROWS, wide + model + head + 256), BF)] * shards
            + [shape((tokens, model), BF)],
            [pltpu.VMEM((tokens, wide), BF), pltpu.VMEM((shards, GAIN_ROWS, 256), F32)]
            + qkv_scratch,
            section=target, pieces=s["pieces"],
        )
        return outs[:shards], outs[shards]

    def exchange(packs, target):
        return [packs[0]] + [links.across(packs[i], target, i) for i in range(1, shards)]

    total_width = 2 * hidden + 512

    def ffn_weights(packs, target):
        return call(
            functools.partial(ffn_weights_kernel, shard, model), info, list(packs),
            [shape((shard, 2 * hidden), BF), shape((shard, hidden), BF)],
            section=target,
        )

    def attn_weights(packs, ffn, target):
        return call(
            functools.partial(weights_kernel, shard, model), info, list(packs) + list(ffn),
            [shape((shard, total_width), BF)] * 2,
            section=target,
        )

    def backward(upstream, s, target, other=None):
        ffn_packs, grad_mixed, rows_ffn = back_ffn(upstream, s, target)
        grad_branch, grad_query, kept, gives, rows_attn = back_attend(grad_mixed, s, target)
        window_grads, ffn_packs, other = back_window(kept, gives, target, (ffn_packs, other))
        ffn_packs = exchange(ffn_packs, target)
        attn_packs, grad_in = back_project(
            window_grads, grad_query, grad_mixed, grad_branch, rows_ffn, rows_attn, s, target
        )
        return ffn_weights(ffn_packs, target), attn_packs, grad_in, other

    x_first = hidden_in.reshape(tokens, model)
    pieces = gather(folded)
    x_window, pieces[5] = fetch(x_first, 0, pieces[5])
    gains = gain_table(pieces, None)
    result_a, saved_a = forward(x_first, pieces, 0, x_window)
    middle = links.cross(result_a, 0)
    result_b, saved_b = forward(middle, pieces, 1)

    ffn, attn_packs, grad_b, _ = backward(cotangent.reshape(tokens, model), saved_b, 1)
    upstream = links.cross(grad_b, 1)
    upstream, attn_packs = tie((upstream, attn_packs))
    b_first, b_second = attn_weights(exchange(attn_packs, 1), ffn, 1)
    upstream, b_first, b_second = tie((upstream, b_first, b_second))
    halves_b = (links.cross(b_first, 1), b_second)

    ffn, attn_packs, grad_a, half_b = backward(upstream, saved_a, 0, halves_b)
    part_b = lax.psum(half_b, "seq")
    a_first, a_second = attn_weights(exchange(attn_packs, 0), ffn, 0)
    a_second, part_b = tie((a_second, part_b))
    part_a = lax.psum(jnp.where(is_first, a_first, links.cross(a_second, 0)), "seq")
    theirs = links.swap(jnp.where(is_first, part_b, part_a))

    part = head // shards
    grads = call(
        finish_kernel, info, [part_a, part_b, theirs],
        [shape((1, shard, heads_width), F32), shape((1, shard, head), F32),
         shape((1, shard, head), F32), shape((1, head, model), F32),
         shape((1, shard, hidden), F32), shape((1, shard, hidden), F32),
         shape((1, quarter, model), F32)]
        + [shape((1, shard), F32)] * 4 + [shape((1, part), F32)] * 2,
    )
    g_query, g_key, g_value, g_out, g_gate, g_up, g_down = grads[:7]
    g_attn, g_post_attn, g_ffn, g_post_ffn, g_query_gain, g_key_gain = grads[7:]
    section_outputs = jnp.where(is_first, result_a, result_b).reshape(1, micro, rows, model)
    input_grads = jnp.where(is_first, grad_a, grad_b).reshape(1, micro, rows, model)
    return (
        section_outputs, input_grads, g_attn, g_query, g_key, g_value, g_query_gain, g_key_gain,
        g_out, g_post_attn, g_ffn, g_gate, g_up, g_down, g_post_ffn,
    )


def solution(mesh):
    rows = P(None, ("seq", "fsdp"), None)
    vector, matrix = P("section", "fsdp"), P("section", "fsdp", None)
    weights = (vector, matrix, matrix, matrix, vector, vector, matrix, vector, vector, matrix,
               matrix, matrix, vector)
    out_rows = P("section", None, ("seq", "fsdp"), None)
    return jax.shard_map(
        functools.partial(body, dict(mesh.shape)),
        mesh=mesh,
        in_specs=(rows, rows, P(None, ("seq", "fsdp"))) + weights,
        out_specs=(out_rows, out_rows) + weights,
        check_vma=False,
    )
```
